32 devices in a mesh: mod: 2 (over x), dp: 16 (over z, y, core).
Axes of the slice: x: 2, y: 2, z: 4, core: 2. Of those that a mesh axis runs over, the one named last changes fastest.
Arguments:
- stream_in: float32 [2, 16, 577, 768], P('mod', 'dp'), may hold values from -6 to 6
- cotangent: float32 [2, 16, 577, 768], P('mod', 'dp'), may hold values from -6 to 6
- patch_count: int32 [16], P('dp'), may hold values from 197 to 577, as said below
- pos_index: int32 [16, 577], P('dp'), may hold values from 0 to 576, as said below
- attn_blocks: float32 [256, 96, 96], P(('mod', 'dp'))
- attn_left: float32 [256, 96, 96], P(('mod', 'dp')), as said below
- attn_right: float32 [256, 96, 96], P(('mod', 'dp')), as said below
- ffn_blocks: float32 [2, 512, 96, 96], P('mod', 'dp')
- ffn_left: float32 [2, 512, 96, 96], P('mod', 'dp'), as said below
- ffn_right: float32 [2, 512, 96, 96], P('mod', 'dp'), as said below
- vectors: float32 [13, 768], replicated
- vectors_mom: float32 [13, 768], replicated, may hold values from -28 to 28
- ffn_bias: float32 [2, 3072], replicated, may hold values from -4 to 4
- ffn_bias_mom: float32 [2, 3072], replicated, may hold values from -16 to 16
- pos_table: float32 [577, 768], replicated, may hold values from -6 to 6
- pos_mom: float32 [577, 768], replicated, may hold values from -4 to 4
Outputs:
- stream_out: float32 [2, 16, 577, 768], P('mod', 'dp')
- stream_grad: float32 [2, 16, 577, 768], P('mod', 'dp')
- attn_grad: float32 [256, 96, 96], P(('mod', 'dp'))
- attn_left_new: float32 [256, 96, 96], P(('mod', 'dp'))
- attn_right_new: float32 [256, 96, 96], P(('mod', 'dp'))
- attn_new: float32 [256, 96, 96], P(('mod', 'dp'))
- ffn_grad: float32 [2, 512, 96, 96], P('mod', 'dp')
- ffn_left_new: float32 [2, 512, 96, 96], P('mod', 'dp')
- ffn_right_new: float32 [2, 512, 96, 96], P('mod', 'dp')
- ffn_new: float32 [2, 512, 96, 96], P('mod', 'dp')
- vectors_mom_new: float32 [13, 768], replicated
- vectors_new: float32 [13, 768], replicated
- ffn_bias_mom_new: float32 [2, 3072], replicated
- ffn_bias_new: float32 [2, 3072], replicated
- pos_mom_new: float32 [577, 768], replicated
- pos_new: float32 [577, 768], replicated
The draws below stay inside these ranges and needn't reach their ends.
Inputs may be any that keep to these rules, and one draw needn't show every extreme that they name: `patch_count`: each item holds 197 or 577 image patches; both numbers occur in every draw. `pos_index`: an item of 577 patches has slot s at row s; for an item of 197 patches slot 0 is at row 0 and the patch in row i, column j of its 14 x 14 grid at row 1 + 24 * a + b, with a = (i * 23 + 13 // 2) // 13 and b likewise of j; unused slots hold 0. `attn_left`: every block is symmetric positive definite. `attn_right`: every block is symmetric positive definite. `ffn_left`: every block is symmetric positive definite. `ffn_right`: every block is symmetric positive definite.
All inputs are finite; a program needn't handle non-finite values.
Results may differ from the reference program's by a relative error of at most 0.011.
The reference program's roundings to bfloat16 on the way count: a program that leaves them out, or rounds other values in their place, can miss the bound.
Values may be sent and summed in bfloat16 or wider, within the bound.
No kernel may reach another device: no remote copies, remote signals or barrier semaphores. Data moves between devices by JAX's collectives and lax.ppermute only.
A program may use at most 256 MiB of HBM per device.

```python
import math
import jax
import jax.numpy as jnp
from jax import lax

D = 768
HEADS = 12
HDIM = 64
FF = 3072
GRID = 24
SMALL_GRID = 14
TEXT = 64
BLOCK = 96
NEWTON = 6
SLOTS = 577
SMALL = 197
MONO = 513
ITEMS = 16
ATT_BLOCKS = 256
FFN_BLOCKS = 512


def item_sizes(key):
    key_pick, key_big, key_small = jax.random.split(key, 3)
    chosen = jax.random.randint(key_pick, (ITEMS,), 0, 2)
    big_item = jax.random.randint(key_big, (), 0, ITEMS)
    offset = jax.random.randint(key_small, (), 1, ITEMS)
    small_item = (big_item + offset) % ITEMS
    item_ids = jnp.arange(ITEMS)
    chosen = jnp.where(item_ids == big_item, 1, chosen)
    chosen = jnp.where(item_ids == small_item, 0, chosen)
    return jnp.where(chosen == 1, SLOTS, SMALL).astype(jnp.int32)


def draw_patch_count(key, part):
    return item_sizes(key)


def draw_pos_index(key, part):
    counts = item_sizes(key)
    slot_ids = jnp.arange(SLOTS, dtype=jnp.int32)
    patch_ids = jnp.maximum(slot_ids - 1, 0)
    row_small = patch_ids // SMALL_GRID
    col_small = patch_ids % SMALL_GRID
    rounding = (SMALL_GRID - 1) // 2
    row_big = (row_small * (GRID - 1) + rounding) // (SMALL_GRID - 1)
    col_big = (col_small * (GRID - 1) + rounding) // (SMALL_GRID - 1)
    mapped = jnp.where(slot_ids == 0, 0, 1 + row_big * GRID + col_big)
    mapped = jnp.where(slot_ids < SMALL, mapped, 0)
    full_items = counts[:, None] == SLOTS
    return jnp.where(full_items, slot_ids[None, :], mapped[None, :]).astype(jnp.int32)


def block_stats(key, block_scales):
    key_diag, key_off = jax.random.split(key)
    count = block_scales.shape[0]
    diagonal = jnp.exp(jax.random.uniform(key_diag, (count, BLOCK), jnp.float32, 0.0, math.log(4.0)))
    noise = jax.random.uniform(key_off, (count, BLOCK, BLOCK), jnp.float32, -0.5, 0.5)
    symmetric = (noise + jnp.swapaxes(noise, 1, 2)) * (0.5 / BLOCK)
    identity = jnp.eye(BLOCK, dtype=jnp.float32)
    stats = symmetric * (1.0 - identity) + identity * diagonal[:, :, None]
    return stats * (BLOCK * block_scales)[:, None, None]


def ffn_scales():
    half_count = FFN_BLOCKS // 2
    per_block = jnp.where(jnp.arange(FFN_BLOCKS) < half_count, 0.1, 0.3) * (ITEMS * SLOTS)
    return jnp.tile(per_block.astype(jnp.float32), 2)


def draw_attn_left(key, part):
    key = jax.random.fold_in(key, 11)
    return block_stats(key, jnp.full((ATT_BLOCKS,), 0.4 * ITEMS * SLOTS, jnp.float32))


def draw_attn_right(key, part):
    key = jax.random.fold_in(key, 12)
    return block_stats(key, jnp.full((ATT_BLOCKS,), 0.4 * ITEMS * SLOTS, jnp.float32))


def draw_ffn_left(key, part):
    key = jax.random.fold_in(key, 13)
    return block_stats(key, ffn_scales()).reshape(2, FFN_BLOCKS, BLOCK, BLOCK)


def draw_ffn_right(key, part):
    key = jax.random.fold_in(key, 14)
    return block_stats(key, ffn_scales()).reshape(2, FFN_BLOCKS, BLOCK, BLOCK)


def draw_attn_blocks(key, part):
    key = jax.random.fold_in(key, 21)
    per_matrix = ATT_BLOCKS // 4
    scales = jnp.array([2.0 * D ** (-0.5), D ** (-0.5), D ** (-0.5), (D // 8) ** (-0.5)], jnp.float32)
    block_scale = jnp.repeat(scales, per_matrix)
    return jax.random.normal(key, (ATT_BLOCKS, BLOCK, BLOCK), jnp.float32) * block_scale[:, None, None]


def draw_ffn_blocks(key, part):
    key = jax.random.fold_in(key, 22)
    half_count = FFN_BLOCKS // 2
    block_scale = jnp.where(jnp.arange(FFN_BLOCKS) < half_count, D ** (-0.5), FF ** (-0.5)).astype(jnp.float32)
    return jax.random.normal(key, (2, FFN_BLOCKS, BLOCK, BLOCK), jnp.float32) * block_scale[None, :, None, None]


def draw_vectors(key, part):
    key = jax.random.fold_in(key, 23)
    key_gain, key_bias = jax.random.split(key)
    gains = jax.random.uniform(key_gain, (13, D), jnp.float32, 0.5, 1.5)
    biases = 0.3 * jax.random.normal(key_bias, (13, D), jnp.float32)
    gain_rows = jnp.array([0, 0, 0, 1, 0, 1, 0, 0, 1, 0, 1, 0, 0], jnp.int32) == 1
    return jnp.where(gain_rows[:, None], gains, biases)


def block_levels(own_key, extent, cuts, least, high):
    level, own = 1.0, jax.random.fold_in(own_key, 6)
    for axis_at, parts in cuts:
        heights = jnp.exp(jax.random.uniform(jax.random.fold_in(own, axis_at), (parts,), jnp.float32, least / len(cuts), high / len(cuts)))
        level = level * jnp.repeat(heights, extent[axis_at] // parts).reshape([-1 if axis == axis_at else 1 for axis in range(len(extent))])
    return level


def gaussian(key, extent, width, limit, cuts=(), held_as=jnp.bfloat16):
    factor_of = block_levels(key, extent, cuts, -0.22, 0.18) if cuts else 1.0
    drawn = jax.random.normal(key, extent, jnp.float32) * width * factor_of
    return jnp.minimum(jnp.maximum(drawn, -limit), limit).astype(held_as)


def setup_inputs(seed: int = 0) -> dict:
    key_list = jax.random.split(jax.random.key(seed), 17)
    return {
        "stream_in": gaussian(key_list[0], (2, ITEMS, SLOTS, D), 1.0, 6.0, ((0, 2), (1, 16)), jnp.float32),
        "cotangent": gaussian(key_list[1], (2, ITEMS, SLOTS, D), 1.0, 6.0, ((0, 2), (1, 16)), jnp.float32),
        "patch_count": draw_patch_count(jax.random.fold_in(key_list[16], 71), 0),
        "pos_index": draw_pos_index(jax.random.fold_in(key_list[16], 71), 0),
        "attn_blocks": draw_attn_blocks(jax.random.fold_in(key_list[16], 71), 0),
        "attn_left": draw_attn_left(jax.random.fold_in(key_list[16], 71), 0),
        "attn_right": draw_attn_right(jax.random.fold_in(key_list[16], 71), 0),
        "ffn_blocks": draw_ffn_blocks(jax.random.fold_in(key_list[16], 71), 0),
        "ffn_left": draw_ffn_left(jax.random.fold_in(key_list[16], 71), 0),
        "ffn_right": draw_ffn_right(jax.random.fold_in(key_list[16], 71), 0),
        "vectors": draw_vectors(jax.random.fold_in(key_list[16], 71), 0),
        "vectors_mom": gaussian(key_list[11], (13, D), (0.05 * (ITEMS * SLOTS) ** 0.5), 28.0, (), jnp.float32),
        "ffn_bias": gaussian(key_list[12], (2, FF), 0.3, 4.0, (), jnp.float32),
        "ffn_bias_mom": gaussian(key_list[13], (2, FF), (0.03 * (ITEMS * SLOTS) ** 0.5), 16.0, (), jnp.float32),
        "pos_table": gaussian(key_list[14], (SLOTS, D), 0.5, 6.0, (), jnp.float32),
        "pos_mom": gaussian(key_list[15], (SLOTS, D), (0.07 * ITEMS ** 0.5), 4.0, (), jnp.float32),
    }


HIGHEST = lax.Precision.HIGHEST
norm_eps = 1e-05
stat_decay = 0.5
matrix_rate = 0.25
moment_keep = 0.9

@jax.custom_vjp
def low(v):
    return lax.optimization_barrier(v.astype(jnp.bfloat16)).astype(jnp.float32)

@jax.custom_vjp
def low_back(v):
    return v

def low_keep(v):
    return (low(v), None)

def low_pass(kept, grad):
    return (grad,)

def back_keep(v):
    return (v, None)

def back_low(kept, grad):
    return (low(grad),)
low.defvjp(low_keep, low_pass)
low_back.defvjp(back_keep, back_low)

def blocks_to_matrix(blocks, row_blocks, col_blocks):
    block_size = blocks.shape[-1]
    leading = blocks.shape[:-3]
    shaped = blocks.reshape(leading + (row_blocks, col_blocks, block_size, block_size))
    moved = jnp.swapaxes(shaped, -3, -2)
    return moved.reshape(leading + (row_blocks * block_size, col_blocks * block_size))

def matrix_to_blocks(matrix, block_size):
    leading = matrix.shape[:-2]
    row_blocks = matrix.shape[-2] // block_size
    col_blocks = matrix.shape[-1] // block_size
    shaped = matrix.reshape(leading + (row_blocks, block_size, col_blocks, block_size))
    moved = jnp.swapaxes(shaped, -3, -2)
    return moved.reshape(leading + (row_blocks * col_blocks, block_size, block_size))

def layer_norm(values, norm_gain, norm_bias):
    row_mean = lax.optimization_barrier(jnp.mean(values, axis=-1, keepdims=True))
    centred = values - row_mean
    spread = lax.optimization_barrier(jnp.mean(centred * centred, axis=-1, keepdims=True))
    return centred * lax.rsqrt(spread + norm_eps) * norm_gain + norm_bias

def attend(queries, key_rows, value_rows, key_mask):
    query_heads = queries.reshape(queries.shape[0], HEADS, HDIM)
    key_heads = key_rows.reshape(key_rows.shape[0], HEADS, HDIM)
    value_heads = value_rows.reshape(value_rows.shape[0], HEADS, HDIM)
    scores = low_back(jnp.einsum('qhd,khd->hqk', query_heads, key_heads, precision=HIGHEST) * HDIM ** (-0.5))
    scores = jnp.where(key_mask[None, None, :], scores, -jnp.inf)
    attn_probs = low(jax.nn.softmax(scores, axis=-1))
    context = jnp.einsum('hqk,khd->qhd', attn_probs, value_heads, precision=HIGHEST)
    return low(low_back(context.reshape(queries.shape[0], D)))

def item_forward(params, image_rows, text_rows, patch_total, item_pos):
    attn_mats, up_mats, down_mats, vectors, ffn_bias, pos_table = params
    low_attn = low(attn_mats)
    image_valid = jnp.arange(SLOTS) < patch_total
    image_hidden = image_rows + pos_table[item_pos]

    def project(hidden, row_base):
        normed = low(layer_norm(hidden, vectors[row_base], vectors[row_base + 1]))
        queries = low(low_back(jnp.dot(normed, low_attn[0], precision=HIGHEST) + vectors[0]))
        key_rows = low(low_back(jnp.dot(normed, low_attn[1], precision=HIGHEST)))
        value_rows = low(low_back(jnp.dot(normed, low_attn[2], precision=HIGHEST) + vectors[1]))
        return (queries, key_rows, value_rows)
    image_q, image_k, image_v = project(image_hidden, 3)
    text_q, text_k, text_v = project(text_rows, 8)
    joint_mask = jnp.concatenate([image_valid, jnp.ones((TEXT,), jnp.bool_)])
    joint_context = attend(jnp.concatenate([image_q, text_q[:TEXT]]), jnp.concatenate([image_k, text_k[:TEXT]]), jnp.concatenate([image_v, text_v[:TEXT]]), joint_mask)
    mono_context = attend(text_q[TEXT:], text_k[TEXT:], text_v[TEXT:], jnp.ones((MONO,), jnp.bool_))
    image_context = joint_context[:SLOTS]
    text_context = jnp.concatenate([joint_context[SLOTS:], mono_context])

    def finish(hidden, context, modality):
        row_base = 3 + 5 * modality
        attn_out = low_back(jnp.dot(context, low_attn[3], precision=HIGHEST) + vectors[2])
        middle = hidden + attn_out
        normed = low(layer_norm(middle, vectors[row_base + 2], vectors[row_base + 3]))
        pre_act = low_back(jnp.dot(normed, low(up_mats[modality]), precision=HIGHEST) + ffn_bias[modality])
        activated = low(jax.nn.gelu(pre_act, approximate=False))
        branch = low_back(jnp.dot(activated, low(down_mats[modality]), precision=HIGHEST) + vectors[row_base + 4])
        return middle + branch
    image_out = jnp.where(image_valid[:, None], finish(image_hidden, image_context, 0), 0.0)
    text_out = finish(text_rows, text_context, 1)
    return (image_out, text_out)

def inverse_root(stats):
    identity = jnp.eye(stats.shape[-1], dtype=stats.dtype)
    norm_value = jnp.sqrt(lax.optimization_barrier(jnp.sum(stats * stats, axis=(-2, -1), keepdims=True)))
    matrix = stats / norm_value
    factor = identity * norm_value ** (-0.25)
    for iteration in range(NEWTON):
        step_mat = (5.0 * identity - matrix) * 0.25
        square = jnp.einsum('bij,bjk->bik', step_mat, step_mat, precision=HIGHEST)
        factor = jnp.einsum('bij,bjk->bik', factor, step_mat, precision=HIGHEST)
        fourth = jnp.einsum('bij,bjk->bik', square, square, precision=HIGHEST)
        matrix = jnp.einsum('bij,bjk->bik', fourth, matrix, precision=HIGHEST)
    return factor

def shampoo_update(grads, lefts, rights, weights):
    left_new = stat_decay * lefts + (1.0 - stat_decay) * jnp.einsum('bij,bkj->bik', grads, grads, precision=HIGHEST)
    right_new = stat_decay * rights + (1.0 - stat_decay) * jnp.einsum('bji,bjk->bik', grads, grads, precision=HIGHEST)
    left_root = inverse_root(left_new)
    right_root = inverse_root(right_new)
    update = jnp.einsum('bij,bjk->bik', jnp.einsum('bij,bjk->bik', left_root, grads, precision=HIGHEST), right_root, precision=HIGHEST)
    return (left_new, right_new, weights - matrix_rate * update)

def reference(stream_in, cotangent, patch_count, pos_index, attn_blocks, attn_left, attn_right, ffn_blocks, ffn_left, ffn_right, vectors, vectors_mom, ffn_bias, ffn_bias_mom, pos_table, pos_mom):
    row_blocks = D // BLOCK
    col_blocks = FF // BLOCK
    split_at = row_blocks * col_blocks
    attn_mats = blocks_to_matrix(attn_blocks.reshape(4, row_blocks * row_blocks, BLOCK, BLOCK), row_blocks, row_blocks)
    up_mats = blocks_to_matrix(ffn_blocks[:, :split_at], row_blocks, col_blocks)
    down_mats = blocks_to_matrix(ffn_blocks[:, split_at:], col_blocks, row_blocks)
    params = (attn_mats, up_mats, down_mats, vectors, ffn_bias, pos_table)

    def one_item(totals, item):
        image_rows, text_rows, image_cot, text_cot, patch_total, item_pos = item

        def forward(params_now, image_now, text_now):
            return item_forward(params_now, image_now, text_now, patch_total, item_pos)
        outputs, pullback = jax.vjp(forward, params, image_rows, text_rows)
        param_grads, image_grad, text_grad = pullback((image_cot, text_cot))
        return (jax.tree.map(jnp.add, totals, param_grads), (outputs[0], outputs[1], image_grad, text_grad))
    totals, per_item = lax.scan(one_item, jax.tree.map(jnp.zeros_like, params), (stream_in[0], stream_in[1], cotangent[0], cotangent[1], patch_count, pos_index))
    stream_out = jnp.stack([per_item[0], per_item[1]])
    stream_grad = jnp.stack([per_item[2], per_item[3]])
    attn_grad = matrix_to_blocks(totals[0], BLOCK).reshape(ATT_BLOCKS, BLOCK, BLOCK)
    ffn_grad = jnp.concatenate([matrix_to_blocks(totals[1], BLOCK), matrix_to_blocks(totals[2], BLOCK)], axis=1)
    attn_left_new, attn_right_new, attn_new = shampoo_update(attn_grad, attn_left, attn_right, attn_blocks)
    flat_shape = (-1, BLOCK, BLOCK)
    ffn_left_flat, ffn_right_flat, ffn_new_flat = shampoo_update(ffn_grad.reshape(flat_shape), ffn_left.reshape(flat_shape), ffn_right.reshape(flat_shape), ffn_blocks.reshape(flat_shape))
    vector_rate = 0.3 / math.sqrt(ITEMS * SLOTS)
    pos_rate = 0.5 / math.sqrt(ITEMS)
    vectors_mom_new = moment_keep * vectors_mom + totals[3]
    vectors_new = vectors - vector_rate * vectors_mom_new
    ffn_bias_mom_new = moment_keep * ffn_bias_mom + totals[4]
    ffn_bias_new = ffn_bias - vector_rate * ffn_bias_mom_new
    pos_mom_new = moment_keep * pos_mom + totals[5]
    pos_new = pos_table - pos_rate * pos_mom_new
    return (stream_out, stream_grad, attn_grad, attn_left_new, attn_right_new, attn_new, ffn_grad, ffn_left_flat.reshape(ffn_blocks.shape), ffn_right_flat.reshape(ffn_blocks.shape), ffn_new_flat.reshape(ffn_blocks.shape), vectors_mom_new, vectors_new, ffn_bias_mom_new, ffn_bias_new, pos_mom_new, pos_new)
```

```python
import functools
import math

import jax
import jax.numpy as jnp
from jax import lax
from jax.experimental import pallas as pl
from jax.experimental.pallas import tpu as pltpu
from jax.sharding import PartitionSpec as P

HEADS = 12
TEXT = 64
NEWTON = 6
PAIR_LANES = 128
QUERY_TILE = 256
VMEM_LIMIT = 56 << 20

f32 = jnp.float32
bf16 = jnp.bfloat16
norm_eps = 1e-05
stat_decay = 0.5
matrix_rate = 0.25
moment_keep = 0.9
masked_score = -1e30


def dot_nn(left, right):
    return lax.dot_general(left, right, (((1,), (0,)), ((), ())), preferred_element_type=f32)


def dot_nt(left, right):
    return lax.dot_general(left, right, (((1,), (1,)), ((), ())), preferred_element_type=f32)


def dot_tn(left, right):
    return lax.dot_general(left, right, (((0,), (0,)), ((), ())), preferred_element_type=f32)


def params(**kwargs):
    return pltpu.CompilerParams(vmem_limit_bytes=VMEM_LIMIT, **kwargs)


def round_up(value, step):
    return (value + step - 1) // step * step


def whole(shape):
    return pl.BlockSpec(shape, lambda *ids: (0,) * len(shape))


SMEM_SPEC = pl.BlockSpec(memory_space=pltpu.SMEM)


def pack_kernel(blocks_ref, out_ref):
    count = blocks_ref.shape[0]
    pieces = [blocks_ref[i] for i in range(count)]
    out_ref[0] = jnp.concatenate(pieces, axis=1).astype(bf16)


def pack_rows(blocks, per_row):
    count, size, _ = blocks.shape
    return pl.pallas_call(
        pack_kernel,
        grid=(count // per_row,),
        in_specs=[pl.BlockSpec((per_row, size, size), lambda i: (i, 0, 0))],
        out_specs=pl.BlockSpec((1, size, per_row * size), lambda i: (i, 0, 0)),
        out_shape=jax.ShapeDtypeStruct((count // per_row, size, per_row * size), bf16),
        compiler_params=params(),
        name="pack_rows",
    )(blocks)


def norm_rows(values):
    centred = values - jnp.mean(values, axis=-1, keepdims=True)
    spread = jnp.mean(centred * centred, axis=-1, keepdims=True)
    inv_std = lax.rsqrt(spread + norm_eps)
    return centred * inv_std, inv_std


def norm_input_grad(grad_out, normal, inv_std, gain):
    grad_norm = grad_out * gain
    mean_grad = jnp.mean(grad_norm, axis=-1, keepdims=True)
    mean_proj = jnp.mean(grad_norm * normal, axis=-1, keepdims=True)
    return inv_std * (grad_norm - mean_grad - normal * mean_proj)


def project_kernel(row_ref, hidden_ref, vec_ref, w_ref, qkv_ref, first_ref):
    step = pl.program_id(0)

    @pl.when(step == 0)
    def _():
        normal, _ = norm_rows(hidden_ref[...])
        first_ref[...] = (normal * vec_ref[0:1, :] + vec_ref[1:2, :]).astype(bf16)

    rows = hidden_ref.shape[0]
    bias = jnp.where(step == 0, vec_ref[5:6, :], jnp.where(step == 2, vec_ref[6:7, :], 0.0))
    out = (dot_nn(first_ref[...], w_ref[0]) + bias).astype(bf16)
    qkv_ref[...] = jnp.zeros(qkv_ref.shape, bf16)
    qkv_ref[pl.ds(pl.multiple_of(row_ref[0], 16), rows), :] = out


def project(rows_info, hidden, vec, attn_mats, seq):
    rows, width = hidden.shape
    return pl.pallas_call(
        project_kernel,
        grid=(3,),
        in_specs=[
            SMEM_SPEC,
            whole((rows, width)),
            whole(vec.shape),
            pl.BlockSpec((1, width, width), lambda i: (i, 0, 0)),
        ],
        out_specs=[pl.BlockSpec((seq, width), lambda i: (0, i)), whole((rows, width))],
        out_shape=[
            jax.ShapeDtypeStruct((seq, 3 * width), bf16),
            jax.ShapeDtypeStruct((rows, width), bf16),
        ],
        compiler_params=params(),
        name="project",
    )(rows_info, hidden, vec, attn_mats)


def key_bias(row_ref, seq):
    rows = lax.broadcasted_iota(jnp.int32, (seq, 1), 0)
    counts = jnp.logical_and(rows >= row_ref[1], rows < row_ref[2])
    return jnp.where(counts, 0.0, masked_score).astype(f32)


def transposed(values):
    return jnp.transpose(values.astype(f32), (1, 0)).astype(bf16)


def attend_kernel(row_ref, q_ref, k_ref, v_ref, ctx_ref, lse_ref):
    seq = q_ref.shape[0]
    half = PAIR_LANES // 2
    scale = half ** (-0.5)
    bias = key_bias(row_ref, seq)
    keys = k_ref[...]
    values_t = transposed(v_ref[...])
    for start in range(0, seq, QUERY_TILE):
        size = min(QUERY_TILE, seq - start)
        tile = slice(start, start + size)
        queries = q_ref[tile, :]
        lane = lax.broadcasted_iota(jnp.int32, (size, PAIR_LANES), 1)
        parts = []
        for head in range(2):
            own = (lane < half) == (head == 0)
            scores = dot_nt(keys, jnp.where(own, queries, jnp.zeros_like(queries))) * scale + bias
            top = jnp.max(scores, axis=0, keepdims=True)
            raised = jnp.exp(scores - top)
            total = jnp.sum(raised, axis=0, keepdims=True)
            probs = (raised * (1.0 / total)).astype(bf16)
            parts.append(dot_nn(values_t[half * head : half * (head + 1), :], probs))
            lse_ref[0, head : head + 1, tile] = top + jnp.log(total)
        ctx_ref[tile, :] = jnp.transpose(jnp.concatenate(parts, axis=0), (1, 0)).astype(bf16)


def attend(rows_info, qkv):
    seq = qkv.shape[0]
    width = qkv.shape[1] // 3
    pairs = width // PAIR_LANES

    def column(base):
        return pl.BlockSpec((seq, PAIR_LANES), lambda i, base=base: (0, base + i))

    return pl.pallas_call(
        attend_kernel,
        grid=(pairs,),
        in_specs=[SMEM_SPEC, column(0), column(pairs), column(2 * pairs)],
        out_specs=[column(0), pl.BlockSpec((1, 8, seq), lambda i: (i, 0, 0))],
        out_shape=[
            jax.ShapeDtypeStruct((seq, width), bf16),
            jax.ShapeDtypeStruct((pairs, 8, seq), f32),
        ],
        compiler_params=params(),
        name="attend",
    )(rows_info, qkv, qkv, qkv)


def attend_grad_kernel(row_ref, q_ref, k_ref, v_ref, g_ref, lse_ref, out_ref, dk_ref, dv_ref):
    seq = q_ref.shape[0]
    half = PAIR_LANES // 2
    scale = half ** (-0.5)
    bias = key_bias(row_ref, seq)
    keys = k_ref[...]
    values = v_ref[...]
    keys_t = transposed(keys)
    for start in range(0, seq, QUERY_TILE):
        size = min(QUERY_TILE, seq - start)
        tile = slice(start, start + size)
        queries = q_ref[tile, :]
        row = lax.broadcasted_iota(jnp.int32, (size, 1), 0) + start
        counts = jnp.logical_and(row >= row_ref[1], row < row_ref[2])
        grads = jnp.where(counts, g_ref[tile, :], jnp.zeros((size, PAIR_LANES), bf16))
        lane = lax.broadcasted_iota(jnp.int32, (size, PAIR_LANES), 1)
        parts = []
        for head in range(2):
            own = (lane < half) == (head == 0)
            own_q = jnp.where(own, queries, jnp.zeros_like(queries))
            own_g = jnp.where(own, grads, jnp.zeros_like(grads))
            scores = dot_nt(keys, own_q) * scale + bias
            probs = jnp.exp(scores - lse_ref[0, head : head + 1, tile])
            grad_probs = dot_nt(values, own_g)
            row_dot = jnp.sum(probs * grad_probs, axis=0, keepdims=True)
            grad_scores = (probs * (grad_probs - row_dot)).astype(bf16)
            grad_v = dot_nn(probs.astype(bf16), own_g)
            grad_k = dot_nn(grad_scores, own_q)
            if start == 0 and head == 0:
                dv_ref[...] = grad_v
                dk_ref[...] = grad_k
            else:
                dv_ref[...] += grad_v
                dk_ref[...] += grad_k
            parts.append(dot_nn(keys_t[half * head : half * (head + 1), :], grad_scores))
        grad_q = jnp.transpose(jnp.concatenate(parts, axis=0) * scale, (1, 0))
        out_ref[0, tile, :] = grad_q.astype(bf16)
    out_ref[1] = (dk_ref[...] * scale).astype(bf16)
    out_ref[2] = dv_ref[...].astype(bf16)


def attend_grad(rows_info, qkv, grad_ctx, lse):
    seq = qkv.shape[0]
    width = qkv.shape[1] // 3
    pairs = width // PAIR_LANES

    def column(base):
        return pl.BlockSpec((seq, PAIR_LANES), lambda i, base=base: (0, base + i))

    return pl.pallas_call(
        attend_grad_kernel,
        grid=(pairs,),
        in_specs=[
            SMEM_SPEC,
            column(0),
            column(pairs),
            column(2 * pairs),
            column(0),
            pl.BlockSpec((1, 8, seq), lambda i: (i, 0, 0)),
        ],
        out_specs=pl.BlockSpec((3, seq, PAIR_LANES), lambda i: (0, 0, i)),
        out_shape=jax.ShapeDtypeStruct((3, seq, width), bf16),
        scratch_shapes=[pltpu.VMEM((seq, PAIR_LANES), f32)] * 2,
        compiler_params=params(),
        name="attend_grad",
    )(rows_info, qkv, qkv, qkv, grad_ctx, lse)


def gelu_pair(values):
    size = jnp.abs(values)
    tail = 1.0 / (1.0 + (0.3275911 * 0.5**0.5) * size)
    poly = tail * (
        0.254829592
        + tail * (-0.284496736 + tail * (1.421413741 + tail * (-1.453152027 + tail * 1.061405429)))
    )
    bell = jnp.exp(-0.5 * values * values)
    upper = 0.5 * poly * bell
    share = jnp.where(values >= 0.0, 1.0 - upper, upper)
    return values * share, share + values * bell * ((2.0 * math.pi) ** -0.5)


def expert_kernel(
    row_ref,
    ctx_ref,
    pair_ref,
    hidden_ref,
    cot_ref,
    vec_ref,
    upb_ref,
    wo_ref,
    up_ref,
    down_ref,
    out_ref,
    gmid_ref,
    gctx_ref,
    dwo_ref,
    dup_ref,
    ddown_ref,
    dvec_ref,
    dupb_ref,
    own_ctx,
    middle,
    second,
    gres,
    gbranch,
    pre,
    gact,
    act,
    gpre,
    branch,
    gsecond,
):
    step = pl.program_id(0)
    last = pl.num_programs(0) - 1
    rows = hidden_ref.shape[0]
    width = hidden_ref.shape[1]
    out_rows = out_ref.shape[0]
    offset = pl.multiple_of(row_ref[0], 16)
    tile = 16
    tiles = rows // tile

    def tile_slice(i):
        return pl.ds(pl.multiple_of(i * tile, tile), tile)

    @pl.when(step == 0)
    def _():
        own_ctx[...] = ctx_ref[pl.ds(offset, rows), :]

        @pl.when(row_ref[3] == 1)
        def _():
            own_ctx[0 : pair_ref.shape[0], :] = pair_ref[...]

        middle[...] = dot_nn(own_ctx[...], wo_ref[...])

        def body(i, total):
            at = tile_slice(i)
            mid = hidden_ref[at, :] + (middle[at, :] + vec_ref[7:8, :])
            middle[at, :] = mid
            normal, _ = norm_rows(mid)
            second[at, :] = (normal * vec_ref[2:3, :] + vec_ref[3:4, :]).astype(bf16)
            row = lax.broadcasted_iota(jnp.int32, (tile, 1), 0) + i * tile
            kept = jnp.where(row < row_ref[4], cot_ref[at, :], 0.0)
            rounded = kept.astype(bf16)
            gbranch[at, :] = rounded
            return total + rounded.astype(f32)

        total = lax.fori_loop(0, tiles, body, jnp.zeros((tile, width), f32))
        dvec_ref[2:3, :] = jnp.sum(total, axis=0, keepdims=True)

    up = up_ref[...].reshape(width, up_ref.shape[3])
    down = down_ref[...]
    pre[...] = dot_nn(second[...], up)
    gact[...] = dot_nt(gbranch[...], down)

    def gelu_body(i, total):
        at = tile_slice(i)
        value, slope = gelu_pair(pre[at, :] + upb_ref[...])
        act[at, :] = value.astype(bf16)
        rounded = (gact[at, :] * slope).astype(bf16)
        gpre[at, :] = rounded
        return total + rounded.astype(f32)

    total = lax.fori_loop(0, tiles, gelu_body, jnp.zeros((tile, act.shape[1]), f32))
    dupb_ref[...] = jnp.sum(total, axis=0, keepdims=True)
    ddown_ref[...] = dot_tn(act[...], gbranch[...]).astype(bf16)
    dup_ref[...] = dot_tn(second[...], gpre[...]).astype(bf16).reshape(dup_ref.shape)
    own_branch = dot_nn(act[...], down)
    own_gsecond = dot_nt(gpre[...], up)

    @pl.when(step == 0)
    def _():
        branch[...] = own_branch
        gsecond[...] = own_gsecond

    @pl.when(step > 0)
    def _():
        branch[...] += own_branch
        gsecond[...] += own_gsecond

    @pl.when(step == last)
    def _():
        def body(i, totals):
            at = tile_slice(i)
            mid = middle[at, :]
            normal, inv_std = norm_rows(mid)
            grad_out = gsecond[at, :]
            row = lax.broadcasted_iota(jnp.int32, (tile, 1), 0) + i * tile
            kept = row < row_ref[4]
            branch[at, :] = jnp.where(kept, mid + (branch[at, :] + vec_ref[4:5, :]), 0.0)
            grad_in = norm_input_grad(grad_out, normal, inv_std, vec_ref[2:3, :])
            grad_mid = jnp.where(kept, cot_ref[at, :], 0.0) + grad_in
            gmid_ref[at, :] = grad_mid
            rounded = grad_mid.astype(bf16)
            gbranch[at, :] = rounded
            return (
                totals[0] + grad_out * normal,
                totals[1] + grad_out,
                totals[2] + rounded.astype(f32),
            )

        zero = jnp.zeros((tile, width), f32)
        gains, shifts, biases = lax.fori_loop(0, tiles, body, (zero, zero, zero))
        dvec_ref[0:1, :] = jnp.sum(gains, axis=0, keepdims=True)
        dvec_ref[1:2, :] = jnp.sum(shifts, axis=0, keepdims=True)
        dvec_ref[3:4, :] = jnp.sum(biases, axis=0, keepdims=True)
        dvec_ref[4:8, :] = jnp.zeros((4, width), f32)
        out_ref[...] = branch[0:out_rows, :]
        dwo_ref[...] = dot_tn(own_ctx[...], gbranch[...]).astype(bf16)
        gctx_ref[...] = jnp.zeros(gctx_ref.shape, bf16)
        gctx_ref[pl.ds(offset, rows), :] = dot_nt(gbranch[...], wo_ref[...]).astype(bf16)


def expert(rows_info, ctx, pair_ctx, hidden, cot, vec, up_bias, w_out, up_parts, down_mat, out_rows):
    rows, width = hidden.shape
    seq = ctx.shape[0]
    row_blocks, chunks, size, chunk = up_parts.shape
    return pl.pallas_call(
        expert_kernel,
        grid=(chunks,),
        in_specs=[
            SMEM_SPEC,
            whole(ctx.shape),
            whole(pair_ctx.shape),
            whole(hidden.shape),
            whole(cot.shape),
            whole(vec.shape),
            pl.BlockSpec((1, chunk), lambda i: (0, i)),
            whole(w_out.shape),
            pl.BlockSpec((row_blocks, 1, size, chunk), lambda i: (0, i, 0, 0)),
            pl.BlockSpec((chunk, width), lambda i: (i, 0)),
        ],
        out_specs=[
            whole((out_rows, width)),
            whole((rows, width)),
            whole((seq, width)),
            whole((width, width)),
            pl.BlockSpec((row_blocks, 1, size, chunk), lambda i: (0, i, 0, 0)),
            pl.BlockSpec((chunk, width), lambda i: (i, 0)),
            whole((8, width)),
            pl.BlockSpec((1, chunk), lambda i: (0, i)),
        ],
        out_shape=[
            jax.ShapeDtypeStruct((out_rows, width), f32),
            jax.ShapeDtypeStruct((rows, width), f32),
            jax.ShapeDtypeStruct((seq, width), bf16),
            jax.ShapeDtypeStruct((width, width), bf16),
            jax.ShapeDtypeStruct(up_parts.shape, bf16),
            jax.ShapeDtypeStruct(down_mat.shape, bf16),
            jax.ShapeDtypeStruct((8, width), f32),
            jax.ShapeDtypeStruct(up_bias.shape, f32),
        ],
        scratch_shapes=[
            pltpu.VMEM((rows, width), bf16),
            pltpu.VMEM((rows, width), f32),
            pltpu.VMEM((rows, width), bf16),
            pltpu.VMEM((8, 128), f32),
            pltpu.VMEM((rows, width), bf16),
            pltpu.VMEM((rows, chunk), f32),
            pltpu.VMEM((rows, chunk), f32),
            pltpu.VMEM((rows, chunk), bf16),
            pltpu.VMEM((rows, chunk), bf16),
            pltpu.VMEM((rows, width), f32),
            pltpu.VMEM((rows, width), f32),
        ],
        compiler_params=params(),
        name="expert",
    )(rows_info, ctx, pair_ctx, hidden, cot, vec, up_bias, w_out, up_parts, down_mat)


def project_grad_kernel(
    row_ref, dqkv_ref, first_ref, hidden_ref, gmid_ref, vec_ref, w_ref, out_ref, dw_ref, dvec_ref, gfirst, own
):
    step = pl.program_id(0)
    rows, width = hidden_ref.shape
    out_rows = out_ref.shape[0]
    tile = 16
    tiles = rows // tile
    own[...] = dqkv_ref[0, pl.ds(pl.multiple_of(row_ref[0], 16), rows), :]
    dw_ref[0] = dot_tn(first_ref[...], own[...]).astype(bf16)
    share = dot_nt(own[...], w_ref[0])

    @pl.when(step == 0)
    def _():
        gfirst[...] = share
        dvec_ref[4:8, :] = jnp.zeros((4, width), f32)
        dvec_ref[2:3, :] = jnp.sum(own[...].astype(f32), axis=0, keepdims=True)

    @pl.when(step > 0)
    def _():
        gfirst[...] += share

    @pl.when(step == 2)
    def _():
        dvec_ref[3:4, :] = jnp.sum(own[...].astype(f32), axis=0, keepdims=True)

        def body(i, totals):
            at = pl.ds(pl.multiple_of(i * tile, tile), tile)
            normal, inv_std = norm_rows(hidden_ref[at, :])
            grad_out = gfirst[at, :]
            grad_in = norm_input_grad(grad_out, normal, inv_std, vec_ref[0:1, :])
            gfirst[at, :] = gmid_ref[at, :] + grad_in
            return totals[0] + grad_out * normal, totals[1] + grad_out

        zero = jnp.zeros((tile, width), f32)
        gains, shifts = lax.fori_loop(0, tiles, body, (zero, zero))
        dvec_ref[0:1, :] = jnp.sum(gains, axis=0, keepdims=True)
        dvec_ref[1:2, :] = jnp.sum(shifts, axis=0, keepdims=True)
        out_ref[...] = gfirst[0:out_rows, :]


def project_grad(rows_info, dqkv, first, hidden, grad_middle, vec, attn_mats, out_rows):
    rows, width = hidden.shape
    seq = dqkv.shape[1]
    square = pl.BlockSpec((1, width, width), lambda i: (i, 0, 0))
    return pl.pallas_call(
        project_grad_kernel,
        grid=(3,),
        in_specs=[
            SMEM_SPEC,
            pl.BlockSpec((1, seq, width), lambda i: (i, 0, 0)),
            whole((rows, width)),
            whole((rows, width)),
            whole((rows, width)),
            whole(vec.shape),
            square,
        ],
        out_specs=[whole((out_rows, width)), square, whole((8, width))],
        out_shape=[
            jax.ShapeDtypeStruct((out_rows, width), f32),
            jax.ShapeDtypeStruct((3, width, width), bf16),
            jax.ShapeDtypeStruct((8, width), f32),
        ],
        scratch_shapes=[pltpu.VMEM((rows, width), f32), pltpu.VMEM((rows, width), bf16)],
        compiler_params=params(),
        name="project_grad",
    )(rows_info, dqkv, first, hidden, grad_middle, vec, attn_mats)


def widen(values):
    rows, cols = values.shape
    return jnp.concatenate([values, jnp.zeros((rows, PAIR_LANES - cols), f32)], axis=1)


def split_parts(values):
    high = values.astype(bf16)
    return high, (values - high.astype(f32)).astype(bf16)


def left_parts(values):
    return jnp.concatenate(split_parts(values), axis=1)


def right_parts(values):
    high, low = split_parts(values)
    rows, cols = high.shape
    gap = jnp.zeros((cols - rows, cols), bf16)
    near = jnp.concatenate([high, gap, high, gap], axis=0)
    far = jnp.concatenate([low, gap, jnp.zeros((cols, cols), bf16)], axis=0)
    return jnp.concatenate([near, far], axis=1)


def times(left, right):
    both = dot_nn(left, right)
    return both[:, :PAIR_LANES] + both[:, PAIR_LANES:]


def inverse_roots(stats, identity):
    size = stats[0].shape[0]
    mats, factors = [], []
    for stat in stats:
        norm = jnp.sqrt(jnp.sum(stat * stat, keepdims=True))
        mats.append(stat * (1.0 / norm))
        factors.append(lax.rsqrt(jnp.sqrt(norm)))
    for iteration in range(NEWTON):
        steps = [1.25 * identity - 0.25 * mat for mat in mats]
        if iteration == 0:
            factors = [step * factor for step, factor in zip(steps, factors)]
            squares = [times(left_parts(step), right_parts(step)) for step in steps]
        elif iteration < NEWTON - 1:
            both = [
                times(
                    jnp.concatenate([left_parts(step), left_parts(factor)], axis=0),
                    right_parts(step),
                )
                for step, factor in zip(steps, factors)
            ]
            squares = [pair[:size] for pair in both]
            factors = [pair[size:] for pair in both]
        else:
            return [
                times(left_parts(factor), right_parts(step)) for step, factor in zip(steps, factors)
            ]
        fourths = [times(left_parts(square), right_parts(square)) for square in squares]
        mats = [times(left_parts(fourth), right_parts(mat)) for fourth, mat in zip(fourths, mats)]


def shampoo_kernel(group, grads_ref, left_ref, right_ref, w_ref, g_out, left_out, right_out, w_out):
    count, size, _ = left_ref.shape
    row = lax.broadcasted_iota(jnp.int32, (size, PAIR_LANES), 0)
    col = lax.broadcasted_iota(jnp.int32, (size, PAIR_LANES), 1)
    identity = (row == col).astype(f32)
    for base in range(0, count, group):
        stats, grads = [], []
        for i in range(base, base + group):
            grad = grads_ref[0, :, i * size : (i + 1) * size]
            g_out[i] = grad
            grad = widen(grad)
            grad_t = widen(jnp.transpose(grad, (1, 0))[:size])
            grads.append(grad)
            outer = times(left_parts(grad), right_parts(grad_t))
            inner = times(left_parts(grad_t), right_parts(grad))
            left_new = stat_decay * left_ref[i] + (1.0 - stat_decay) * outer[:, :size]
            right_new = stat_decay * right_ref[i] + (1.0 - stat_decay) * inner[:, :size]
            left_out[i] = left_new
            right_out[i] = right_new
            stats += [widen(left_new), widen(right_new)]
        roots = inverse_roots(stats, identity)
        for at in range(group):
            half_way = times(left_parts(roots[2 * at]), right_parts(grads[at]))
            update = times(left_parts(half_way), right_parts(roots[2 * at + 1]))
            w_out[base + at] = w_ref[base + at] - matrix_rate * update[:, :size]


def shampoo(grad_rows, lefts, rights, weights):
    parts, size, span = grad_rows.shape
    count = span // size
    group = math.gcd(count, 4)
    blocks = pl.BlockSpec((count, size, size), lambda i: (i, 0, 0))
    shape = jax.ShapeDtypeStruct(lefts.shape, f32)
    return pl.pallas_call(
        functools.partial(shampoo_kernel, group),
        grid=(parts,),
        in_specs=[pl.BlockSpec((1, size, span), lambda i: (i, 0, 0)), blocks, blocks, blocks],
        out_specs=[blocks] * 4,
        out_shape=[shape] * 4,
        compiler_params=params(),
        name="shampoo",
    )(grad_rows, lefts, rights, weights)


def blocks_to_matrix(blocks, row_blocks, col_blocks):
    block_size = blocks.shape[-1]
    leading = blocks.shape[:-3]
    shaped = blocks.reshape(leading + (row_blocks, col_blocks, block_size, block_size))
    moved = jnp.swapaxes(shaped, -3, -2)
    return moved.reshape(leading + (row_blocks * block_size, col_blocks * block_size))


def local(
    stream_in,
    cotangent,
    patch_count,
    pos_index,
    attn_blocks,
    attn_left,
    attn_right,
    ffn_blocks,
    ffn_left,
    ffn_right,
    vectors,
    vectors_mom,
    ffn_bias,
    ffn_bias_mom,
    pos_table,
    pos_mom,
):
    size = attn_blocks.shape[-1]
    width = vectors.shape[1]
    hidden_units = ffn_bias.shape[1]
    slots = stream_in.shape[2]
    row_blocks = width // size
    chunks = hidden_units // width
    rows = round_up(slots, 16)
    seq = round_up(slots + TEXT, 32)
    own_attn = attn_blocks.shape[0]
    ffn_flat = ffn_blocks.shape[1]
    modality = lax.axis_index("mod")
    is_text = modality == 1
    image_flag = (1 - modality).astype(f32)

    attn_span = math.gcd(own_attn, row_blocks)
    ffn_span = math.gcd(ffn_flat, row_blocks)
    attn_rows = pack_rows(attn_blocks, attn_span)
    ffn_rows = pack_rows(ffn_blocks[0], ffn_span)
    attn_all = lax.all_gather(attn_rows, ("mod", "dp"), axis=0, tiled=True)
    ffn_all = lax.all_gather(ffn_rows, "dp", axis=0, tiled=True)

    def join(parts):
        lead, _, span = parts.shape
        if span == width:
            return parts
        shaped = parts.reshape(-1, width // span, size, span)
        return jnp.swapaxes(shaped, 1, 2).reshape(-1, size, width)

    attn_mats = join(attn_all).reshape(4, width, width)
    ffn_parts = join(ffn_all).reshape(2, -1, size, width)
    up_parts = ffn_parts[0].reshape(row_blocks, chunks, size, width)
    down_mat = ffn_parts[1].reshape(hidden_units, width)

    own_vec = lax.dynamic_slice_in_dim(vectors, 3 + 5 * modality, 5, 0)
    vec = jnp.concatenate([own_vec, vectors[0:3][jnp.array([0, 1, 2])]], axis=0)
    up_bias = lax.dynamic_slice_in_dim(ffn_bias, modality, 1, 0)
    count = patch_count[0]
    offset = TEXT * (1 - modality)
    first_key = jnp.where(is_text, TEXT, 0)
    end_key = jnp.where(is_text, slots, TEXT + count)
    kept_rows = jnp.where(is_text, slots, count)
    rows_info = jnp.stack([offset, first_key, end_key, modality, kept_rows]).astype(jnp.int32)
    pad = ((0, rows - slots), (0, 0))
    hidden = stream_in[0, 0] + image_flag * jnp.take(pos_table, pos_index[0], axis=0)
    hidden = jnp.pad(hidden, pad)
    cot = jnp.pad(cotangent[0, 0], pad)

    to_image = [(1, 0)]
    to_text = [(0, 1)]
    qkv, first = project(rows_info, hidden, vec, attn_mats, seq)
    pair_qkv = lax.ppermute(qkv[:TEXT], "mod", to_image)
    qkv = lax.dynamic_update_slice(qkv, jnp.where(is_text, qkv[:TEXT], pair_qkv), (0, 0))
    ctx, lse = attend(rows_info, qkv)
    pair_ctx = lax.ppermute(ctx[:TEXT], "mod", to_text)
    stream_out, grad_middle, grad_ctx, grad_wo, grad_up, grad_down, late_vec, grad_up_bias = expert(
        rows_info, ctx, pair_ctx, hidden, cot, vec, up_bias, attn_mats[3], up_parts, down_mat, slots
    )
    pair_grad = lax.ppermute(grad_ctx[:TEXT], "mod", to_image)
    grad_ctx = lax.dynamic_update_slice(
        grad_ctx, jnp.where(is_text, grad_ctx[:TEXT], pair_grad), (0, 0)
    )
    grad_qkv = attend_grad(rows_info, qkv, grad_ctx, lse)
    pair_dqkv = lax.ppermute(grad_qkv[:, :TEXT], "mod", to_text)
    grad_qkv = lax.dynamic_update_slice(
        grad_qkv, jnp.where(is_text, pair_dqkv, grad_qkv[:, :TEXT]), (0, 0, 0)
    )
    stream_grad, grad_wqkv, early_vec = project_grad(
        rows_info, grad_qkv, first, hidden, grad_middle, vec, attn_mats, slots
    )

    def spread(parts, span):
        if span == width:
            return parts
        shaped = parts.reshape(-1, size, width // span, span)
        return jnp.swapaxes(shaped, 1, 2).reshape(-1, size, span)

    ffn_full = jnp.concatenate(
        [grad_up.reshape(-1, size, width), grad_down.reshape(-1, size, width)], axis=0
    )
    ffn_sum = lax.psum_scatter(
        spread(ffn_full, ffn_span * size), "dp", scatter_dimension=0, tiled=True
    )
    attn_full = jnp.concatenate([grad_wqkv, grad_wo[None]], axis=0).reshape(-1, size, width)
    attn_sum = lax.psum_scatter(
        spread(attn_full, attn_span * size), ("mod", "dp"), scatter_dimension=0, tiled=True
    )
    grad_pos = jax.ops.segment_sum(image_flag * stream_grad, pos_index[0], num_segments=slots)
    selector = (jnp.arange(2) == modality).astype(f32)
    own_rows = jnp.stack([early_vec[0], early_vec[1], late_vec[0], late_vec[1], late_vec[2]])
    shared_rows = jnp.stack([early_vec[2], early_vec[3], late_vec[3]])
    vector_grad = jnp.concatenate(
        [shared_rows, (selector[:, None, None] * own_rows[None]).reshape(10, width)], axis=0
    )
    up_bias_grad = selector[:, None] * grad_up_bias
    vector_sum, up_bias_sum, pos_sum = lax.psum((vector_grad, up_bias_grad, grad_pos), ("mod", "dp"))

    items_total = lax.axis_size("dp")
    vector_rate = 0.3 / math.sqrt(items_total * slots)
    pos_rate = 0.5 / math.sqrt(items_total)
    vectors_mom_new = moment_keep * vectors_mom + vector_sum
    vectors_new = vectors - vector_rate * vectors_mom_new
    ffn_bias_mom_new = moment_keep * ffn_bias_mom + up_bias_sum
    ffn_bias_new = ffn_bias - vector_rate * ffn_bias_mom_new
    pos_mom_new = moment_keep * pos_mom + pos_sum
    pos_new = pos_table - pos_rate * pos_mom_new
    ffn_out = shampoo(ffn_sum.astype(f32), ffn_left[0], ffn_right[0], ffn_blocks[0])
    attn_out = shampoo(attn_sum.astype(f32), attn_left, attn_right, attn_blocks)
    return (
        stream_out[None, None],
        stream_grad[None, None],
        *attn_out,
        *(part[None] for part in ffn_out),
        vectors_mom_new,
        vectors_new,
        ffn_bias_mom_new,
        ffn_bias_new,
        pos_mom_new,
        pos_new,
    )


def solution(mesh):
    items = P("mod", "dp", None, None)
    owned = P(("mod", "dp"), None, None)
    return jax.shard_map(
        local,
        mesh=mesh,
        in_specs=(items, items, P("dp"), P("dp", None), owned, owned, owned, items, items, items)
        + (P(),) * 6,
        out_specs=(items, items, owned, owned, owned, owned, items, items, items, items)
        + (P(),) * 6,
        check_vma=False,
    )
```

```python
import functools
import math

import jax
import jax.numpy as jnp
from jax import lax
from jax.experimental import pallas as pl
from jax.experimental.pallas import tpu as pltpu
from jax.sharding import PartitionSpec as P

HEADS = 12
TEXT = 64
NEWTON = 6
PAIR_LANES = 128
QUERY_TILE = 256
VMEM_LIMIT = 56 << 20

f32 = jnp.float32
bf16 = jnp.bfloat16
norm_eps = 1e-05
stat_decay = 0.5
matrix_rate = 0.25
moment_keep = 0.9
masked_score = -1e30


def dot_nn(left, right):
    return lax.dot_general(left, right, (((1,), (0,)), ((), ())), preferred_element_type=f32)


def dot_nt(left, right):
    return lax.dot_general(left, right, (((1,), (1,)), ((), ())), preferred_element_type=f32)


def dot_tn(left, right):
    return lax.dot_general(left, right, (((0,), (0,)), ((), ())), preferred_element_type=f32)


def params():
    return pltpu.CompilerParams(vmem_limit_bytes=VMEM_LIMIT)


def cost(microseconds):
    return pl.CostEstimate(flops=int(microseconds * 1e8), bytes_accessed=0, transcendentals=0)


def round_up(value, step):
    return (value + step - 1) // step * step


def whole(shape):
    return pl.BlockSpec(shape, lambda *ids: (0,) * len(shape))


SMEM_SPEC = pl.BlockSpec(memory_space=pltpu.SMEM)


def pack_kernel(up_ref, blocks_ref, out_ref):
    part = pl.program_id(0)
    parts = pl.num_programs(0)
    per_row = blocks_ref.shape[0] // parts
    pieces = []
    for i in range(per_row):
        at = jnp.where(up_ref[0] == 1, i * parts + part, part * per_row + i)
        pieces.append(blocks_ref[at])
    out_ref[0] = jnp.concatenate(pieces, axis=1).astype(bf16)


def pack_rows(is_up, blocks, per_row):
    count, size, _ = blocks.shape
    return pl.pallas_call(
        pack_kernel,
        grid=(count // per_row,),
        in_specs=[SMEM_SPEC, whole(blocks.shape)],
        out_specs=pl.BlockSpec((1, size, per_row * size), lambda i: (i, 0, 0)),
        out_shape=jax.ShapeDtypeStruct((count // per_row, size, per_row * size), bf16),
        compiler_params=params(),
        cost_estimate=cost(3),
        name="pack_rows",
    )(is_up, blocks)


def norm_rows(values):
    centred = values - jnp.mean(values, axis=-1, keepdims=True)
    spread = jnp.mean(centred * centred, axis=-1, keepdims=True)
    inv_std = lax.rsqrt(spread + norm_eps)
    return centred * inv_std, inv_std


def norm_input_grad(grad_out, normal, inv_std, gain):
    grad_norm = grad_out * gain
    mean_grad = jnp.mean(grad_norm, axis=-1, keepdims=True)
    mean_proj = jnp.mean(grad_norm * normal, axis=-1, keepdims=True)
    return inv_std * (grad_norm - mean_grad - normal * mean_proj)


def first_norm_kernel(row_ref, hidden_ref, vec_ref, first_ref):
    rows = hidden_ref.shape[0]
    normal, _ = norm_rows(hidden_ref[...])
    first_ref[...] = jnp.zeros(first_ref.shape, bf16)
    first = normal * vec_ref[0:1, :] + vec_ref[1:2, :]
    first_ref[pl.ds(pl.multiple_of(row_ref[0], 16), rows), :] = first.astype(bf16)


def first_norm(rows_info, hidden, vec, seq):
    return pl.pallas_call(
        first_norm_kernel,
        in_specs=[SMEM_SPEC, whole(hidden.shape), whole(vec.shape)],
        out_specs=whole((seq, hidden.shape[1])),
        out_shape=jax.ShapeDtypeStruct((seq, hidden.shape[1]), bf16),
        compiler_params=params(),
        cost_estimate=cost(4),
        name="first_norm",
    )(rows_info, hidden, vec)


def project_kernel(row_ref, first_ref, vec_ref, *refs):
    weight_refs, (qkv_ref, w_ref) = refs[:-2], refs[-2:]
    step = pl.program_id(0)
    if len(weight_refs) == 1:
        w_ref[...] = weight_refs[0][...]
    else:
        upper, upper_far, lower, lower_far = weight_refs
        half, size = upper.shape[3], 2 * upper.shape[3]
        on_one = row_ref[5] == 1
        for z in range(2):
            for y in range(2):
                for base, near, far in (
                    (0, upper[0, y, z], upper_far[0, y, z]),
                    (half, lower[y, 0, z], lower_far[y, 0, z]),
                ):
                    start = (4 * z + 2 * y) * size + base
                    w_ref[0, start : start + half, :] = jnp.where(on_one, far, near)
                    start += size
                    w_ref[0, start : start + half, :] = jnp.where(on_one, near, far)

    @pl.when(step < 3)
    def _():
        bias = jnp.where(step == 0, vec_ref[5:6, :], jnp.where(step == 2, vec_ref[6:7, :], 0.0))
        qkv_ref[...] = (dot_nn(first_ref[...], w_ref[0]) + bias).astype(bf16)


def project(rows_info, first, vec, attn_parts):
    seq, width = first.shape
    if len(attn_parts) == 1:
        weight_specs = [pl.BlockSpec((1, width, width), lambda i: (i, 0, 0))]
    else:
        half = attn_parts[0].shape[3]
        upper = pl.BlockSpec((1, 2, 2, half, width), lambda i: (i // 2, 0, i % 2, 0, 0))
        lower = pl.BlockSpec((2, 1, 2, half, width), lambda i: (0, i // 2, i % 2, 0, 0))
        weight_specs = [upper, upper, lower, lower]
    return pl.pallas_call(
        project_kernel,
        grid=(4,),
        in_specs=[SMEM_SPEC, whole((seq, width)), whole(vec.shape), *weight_specs],
        out_specs=[
            pl.BlockSpec((seq, width), lambda i: (0, jnp.minimum(i, 2))),
            pl.BlockSpec((1, width, width), lambda i: (i, 0, 0)),
        ],
        out_shape=[
            jax.ShapeDtypeStruct((seq, 3 * width), bf16),
            jax.ShapeDtypeStruct((4, width, width), bf16),
        ],
        compiler_params=params(),
        cost_estimate=cost(8),
        name="project",
    )(rows_info, first, vec, *attn_parts)


def key_bias(row_ref, seq):
    rows = lax.broadcasted_iota(jnp.int32, (seq, 1), 0)
    counts = jnp.logical_and(rows >= row_ref[1], rows < row_ref[2])
    return jnp.where(counts, 0.0, masked_score).astype(f32)


def transposed(values):
    return jnp.transpose(values.astype(f32), (1, 0)).astype(bf16)


def attend_kernel(row_ref, q_ref, k_ref, v_ref, ctx_ref, lse_ref, pair_ref):
    seq = q_ref.shape[0]
    half = PAIR_LANES // 2
    scale = half ** (-0.5)
    bias = key_bias(row_ref, seq)
    keys = k_ref[...]
    values_t = transposed(v_ref[...])
    for start in range(0, seq, QUERY_TILE):
        size = min(QUERY_TILE, seq - start)
        tile = slice(start, start + size)
        queries = q_ref[tile, :]
        lane = lax.broadcasted_iota(jnp.int32, (size, PAIR_LANES), 1)
        parts = []
        for head in range(2):
            own = (lane < half) == (head == 0)
            scores = dot_nt(keys, jnp.where(own, queries, jnp.zeros_like(queries))) * scale + bias
            top = jnp.max(scores, axis=0, keepdims=True)
            raised = jnp.exp(scores - top)
            total = jnp.sum(raised, axis=0, keepdims=True)
            probs = (raised * (1.0 / total)).astype(bf16)
            parts.append(dot_nn(values_t[half * head : half * (head + 1), :], probs))
            lse_ref[0, head : head + 1, tile] = top + jnp.log(total)
        context = jnp.transpose(jnp.concatenate(parts, axis=0), (1, 0)).astype(bf16)
        ctx_ref[tile, :] = context
        if start == 0:
            pair_ref[...] = context[: pair_ref.shape[0]]


def attend(rows_info, qkv):
    seq = qkv.shape[0]
    width = qkv.shape[1] // 3
    pairs = width // PAIR_LANES

    def column(base):
        return pl.BlockSpec((seq, PAIR_LANES), lambda i, base=base: (0, base + i))

    return pl.pallas_call(
        attend_kernel,
        grid=(pairs,),
        in_specs=[SMEM_SPEC, column(0), column(pairs), column(2 * pairs)],
        out_specs=[
            column(0),
            pl.BlockSpec((1, 8, seq), lambda i: (i, 0, 0)),
            pl.BlockSpec((TEXT, PAIR_LANES), lambda i: (0, i)),
        ],
        out_shape=[
            jax.ShapeDtypeStruct((seq, width), bf16),
            jax.ShapeDtypeStruct((pairs, 8, seq), f32),
            jax.ShapeDtypeStruct((TEXT, width), bf16),
        ],
        compiler_params=params(),
        cost_estimate=cost(22),
        name="attend",
    )(rows_info, qkv, qkv, qkv)


def attend_grad_kernel(
    row_ref, q_ref, k_ref, v_ref, g_ref, pair_ref, lse_ref, out_ref, dk_ref, dv_ref
):
    seq = q_ref.shape[0]
    half = PAIR_LANES // 2
    scale = half ** (-0.5)
    bias = key_bias(row_ref, seq)
    keys = k_ref[...]
    values = v_ref[...]
    keys_t = transposed(keys)
    for start in range(0, seq, QUERY_TILE):
        size = min(QUERY_TILE, seq - start)
        tile = slice(start, start + size)
        queries = q_ref[tile, :]
        row = lax.broadcasted_iota(jnp.int32, (size, 1), 0) + start
        counts = jnp.logical_and(row >= row_ref[1], row < row_ref[2])
        grads = g_ref[tile, :]
        if start == 0:
            grads = jnp.concatenate([pair_ref[...], grads[pair_ref.shape[0] :]], axis=0)
        grads = jnp.where(counts, grads, jnp.zeros((size, PAIR_LANES), bf16))
        lane = lax.broadcasted_iota(jnp.int32, (size, PAIR_LANES), 1)
        parts = []
        for head in range(2):
            own = (lane < half) == (head == 0)
            own_q = jnp.where(own, queries, jnp.zeros_like(queries))
            own_g = jnp.where(own, grads, jnp.zeros_like(grads))
            scores = dot_nt(keys, own_q) * scale + bias
            probs = jnp.exp(scores - lse_ref[0, head : head + 1, tile])
            grad_probs = dot_nt(values, own_g)
            row_dot = jnp.sum(probs * grad_probs, axis=0, keepdims=True)
            grad_scores = (probs * (grad_probs - row_dot)).astype(bf16)
            grad_v = dot_nn(probs.astype(bf16), own_g)
            grad_k = dot_nn(grad_scores, own_q)
            if start == 0 and head == 0:
                dv_ref[...] = grad_v
                dk_ref[...] = grad_k
            else:
                dv_ref[...] += grad_v
                dk_ref[...] += grad_k
            parts.append(dot_nn(keys_t[half * head : half * (head + 1), :], grad_scores))
        grad_q = jnp.transpose(jnp.concatenate(parts, axis=0) * scale, (1, 0))
        out_ref[0, tile, :] = grad_q.astype(bf16)
    out_ref[1] = (dk_ref[...] * scale).astype(bf16)
    out_ref[2] = dv_ref[...].astype(bf16)


def attend_grad(rows_info, qkv, grad_ctx, pair_grad, lse):
    seq = qkv.shape[0]
    width = qkv.shape[1] // 3
    pairs = width // PAIR_LANES

    def column(base):
        return pl.BlockSpec((seq, PAIR_LANES), lambda i, base=base: (0, base + i))

    return pl.pallas_call(
        attend_grad_kernel,
        grid=(pairs,),
        in_specs=[
            SMEM_SPEC,
            column(0),
            column(pairs),
            column(2 * pairs),
            column(0),
            pl.BlockSpec((TEXT, PAIR_LANES), lambda i: (0, i)),
            pl.BlockSpec((1, 8, seq), lambda i: (i, 0, 0)),
        ],
        out_specs=pl.BlockSpec((3, seq, PAIR_LANES), lambda i: (0, 0, i)),
        out_shape=jax.ShapeDtypeStruct((3, seq, width), bf16),
        scratch_shapes=[pltpu.VMEM((seq, PAIR_LANES), f32)] * 2,
        compiler_params=params(),
        cost_estimate=cost(25),
        name="attend_grad",
    )(rows_info, qkv, qkv, qkv, grad_ctx, pair_grad, lse)


def gelu_pair(values):
    size = jnp.abs(values)
    tail = 1.0 / (1.0 + (0.3275911 * 0.5**0.5) * size)
    poly = tail * (
        0.254829592
        + tail * (-0.284496736 + tail * (1.421413741 + tail * (-1.453152027 + tail * 1.061405429)))
    )
    bell = jnp.exp(-0.5 * values * values)
    upper = 0.5 * poly * bell
    share = jnp.where(values >= 0.0, 1.0 - upper, upper)
    return values * share, share + values * bell * ((2.0 * math.pi) ** -0.5)


def split_by_core(row_ref, grad, shape):
    size, width = shape[-2:]
    blocks = grad.reshape(-1, 2, size, width)
    near, far = blocks[:, 0], blocks[:, 1]
    on_one = row_ref[5] == 1
    return jnp.where(on_one, far, near).reshape(shape), jnp.where(on_one, near, far).reshape(shape)


def expert_chunk(
    row_ref, second, gbranch, upb, up_ref, down_ref, grad_refs, dupb_ref, branch, gsecond, scratch, begin
):
    pre, gact, act, gpre = scratch
    rows, width = act.shape
    tile = 16
    up = up_ref[...].reshape(width, width)
    down = down_ref[...].reshape(width, width)
    pre[...] = dot_nn(second[...], up)
    gact[...] = dot_nt(gbranch[...], down)

    def body(i, total):
        at = pl.ds(pl.multiple_of(i * tile, tile), tile)
        value, slope = gelu_pair(pre[at, :] + upb[...])
        act[at, :] = value.astype(bf16)
        rounded = (gact[at, :] * slope).astype(bf16)
        gpre[at, :] = rounded
        return total + rounded.astype(f32)

    total = lax.fori_loop(0, rows // tile, body, jnp.zeros((tile, width), f32))
    dupb_ref[...] = jnp.sum(total, axis=0, keepdims=True)
    for which, grad in enumerate(
        (dot_tn(second[...], gpre[...]), dot_tn(act[...], gbranch[...]))
    ):
        grad, shape = grad.astype(bf16), grad_refs[0].shape[1:]
        if len(grad_refs) == 1:
            grad_refs[0][which] = grad.reshape(shape)
        else:
            grad_refs[0][which], grad_refs[1][which] = split_by_core(row_ref, grad, shape)
    own_branch = dot_nn(act[...], down)
    own_gsecond = dot_nt(gpre[...], up)

    @pl.when(begin)
    def _():
        branch[...] = own_branch
        gsecond[...] = own_gsecond

    @pl.when(jnp.logical_not(begin))
    def _():
        branch[...] += own_branch
        gsecond[...] += own_gsecond


def expert_begin_kernel(
    row_ref,
    ctx_ref,
    pair_ref,
    hidden_ref,
    cot_ref,
    vec_ref,
    upb_ref,
    wo_ref,
    up_ref,
    down_ref,
    own_ctx,
    middle,
    second,
    gbranch,
    branch,
    gsecond,
    grad_ref,
    dvec_ref,
    dupb_ref,
    *scratch,
):
    step = pl.program_id(0)
    rows, width = hidden_ref.shape
    tile = 16

    @pl.when(step == 0)
    def _():
        own_ctx[...] = ctx_ref[pl.ds(pl.multiple_of(row_ref[0], 16), rows), :]

        @pl.when(row_ref[3] == 1)
        def _():
            own_ctx[0 : pair_ref.shape[0], :] = pair_ref[...]

        middle[...] = dot_nn(own_ctx[...], wo_ref[0])

        def body(i, total):
            at = pl.ds(pl.multiple_of(i * tile, tile), tile)
            mid = hidden_ref[at, :] + (middle[at, :] + vec_ref[7:8, :])
            middle[at, :] = mid
            normal, _ = norm_rows(mid)
            second[at, :] = (normal * vec_ref[2:3, :] + vec_ref[3:4, :]).astype(bf16)
            row = lax.broadcasted_iota(jnp.int32, (tile, 1), 0) + i * tile
            kept = jnp.where(row < row_ref[4], cot_ref[at, :], 0.0)
            rounded = kept.astype(bf16)
            gbranch[at, :] = rounded
            return total + rounded.astype(f32)

        total = lax.fori_loop(0, rows // tile, body, jnp.zeros((tile, width), f32))
        dvec_ref[...] = jnp.zeros(dvec_ref.shape, f32)
        dvec_ref[2:3, :] = jnp.sum(total, axis=0, keepdims=True)

    expert_chunk(
        row_ref,
        second,
        gbranch,
        upb_ref,
        up_ref,
        down_ref,
        (grad_ref,),
        dupb_ref,
        branch,
        gsecond,
        scratch,
        step == 0,
    )


def expert_end_kernel(
    row_ref,
    own_ctx,
    middle,
    second,
    gbranch,
    branch_in,
    gsecond_in,
    dvec_in,
    cot_ref,
    vec_ref,
    upb_ref,
    wo_ref,
    up_ref,
    down_ref,
    out_ref,
    gmid_ref,
    gctx_ref,
    pair_ref,
    dwo_ref,
    keep_ref,
    send_ref,
    dvec_ref,
    dupb_ref,
    branch,
    gsecond,
    rounded_ref,
    *scratch,
):
    step = pl.program_id(0)
    rows, width = middle.shape
    out_rows = out_ref.shape[0]
    tile = 16

    @pl.when(step == 0)
    def _():
        branch[...] = branch_in[...]
        gsecond[...] = gsecond_in[...]

    expert_chunk(
        row_ref,
        second,
        gbranch,
        upb_ref,
        up_ref,
        down_ref,
        (keep_ref, send_ref),
        dupb_ref,
        branch,
        gsecond,
        scratch,
        step < 0,
    )

    @pl.when(step == pl.num_programs(0) - 1)
    def _():
        def body(i, totals):
            at = pl.ds(pl.multiple_of(i * tile, tile), tile)
            mid = middle[at, :]
            normal, inv_std = norm_rows(mid)
            grad_out = gsecond[at, :]
            row = lax.broadcasted_iota(jnp.int32, (tile, 1), 0) + i * tile
            kept = row < row_ref[4]
            branch[at, :] = jnp.where(kept, mid + (branch[at, :] + vec_ref[4:5, :]), 0.0)
            grad_in = norm_input_grad(grad_out, normal, inv_std, vec_ref[2:3, :])
            grad_mid = jnp.where(kept, cot_ref[at, :], 0.0) + grad_in
            gmid_ref[at, :] = grad_mid
            rounded = grad_mid.astype(bf16)
            rounded_ref[at, :] = rounded
            return (
                totals[0] + grad_out * normal,
                totals[1] + grad_out,
                totals[2] + rounded.astype(f32),
            )

        zero = jnp.zeros((tile, width), f32)
        gains, shifts, biases = lax.fori_loop(0, rows // tile, body, (zero, zero, zero))
        dvec_ref[...] = dvec_in[...]
        dvec_ref[0:1, :] = jnp.sum(gains, axis=0, keepdims=True)
        dvec_ref[1:2, :] = jnp.sum(shifts, axis=0, keepdims=True)
        dvec_ref[3:4, :] = jnp.sum(biases, axis=0, keepdims=True)
        out_ref[...] = branch[0:out_rows, :]
        dwo_ref[...] = dot_tn(own_ctx[...], rounded_ref[...]).astype(bf16)
        grad_ctx = dot_nt(rounded_ref[...], wo_ref[0]).astype(bf16)
        gctx_ref[...] = jnp.zeros(gctx_ref.shape, bf16)
        gctx_ref[pl.ds(pl.multiple_of(row_ref[0], 16), rows), :] = grad_ctx
        pair_ref[...] = grad_ctx[: pair_ref.shape[0]]


def expert_specs(rows, width, ffn_parts, half):
    _, row_blocks, chunks, size, _ = ffn_parts.shape
    base = half * (chunks // 2)

    def weights(which):
        return pl.BlockSpec(
            (1, row_blocks, 1, size, width), lambda i: (which, 0, base + i, 0, 0)
        )

    inputs = [
        pl.BlockSpec((1, width), lambda i: (0, base + i)),
        pl.BlockSpec((1, width, width), lambda i: (3, 0, 0)),
        weights(0),
        weights(1),
    ]
    outs = 1 + half
    per_out = row_blocks // outs
    grad_spec = [pl.BlockSpec((2, per_out, 1, size, width), lambda i: (0, 0, i, 0, 0))] * outs
    grad_shape = [jax.ShapeDtypeStruct((2, per_out, chunks // 2, size, width), bf16)] * outs
    bias_spec = pl.BlockSpec((1, width), lambda i: (0, i))
    bias_shape = jax.ShapeDtypeStruct((1, chunks // 2 * width), f32)
    scratch = [pltpu.VMEM((rows, width), f32)] * 2 + [pltpu.VMEM((rows, width), bf16)] * 2
    return inputs, (grad_spec, grad_shape), (bias_spec, bias_shape), scratch


def expert_begin(rows_info, ctx, pair_ctx, hidden, cot, vec, up_bias, w_attn, ffn_parts):
    rows, width = hidden.shape
    inputs, grads, biases, scratch = expert_specs(rows, width, ffn_parts, 0)
    kept = [bf16, f32, bf16, bf16, f32, f32]
    return pl.pallas_call(
        expert_begin_kernel,
        grid=(ffn_parts.shape[2] // 2,),
        in_specs=[
            SMEM_SPEC,
            whole(ctx.shape),
            whole(pair_ctx.shape),
            whole(hidden.shape),
            whole(cot.shape),
            whole(vec.shape),
            *inputs,
        ],
        out_specs=[whole((rows, width))] * 6 + [*grads[0], whole((8, width)), biases[0]],
        out_shape=[jax.ShapeDtypeStruct((rows, width), kind) for kind in kept]
        + [*grads[1], jax.ShapeDtypeStruct((8, width), f32), biases[1]],
        scratch_shapes=scratch,
        compiler_params=params(),
        cost_estimate=cost(28),
        name="expert_begin",
    )(rows_info, ctx, pair_ctx, hidden, cot, vec, up_bias, w_attn, ffn_parts, ffn_parts)


def expert_end(rows_info, kept, late, cot, vec, up_bias, w_attn, ffn_parts, seq, out_rows):
    rows, width = cot.shape
    inputs, grads, biases, scratch = expert_specs(rows, width, ffn_parts, 1)
    return pl.pallas_call(
        expert_end_kernel,
        grid=(ffn_parts.shape[2] // 2,),
        in_specs=[SMEM_SPEC]
        + [whole((rows, width))] * 6
        + [whole(late.shape), whole(cot.shape), whole(vec.shape), *inputs],
        out_specs=[
            whole((out_rows, width)),
            whole((rows, width)),
            whole((seq, width)),
            whole((TEXT, width)),
            whole((width, width)),
            *grads[0],
            whole((8, width)),
            biases[0],
        ],
        out_shape=[
            jax.ShapeDtypeStruct((out_rows, width), f32),
            jax.ShapeDtypeStruct((rows, width), f32),
            jax.ShapeDtypeStruct((seq, width), bf16),
            jax.ShapeDtypeStruct((TEXT, width), bf16),
            jax.ShapeDtypeStruct((width, width), bf16),
            *grads[1],
            jax.ShapeDtypeStruct((8, width), f32),
            biases[1],
        ],
        scratch_shapes=[
            pltpu.VMEM((rows, width), f32),
            pltpu.VMEM((rows, width), f32),
            pltpu.VMEM((rows, width), bf16),
            *scratch,
        ],
        compiler_params=params(),
        cost_estimate=cost(30),
        name="expert_end",
    )(rows_info, *kept, late, cot, vec, up_bias, w_attn, ffn_parts, ffn_parts)


def project_grad_kernel(
    row_ref, dqkv_ref, first_ref, w_ref, dwo_ref, keep_ref, send_ref, gfirst, pair_ref, sums_ref
):
    step = pl.program_id(0)

    def put(grad):
        keep_ref[0], send_ref[0] = split_by_core(row_ref, grad, keep_ref.shape[1:])

    @pl.when(step < 3)
    def _():
        own = dqkv_ref[0]
        put(dot_tn(first_ref[...], own).astype(bf16))
        share = dot_nt(own, w_ref[0])
        sums = jnp.sum(own.astype(f32), axis=0, keepdims=True)

        @pl.when(step == 0)
        def _():
            gfirst[...] = share
            sums_ref[...] = jnp.zeros(sums_ref.shape, f32)
            sums_ref[0:1, :] = sums

        @pl.when(step > 0)
        def _():
            gfirst[...] += share
            sums_ref[1:2, :] = sums

    @pl.when(step == 3)
    def _():
        put(dwo_ref[...])
        pair_ref[...] = gfirst[0 : pair_ref.shape[0], :]


def project_grad(rows_info, dqkv, first, w_attn, grad_wo, size):
    seq, width = first.shape
    pairs = width // size // 2
    part = pl.BlockSpec((1, pairs, size, width), lambda i: (i, 0, 0, 0))

    def early_index(i):
        return (jnp.minimum(i, 2), 0, 0)

    return pl.pallas_call(
        project_grad_kernel,
        grid=(4,),
        in_specs=[
            SMEM_SPEC,
            pl.BlockSpec((1, seq, width), early_index),
            whole((seq, width)),
            pl.BlockSpec((1, width, width), early_index),
            whole(grad_wo.shape),
        ],
        out_specs=[part, part, whole((seq, width)), whole((TEXT, width)), whole((8, width))],
        out_shape=[
            jax.ShapeDtypeStruct((4, pairs, size, width), bf16),
            jax.ShapeDtypeStruct((4, pairs, size, width), bf16),
            jax.ShapeDtypeStruct((seq, width), f32),
            jax.ShapeDtypeStruct((TEXT, width), f32),
            jax.ShapeDtypeStruct((8, width), f32),
        ],
        compiler_params=params(),
        cost_estimate=cost(15),
        name="project_grad",
    )(rows_info, dqkv, first, w_attn, grad_wo)


def first_grad_kernel(
    row_ref,
    gfirst_ref,
    pair_ref,
    hidden_ref,
    gmid_ref,
    vec_ref,
    sums_ref,
    late_ref,
    upb_ref,
    pos_ref,
    out_ref,
    small_ref,
    own,
):
    rows, width = hidden_ref.shape
    tile = 16
    own[...] = gfirst_ref[pl.ds(pl.multiple_of(row_ref[0], 16), rows), :]

    @pl.when(row_ref[3] == 1)
    def _():
        own[0 : pair_ref.shape[0], :] = pair_ref[...]

    def body(i, totals):
        at = pl.ds(pl.multiple_of(i * tile, tile), tile)
        normal, inv_std = norm_rows(hidden_ref[at, :])
        grad_out = own[at, :]
        grad_in = norm_input_grad(grad_out, normal, inv_std, vec_ref[0:1, :])
        own[at, :] = gmid_ref[at, :] + grad_in
        return totals[0] + grad_out * normal, totals[1] + grad_out

    zero = jnp.zeros((tile, width), f32)
    gains, shifts = lax.fori_loop(0, rows // tile, body, (zero, zero))
    out_ref[...] = own[0 : out_ref.shape[0], :]
    own_rows = (
        jnp.sum(gains, axis=0, keepdims=True),
        jnp.sum(shifts, axis=0, keepdims=True),
        late_ref[0:1, :],
        late_ref[1:2, :],
        late_ref[2:3, :],
    )
    row = lax.broadcasted_iota(jnp.int32, (16, width), 0)
    top = jnp.where(row == 0, sums_ref[0:1, :], 0.0)
    top = jnp.where(row == 1, sums_ref[1:2, :], top)
    top = jnp.where(row == 2, late_ref[3:4, :], top)
    for i, value in enumerate(own_rows):
        top = jnp.where(row == 3 + 5 * row_ref[3] + i, value, top)
    small_ref[0:16, :] = top
    row = lax.broadcasted_iota(jnp.int32, (8, width), 0)
    bias = jnp.zeros((8, width), f32)
    for i in range(upb_ref.shape[0]):
        bias = jnp.where(row == upb_ref.shape[0] * row_ref[3] + i, upb_ref[i : i + 1, :], bias)
    small_ref[16:24, :] = bias
    grads = own[...]
    high = grads.astype(bf16)
    low = (grads - high.astype(f32)).astype(bf16)
    table = lax.broadcasted_iota(jnp.int32, (rows, rows), 0)
    chosen = jnp.where(row_ref[3] == 0, pos_ref[...], -1) == table
    chosen = jnp.where(chosen, 1.0, 0.0).astype(bf16)
    small_ref[24 : 24 + rows, :] = dot_nn(chosen, high) + dot_nn(chosen, low)
    small_ref[24 + rows :, :] = jnp.zeros((small_ref.shape[0] - 24 - rows, width), f32)


def first_grad(
    rows_info, gfirst, pair_grad, hidden, grad_middle, vec, sums, late, up_bias, pos, out_rows
):
    rows, width = hidden.shape
    small = round_up(24 + rows, 128)
    args = (gfirst, pair_grad, hidden, grad_middle, vec, sums, late, up_bias, pos)
    return pl.pallas_call(
        first_grad_kernel,
        in_specs=[SMEM_SPEC] + [whole(arg.shape) for arg in args],
        out_specs=[whole((out_rows, width)), whole((small, width))],
        out_shape=[
            jax.ShapeDtypeStruct((out_rows, width), f32),
            jax.ShapeDtypeStruct((small, width), f32),
        ],
        scratch_shapes=[pltpu.VMEM((rows, width), f32)],
        compiler_params=params(),
        cost_estimate=cost(8),
        name="first_grad",
    )(rows_info, *args)


def widen(values):
    rows, cols = values.shape
    return jnp.concatenate([values, jnp.zeros((rows, PAIR_LANES - cols), f32)], axis=1)


def split_parts(values):
    high = values.astype(bf16)
    return high, (values - high.astype(f32)).astype(bf16)


def left_parts(values):
    return jnp.concatenate(split_parts(values), axis=1)


def right_parts(values):
    high, low = split_parts(values)
    rows, cols = high.shape
    gap = jnp.zeros((cols - rows, cols), bf16)
    near = jnp.concatenate([high, gap, high, gap], axis=0)
    far = jnp.concatenate([low, gap, jnp.zeros((cols, cols), bf16)], axis=0)
    return jnp.concatenate([near, far], axis=1)


def times(left, right):
    both = dot_nn(left, right)
    return both[:, :PAIR_LANES] + both[:, PAIR_LANES:]


def inverse_roots(stats, identity):
    size = stats[0].shape[0]
    mats, factors = [], []
    for stat in stats:
        norm = jnp.sqrt(jnp.sum(stat * stat, keepdims=True))
        mats.append(stat * (1.0 / norm))
        factors.append(lax.rsqrt(jnp.sqrt(norm)))
    for iteration in range(NEWTON):
        steps = [1.25 * identity - 0.25 * mat for mat in mats]
        if iteration == 0:
            factors = [step * factor for step, factor in zip(steps, factors)]
            squares = [times(left_parts(step), right_parts(step)) for step in steps]
        elif iteration < NEWTON - 1:
            both = [
                times(
                    jnp.concatenate([left_parts(step), left_parts(factor)], axis=0),
                    right_parts(step),
                )
                for step, factor in zip(steps, factors)
            ]
            squares = [pair[:size] for pair in both]
            factors = [pair[size:] for pair in both]
        else:
            return [
                times(left_parts(factor), right_parts(step)) for step, factor in zip(steps, factors)
            ]
        fourths = [times(left_parts(square), right_parts(square)) for square in squares]
        mats = [times(left_parts(fourth), right_parts(mat)) for fourth, mat in zip(fourths, mats)]


def shampoo_kernel(group, part, parts, grad_count, earlier, up_ref, *refs):
    grad_refs = refs[:grad_count]
    left_ref, right_ref, w_ref = refs[grad_count : grad_count + 3]
    outs = refs[grad_count + 3 + earlier : grad_count + 7 + earlier]
    results, sems = refs[-2:]
    _, count, size, _ = left_ref.shape
    row = lax.broadcasted_iota(jnp.int32, (size, PAIR_LANES), 0)
    col = lax.broadcasted_iota(jnp.int32, (size, PAIR_LANES), 1)
    identity = (row == col).astype(f32)
    copies = []

    def store(kind, i, at, value):
        results[kind, i] = value
        copy = pltpu.make_async_copy(results.at[kind, i], outs[kind].at[at], sems.at[kind, i])
        copy.start()
        copies.append(copy)

    for base in range(0, count, group):
        places, stats, grads = [], [], []
        for i in range(base, base + group):
            at = jnp.where(up_ref[0] == 1, i * parts + part, part * count + i)
            places.append(at)
            span = slice(i * size, (i + 1) * size)
            grad = grad_refs[0][0, :, span].astype(f32)
            for ref in grad_refs[1:]:
                grad = grad + ref[0, :, span].astype(f32)
            store(0, i, at, grad)
            grad = widen(grad)
            grad_t = widen(jnp.transpose(grad, (1, 0))[:size])
            grads.append(grad)
            outer = times(left_parts(grad), right_parts(grad_t))
            inner = times(left_parts(grad_t), right_parts(grad))
            left_new = stat_decay * left_ref[0, i] + (1.0 - stat_decay) * outer[:, :size]
            right_new = stat_decay * right_ref[0, i] + (1.0 - stat_decay) * inner[:, :size]
            store(1, i, at, left_new)
            store(2, i, at, right_new)
            stats += [widen(left_new), widen(right_new)]
        roots = inverse_roots(stats, identity)
        for i, at in enumerate(places):
            half_way = times(left_parts(roots[2 * i]), right_parts(grads[i]))
            update = times(left_parts(half_way), right_parts(roots[2 * i + 1]))
            store(3, base + i, at, w_ref[0, base + i] - matrix_rate * update[:, :size])
    for copy in copies:
        copy.wait()


def shampoo(is_up, part, at, grad_rows, lefts, rights, weights, earlier=()):
    parts, count, size, _ = lefts.shape
    span = count * size
    blocks = pl.BlockSpec((1, count, size, size), lambda i: (part, 0, 0, 0))
    shape = jax.ShapeDtypeStruct((parts * count, size, size), f32)
    anywhere = pl.BlockSpec(memory_space=pl.ANY)
    first_earlier = 4 + len(grad_rows)
    kernel = functools.partial(
        shampoo_kernel, math.gcd(count, 4), part, parts, len(grad_rows), len(earlier)
    )
    return pl.pallas_call(
        kernel,
        grid=(1,),
        in_specs=[SMEM_SPEC]
        + [pl.BlockSpec((1, size, span), lambda i: (at, 0, 0))] * len(grad_rows)
        + [blocks] * 3
        + [anywhere] * len(earlier),
        out_specs=[anywhere] * 4,
        out_shape=[shape] * 4,
        scratch_shapes=[
            pltpu.VMEM((4, count, size, size), f32),
            pltpu.SemaphoreType.DMA((4, count)),
        ],
        input_output_aliases={first_earlier + i: i for i in range(len(earlier))},
        compiler_params=params(),
        cost_estimate=cost(9),
        name="shampoo",
    )(is_up, *grad_rows, lefts, rights, weights, *earlier)


CORE, Y, Z_LOW, Z_HIGH = 1, 2, 4, 8


def flip(values, bits):
    size = lax.axis_size("dp")
    return lax.ppermute(values, "dp", [(i, i ^ bits) for i in range(size)])


def flip_mod(values):
    return lax.ppermute(values, "mod", [(0, 1), (1, 0)])


def in_order(bit, own, other):
    return jnp.stack([jnp.where(bit == 1, other, own), jnp.where(bit == 1, own, other)])


def place():
    index = lax.axis_index("dp")
    return index % 2, index // 2 % 2, index // 4


def sync(*values):
    return lax.optimization_barrier(values)


def pick(values, index, axis):
    return lax.dynamic_index_in_dim(values, index, axis, keepdims=False)


def plus(left, right):
    return (left.astype(f32) + right.astype(f32)).astype(bf16)


def square_parts(blocks, rows, cols):
    size = blocks.shape[-1]
    shaped = blocks.reshape(rows, cols, size, size)
    return jnp.swapaxes(shaped, 1, 2).reshape(rows, size, cols * size)


def parts_to_blocks(parts):
    rows, size, span = parts.shape
    shaped = parts.reshape(rows, size, span // size, size)
    return jnp.swapaxes(shaped, 1, 2).reshape(-1, size, size)


def local(
    stream_in,
    cotangent,
    patch_count,
    pos_index,
    attn_blocks,
    attn_left,
    attn_right,
    ffn_blocks,
    ffn_left,
    ffn_right,
    vectors,
    vectors_mom,
    ffn_bias,
    ffn_bias_mom,
    pos_table,
    pos_mom,
):
    size = attn_blocks.shape[-1]
    width = vectors.shape[1]
    hidden_units = ffn_bias.shape[1]
    slots = stream_in.shape[2]
    row_blocks = width // size
    chunks = hidden_units // width
    rows = round_up(slots, 16)
    seq = round_up(slots + TEXT, 32)
    by_rows = lax.axis_size("dp") == 16 and attn_blocks.shape[0] == row_blocks
    modality = lax.axis_index("mod")
    is_text = modality == 1
    image_flag = (1 - modality).astype(f32)
    along = lax.axis_index("dp")
    is_up = jnp.where(along < lax.axis_size("dp") // 2, 1, 0).astype(jnp.int32)[None]
    is_not = jnp.zeros((1,), jnp.int32)

    core, y, z = place()
    to_image = [(1, 0)]
    to_text = [(0, 1)]

    if by_rows:
        own_attn = pack_rows(is_not, attn_blocks, row_blocks)[0]
        along_z = [flip(own_attn, bits) for bits in (Z_LOW, Z_HIGH, Z_LOW | Z_HIGH)]
        ffn_rows = pack_rows(is_up, ffn_blocks[0], row_blocks)

    own_vec = lax.dynamic_slice_in_dim(vectors, 3 + 5 * modality, 5, 0)
    vec = jnp.concatenate([own_vec, vectors[0:3]], axis=0)
    up_bias = lax.dynamic_index_in_dim(ffn_bias, modality, 0, keepdims=False)
    up_bias = jnp.swapaxes(up_bias.reshape(row_blocks, chunks, size), 0, 1).reshape(1, hidden_units)
    count = patch_count[0]
    offset = TEXT * (1 - modality)
    first_key = jnp.where(is_text, TEXT, 0)
    end_key = jnp.where(is_text, slots, TEXT + count)
    kept_rows = jnp.where(is_text, slots, count)
    own_core = core if by_rows else 0 * along
    rows_info = jnp.stack([offset, first_key, end_key, modality, kept_rows, own_core])
    rows_info = rows_info.astype(jnp.int32)
    pad = ((0, rows - slots), (0, 0))
    hidden = stream_in[0, 0] + image_flag * jnp.take(pos_table, pos_index[0], axis=0)
    hidden = jnp.pad(hidden, pad)
    pos = jnp.pad(pos_index[0], pad[0], constant_values=-1)[None]
    if by_rows:
        along_z, ffn_rows, hidden, cotangent = sync(along_z, ffn_rows, hidden, cotangent)
        ffn_parts = lax.all_gather(ffn_rows, "dp", axis=0, tiled=True)
        ffn_parts = ffn_parts.reshape(2, row_blocks, chunks, size, width)
        near = in_order(z % 2, own_attn, along_z[0])
        far = in_order(z % 2, along_z[1], along_z[2])
        attn_z = in_order(z // 2, near, far).reshape(4, size, width)
        upper, lower = attn_z[:, : size // 2], attn_z[:, size // 2 :]
        upper_y, lower_x = flip(upper, Y), flip_mod(lower)
    first = first_norm(rows_info, hidden, vec, seq)
    pair_first = lax.ppermute(first[:TEXT], "mod", to_image)
    if by_rows:
        upper_y, lower_x, first, pair_first, cotangent = sync(
            upper_y, lower_x, first, pair_first, cotangent
        )
        upper, lower = in_order(y, upper, upper_y), in_order(modality, lower, lower_x)
        upper_x, lower_y = flip_mod(upper), flip(lower, Y)
    first = lax.dynamic_update_slice(first, jnp.where(is_text, first[:TEXT], pair_first), (0, 0))
    cot = jnp.pad(cotangent[0, 0], pad)

    def by_parts(blocks):
        by_chunk = blocks.reshape(chunks, -1, size, size)
        spread = jnp.swapaxes(blocks.reshape(-1, chunks, size, size), 0, 1)
        return jnp.where(is_up[0] == 1, spread, by_chunk)

    if by_rows:
        ffn_old = [by_parts(part[0]) for part in (ffn_left, ffn_right, ffn_blocks)]
        upper_x, lower_y, first, cot, ffn_old = sync(upper_x, lower_y, first, cot, ffn_old)
        upper, lower = in_order(modality, upper, upper_x), in_order(y, lower, lower_y)
        attn_parts = [upper, flip(upper, CORE), lower, flip(lower, CORE)]
    else:
        attn_all = lax.all_gather(attn_blocks.astype(bf16), ("mod", "dp"), axis=0, tiled=True)
        attn_parts = [square_parts(attn_all, 4 * row_blocks, row_blocks).reshape(4, width, width)]
        ffn_all = lax.all_gather(ffn_blocks[0].astype(bf16), "dp", axis=0, tiled=True)
        shape = (2, row_blocks, row_blocks, chunks, size, size)
        up = ffn_all.reshape(shape)[0].transpose(0, 2, 3, 1, 4)
        down = ffn_all.reshape(2, row_blocks, chunks, row_blocks, size, size)[1]
        down = down.transpose(0, 1, 3, 2, 4)
        ffn_parts = jnp.stack([p.reshape(row_blocks, chunks, size, width) for p in (up, down)])

    qkv, w_attn = project(rows_info, first, vec, attn_parts)
    ctx, lse, pair_ctx = attend(rows_info, qkv)
    pair_ctx = lax.ppermute(pair_ctx, "mod", to_text)
    *kept, grad_1, late_vec, up_bias_grad_1 = expert_begin(
        rows_info, ctx, pair_ctx, hidden, cot, vec, up_bias, w_attn, ffn_parts
    )
    ended = expert_end(rows_info, kept, late_vec, cot, vec, up_bias, w_attn, ffn_parts, seq, slots)
    stream_out, grad_middle, grad_ctx, pair_grad, grad_wo, keep_2, send_2, late_vec, up_bias_grad_2 = ended
    pair_grad = lax.ppermute(pair_grad, "mod", to_image)

    def along_z_of(parts):
        return [flip(part, bits * Z_LOW) for bits, part in enumerate(parts) if bits]

    if by_rows:
        ffn_1 = lax.psum_scatter(
            grad_1.reshape(-1, chunks // 2, size, width), "dp", scatter_dimension=0, tiled=True
        )[0]
        got_2 = flip(send_2, CORE)
        pair_grad, got_2, grad_ctx = sync(pair_grad, got_2, grad_ctx)
        both = plus(keep_2, got_2).reshape((4, 2) + keep_2.shape[2:])
        keep_2, send_2, grad_ctx = sync(pick(both, y, 1), pick(both, 1 - y, 1), grad_ctx)
        got_2 = flip(send_2, Y)
    grad_qkv = attend_grad(rows_info, qkv, grad_ctx, pair_grad, lse)
    if by_rows:
        got_2, grad_qkv = sync(got_2, grad_qkv)
        both = plus(keep_2, got_2)
        ffn_2 = [pick(both, z ^ bits, 0) for bits in range(4)]
        ffn_2, grad_qkv = sync(ffn_2, grad_qkv)
        got_2 = along_z_of(ffn_2)
    projected = project_grad(rows_info, grad_qkv, first, w_attn, grad_wo, size)
    if by_rows:
        projected, ffn_1, got_2 = sync(projected, ffn_1, got_2)
    attn_keep, attn_send, grad_first, pair_first_grad, sums = projected
    pair_first_grad = lax.ppermute(pair_first_grad, "mod", to_text)
    up_bias_grad = jnp.concatenate([up_bias_grad_1, up_bias_grad_2], axis=1)
    up_bias_grad = jnp.swapaxes(up_bias_grad.reshape(chunks, row_blocks, size), 0, 1)
    if by_rows:
        attn_got = flip(attn_send, CORE)
        attn_got, pair_first_grad = sync(attn_got, pair_first_grad)
        both = plus(attn_keep, attn_got).reshape(2, 4, 2, size, width)
        upper, lower = both[..., : size // 2, :], both[..., size // 2 :, :]
        upper_keep, upper_send = pick(upper, modality, 0), pick(upper, 1 - modality, 0)
        lower_keep, lower_send = pick(lower, y, 2), pick(lower, 1 - y, 2)
        upper_keep, upper_send, lower_keep, lower_send, pair_first_grad = sync(
            upper_keep, upper_send, lower_keep, lower_send, pair_first_grad
        )
        upper_got, lower_got = flip_mod(upper_send), flip(lower_send, Y)
    stream_grad, small = first_grad(
        rows_info,
        grad_first,
        pair_first_grad,
        hidden,
        grad_middle,
        vec,
        sums,
        late_vec,
        up_bias_grad.reshape(chunks, width),
        pos,
        slots,
    )
    if by_rows:
        small = small.astype(bf16).reshape(2, 2, 4, -1, width)
        small_keep, small_send = pick(small, core, 0), pick(small, 1 - core, 0)
        small_got = flip(small_send, CORE)
        upper_got, lower_got, small_got = sync(upper_got, lower_got, small_got)
        upper, lower = plus(upper_keep, upper_got), plus(lower_keep, lower_got)
        upper_keep, upper_send = pick(upper, y, 1), pick(upper, 1 - y, 1)
        lower_keep, lower_send = pick(lower, modality, 0), pick(lower, 1 - modality, 0)
        small = plus(small_keep, small_got)
        small_keep, small_send = pick(small, y, 0), pick(small, 1 - y, 0)
        small_keep, small_send, upper_keep, upper_send, lower_keep, lower_send, ffn_1 = sync(
            small_keep, small_send, upper_keep, upper_send, lower_keep, lower_send, ffn_1
        )
        upper_got, lower_got = flip(upper_send, Y), flip_mod(lower_send)
        small_got = flip(small_send, Y)
        ffn_new = shampoo(is_up, 0, 0, [ffn_1], *ffn_old)
        ffn_new, small_got, upper_got, lower_got = sync(ffn_new, small_got, upper_got, lower_got)
        attn = jnp.concatenate([plus(upper_keep, upper_got), plus(lower_keep, lower_got)], axis=1)
        attn_z = [pick(attn, z ^ bits, 0) for bits in range(4)]
        small = plus(small_keep, small_got)
        small_z = [pick(small, z ^ bits, 0) for bits in range(4)]
        small_z, attn_z, ffn_new = sync(small_z, attn_z, ffn_new)
        attn_got = along_z_of(attn_z)
        small_got = along_z_of(small_z)
        ffn_new = shampoo(is_up, 1, 1, [ffn_1], *ffn_old, ffn_new)
        ffn_new, small_got = sync(ffn_new, small_got)
        small = sum(part.astype(f32) for part in (small_z[0], *small_got))
        small, ffn_new = sync(small, ffn_new)
        small_got = flip_mod(small)
        ffn_new = shampoo(is_up, 2, 0, [ffn_2[0], *got_2], *ffn_old, ffn_new)
        ffn_new, small_got = sync(ffn_new, small_got)
        small = (small + small_got).astype(bf16)
        small, ffn_new = sync(small, ffn_new)
        small_got = [flip(small, bits * Z_LOW) for bits in (1, 2, 3)]
        ffn_out = shampoo(is_up, 3, 1, [ffn_2[0], *got_2], *ffn_old, ffn_new)
        small_got, attn_got, ffn_out = sync(small_got, attn_got, ffn_out)
        near = in_order(z % 2, small, small_got[0])
        far = in_order(z % 2, small_got[1], small_got[2])
        small = in_order(z // 2, near, far)
        small, attn_got = sync(small, attn_got)
        small_got = flip(small, Y)
        attn_rows = [part[None] for part in (attn_z[0], *attn_got)]
        attn_old = [part[None] for part in (attn_left, attn_right, attn_blocks)]
        attn_out = shampoo(is_not, 0, 0, attn_rows, *attn_old)
        small_got, attn_out = sync(small_got, attn_out)
        small = in_order(y, small, small_got)
        small_sum = in_order(core, small, flip(small, CORE)).astype(f32).reshape(-1, width)
    else:
        grad_2 = jnp.stack([keep_2, send_2], axis=2).reshape(grad_1.shape)
        grads = jnp.concatenate([grad_1, grad_2], axis=2)
        up = grads[0].reshape(row_blocks, chunks, size, row_blocks, size)
        down = grads[1].reshape(row_blocks, chunks, size, row_blocks, size)
        up = up.transpose(0, 3, 1, 2, 4).reshape(-1, size, size)
        down = down.transpose(0, 1, 3, 2, 4).reshape(-1, size, size)
        ffn_sum = lax.psum_scatter(
            jnp.concatenate([up, down], axis=0), "dp", scatter_dimension=0, tiled=True
        )
        attn_full = jnp.stack([attn_keep, attn_send], axis=2).reshape(-1, size, width)
        attn_sum = lax.psum_scatter(
            parts_to_blocks(attn_full), ("mod", "dp"), scatter_dimension=0, tiled=True
        )
        small_sum = lax.psum(small, ("mod", "dp"))
        ffn_old = [part for part in (ffn_left, ffn_right, ffn_blocks)]
        attn_old = [part[None] for part in (attn_left, attn_right, attn_blocks)]
        ffn_out = shampoo(is_not, 0, 0, [square_parts(ffn_sum, 1, ffn_sum.shape[0])], *ffn_old)
        attn_out = shampoo(is_not, 0, 0, [square_parts(attn_sum, 1, attn_sum.shape[0])], *attn_old)

    items_total = lax.axis_size("dp")
    vector_rate = 0.3 / math.sqrt(items_total * slots)
    pos_rate = 0.5 / math.sqrt(items_total)
    vectors_mom_new = moment_keep * vectors_mom + small_sum[: vectors.shape[0]]
    vectors_new = vectors - vector_rate * vectors_mom_new
    ffn_bias_mom_new = moment_keep * ffn_bias_mom + small_sum[16:24].reshape(ffn_bias.shape)
    ffn_bias_new = ffn_bias - vector_rate * ffn_bias_mom_new
    pos_mom_new = moment_keep * pos_mom + small_sum[24 : 24 + slots]
    pos_new = pos_table - pos_rate * pos_mom_new
    return (
        stream_out[None, None],
        stream_grad[None, None],
        *attn_out,
        *(part[None] for part in ffn_out),
        vectors_mom_new,
        vectors_new,
        ffn_bias_mom_new,
        ffn_bias_new,
        pos_mom_new,
        pos_new,
    )


def solution(mesh):
    items = P("mod", "dp", None, None)
    owned = P(("mod", "dp"), None, None)
    return jax.shard_map(
        local,
        mesh=mesh,
        in_specs=(items, items, P("dp"), P("dp", None), owned, owned, owned, items, items, items)
        + (P(),) * 6,
        out_specs=(items, items, owned, owned, owned, owned, items, items, items, items)
        + (P(),) * 6,
        check_vma=False,
    )
```

```python
import functools
import math

import jax
import jax.numpy as jnp
from jax import lax
from jax.experimental import pallas as pl
from jax.experimental.pallas import tpu as pltpu
from jax.sharding import PartitionSpec as P

HEADS = 12
TEXT = 64
NEWTON = 6
PAIR_LANES = 128
QUERY_TILE = 336
GRAD_TILE = 256

f32 = jnp.float32
bf16 = jnp.bfloat16
norm_eps = 1e-05
stat_decay = 0.5
matrix_rate = 0.25
moment_keep = 0.9
masked_score = -1e30


def dot_nn(left, right):
    return lax.dot_general(left, right, (((1,), (0,)), ((), ())), preferred_element_type=f32)


def dot_nt(left, right):
    return lax.dot_general(left, right, (((1,), (1,)), ((), ())), preferred_element_type=f32)


def dot_tn(left, right):
    return lax.dot_general(left, right, (((0,), (0,)), ((), ())), preferred_element_type=f32)


def params(mebibytes=56):
    return pltpu.CompilerParams(vmem_limit_bytes=mebibytes << 20)


def cost(microseconds):
    return pl.CostEstimate(flops=int(microseconds), bytes_accessed=0, transcendentals=0)


def round_up(value, step):
    return (value + step - 1) // step * step


def whole(shape):
    return pl.BlockSpec(shape, lambda *ids: (0,) * len(shape))


SMEM_SPEC = pl.BlockSpec(memory_space=pltpu.SMEM)


def pack_kernel(up_ref, blocks_ref, out_ref):
    part = pl.program_id(0)
    parts = pl.num_programs(0)
    per_row = blocks_ref.shape[0] // parts
    pieces = []
    for i in range(per_row):
        at = jnp.where(up_ref[0] == 1, i * parts + part, part * per_row + i)
        pieces.append(blocks_ref[at])
    out_ref[0] = jnp.concatenate(pieces, axis=1).astype(bf16)


def pack_rows(is_up, blocks, per_row):
    count, size, _ = blocks.shape
    return pl.pallas_call(
        pack_kernel,
        grid=(count // per_row,),
        in_specs=[SMEM_SPEC, whole(blocks.shape)],
        out_specs=pl.BlockSpec((1, size, per_row * size), lambda i: (i, 0, 0)),
        out_shape=jax.ShapeDtypeStruct((count // per_row, size, per_row * size), bf16),
        compiler_params=params(),
        cost_estimate=cost(3),
        name="pack_rows",
    )(is_up, blocks)


def norm_rows(values):
    centred = values - jnp.mean(values, axis=-1, keepdims=True)
    spread = jnp.mean(centred * centred, axis=-1, keepdims=True)
    inv_std = lax.rsqrt(spread + norm_eps)
    return centred * inv_std, inv_std


def norm_input_grad(grad_out, normal, inv_std, gain):
    grad_norm = grad_out * gain
    mean_grad = jnp.mean(grad_norm, axis=-1, keepdims=True)
    mean_proj = jnp.mean(grad_norm * normal, axis=-1, keepdims=True)
    return inv_std * (grad_norm - mean_grad - normal * mean_proj)


def first_norm_kernel(row_ref, hidden_ref, vec_ref, first_ref):
    rows = hidden_ref.shape[0]
    normal, _ = norm_rows(hidden_ref[...])
    first_ref[...] = jnp.zeros(first_ref.shape, bf16)
    first = normal * vec_ref[0:1, :] + vec_ref[1:2, :]
    first_ref[pl.ds(pl.multiple_of(row_ref[0], 16), rows), :] = first.astype(bf16)


def first_norm(rows_info, hidden, vec, seq):
    return pl.pallas_call(
        first_norm_kernel,
        in_specs=[SMEM_SPEC, whole(hidden.shape), whole(vec.shape)],
        out_specs=whole((seq, hidden.shape[1])),
        out_shape=jax.ShapeDtypeStruct((seq, hidden.shape[1]), bf16),
        compiler_params=params(),
        cost_estimate=cost(4),
        name="first_norm",
    )(rows_info, hidden, vec)


def project_kernel(row_ref, first_ref, vec_ref, *refs):
    weight_refs, (qkv_ref, w_ref) = refs[:-2], refs[-2:]
    step = pl.program_id(0)
    if len(weight_refs) == 1:
        w_ref[...] = weight_refs[0][...]
    else:
        upper, upper_far, lower, lower_far = weight_refs
        half, size = upper.shape[3], 2 * upper.shape[3]
        on_one = row_ref[5] == 1
        for z in range(2):
            for y in range(2):
                for base, near, far in (
                    (0, upper[0, y, z], upper_far[0, y, z]),
                    (half, lower[y, 0, z], lower_far[y, 0, z]),
                ):
                    start = (4 * z + 2 * y) * size + base
                    w_ref[0, start : start + half, :] = jnp.where(on_one, far, near)
                    start += size
                    w_ref[0, start : start + half, :] = jnp.where(on_one, near, far)

    @pl.when(step < 3)
    def _():
        bias = jnp.where(step == 0, vec_ref[5:6, :], jnp.where(step == 2, vec_ref[6:7, :], 0.0))
        qkv_ref[...] = (dot_nn(first_ref[...], w_ref[0]) + bias).astype(bf16)


def project(rows_info, first, vec, attn_parts):
    seq, width = first.shape
    if len(attn_parts) == 1:
        weight_specs = [pl.BlockSpec((1, width, width), lambda i: (i, 0, 0))]
    else:
        half = attn_parts[0].shape[3]
        upper = pl.BlockSpec((1, 2, 2, half, width), lambda i: (i // 2, 0, i % 2, 0, 0))
        lower = pl.BlockSpec((2, 1, 2, half, width), lambda i: (0, i // 2, i % 2, 0, 0))
        weight_specs = [upper, upper, lower, lower]
    return pl.pallas_call(
        project_kernel,
        grid=(4,),
        in_specs=[SMEM_SPEC, whole((seq, width)), whole(vec.shape), *weight_specs],
        out_specs=[
            pl.BlockSpec((seq, width), lambda i: (0, jnp.minimum(i, 2))),
            pl.BlockSpec((1, width, width), lambda i: (i, 0, 0)),
        ],
        out_shape=[
            jax.ShapeDtypeStruct((seq, 3 * width), bf16),
            jax.ShapeDtypeStruct((4, width, width), bf16),
        ],
        compiler_params=params(),
        cost_estimate=cost(8),
        name="project",
    )(rows_info, first, vec, *attn_parts)


def key_bias(row_ref, seq):
    rows = lax.broadcasted_iota(jnp.int32, (seq, 1), 0)
    counts = jnp.logical_and(rows >= row_ref[1], rows < row_ref[2])
    return jnp.where(counts, 0.0, masked_score).astype(f32)


def transposed(values):
    return jnp.transpose(values.astype(f32), (1, 0)).astype(bf16)


def attend_kernel(row_ref, q_ref, k_ref, v_ref, ctx_ref, lse_ref, pair_ref):
    seq = q_ref.shape[0]
    half = PAIR_LANES // 2
    scale = half ** (-0.5)
    lane = lax.broadcasted_iota(jnp.int32, (seq, PAIR_LANES), 1)
    bias = key_bias(row_ref, seq).astype(bf16)
    queries = q_ref[...] * jnp.asarray(scale, bf16)
    keys = k_ref[...]
    values = v_ref[...]
    one = jnp.ones((seq, PAIR_LANES), bf16)
    heads = []
    for head in range(2):
        own = (lane < half) == (head == 0)
        spare = lane == half * (1 - head)
        head_q = jnp.where(own, queries, jnp.where(spare, one, jnp.zeros_like(one)))
        head_k = jnp.where(own, keys, jnp.where(spare, bias, jnp.zeros_like(one)))
        head_v = jnp.where(own, values, one)
        heads.append((head_q, head_k, head_v))
    for start in range(0, seq, QUERY_TILE):
        size = min(QUERY_TILE, seq - start)
        tile = slice(start, start + size)
        parts, lses = [], []
        for head, (head_q, head_k, head_v) in enumerate(heads):
            scores = dot_nt(head_q[tile], head_k)
            top = jnp.max(scores, axis=1, keepdims=True)
            raised = jnp.exp(scores - top).astype(bf16)
            summed = dot_nn(raised, head_v)
            at = half * (1 - head)
            total = summed[:, at : at + 1]
            parts.append(summed * (1.0 / total))
            lses.append(top + jnp.log(total))
        low = lax.broadcasted_iota(jnp.int32, (size, PAIR_LANES), 1) < half
        context = jnp.where(low, parts[0], parts[1]).astype(bf16)
        ctx_ref[tile, :] = context
        if start == 0:
            pair_ref[...] = context[: pair_ref.shape[0]]
        lane8 = lax.broadcasted_iota(jnp.int32, (size, 8), 1)
        lse_ref[0, tile, :] = jnp.where(lane8 == 0, lses[0], lses[1])


def attend(rows_info, qkv):
    seq = qkv.shape[0]
    width = qkv.shape[1] // 3
    pairs = width // PAIR_LANES

    def column(base):
        return pl.BlockSpec((seq, PAIR_LANES), lambda i, base=base: (0, base + i))

    return pl.pallas_call(
        attend_kernel, grid=(pairs,),
        in_specs=[SMEM_SPEC, column(0), column(pairs), column(2 * pairs)],
        out_specs=[column(0), pl.BlockSpec((1, seq, 8), lambda i: (i, 0, 0)), pl.BlockSpec((TEXT, PAIR_LANES), lambda i: (0, i))],
        out_shape=[jax.ShapeDtypeStruct((seq, width), bf16), jax.ShapeDtypeStruct((pairs, seq, 8), f32), jax.ShapeDtypeStruct((TEXT, width), bf16)],
        compiler_params=params(), cost_estimate=cost(12), name="attend",
    )(rows_info, qkv, qkv, qkv)


def three_parts(values):
    high = values.astype(bf16)
    rest = values - high.astype(f32)
    middle = rest.astype(bf16)
    return high, middle, (rest - middle.astype(f32)).astype(bf16)


def attend_grad_kernel(
    row_ref, q_ref, k_ref, v_ref, g_ref, pair_ref, ctx_ref, lse_ref, out_ref, dk_ref, dv_ref
):
    seq = q_ref.shape[0]
    half = PAIR_LANES // 2
    scale = half ** (-0.5)
    lane = lax.broadcasted_iota(jnp.int32, (seq, PAIR_LANES), 1)
    bias = key_bias(row_ref, seq).astype(bf16)
    queries = q_ref[...]
    scaled = queries * jnp.asarray(scale, bf16)
    keys = k_ref[...]
    values = v_ref[...]
    keys_t = transposed(keys)
    row = lax.broadcasted_iota(jnp.int32, (seq, 1), 0)
    counts = jnp.logical_and(row >= row_ref[1], row < row_ref[2])
    grads = jnp.concatenate([pair_ref[...], g_ref[pair_ref.shape[0] :, :]], axis=0)
    grads = jnp.where(counts, grads, jnp.zeros((seq, PAIR_LANES), bf16))
    products = grads.astype(f32) * ctx_ref[...].astype(f32)
    one = jnp.ones((seq, PAIR_LANES), bf16)
    zero = jnp.zeros((seq, PAIR_LANES), bf16)
    heads = []
    for head in range(2):
        own = (lane < half) == (head == 0)
        spare = lane - half * (1 - head)
        lse = three_parts(-lse_ref[0, :, head : head + 1])
        dots = three_parts(-jnp.sum(jnp.where(own, products, 0.0), axis=1, keepdims=True))
        own_q = jnp.where(own, queries, zero)
        own_g = jnp.where(own, grads, zero)
        head_q = jnp.where(own, scaled, jnp.where(spare == 3, one, zero))
        head_g = own_g
        for i in range(3):
            head_q = jnp.where(spare == i, lse[i], head_q)
            head_g = jnp.where(spare == i, dots[i], head_g)
        head_k = jnp.where(own, keys, jnp.where(spare == 3, bias, one))
        head_v = jnp.where(own, values, one)
        heads.append((head_q, head_g, head_k, head_v, own_q, own_g))
    for start in range(0, seq, GRAD_TILE):
        size = min(GRAD_TILE, seq - start)
        tile = slice(start, start + size)
        parts = []
        for head, (head_q, head_g, head_k, head_v, own_q, own_g) in enumerate(heads):
            probs = jnp.exp(dot_nt(head_k, head_q[tile]))
            grad_scores = (probs * dot_nt(head_v, head_g[tile])).astype(bf16)
            grad_v = dot_nn(probs.astype(bf16), own_g[tile])
            grad_k = dot_nn(grad_scores, own_q[tile])
            if start == 0 and head == 0:
                dv_ref[...] = grad_v
                dk_ref[...] = grad_k
            else:
                dv_ref[...] += grad_v
                dk_ref[...] += grad_k
            parts.append(dot_nn(keys_t[half * head : half * (head + 1), :], grad_scores))
        grad_q = jnp.transpose(jnp.concatenate(parts, axis=0) * scale, (1, 0))
        out_ref[0, tile, :] = grad_q.astype(bf16)
    out_ref[1] = (dk_ref[...] * scale).astype(bf16)
    out_ref[2] = dv_ref[...].astype(bf16)


def attend_grad(rows_info, qkv, grad_ctx, pair_grad, ctx, lse):
    seq = qkv.shape[0]
    width = qkv.shape[1] // 3
    pairs = width // PAIR_LANES

    def column(base):
        return pl.BlockSpec((seq, PAIR_LANES), lambda i, base=base: (0, base + i))

    return pl.pallas_call(
        attend_grad_kernel,
        grid=(pairs,),
        in_specs=[
            SMEM_SPEC,
            column(0),
            column(pairs),
            column(2 * pairs),
            column(0),
            pl.BlockSpec((TEXT, PAIR_LANES), lambda i: (0, i)),
            column(0),
            pl.BlockSpec((1, seq, 8), lambda i: (i, 0, 0)),
        ],
        out_specs=pl.BlockSpec((3, seq, PAIR_LANES), lambda i: (0, 0, i)),
        out_shape=jax.ShapeDtypeStruct((3, seq, width), bf16),
        scratch_shapes=[pltpu.VMEM((seq, PAIR_LANES), f32)] * 2,
        compiler_params=params(),
        cost_estimate=cost(15),
        name="attend_grad",
    )(rows_info, qkv, qkv, qkv, grad_ctx, pair_grad, ctx, lse)


def gelu_pair(values):
    size = jnp.abs(values)
    tail = 1.0 / (1.0 + (0.3275911 * 0.5**0.5) * size)
    poly = tail * (
        0.254829592
        + tail * (-0.284496736 + tail * (1.421413741 + tail * (-1.453152027 + tail * 1.061405429)))
    )
    bell = jnp.exp(-0.5 * values * values)
    upper = 0.5 * poly * bell
    share = jnp.where(values >= 0.0, 1.0 - upper, upper)
    return values * share, share + values * bell * ((2.0 * math.pi) ** -0.5)


def split_by_core(row_ref, grad, shape):
    size, width = shape[-2:]
    blocks = grad.reshape(-1, 2, size, width)
    near, far = blocks[:, 0], blocks[:, 1]
    on_one = row_ref[5] == 1
    return jnp.where(on_one, far, near).reshape(shape), jnp.where(on_one, near, far).reshape(shape)


def expert_chunk(
    second, gbranch, upb, up_ref, down_ref, grad_ref, dupb_ref, branch, gsecond, scratch, begin
):
    pre, gact, act, gpre = scratch
    rows, width = act.shape
    tile = 16
    up = up_ref[...].reshape(width, width)
    down = down_ref[...].reshape(width, width)
    pre[...] = dot_nn(second[...], up)
    gact[...] = dot_nt(gbranch[...], down)

    def body(i, total):
        at = pl.ds(pl.multiple_of(i * tile, tile), tile)
        value, slope = gelu_pair(pre[at, :] + upb[...])
        act[at, :] = value.astype(bf16)
        rounded = (gact[at, :] * slope).astype(bf16)
        gpre[at, :] = rounded
        return total + rounded.astype(f32)

    total = lax.fori_loop(0, rows // tile, body, jnp.zeros((tile, width), f32), unroll=True)
    dupb_ref[...] = jnp.sum(total, axis=0, keepdims=True)
    for which, grad in enumerate(
        (dot_tn(second[...], gpre[...]), dot_tn(act[...], gbranch[...]))
    ):
        grad_ref[which] = grad.astype(bf16).reshape(grad_ref.shape[1:])
    own_branch = dot_nn(act[...], down)
    own_gsecond = dot_nt(gpre[...], up)

    @pl.when(begin)
    def _():
        branch[...] = own_branch
        gsecond[...] = own_gsecond

    @pl.when(jnp.logical_not(begin))
    def _():
        branch[...] += own_branch
        gsecond[...] += own_gsecond


def expert_kernel(
    row_ref,
    ctx_ref,
    pair_ref,
    hidden_ref,
    cot_ref,
    vec_ref,
    upb_ref,
    wo_ref,
    up_ref,
    down_ref,
    out_ref,
    gmid_ref,
    gctx_ref,
    pair_grad_ref,
    dwo_ref,
    grad_ref,
    dvec_ref,
    dupb_ref,
    own_ctx,
    middle,
    second,
    gbranch,
    branch,
    gsecond,
    *scratch,
):
    step = pl.program_id(0)
    rows, width = hidden_ref.shape
    out_rows = out_ref.shape[0]
    tile = 16

    @pl.when(step == 0)
    def _():
        own_ctx[...] = ctx_ref[pl.ds(pl.multiple_of(row_ref[0], 16), rows), :]

        @pl.when(row_ref[3] == 1)
        def _():
            own_ctx[0 : pair_ref.shape[0], :] = pair_ref[...]

        middle[...] = dot_nn(own_ctx[...], wo_ref[0])

        def body(i, total):
            at = pl.ds(pl.multiple_of(i * tile, tile), tile)
            mid = hidden_ref[at, :] + (middle[at, :] + vec_ref[7:8, :])
            middle[at, :] = mid
            normal, _ = norm_rows(mid)
            second[at, :] = (normal * vec_ref[2:3, :] + vec_ref[3:4, :]).astype(bf16)
            row = lax.broadcasted_iota(jnp.int32, (tile, 1), 0) + i * tile
            kept = jnp.where(row < row_ref[4], cot_ref[at, :], 0.0)
            rounded = kept.astype(bf16)
            gbranch[at, :] = rounded
            return total + rounded.astype(f32)

        total = lax.fori_loop(
            0, rows // tile, body, jnp.zeros((tile, width), f32), unroll=True
        )
        dvec_ref[...] = jnp.zeros(dvec_ref.shape, f32)
        dvec_ref[2:3, :] = jnp.sum(total, axis=0, keepdims=True)

    expert_chunk(
        second,
        gbranch,
        upb_ref,
        up_ref,
        down_ref,
        grad_ref,
        dupb_ref,
        branch,
        gsecond,
        scratch,
        step == 0,
    )

    @pl.when(step == pl.num_programs(0) - 1)
    def _():
        def body(i, totals):
            at = pl.ds(pl.multiple_of(i * tile, tile), tile)
            mid = middle[at, :]
            normal, inv_std = norm_rows(mid)
            grad_out = gsecond[at, :]
            row = lax.broadcasted_iota(jnp.int32, (tile, 1), 0) + i * tile
            kept = row < row_ref[4]
            branch[at, :] = jnp.where(kept, mid + (branch[at, :] + vec_ref[4:5, :]), 0.0)
            grad_in = norm_input_grad(grad_out, normal, inv_std, vec_ref[2:3, :])
            grad_mid = jnp.where(kept, cot_ref[at, :], 0.0) + grad_in
            gmid_ref[at, :] = grad_mid
            rounded = grad_mid.astype(bf16)
            gbranch[at, :] = rounded
            return (
                totals[0] + grad_out * normal,
                totals[1] + grad_out,
                totals[2] + rounded.astype(f32),
            )

        zero = jnp.zeros((tile, width), f32)
        gains, shifts, biases = lax.fori_loop(
            0, rows // tile, body, (zero, zero, zero), unroll=True
        )
        dvec_ref[0:1, :] = jnp.sum(gains, axis=0, keepdims=True)
        dvec_ref[1:2, :] = jnp.sum(shifts, axis=0, keepdims=True)
        dvec_ref[3:4, :] = jnp.sum(biases, axis=0, keepdims=True)
        out_ref[...] = branch[0:out_rows, :].reshape(out_ref.shape)
        dwo_ref[...] = dot_tn(own_ctx[...], gbranch[...]).astype(bf16)
        grad_ctx = dot_nt(gbranch[...], wo_ref[0]).astype(bf16)
        gctx_ref[...] = jnp.zeros(gctx_ref.shape, bf16)
        gctx_ref[pl.ds(pl.multiple_of(row_ref[0], 16), rows), :] = grad_ctx
        pair_grad_ref[...] = grad_ctx[: pair_grad_ref.shape[0]]


def expert(rows_info, ctx, pair_ctx, hidden, cot, vec, up_bias, w_attn, ffn_parts, out_rows):
    rows, width = hidden.shape
    seq = ctx.shape[0]
    _, row_blocks, chunks, size, _ = ffn_parts.shape

    def weights(which):
        return pl.BlockSpec((1, row_blocks, 1, size, width), lambda i: (which, 0, i, 0, 0))

    return pl.pallas_call(
        expert_kernel,
        grid=(chunks,),
        in_specs=[
            SMEM_SPEC,
            whole(ctx.shape),
            whole(pair_ctx.shape),
            whole(hidden.shape),
            whole(cot.shape),
            whole(vec.shape),
            pl.BlockSpec((1, width), lambda i: (0, i)),
            pl.BlockSpec((1, width, width), lambda i: (3, 0, 0)),
            weights(0),
            weights(1),
        ],
        out_specs=[
            whole((out_rows, 1, width)),
            whole((rows, width)),
            whole((seq, width)),
            whole((TEXT, width)),
            whole((width, width)),
            pl.BlockSpec((2, row_blocks, 1, size, width), lambda i: (0, 0, i, 0, 0)),
            whole((8, width)),
            pl.BlockSpec((1, width), lambda i: (0, i)),
        ],
        out_shape=[
            jax.ShapeDtypeStruct((out_rows, 1, width), f32),
            jax.ShapeDtypeStruct((rows, width), f32),
            jax.ShapeDtypeStruct((seq, width), bf16),
            jax.ShapeDtypeStruct((TEXT, width), bf16),
            jax.ShapeDtypeStruct((width, width), bf16),
            jax.ShapeDtypeStruct(ffn_parts.shape, bf16),
            jax.ShapeDtypeStruct((8, width), f32),
            jax.ShapeDtypeStruct((1, chunks * width), f32),
        ],
        scratch_shapes=[
            pltpu.VMEM((rows, width), bf16),
            pltpu.VMEM((rows, width), f32),
            pltpu.VMEM((rows, width), bf16),
            pltpu.VMEM((rows, width), bf16),
            pltpu.VMEM((rows, width), f32),
            pltpu.VMEM((rows, width), f32),
            pltpu.VMEM((rows, width), f32),
            pltpu.VMEM((rows, width), f32),
            pltpu.VMEM((rows, width), bf16),
            pltpu.VMEM((rows, width), bf16),
        ],
        compiler_params=params(),
        cost_estimate=cost(43),
        name="expert",
    )(rows_info, ctx, pair_ctx, hidden, cot, vec, up_bias, w_attn, ffn_parts, ffn_parts)


def project_grad_kernel(
    row_ref, dqkv_ref, first_ref, w_ref, dwo_ref, keep_ref, send_ref, gfirst, pair_ref, sums_ref
):
    step = pl.program_id(0)

    def put(grad):
        keep_ref[0], send_ref[0] = split_by_core(row_ref, grad, keep_ref.shape[1:])

    @pl.when(step < 3)
    def _():
        own = dqkv_ref[0]
        put(dot_tn(first_ref[...], own).astype(bf16))
        share = dot_nt(own, w_ref[0])
        sums = jnp.sum(own.astype(f32), axis=0, keepdims=True)

        @pl.when(step == 0)
        def _():
            gfirst[...] = share
            sums_ref[...] = jnp.zeros(sums_ref.shape, f32)
            sums_ref[0:1, :] = sums

        @pl.when(step > 0)
        def _():
            gfirst[...] += share
            sums_ref[1:2, :] = sums

    @pl.when(step == 3)
    def _():
        put(dwo_ref[...])
        pair_ref[...] = gfirst[0 : pair_ref.shape[0], :]


def project_grad(rows_info, dqkv, first, w_attn, grad_wo, size):
    seq, width = first.shape
    pairs = width // size // 2
    part = pl.BlockSpec((1, pairs, size, width), lambda i: (i, 0, 0, 0))

    def early_index(i):
        return (jnp.minimum(i, 2), 0, 0)

    return pl.pallas_call(
        project_grad_kernel,
        grid=(4,),
        in_specs=[
            SMEM_SPEC,
            pl.BlockSpec((1, seq, width), early_index),
            whole((seq, width)),
            pl.BlockSpec((1, width, width), early_index),
            whole(grad_wo.shape),
        ],
        out_specs=[part, part, whole((seq, width)), whole((TEXT, width)), whole((8, width))],
        out_shape=[
            jax.ShapeDtypeStruct((4, pairs, size, width), bf16),
            jax.ShapeDtypeStruct((4, pairs, size, width), bf16),
            jax.ShapeDtypeStruct((seq, width), f32),
            jax.ShapeDtypeStruct((TEXT, width), f32),
            jax.ShapeDtypeStruct((8, width), f32),
        ],
        compiler_params=params(),
        cost_estimate=cost(15),
        name="project_grad",
    )(rows_info, dqkv, first, w_attn, grad_wo)


def first_grad_kernel(
    row_ref,
    gfirst_ref,
    pair_ref,
    hidden_ref,
    gmid_ref,
    vec_ref,
    sums_ref,
    late_ref,
    upb_ref,
    pos_ref,
    out_ref,
    small_ref,
    own,
):
    rows, width = hidden_ref.shape
    tile = 16
    own[...] = gfirst_ref[pl.ds(pl.multiple_of(row_ref[0], 16), rows), :]

    @pl.when(row_ref[3] == 1)
    def _():
        own[0 : pair_ref.shape[0], :] = pair_ref[...]

    def body(i, totals):
        at = pl.ds(pl.multiple_of(i * tile, tile), tile)
        normal, inv_std = norm_rows(hidden_ref[at, :])
        grad_out = own[at, :]
        grad_in = norm_input_grad(grad_out, normal, inv_std, vec_ref[0:1, :])
        own[at, :] = gmid_ref[at, :] + grad_in
        return totals[0] + grad_out * normal, totals[1] + grad_out

    zero = jnp.zeros((tile, width), f32)
    gains, shifts = lax.fori_loop(0, rows // tile, body, (zero, zero), unroll=True)
    out_ref[...] = own[0 : out_ref.shape[0], :].reshape(out_ref.shape)
    own_rows = (
        jnp.sum(gains, axis=0, keepdims=True),
        jnp.sum(shifts, axis=0, keepdims=True),
        late_ref[0:1, :],
        late_ref[1:2, :],
        late_ref[2:3, :],
    )
    row = lax.broadcasted_iota(jnp.int32, (16, width), 0)
    top = jnp.where(row == 0, sums_ref[0:1, :], 0.0)
    top = jnp.where(row == 1, sums_ref[1:2, :], top)
    top = jnp.where(row == 2, late_ref[3:4, :], top)
    for i, value in enumerate(own_rows):
        top = jnp.where(row == 3 + 5 * row_ref[3] + i, value, top)
    small_ref[0:16, :] = top.astype(small_ref.dtype)
    row = lax.broadcasted_iota(jnp.int32, (8, width), 0)
    bias = jnp.zeros((8, width), f32)
    for i in range(upb_ref.shape[0]):
        bias = jnp.where(row == upb_ref.shape[0] * row_ref[3] + i, upb_ref[i : i + 1, :], bias)
    small_ref[16:32, :] = jnp.concatenate([bias, jnp.zeros_like(bias)], axis=0).astype(small_ref.dtype)
    grads = own[...]
    high = grads.astype(bf16)
    low = (grads - high.astype(f32)).astype(bf16)
    table = lax.broadcasted_iota(jnp.int32, (rows, rows), 0)
    chosen = jnp.where(row_ref[3] == 0, pos_ref[...], -1) == table
    chosen = jnp.where(chosen, 1.0, 0.0).astype(bf16)
    sums = dot_nn(chosen, high) + dot_nn(chosen, low)
    small_ref[32 : 32 + rows, :] = sums.astype(small_ref.dtype)
    spare = small_ref.shape[0] - 32 - rows
    if spare:
        small_ref[32 + rows :, :] = jnp.zeros((spare, width), small_ref.dtype)


def first_grad(
    rows_info, gfirst, pair_grad, hidden, grad_middle, vec, sums, late, up_bias, pos, out_rows
):
    rows, width = hidden.shape
    small = round_up(32 + rows, 128)
    args = (gfirst, pair_grad, hidden, grad_middle, vec, sums, late, up_bias, pos)
    return pl.pallas_call(
        first_grad_kernel,
        in_specs=[SMEM_SPEC] + [whole(arg.shape) for arg in args],
        out_specs=[whole((out_rows, 1, width)), whole((small, width))],
        out_shape=[
            jax.ShapeDtypeStruct((out_rows, 1, width), f32),
            jax.ShapeDtypeStruct((small, width), bf16),
        ],
        scratch_shapes=[pltpu.VMEM((rows, width), f32)],
        compiler_params=params(24),
        cost_estimate=cost(8),
        name="first_grad",
    )(rows_info, *args)


def widen(values):
    rows, cols = values.shape
    return jnp.concatenate([values, jnp.zeros((rows, PAIR_LANES - cols), f32)], axis=1)


def split_parts(values):
    high = values.astype(bf16)
    return high, (values - high.astype(f32)).astype(bf16)


def left_parts(values):
    return jnp.concatenate(split_parts(values), axis=1)


def right_parts(values):
    high, low = split_parts(values)
    rows, cols = high.shape
    gap = jnp.zeros((cols - rows, cols), bf16)
    near = jnp.concatenate([high, gap, high, gap], axis=0)
    far = jnp.concatenate([low, gap, jnp.zeros((cols, cols), bf16)], axis=0)
    return jnp.concatenate([near, far], axis=1)


def times(left, right):
    both = dot_nn(left, right)
    return both[:, :PAIR_LANES] + both[:, PAIR_LANES:]


def inverse_roots(stats, identity):
    size = stats[0].shape[0]
    mats, factors = [], []
    for stat in stats:
        norm = jnp.sqrt(jnp.sum(stat * stat, keepdims=True))
        mats.append(stat * (1.0 / norm))
        factors.append(lax.rsqrt(jnp.sqrt(norm)))
    for iteration in range(NEWTON):
        steps = [1.25 * identity - 0.25 * mat for mat in mats]
        if iteration == 0:
            factors = [step * factor for step, factor in zip(steps, factors)]
            squares = [times(left_parts(step), right_parts(step)) for step in steps]
        elif iteration < NEWTON - 1:
            both = [
                times(
                    jnp.concatenate([left_parts(step), left_parts(factor)], axis=0),
                    right_parts(step),
                )
                for step, factor in zip(steps, factors)
            ]
            squares = [pair[:size] for pair in both]
            factors = [pair[size:] for pair in both]
        else:
            return [
                times(left_parts(factor), right_parts(step)) for step, factor in zip(steps, factors)
            ]
        fourths = [times(left_parts(square), right_parts(square)) for square in squares]
        mats = [times(left_parts(fourth), right_parts(mat)) for fourth, mat in zip(fourths, mats)]


def shampoo_kernel(group, begin, parts, grad_count, earlier, up_ref, *refs):
    part = begin + pl.program_id(0)
    grad_refs = refs[:grad_count]
    left_ref, right_ref, w_ref = refs[grad_count : grad_count + 3]
    outs = refs[grad_count + 3 + earlier : grad_count + 7 + earlier]
    results, sems = refs[-2:]
    _, count, size, _ = left_ref.shape
    row = lax.broadcasted_iota(jnp.int32, (size, PAIR_LANES), 0)
    col = lax.broadcasted_iota(jnp.int32, (size, PAIR_LANES), 1)
    identity = (row == col).astype(f32)
    copies = []

    def store(kind, i, at, value):
        results[kind, i] = value
        copy = pltpu.make_async_copy(results.at[kind, i], outs[kind].at[at], sems.at[kind, i])
        copy.start()
        copies.append(copy)

    for base in range(0, count, group):
        places, stats, grads = [], [], []
        for i in range(base, base + group):
            at = jnp.where(up_ref[0] == 1, i * parts + part, part * count + i)
            places.append(at)
            span = slice(i * size, (i + 1) * size)
            grad = grad_refs[0][0, :, span].astype(f32)
            for ref in grad_refs[1:]:
                grad = grad + ref[0, :, span].astype(f32)
            store(0, i, at, grad)
            grad = widen(grad)
            grad_t = widen(jnp.transpose(grad, (1, 0))[:size])
            grads.append(grad)
            outer = times(left_parts(grad), right_parts(grad_t))
            inner = times(left_parts(grad_t), right_parts(grad))
            left_new = stat_decay * left_ref[0, i] + (1.0 - stat_decay) * outer[:, :size]
            right_new = stat_decay * right_ref[0, i] + (1.0 - stat_decay) * inner[:, :size]
            store(1, i, at, left_new)
            store(2, i, at, right_new)
            stats += [widen(left_new), widen(right_new)]
        roots = inverse_roots(stats, identity)
        for i, at in enumerate(places):
            half_way = times(left_parts(roots[2 * i]), right_parts(grads[i]))
            update = times(left_parts(half_way), right_parts(roots[2 * i + 1]))
            store(3, base + i, at, w_ref[0, base + i] - matrix_rate * update[:, :size])
    for copy in copies:
        copy.wait()


def shampoo(is_up, begin, end, grad_rows, lefts, rights, weights, earlier=(), mebibytes=24):
    parts, count, size, _ = lefts.shape
    span = count * size
    blocks = pl.BlockSpec((1, count, size, size), lambda i: (begin + i, 0, 0, 0))
    shape = jax.ShapeDtypeStruct((parts * count, size, size), f32)
    anywhere = pl.BlockSpec(memory_space=pl.ANY)
    first_earlier = 4 + len(grad_rows)
    kernel = functools.partial(
        shampoo_kernel, math.gcd(count, 8), begin, parts, len(grad_rows), len(earlier)
    )
    return pl.pallas_call(
        kernel,
        grid=(end - begin,),
        in_specs=[SMEM_SPEC]
        + [pl.BlockSpec((1, size, span), lambda i: (begin + i, 0, 0))] * len(grad_rows)
        + [blocks] * 3
        + [anywhere] * len(earlier),
        out_specs=[anywhere] * 4,
        out_shape=[shape] * 4,
        scratch_shapes=[
            pltpu.VMEM((4, count, size, size), f32),
            pltpu.SemaphoreType.DMA((4, count)),
        ],
        input_output_aliases={first_earlier + i: i for i in range(len(earlier))},
        compiler_params=params(mebibytes),
        cost_estimate=cost(9),
        name="shampoo",
    )(is_up, *grad_rows, lefts, rights, weights, *earlier)


def momentum_kernel(
    vector_rate, pos_rate, sum_ref, v_ref, vm_ref, b_ref, bm_ref, p_ref, pm_ref, vm_out, v_out, bm_out, b_out, pm_out, p_out
):
    width = v_ref.shape[1]
    new = moment_keep * vm_ref[...] + sum_ref[0 : v_ref.shape[0], :].astype(f32)
    vm_out[...] = new
    v_out[...] = v_ref[...] - vector_rate * new
    per_row = b_ref.shape[1] // width
    rows = sum_ref[16:32, :].astype(f32)
    for i in range(b_ref.shape[0]):
        for j in range(per_row):
            at = (slice(i, i + 1), slice(j * width, (j + 1) * width))
            row = i * per_row + j
            new = moment_keep * bm_ref[at] + rows[row : row + 1, :]
            bm_out[at] = new
            b_out[at] = b_ref[at] - vector_rate * new
    new = moment_keep * pm_ref[...] + sum_ref[32 : 32 + p_ref.shape[0], :].astype(f32)
    pm_out[...] = new
    p_out[...] = p_ref[...] - pos_rate * new


def momentum_step(sums, vectors, vectors_mom, bias, bias_mom, table, table_mom, vector_rate, pos_rate):
    args = (sums, vectors, vectors_mom, bias, bias_mom, table, table_mom)
    outs = (vectors, vectors, bias, bias, table, table)
    return pl.pallas_call(
        functools.partial(momentum_kernel, vector_rate, pos_rate),
        in_specs=[whole(arg.shape) for arg in args],
        out_specs=[whole(out.shape) for out in outs],
        out_shape=[jax.ShapeDtypeStruct(out.shape, f32) for out in outs],
        compiler_params=params(),
        cost_estimate=cost(3),
        name="momentum",
    )(*args)


CORE, Y, Z_LOW, Z_HIGH = 1, 2, 4, 8


def flip(values, bits):
    size = lax.axis_size("dp")
    return lax.ppermute(values, "dp", [(i, i ^ bits) for i in range(size)])


def flip_mod(values):
    return lax.ppermute(values, "mod", [(0, 1), (1, 0)])


def in_order(bit, own, other):
    return jnp.stack([jnp.where(bit == 1, other, own), jnp.where(bit == 1, own, other)])


def place():
    index = lax.axis_index("dp")
    return index % 2, index // 2 % 2, index // 4


def sync(*values):
    return lax.optimization_barrier(values)


def pick(values, index, axis):
    return lax.dynamic_index_in_dim(values, index, axis, keepdims=False)


def plus(left, right):
    return (left.astype(f32) + right.astype(f32)).astype(bf16)


def square_parts(blocks, rows, cols):
    size = blocks.shape[-1]
    shaped = blocks.reshape(rows, cols, size, size)
    return jnp.swapaxes(shaped, 1, 2).reshape(rows, size, cols * size)


def parts_to_blocks(parts):
    rows, size, span = parts.shape
    shaped = parts.reshape(rows, size, span // size, size)
    return jnp.swapaxes(shaped, 1, 2).reshape(-1, size, size)


def local(
    stream_in,
    cotangent,
    patch_count,
    pos_index,
    attn_blocks,
    attn_left,
    attn_right,
    ffn_blocks,
    ffn_left,
    ffn_right,
    vectors,
    vectors_mom,
    ffn_bias,
    ffn_bias_mom,
    pos_table,
    pos_mom,
):
    size = attn_blocks.shape[-1]
    width = vectors.shape[1]
    hidden_units = ffn_bias.shape[1]
    slots = stream_in.shape[2]
    row_blocks = width // size
    chunks = hidden_units // width
    rows = round_up(slots, 16)
    seq = round_up(slots + TEXT, 32)
    by_rows = lax.axis_size("dp") == 16 and attn_blocks.shape[0] == row_blocks
    modality = lax.axis_index("mod")
    is_text = modality == 1
    image_flag = (1 - modality).astype(f32)
    along = lax.axis_index("dp")
    is_up = jnp.where(along < lax.axis_size("dp") // 2, 1, 0).astype(jnp.int32)[None]
    is_not = jnp.zeros((1,), jnp.int32)

    core, y, z = place()
    to_image = [(1, 0)]
    to_text = [(0, 1)]

    if by_rows:
        own_attn = pack_rows(is_not, attn_blocks, row_blocks)[0]
        along_z = [flip(own_attn, bits) for bits in (Z_LOW, Z_HIGH, Z_LOW | Z_HIGH)]
        ffn_rows = pack_rows(is_up, ffn_blocks[0], row_blocks)

    own_vec = lax.dynamic_slice_in_dim(vectors, 3 + 5 * modality, 5, 0)
    vec = jnp.concatenate([own_vec, vectors[0:3]], axis=0)
    up_bias = lax.dynamic_index_in_dim(ffn_bias, modality, 0, keepdims=False)
    up_bias = jnp.swapaxes(up_bias.reshape(row_blocks, chunks, size), 0, 1).reshape(1, hidden_units)
    count = patch_count[0]
    offset = TEXT * (1 - modality)
    first_key = jnp.where(is_text, TEXT, 0)
    end_key = jnp.where(is_text, slots, TEXT + count)
    kept_rows = jnp.where(is_text, slots, count)
    own_core = core if by_rows else 0 * along
    rows_info = jnp.stack([offset, first_key, end_key, modality, kept_rows, own_core])
    rows_info = rows_info.astype(jnp.int32)
    pad = ((0, rows - slots), (0, 0))
    hidden = stream_in[0, 0] + image_flag * jnp.take(pos_table, pos_index[0], axis=0)
    hidden = jnp.pad(hidden, pad)
    pos = jnp.pad(pos_index[0], pad[0], constant_values=-1)[None]
    first = first_norm(rows_info, hidden, vec, seq)
    if by_rows:
        along_z, hidden, first, cotangent, up_bias, pos = sync(
            along_z, hidden, first, cotangent, up_bias, pos
        )
        ffn_parts = lax.all_gather(ffn_rows, "dp", axis=0, tiled=True)
        ffn_parts = ffn_parts.reshape(2, row_blocks, chunks, size, width)
        near = in_order(z % 2, own_attn, along_z[0])
        far = in_order(z % 2, along_z[1], along_z[2])
        attn_z = in_order(z // 2, near, far).reshape(4, size, width)
        upper, lower = attn_z[:, : size // 2], attn_z[:, size // 2 :]
        upper_y, lower_x = flip(upper, Y), flip_mod(lower)
    pair_first = lax.ppermute(first[:TEXT], "mod", to_image)
    if by_rows:
        upper_y, lower_x, first, pair_first, cotangent = sync(
            upper_y, lower_x, first, pair_first, cotangent
        )
        upper, lower = in_order(y, upper, upper_y), in_order(modality, lower, lower_x)
        upper_x, lower_y = flip_mod(upper), flip(lower, Y)
    first = lax.dynamic_update_slice(first, jnp.where(is_text, first[:TEXT], pair_first), (0, 0))
    cot = jnp.pad(cotangent[0, 0], pad)

    def by_parts(blocks):
        by_chunk = blocks.reshape(chunks, -1, size, size)
        spread = jnp.swapaxes(blocks.reshape(-1, chunks, size, size), 0, 1)
        return jnp.where(is_up[0] == 1, spread, by_chunk)

    if by_rows:
        ffn_old = [by_parts(part[0]) for part in (ffn_left, ffn_right, ffn_blocks)]
        upper_x, lower_y, first, cot, ffn_old = sync(upper_x, lower_y, first, cot, ffn_old)
        upper, lower = in_order(modality, upper, upper_x), in_order(y, lower, lower_y)
        attn_parts = [upper, flip(upper, CORE), lower, flip(lower, CORE)]
    else:
        attn_all = lax.all_gather(attn_blocks.astype(bf16), ("mod", "dp"), axis=0, tiled=True)
        attn_parts = [square_parts(attn_all, 4 * row_blocks, row_blocks).reshape(4, width, width)]
        ffn_all = lax.all_gather(ffn_blocks[0].astype(bf16), "dp", axis=0, tiled=True)
        shape = (2, row_blocks, row_blocks, chunks, size, size)
        up = ffn_all.reshape(shape)[0].transpose(0, 2, 3, 1, 4)
        down = ffn_all.reshape(2, row_blocks, chunks, row_blocks, size, size)[1]
        down = down.transpose(0, 1, 3, 2, 4)
        ffn_parts = jnp.stack([p.reshape(row_blocks, chunks, size, width) for p in (up, down)])

    qkv, w_attn = project(rows_info, first, vec, attn_parts)
    ctx, lse, pair_ctx = attend(rows_info, qkv)
    pair_ctx = lax.ppermute(pair_ctx, "mod", to_text)
    stream_out, grad_middle, grad_ctx, pair_grad, grad_wo, grad_ffn, late_vec, up_bias_grad = expert(
        rows_info, ctx, pair_ctx, hidden, cot, vec, up_bias, w_attn, ffn_parts, slots
    )
    pair_grad = lax.ppermute(pair_grad, "mod", to_image)

    def along_z_of(parts):
        return [flip(part, bits * Z_LOW) for bits, part in enumerate(parts) if bits]

    if by_rows:
        ffn_sum = lax.psum_scatter(
            grad_ffn.reshape(-1, chunks, size, width), "dp", scatter_dimension=0, tiled=True
        )[0]
    grad_qkv = attend_grad(rows_info, qkv, grad_ctx, pair_grad, ctx, lse)
    attn_keep, attn_send, grad_first, pair_first_grad, sums = project_grad(
        rows_info, grad_qkv, first, w_attn, grad_wo, size
    )
    pair_first_grad = lax.ppermute(pair_first_grad, "mod", to_text)
    up_bias_grad = jnp.swapaxes(up_bias_grad.reshape(chunks, row_blocks, size), 0, 1)
    if by_rows:
        attn_got = flip(attn_send, CORE)
        attn_got, pair_first_grad = sync(attn_got, pair_first_grad)
        both = plus(attn_keep, attn_got).reshape(2, 4, 2, size, width)
        upper, lower = both[..., : size // 2, :], both[..., size // 2 :, :]
        upper_keep, upper_send = pick(upper, modality, 0), pick(upper, 1 - modality, 0)
        lower_keep, lower_send = pick(lower, y, 2), pick(lower, 1 - y, 2)
        upper_keep, upper_send, lower_keep, lower_send, pair_first_grad = sync(
            upper_keep, upper_send, lower_keep, lower_send, pair_first_grad
        )
        upper_got, lower_got = flip_mod(upper_send), flip(lower_send, Y)
    stream_grad, small = first_grad(
        rows_info,
        grad_first,
        pair_first_grad,
        hidden,
        grad_middle,
        vec,
        sums,
        late_vec,
        up_bias_grad.reshape(chunks, width),
        pos,
        slots,
    )
    stream_out = stream_out.reshape(stream_in.shape)
    stream_grad = stream_grad.reshape(stream_in.shape)
    if by_rows:
        small = small.reshape(2, 2, 4, -1, width)
        small_keep, small_send = pick(small, core, 0), pick(small, 1 - core, 0)
        small_got = flip(small_send, CORE)
        upper_got, lower_got, small_got = sync(upper_got, lower_got, small_got)
        upper, lower = plus(upper_keep, upper_got), plus(lower_keep, lower_got)
        small = plus(small_keep, small_got)
        upper = jnp.concatenate([upper, jnp.swapaxes(small, 0, 1)], axis=2)
        upper_keep, upper_send = pick(upper, y, 1), pick(upper, 1 - y, 1)
        lower_keep, lower_send = pick(lower, modality, 0), pick(lower, 1 - modality, 0)
        upper_keep, upper_send, lower_keep, lower_send = sync(
            upper_keep, upper_send, lower_keep, lower_send
        )
        upper_got, lower_got = flip(upper_send, Y), flip_mod(lower_send)
        attn = jnp.concatenate([plus(lower_keep, lower_got), plus(upper_keep, upper_got)], axis=1)
        attn_z = [pick(attn, z ^ bits, 0) for bits in range(4)]
        attn_got = along_z_of(attn_z)
        attn_got = sync(*attn_got)
        small = sum(part[size:].astype(f32) for part in (attn_z[0], *attn_got))
        half = size // 2
        attn_rows = [
            jnp.concatenate([part[half:size], part[:half]], axis=0)[None]
            for part in (attn_z[0], *attn_got)
        ]
        small, attn_rows = sync(small, attn_rows)
        small_got = flip_mod(small)
        attn_old = [part[None] for part in (attn_left, attn_right, attn_blocks)]
        attn_out = shampoo(is_not, 0, 1, attn_rows, *attn_old, mebibytes=56)
        attn_out, small_got = sync(attn_out, small_got)
        small = (small + small_got).astype(bf16)
        small, ffn_sum = sync(small, ffn_sum)
        small_got = flip(small, Z_LOW)
        ffn_new = shampoo(is_up, 0, 1, [ffn_sum], *ffn_old)
        small_got, ffn_new = sync(small_got, ffn_new)
        small, ffn_new = sync(in_order(z % 2, small, small_got), ffn_new)
        small_got = flip(small, Z_HIGH)
        ffn_new = shampoo(is_up, 1, 2, [ffn_sum], *ffn_old, ffn_new)
        small_got, ffn_new = sync(small_got, ffn_new)
        small, ffn_new = sync(in_order(z // 2, small, small_got), ffn_new)
        small_got = flip(small, Y)
        ffn_new = shampoo(is_up, 2, 3, [ffn_sum], *ffn_old, ffn_new)
        small_got, ffn_new = sync(small_got, ffn_new)
        small, ffn_new = sync(in_order(y, small, small_got), ffn_new)
        small_got = flip(small, CORE)
        ffn_out = shampoo(is_up, 3, 4, [ffn_sum], *ffn_old, ffn_new)
        small_got, ffn_out = sync(small_got, ffn_out)
        small_sum = in_order(core, small, small_got).reshape(-1, width)
    else:
        up = grad_ffn[0].reshape(row_blocks, chunks, size, row_blocks, size)
        down = grad_ffn[1].reshape(row_blocks, chunks, size, row_blocks, size)
        up = up.transpose(0, 3, 1, 2, 4).reshape(-1, size, size)
        down = down.transpose(0, 1, 3, 2, 4).reshape(-1, size, size)
        ffn_sum = lax.psum_scatter(
            jnp.concatenate([up, down], axis=0), "dp", scatter_dimension=0, tiled=True
        )
        attn_full = jnp.stack([attn_keep, attn_send], axis=2).reshape(-1, size, width)
        attn_sum = lax.psum_scatter(
            parts_to_blocks(attn_full), ("mod", "dp"), scatter_dimension=0, tiled=True
        )
        small_sum = lax.psum(small.astype(f32), ("mod", "dp")).astype(bf16)
        ffn_old = [part for part in (ffn_left, ffn_right, ffn_blocks)]
        attn_old = [part[None] for part in (attn_left, attn_right, attn_blocks)]
        ffn_out = shampoo(is_not, 0, 1, [square_parts(ffn_sum, 1, ffn_sum.shape[0])], *ffn_old)
        attn_out = shampoo(is_not, 0, 1, [square_parts(attn_sum, 1, attn_sum.shape[0])], *attn_old)

    items_total = lax.axis_size("dp")
    vector_rate = 0.3 / math.sqrt(items_total * slots)
    pos_rate = 0.5 / math.sqrt(items_total)
    vector_news = momentum_step(
        small_sum, vectors, vectors_mom, ffn_bias, ffn_bias_mom, pos_table, pos_mom, vector_rate, pos_rate
    )
    return (
        stream_out,
        stream_grad,
        *attn_out,
        *(part[None] for part in ffn_out),
        *vector_news,
    )


def solution(mesh):
    items = P("mod", "dp", None, None)
    owned = P(("mod", "dp"), None, None)
    return jax.shard_map(
        local,
        mesh=mesh,
        in_specs=(items, items, P("dp"), P("dp", None), owned, owned, owned, items, items, items)
        + (P(),) * 6,
        out_specs=(items, items, owned, owned, owned, owned, items, items, items, items)
        + (P(),) * 6,
        check_vma=False,
    )
```

```python
import functools
import math

import jax
import jax.numpy as jnp
from jax import lax
from jax.experimental import pallas as pl
from jax.experimental.pallas import tpu as pltpu
from jax.sharding import PartitionSpec as P

HEADS = 12
TEXT = 64
NEWTON = 6
PAIR_LANES = 128
QUERY_TILE = 336
GRAD_TILE = 256

f32 = jnp.float32
bf16 = jnp.bfloat16
norm_eps = 1e-05
stat_decay = 0.5
matrix_rate = 0.25
moment_keep = 0.9
masked_score = -1e30


def dot_nn(left, right):
    return lax.dot_general(left, right, (((1,), (0,)), ((), ())), preferred_element_type=f32)


def dot_nt(left, right):
    return lax.dot_general(left, right, (((1,), (1,)), ((), ())), preferred_element_type=f32)


def dot_tn(left, right):
    return lax.dot_general(left, right, (((0,), (0,)), ((), ())), preferred_element_type=f32)


def params(mebibytes=56):
    return pltpu.CompilerParams(vmem_limit_bytes=mebibytes << 20)


def cost(microseconds):
    return pl.CostEstimate(flops=int(microseconds), bytes_accessed=0, transcendentals=0)


def round_up(value, step):
    return (value + step - 1) // step * step


def whole(shape):
    return pl.BlockSpec(shape, lambda *ids: (0,) * len(shape))


SMEM_SPEC = pl.BlockSpec(memory_space=pltpu.SMEM)


def pack_kernel(up_ref, blocks_ref, out_ref):
    part = pl.program_id(0)
    parts = pl.num_programs(0)
    per_row = blocks_ref.shape[0] // parts
    pieces = []
    for i in range(per_row):
        at = jnp.where(up_ref[0] == 1, i * parts + part, part * per_row + i)
        pieces.append(blocks_ref[at])
    out_ref[0] = jnp.concatenate(pieces, axis=1).astype(bf16)


def pack_rows(is_up, blocks, per_row):
    count, size, _ = blocks.shape
    return pl.pallas_call(
        pack_kernel,
        grid=(count // per_row,),
        in_specs=[SMEM_SPEC, whole(blocks.shape)],
        out_specs=pl.BlockSpec((1, size, per_row * size), lambda i: (i, 0, 0)),
        out_shape=jax.ShapeDtypeStruct((count // per_row, size, per_row * size), bf16),
        compiler_params=params(),
        cost_estimate=cost(3),
        name="pack_rows",
    )(is_up, blocks)


def norm_rows(values):
    centred = values - jnp.mean(values, axis=-1, keepdims=True)
    spread = jnp.mean(centred * centred, axis=-1, keepdims=True)
    inv_std = lax.rsqrt(spread + norm_eps)
    return centred * inv_std, inv_std


def norm_input_grad(grad_out, normal, inv_std, gain):
    grad_norm = grad_out * gain
    mean_grad = jnp.mean(grad_norm, axis=-1, keepdims=True)
    mean_proj = jnp.mean(grad_norm * normal, axis=-1, keepdims=True)
    return inv_std * (grad_norm - mean_grad - normal * mean_proj)


def first_norm_kernel(row_ref, hidden_ref, vec_ref, first_ref):
    rows = hidden_ref.shape[0]
    normal, _ = norm_rows(hidden_ref[...])
    first_ref[...] = jnp.zeros(first_ref.shape, bf16)
    first = normal * vec_ref[0:1, :] + vec_ref[1:2, :]
    first_ref[pl.ds(pl.multiple_of(row_ref[0], 16), rows), :] = first.astype(bf16)


def first_norm(rows_info, hidden, vec, seq):
    return pl.pallas_call(
        first_norm_kernel,
        in_specs=[SMEM_SPEC, whole(hidden.shape), whole(vec.shape)],
        out_specs=whole((seq, hidden.shape[1])),
        out_shape=jax.ShapeDtypeStruct((seq, hidden.shape[1]), bf16),
        compiler_params=params(),
        cost_estimate=cost(4),
        name="first_norm",
    )(rows_info, hidden, vec)


def project_kernel(row_ref, first_ref, vec_ref, *refs):
    weight_refs, (qkv_ref, w_ref) = refs[:-2], refs[-2:]
    step = pl.program_id(0)
    if len(weight_refs) == 1:
        w_ref[...] = weight_refs[0][...]
    else:
        upper, upper_far, lower, lower_far = weight_refs
        half = upper.shape[3]
        size = half + lower.shape[3]
        on_one = row_ref[5] == 1
        for z in range(2):
            for y in range(2):
                for base, near, far in (
                    (0, upper[0, y, z], upper_far[0, y, z]),
                    (half, lower[y, 0, z], lower_far[y, 0, z]),
                ):
                    start = (4 * z + 2 * y) * size + base
                    end = start + near.shape[0]
                    w_ref[0, start:end, :] = jnp.where(on_one, far, near)
                    w_ref[0, start + size : end + size, :] = jnp.where(on_one, near, far)

    @pl.when(step < 3)
    def _():
        bias = jnp.where(step == 0, vec_ref[5:6, :], jnp.where(step == 2, vec_ref[6:7, :], 0.0))
        qkv_ref[...] = (dot_nn(first_ref[...], w_ref[0]) + bias).astype(bf16)


def project(rows_info, first, vec, attn_parts):
    seq, width = first.shape
    if len(attn_parts) == 1:
        weight_specs = [pl.BlockSpec((1, width, width), lambda i: (i, 0, 0))]
    else:
        rows = [part.shape[3] for part in attn_parts]
        upper = pl.BlockSpec((1, 2, 2, rows[0], width), lambda i: (i // 2, 0, i % 2, 0, 0))
        lower = pl.BlockSpec((2, 1, 2, rows[2], width), lambda i: (0, i // 2, i % 2, 0, 0))
        weight_specs = [upper, upper, lower, lower]
    return pl.pallas_call(
        project_kernel,
        grid=(4,),
        in_specs=[SMEM_SPEC, whole((seq, width)), whole(vec.shape), *weight_specs],
        out_specs=[
            pl.BlockSpec((seq, width), lambda i: (0, jnp.minimum(i, 2))),
            pl.BlockSpec((1, width, width), lambda i: (i, 0, 0)),
        ],
        out_shape=[
            jax.ShapeDtypeStruct((seq, 3 * width), bf16),
            jax.ShapeDtypeStruct((4, width, width), bf16),
        ],
        compiler_params=params(),
        cost_estimate=cost(8),
        name="project",
    )(rows_info, first, vec, *attn_parts)


def key_bias(row_ref, seq):
    rows = lax.broadcasted_iota(jnp.int32, (seq, 1), 0)
    counts = jnp.logical_and(rows >= row_ref[1], rows < row_ref[2])
    return jnp.where(counts, 0.0, masked_score).astype(f32)


def transposed(values):
    return jnp.transpose(values.astype(f32), (1, 0)).astype(bf16)


def attend_kernel(row_ref, q_ref, k_ref, v_ref, ctx_ref, lse_ref, pair_ref):
    seq = q_ref.shape[0]
    half = PAIR_LANES // 2
    scale = half ** (-0.5)
    lane = lax.broadcasted_iota(jnp.int32, (seq, PAIR_LANES), 1)
    bias = key_bias(row_ref, seq).astype(bf16)
    queries = q_ref[...] * jnp.asarray(scale, bf16)
    keys = k_ref[...]
    values = v_ref[...]
    one = jnp.ones((seq, PAIR_LANES), bf16)
    heads = []
    for head in range(2):
        own = (lane < half) == (head == 0)
        spare = lane == half * (1 - head)
        head_q = jnp.where(own, queries, jnp.where(spare, one, jnp.zeros_like(one)))
        head_k = jnp.where(own, keys, jnp.where(spare, bias, jnp.zeros_like(one)))
        head_v = jnp.where(own, values, one)
        heads.append((head_q, head_k, head_v))
    for start in range(0, seq, QUERY_TILE):
        size = min(QUERY_TILE, seq - start)
        tile = slice(start, start + size)
        parts, lses = [], []
        for head, (head_q, head_k, head_v) in enumerate(heads):
            scores = dot_nt(head_q[tile], head_k)
            top = jnp.max(scores, axis=1, keepdims=True)
            raised = jnp.exp(scores - top).astype(bf16)
            summed = dot_nn(raised, head_v)
            at = half * (1 - head)
            total = summed[:, at : at + 1]
            parts.append(summed * (1.0 / total))
            lses.append(top + jnp.log(total))
        low = lax.broadcasted_iota(jnp.int32, (size, PAIR_LANES), 1) < half
        context = jnp.where(low, parts[0], parts[1]).astype(bf16)
        ctx_ref[tile, :] = context
        if start == 0:
            pair_ref[...] = context[: pair_ref.shape[0]]
        lane8 = lax.broadcasted_iota(jnp.int32, (size, 8), 1)
        lse_ref[0, tile, :] = jnp.where(lane8 == 0, lses[0], lses[1])


def attend(rows_info, qkv):
    seq = qkv.shape[0]
    width = qkv.shape[1] // 3
    pairs = width // PAIR_LANES

    def column(base):
        return pl.BlockSpec((seq, PAIR_LANES), lambda i, base=base: (0, base + i))

    return pl.pallas_call(
        attend_kernel, grid=(pairs,),
        in_specs=[SMEM_SPEC, column(0), column(pairs), column(2 * pairs)],
        out_specs=[column(0), pl.BlockSpec((1, seq, 8), lambda i: (i, 0, 0)), pl.BlockSpec((TEXT, PAIR_LANES), lambda i: (0, i))],
        out_shape=[jax.ShapeDtypeStruct((seq, width), bf16), jax.ShapeDtypeStruct((pairs, seq, 8), f32), jax.ShapeDtypeStruct((TEXT, width), bf16)],
        compiler_params=params(), cost_estimate=cost(12), name="attend",
    )(rows_info, qkv, qkv, qkv)


def three_parts(values):
    high = values.astype(bf16)
    rest = values - high.astype(f32)
    middle = rest.astype(bf16)
    return high, middle, (rest - middle.astype(f32)).astype(bf16)


def attend_grad_kernel(
    row_ref, q_ref, k_ref, v_ref, g_ref, pair_ref, ctx_ref, lse_ref, out_ref, dk_ref, dv_ref
):
    seq = q_ref.shape[0]
    half = PAIR_LANES // 2
    scale = half ** (-0.5)
    lane = lax.broadcasted_iota(jnp.int32, (seq, PAIR_LANES), 1)
    bias = key_bias(row_ref, seq).astype(bf16)
    queries = q_ref[...]
    scaled = queries * jnp.asarray(scale, bf16)
    keys = k_ref[...]
    values = v_ref[...]
    keys_t = transposed(keys)
    row = lax.broadcasted_iota(jnp.int32, (seq, 1), 0)
    counts = jnp.logical_and(row >= row_ref[1], row < row_ref[2])
    grads = jnp.concatenate([pair_ref[...], g_ref[pair_ref.shape[0] :, :]], axis=0)
    grads = jnp.where(counts, grads, jnp.zeros((seq, PAIR_LANES), bf16))
    products = grads.astype(f32) * ctx_ref[...].astype(f32)
    one = jnp.ones((seq, PAIR_LANES), bf16)
    zero = jnp.zeros((seq, PAIR_LANES), bf16)
    heads = []
    for head in range(2):
        own = (lane < half) == (head == 0)
        spare = lane - half * (1 - head)
        lse = three_parts(-lse_ref[0, :, head : head + 1])
        dots = three_parts(-jnp.sum(jnp.where(own, products, 0.0), axis=1, keepdims=True))
        own_q = jnp.where(own, queries, zero)
        own_g = jnp.where(own, grads, zero)
        head_q = jnp.where(own, scaled, jnp.where(spare == 3, one, zero))
        head_g = own_g
        for i in range(3):
            head_q = jnp.where(spare == i, lse[i], head_q)
            head_g = jnp.where(spare == i, dots[i], head_g)
        head_k = jnp.where(own, keys, jnp.where(spare == 3, bias, one))
        head_v = jnp.where(own, values, one)
        heads.append((head_q, head_g, head_k, head_v, own_q, own_g))
    for start in range(0, seq, GRAD_TILE):
        size = min(GRAD_TILE, seq - start)
        tile = slice(start, start + size)
        parts = []
        for head, (head_q, head_g, head_k, head_v, own_q, own_g) in enumerate(heads):
            probs = jnp.exp(dot_nt(head_k, head_q[tile]))
            grad_scores = (probs * dot_nt(head_v, head_g[tile])).astype(bf16)
            grad_v = dot_nn(probs.astype(bf16), own_g[tile])
            grad_k = dot_nn(grad_scores, own_q[tile])
            if start == 0 and head == 0:
                dv_ref[...] = grad_v
                dk_ref[...] = grad_k
            else:
                dv_ref[...] += grad_v
                dk_ref[...] += grad_k
            parts.append(dot_nn(keys_t[half * head : half * (head + 1), :], grad_scores))
        grad_q = jnp.transpose(jnp.concatenate(parts, axis=0) * scale, (1, 0))
        out_ref[0, tile, :] = grad_q.astype(bf16)
    out_ref[1] = (dk_ref[...] * scale).astype(bf16)
    out_ref[2] = dv_ref[...].astype(bf16)


def attend_grad(rows_info, qkv, grad_ctx, pair_grad, ctx, lse):
    seq = qkv.shape[0]
    width = qkv.shape[1] // 3
    pairs = width // PAIR_LANES

    def column(base):
        return pl.BlockSpec((seq, PAIR_LANES), lambda i, base=base: (0, base + i))

    return pl.pallas_call(
        attend_grad_kernel,
        grid=(pairs,),
        in_specs=[
            SMEM_SPEC,
            column(0),
            column(pairs),
            column(2 * pairs),
            column(0),
            pl.BlockSpec((TEXT, PAIR_LANES), lambda i: (0, i)),
            column(0),
            pl.BlockSpec((1, seq, 8), lambda i: (i, 0, 0)),
        ],
        out_specs=pl.BlockSpec((3, seq, PAIR_LANES), lambda i: (0, 0, i)),
        out_shape=jax.ShapeDtypeStruct((3, seq, width), bf16),
        scratch_shapes=[pltpu.VMEM((seq, PAIR_LANES), f32)] * 2,
        compiler_params=params(),
        cost_estimate=cost(15),
        name="attend_grad",
    )(rows_info, qkv, qkv, qkv, grad_ctx, pair_grad, ctx, lse)


def gelu_pair(values):
    size = jnp.abs(values)
    tail = 1.0 / (1.0 + (0.3275911 * 0.5**0.5) * size)
    poly = tail * (
        0.254829592
        + tail * (-0.284496736 + tail * (1.421413741 + tail * (-1.453152027 + tail * 1.061405429)))
    )
    bell = jnp.exp(-0.5 * values * values)
    upper = 0.5 * poly * bell
    share = jnp.where(values >= 0.0, 1.0 - upper, upper)
    return values * share, share + values * bell * ((2.0 * math.pi) ** -0.5)


def split_by_core(row_ref, grad, shape):
    size, width = shape[-2:]
    blocks = grad.reshape(-1, 2, size, width)
    near, far = blocks[:, 0], blocks[:, 1]
    on_one = row_ref[5] == 1
    return jnp.where(on_one, far, near).reshape(shape), jnp.where(on_one, near, far).reshape(shape)


def expert_chunk(
    order, second, gbranch, upb, parts_ref, grad_ref, dupb_ref, branch, gsecond, scratch, begin
):
    pre, gact, act, gpre, up, down = scratch
    rows, width = act.shape
    tile = 16
    size = parts_ref.shape[2]
    places = [(which, slice(i * size, (i + 1) * size)) for which in range(2) for i in range(len(order) // 2)]
    for at, (which, span) in zip(order, places):
        (up, down)[which][span, :] = parts_ref[at, 0]
    pre[...] = dot_nn(second[...], up[...])
    gact[...] = dot_nt(gbranch[...], down[...])

    def body(i, total):
        at = pl.ds(pl.multiple_of(i * tile, tile), tile)
        value, slope = gelu_pair(pre[at, :] + upb[...])
        act[at, :] = value.astype(bf16)
        rounded = (gact[at, :] * slope).astype(bf16)
        gpre[at, :] = rounded
        return total + rounded.astype(f32)

    total = lax.fori_loop(0, rows // tile, body, jnp.zeros((tile, width), f32), unroll=True)
    dupb_ref[...] = jnp.sum(total, axis=0, keepdims=True)
    grads = [
        dot_tn(second[...], gpre[...]).astype(bf16),
        dot_tn(act[...], gbranch[...]).astype(bf16),
    ]
    for at, (which, span) in zip(order, places):
        grad_ref[at, 0] = grads[which][span, :]
    own_branch = dot_nn(act[...], down[...])
    own_gsecond = dot_nt(gpre[...], up[...])

    @pl.when(begin)
    def _():
        branch[...] = own_branch
        gsecond[...] = own_gsecond

    @pl.when(jnp.logical_not(begin))
    def _():
        branch[...] += own_branch
        gsecond[...] += own_gsecond


def expert_kernel(
    order,
    row_ref,
    ctx_ref,
    pair_ref,
    hidden_ref,
    cot_ref,
    vec_ref,
    upb_ref,
    wo_ref,
    parts_ref,
    out_ref,
    gmid_ref,
    gctx_ref,
    pair_grad_ref,
    dwo_ref,
    grad_ref,
    dvec_ref,
    dupb_ref,
    own_ctx,
    middle,
    second,
    gbranch,
    branch,
    gsecond,
    *scratch,
):
    step = pl.program_id(0)
    rows, width = hidden_ref.shape
    out_rows = out_ref.shape[0]
    tile = 16

    @pl.when(step == 0)
    def _():
        own_ctx[...] = ctx_ref[pl.ds(pl.multiple_of(row_ref[0], 16), rows), :]

        @pl.when(row_ref[3] == 1)
        def _():
            own_ctx[0 : pair_ref.shape[0], :] = pair_ref[...]

        middle[...] = dot_nn(own_ctx[...], wo_ref[0])

        def body(i, total):
            at = pl.ds(pl.multiple_of(i * tile, tile), tile)
            mid = hidden_ref[at, :] + (middle[at, :] + vec_ref[7:8, :])
            middle[at, :] = mid
            normal, _ = norm_rows(mid)
            second[at, :] = (normal * vec_ref[2:3, :] + vec_ref[3:4, :]).astype(bf16)
            row = lax.broadcasted_iota(jnp.int32, (tile, 1), 0) + i * tile
            kept = jnp.where(row < row_ref[4], cot_ref[at, :], 0.0)
            rounded = kept.astype(bf16)
            gbranch[at, :] = rounded
            return total + rounded.astype(f32)

        total = lax.fori_loop(
            0, rows // tile, body, jnp.zeros((tile, width), f32), unroll=True
        )
        dvec_ref[...] = jnp.zeros(dvec_ref.shape, f32)
        dvec_ref[2:3, :] = jnp.sum(total, axis=0, keepdims=True)

    expert_chunk(
        order,
        second,
        gbranch,
        upb_ref,
        parts_ref,
        grad_ref,
        dupb_ref,
        branch,
        gsecond,
        scratch,
        step == 0,
    )

    @pl.when(step == pl.num_programs(0) - 1)
    def _():
        def body(i, totals):
            at = pl.ds(pl.multiple_of(i * tile, tile), tile)
            mid = middle[at, :]
            normal, inv_std = norm_rows(mid)
            grad_out = gsecond[at, :]
            row = lax.broadcasted_iota(jnp.int32, (tile, 1), 0) + i * tile
            kept = row < row_ref[4]
            branch[at, :] = jnp.where(kept, mid + (branch[at, :] + vec_ref[4:5, :]), 0.0)
            grad_in = norm_input_grad(grad_out, normal, inv_std, vec_ref[2:3, :])
            grad_mid = jnp.where(kept, cot_ref[at, :], 0.0) + grad_in
            gmid_ref[at, :] = grad_mid
            rounded = grad_mid.astype(bf16)
            gbranch[at, :] = rounded
            return (
                totals[0] + grad_out * normal,
                totals[1] + grad_out,
                totals[2] + rounded.astype(f32),
            )

        zero = jnp.zeros((tile, width), f32)
        gains, shifts, biases = lax.fori_loop(
            0, rows // tile, body, (zero, zero, zero), unroll=True
        )
        dvec_ref[0:1, :] = jnp.sum(gains, axis=0, keepdims=True)
        dvec_ref[1:2, :] = jnp.sum(shifts, axis=0, keepdims=True)
        dvec_ref[3:4, :] = jnp.sum(biases, axis=0, keepdims=True)
        out_ref[...] = branch[0:out_rows, :].reshape(out_ref.shape)
        dwo_ref[...] = dot_tn(own_ctx[...], gbranch[...]).astype(bf16)
        grad_ctx = dot_nt(gbranch[...], wo_ref[0]).astype(bf16)
        gctx_ref[...] = jnp.zeros(gctx_ref.shape, bf16)
        gctx_ref[pl.ds(pl.multiple_of(row_ref[0], 16), rows), :] = grad_ctx
        pair_grad_ref[...] = grad_ctx[: pair_grad_ref.shape[0]]


def expert(rows_info, ctx, pair_ctx, hidden, cot, vec, up_bias, w_attn, ffn_parts, order, out_rows):
    rows, width = hidden.shape
    seq = ctx.shape[0]
    blocks, chunks, size, _ = ffn_parts.shape
    parts = pl.BlockSpec((blocks, 1, size, width), lambda i: (0, i, 0, 0))
    return pl.pallas_call(
        functools.partial(expert_kernel, order),
        grid=(chunks,),
        in_specs=[
            SMEM_SPEC,
            whole(ctx.shape),
            whole(pair_ctx.shape),
            whole(hidden.shape),
            whole(cot.shape),
            whole(vec.shape),
            pl.BlockSpec((1, width), lambda i: (0, i)),
            pl.BlockSpec((1, width, width), lambda i: (3, 0, 0)),
            parts,
        ],
        out_specs=[
            whole((out_rows, 1, width)),
            whole((rows, width)),
            whole((seq, width)),
            whole((TEXT, width)),
            whole((width, width)),
            parts,
            whole((8, width)),
            pl.BlockSpec((1, width), lambda i: (0, i)),
        ],
        out_shape=[
            jax.ShapeDtypeStruct((out_rows, 1, width), f32),
            jax.ShapeDtypeStruct((rows, width), f32),
            jax.ShapeDtypeStruct((seq, width), bf16),
            jax.ShapeDtypeStruct((TEXT, width), bf16),
            jax.ShapeDtypeStruct((width, width), bf16),
            jax.ShapeDtypeStruct(ffn_parts.shape, bf16),
            jax.ShapeDtypeStruct((8, width), f32),
            jax.ShapeDtypeStruct((1, chunks * width), f32),
        ],
        scratch_shapes=[
            pltpu.VMEM((rows, width), bf16),
            pltpu.VMEM((rows, width), f32),
            pltpu.VMEM((rows, width), bf16),
            pltpu.VMEM((rows, width), bf16),
            pltpu.VMEM((rows, width), f32),
            pltpu.VMEM((rows, width), f32),
            pltpu.VMEM((rows, width), f32),
            pltpu.VMEM((rows, width), f32),
            pltpu.VMEM((rows, width), bf16),
            pltpu.VMEM((rows, width), bf16),
            pltpu.VMEM((width, width), bf16),
            pltpu.VMEM((width, width), bf16),
        ],
        compiler_params=params(),
        cost_estimate=cost(43),
        name="expert",
    )(rows_info, ctx, pair_ctx, hidden, cot, vec, up_bias, w_attn, ffn_parts)


def project_grad_kernel(
    row_ref, dqkv_ref, first_ref, w_ref, dwo_ref, keep_ref, send_ref, gfirst, pair_ref, sums_ref
):
    step = pl.program_id(0)

    def put(grad):
        keep_ref[0], send_ref[0] = split_by_core(row_ref, grad, keep_ref.shape[1:])

    @pl.when(step < 3)
    def _():
        own = dqkv_ref[0]
        put(dot_tn(first_ref[...], own).astype(bf16))
        share = dot_nt(own, w_ref[0])
        sums = jnp.sum(own.astype(f32), axis=0, keepdims=True)

        @pl.when(step == 0)
        def _():
            gfirst[...] = share
            sums_ref[...] = jnp.zeros(sums_ref.shape, f32)
            sums_ref[0:1, :] = sums

        @pl.when(step > 0)
        def _():
            gfirst[...] += share
            sums_ref[1:2, :] = sums

    @pl.when(step == 3)
    def _():
        put(dwo_ref[...])
        pair_ref[...] = gfirst[0 : pair_ref.shape[0], :]


def project_grad(rows_info, dqkv, first, w_attn, grad_wo, size):
    seq, width = first.shape
    pairs = width // size // 2
    part = pl.BlockSpec((1, pairs, size, width), lambda i: (i, 0, 0, 0))

    def early_index(i):
        return (jnp.minimum(i, 2), 0, 0)

    return pl.pallas_call(
        project_grad_kernel,
        grid=(4,),
        in_specs=[
            SMEM_SPEC,
            pl.BlockSpec((1, seq, width), early_index),
            whole((seq, width)),
            pl.BlockSpec((1, width, width), early_index),
            whole(grad_wo.shape),
        ],
        out_specs=[part, part, whole((seq, width)), whole((TEXT, width)), whole((8, width))],
        out_shape=[
            jax.ShapeDtypeStruct((4, pairs, size, width), bf16),
            jax.ShapeDtypeStruct((4, pairs, size, width), bf16),
            jax.ShapeDtypeStruct((seq, width), f32),
            jax.ShapeDtypeStruct((TEXT, width), f32),
            jax.ShapeDtypeStruct((8, width), f32),
        ],
        compiler_params=params(),
        cost_estimate=cost(15),
        name="project_grad",
    )(rows_info, dqkv, first, w_attn, grad_wo)


def first_grad_kernel(
    row_ref,
    gfirst_ref,
    pair_ref,
    hidden_ref,
    gmid_ref,
    vec_ref,
    sums_ref,
    late_ref,
    upb_ref,
    pos_ref,
    out_ref,
    small_ref,
    own,
):
    rows, width = hidden_ref.shape
    tile = 16
    own[...] = gfirst_ref[pl.ds(pl.multiple_of(row_ref[0], 16), rows), :]

    @pl.when(row_ref[3] == 1)
    def _():
        own[0 : pair_ref.shape[0], :] = pair_ref[...]

    def body(i, totals):
        at = pl.ds(pl.multiple_of(i * tile, tile), tile)
        normal, inv_std = norm_rows(hidden_ref[at, :])
        grad_out = own[at, :]
        grad_in = norm_input_grad(grad_out, normal, inv_std, vec_ref[0:1, :])
        own[at, :] = gmid_ref[at, :] + grad_in
        return totals[0] + grad_out * normal, totals[1] + grad_out

    zero = jnp.zeros((tile, width), f32)
    gains, shifts = lax.fori_loop(0, rows // tile, body, (zero, zero), unroll=True)
    out_ref[...] = own[0 : out_ref.shape[0], :].reshape(out_ref.shape)
    own_rows = (
        jnp.sum(gains, axis=0, keepdims=True),
        jnp.sum(shifts, axis=0, keepdims=True),
        late_ref[0:1, :],
        late_ref[1:2, :],
        late_ref[2:3, :],
    )
    row = lax.broadcasted_iota(jnp.int32, (16, width), 0)
    top = jnp.where(row == 0, sums_ref[0:1, :], 0.0)
    top = jnp.where(row == 1, sums_ref[1:2, :], top)
    top = jnp.where(row == 2, late_ref[3:4, :], top)
    for i, value in enumerate(own_rows):
        top = jnp.where(row == 3 + 5 * row_ref[3] + i, value, top)
    small_ref[0:16, :] = top.astype(small_ref.dtype)
    row = lax.broadcasted_iota(jnp.int32, (8, width), 0)
    bias = jnp.zeros((8, width), f32)
    for i in range(upb_ref.shape[0]):
        bias = jnp.where(row == upb_ref.shape[0] * row_ref[3] + i, upb_ref[i : i + 1, :], bias)
    small_ref[16:32, :] = jnp.concatenate([bias, jnp.zeros_like(bias)], axis=0).astype(small_ref.dtype)
    grads = own[...]
    high = grads.astype(bf16)
    low = (grads - high.astype(f32)).astype(bf16)
    table = lax.broadcasted_iota(jnp.int32, (rows, rows), 0)
    chosen = jnp.where(row_ref[3] == 0, pos_ref[...], -1) == table
    chosen = jnp.where(chosen, 1.0, 0.0).astype(bf16)
    sums = dot_nn(chosen, high) + dot_nn(chosen, low)
    small_ref[32 : 32 + rows, :] = sums.astype(small_ref.dtype)
    spare = small_ref.shape[0] - 32 - rows
    if spare:
        small_ref[32 + rows :, :] = jnp.zeros((spare, width), small_ref.dtype)


def first_grad(
    rows_info, gfirst, pair_grad, hidden, grad_middle, vec, sums, late, up_bias, pos, out_rows
):
    rows, width = hidden.shape
    small = round_up(32 + rows, 128)
    args = (gfirst, pair_grad, hidden, grad_middle, vec, sums, late, up_bias, pos)
    return pl.pallas_call(
        first_grad_kernel,
        in_specs=[SMEM_SPEC] + [whole(arg.shape) for arg in args],
        out_specs=[whole((out_rows, 1, width)), whole((small, width))],
        out_shape=[
            jax.ShapeDtypeStruct((out_rows, 1, width), f32),
            jax.ShapeDtypeStruct((small, width), bf16),
        ],
        scratch_shapes=[pltpu.VMEM((rows, width), f32)],
        compiler_params=params(24),
        cost_estimate=cost(8),
        name="first_grad",
    )(rows_info, *args)


def widen(values):
    rows, cols = values.shape
    return jnp.concatenate([values, jnp.zeros((rows, PAIR_LANES - cols), f32)], axis=1)


def split_parts(values):
    high = values.astype(bf16)
    return high, (values - high.astype(f32)).astype(bf16)


def left_parts(values):
    return jnp.concatenate(split_parts(values), axis=1)


def right_parts(values):
    high, low = split_parts(values)
    rows, cols = high.shape
    gap = jnp.zeros((cols - rows, cols), bf16)
    near = jnp.concatenate([high, gap, high, gap], axis=0)
    far = jnp.concatenate([low, gap, jnp.zeros((cols, cols), bf16)], axis=0)
    return jnp.concatenate([near, far], axis=1)


def times(left, right):
    both = dot_nn(left, right)
    return both[:, :PAIR_LANES] + both[:, PAIR_LANES:]


def inverse_roots(stats, identity):
    size = stats[0].shape[0]
    mats, factors = [], []
    for stat in stats:
        norm = jnp.sqrt(jnp.sum(stat * stat, keepdims=True))
        mats.append(stat * (1.0 / norm))
        factors.append(lax.rsqrt(jnp.sqrt(norm)))
    for iteration in range(NEWTON):
        steps = [1.25 * identity - 0.25 * mat for mat in mats]
        if iteration == 0:
            factors = [step * factor for step, factor in zip(steps, factors)]
            squares = [times(left_parts(step), right_parts(step)) for step in steps]
        elif iteration < NEWTON - 1:
            both = [
                times(
                    jnp.concatenate([left_parts(step), left_parts(factor)], axis=0),
                    right_parts(step),
                )
                for step, factor in zip(steps, factors)
            ]
            squares = [pair[:size] for pair in both]
            factors = [pair[size:] for pair in both]
        else:
            return [
                times(left_parts(factor), right_parts(step)) for step, factor in zip(steps, factors)
            ]
        fourths = [times(left_parts(square), right_parts(square)) for square in squares]
        mats = [times(left_parts(fourth), right_parts(mat)) for fourth, mat in zip(fourths, mats)]


def shampoo_kernel(group, begin, parts, grad_count, earlier, up_ref, *refs):
    part = begin + pl.program_id(0)
    grad_refs = refs[:grad_count]
    left_ref, right_ref, w_ref = refs[grad_count : grad_count + 3]
    outs = refs[grad_count + 3 + earlier : grad_count + 7 + earlier]
    results, sems = refs[-2:]
    _, count, size, _ = left_ref.shape
    row = lax.broadcasted_iota(jnp.int32, (size, PAIR_LANES), 0)
    col = lax.broadcasted_iota(jnp.int32, (size, PAIR_LANES), 1)
    identity = (row == col).astype(f32)
    copies = []

    def store(kind, i, at, value):
        results[kind, i] = value
        copy = pltpu.make_async_copy(results.at[kind, i], outs[kind].at[at], sems.at[kind, i])
        copy.start()
        copies.append(copy)

    for base in range(0, count, group):
        places, stats, grads = [], [], []
        for i in range(base, base + group):
            at = jnp.where(up_ref[0] == 1, i * parts + part, part * count + i)
            places.append(at)
            span = slice(i * size, (i + 1) * size)
            grad = grad_refs[0][0, :, span].astype(f32)
            for ref in grad_refs[1:]:
                grad = grad + ref[0, :, span].astype(f32)
            store(0, i, at, grad)
            grad = widen(grad)
            grad_t = widen(jnp.transpose(grad, (1, 0))[:size])
            grads.append(grad)
            outer = times(left_parts(grad), right_parts(grad_t))
            inner = times(left_parts(grad_t), right_parts(grad))
            left_new = stat_decay * left_ref[0, i] + (1.0 - stat_decay) * outer[:, :size]
            right_new = stat_decay * right_ref[0, i] + (1.0 - stat_decay) * inner[:, :size]
            store(1, i, at, left_new)
            store(2, i, at, right_new)
            stats += [widen(left_new), widen(right_new)]
        roots = inverse_roots(stats, identity)
        for i, at in enumerate(places):
            half_way = times(left_parts(roots[2 * i]), right_parts(grads[i]))
            update = times(left_parts(half_way), right_parts(roots[2 * i + 1]))
            store(3, base + i, at, w_ref[0, base + i] - matrix_rate * update[:, :size])
    for copy in copies:
        copy.wait()


def shampoo(is_up, begin, end, grad_rows, lefts, rights, weights, earlier=(), mebibytes=24):
    parts, count, size, _ = lefts.shape
    span = count * size
    blocks = pl.BlockSpec((1, count, size, size), lambda i: (begin + i, 0, 0, 0))
    shape = jax.ShapeDtypeStruct((parts * count, size, size), f32)
    anywhere = pl.BlockSpec(memory_space=pl.ANY)
    first_earlier = 4 + len(grad_rows)
    kernel = functools.partial(
        shampoo_kernel, math.gcd(count, 8), begin, parts, len(grad_rows), len(earlier)
    )
    return pl.pallas_call(
        kernel,
        grid=(end - begin,),
        in_specs=[SMEM_SPEC]
        + [pl.BlockSpec((1, size, span), lambda i: (begin + i, 0, 0))] * len(grad_rows)
        + [blocks] * 3
        + [anywhere] * len(earlier),
        out_specs=[anywhere] * 4,
        out_shape=[shape] * 4,
        scratch_shapes=[
            pltpu.VMEM((4, count, size, size), f32),
            pltpu.SemaphoreType.DMA((4, count)),
        ],
        input_output_aliases={first_earlier + i: i for i in range(len(earlier))},
        compiler_params=params(mebibytes),
        cost_estimate=cost(9),
        name="shampoo",
    )(is_up, *grad_rows, lefts, rights, weights, *earlier)


def momentum_kernel(
    vector_rate, pos_rate, sum_ref, v_ref, vm_ref, b_ref, bm_ref, p_ref, pm_ref, vm_out, v_out, bm_out, b_out, pm_out, p_out
):
    width = v_ref.shape[1]
    new = moment_keep * vm_ref[...] + sum_ref[0 : v_ref.shape[0], :].astype(f32)
    vm_out[...] = new
    v_out[...] = v_ref[...] - vector_rate * new
    per_row = b_ref.shape[1] // width
    rows = sum_ref[16:32, :].astype(f32)
    for i in range(b_ref.shape[0]):
        for j in range(per_row):
            at = (slice(i, i + 1), slice(j * width, (j + 1) * width))
            row = i * per_row + j
            new = moment_keep * bm_ref[at] + rows[row : row + 1, :]
            bm_out[at] = new
            b_out[at] = b_ref[at] - vector_rate * new
    new = moment_keep * pm_ref[...] + sum_ref[32 : 32 + p_ref.shape[0], :].astype(f32)
    pm_out[...] = new
    p_out[...] = p_ref[...] - pos_rate * new


def momentum_step(sums, vectors, vectors_mom, bias, bias_mom, table, table_mom, vector_rate, pos_rate):
    args = (sums, vectors, vectors_mom, bias, bias_mom, table, table_mom)
    outs = (vectors, vectors, bias, bias, table, table)
    return pl.pallas_call(
        functools.partial(momentum_kernel, vector_rate, pos_rate),
        in_specs=[whole(arg.shape) for arg in args],
        out_specs=[whole(out.shape) for out in outs],
        out_shape=[jax.ShapeDtypeStruct(out.shape, f32) for out in outs],
        compiler_params=params(),
        cost_estimate=cost(3),
        name="momentum",
    )(*args)


CORE, Y, Z_LOW, Z_HIGH = 1, 2, 4, 8


def flip(values, bits):
    size = lax.axis_size("dp")
    return lax.ppermute(values, "dp", [(i, i ^ bits) for i in range(size)])


def flip_mod(values):
    return lax.ppermute(values, "mod", [(0, 1), (1, 0)])


def in_order(bit, own, other):
    return jnp.stack([jnp.where(bit == 1, other, own), jnp.where(bit == 1, own, other)])


def ring_order():
    chips = [(z, 0) for z in range(4)] + [(z, 1) for z in reversed(range(4))]
    return [z * 4 + y * 2 + core for z, y in chips for core in range(2)]


def place():
    index = lax.axis_index("dp")
    return index % 2, index // 2 % 2, index // 4


def sync(*values):
    return lax.optimization_barrier(values)


def pick(values, index, axis):
    return lax.dynamic_index_in_dim(values, index, axis, keepdims=False)


def plus(left, right):
    return (left.astype(f32) + right.astype(f32)).astype(bf16)


def square_parts(blocks, rows, cols):
    size = blocks.shape[-1]
    shaped = blocks.reshape(rows, cols, size, size)
    return jnp.swapaxes(shaped, 1, 2).reshape(rows, size, cols * size)


def parts_to_blocks(parts):
    rows, size, span = parts.shape
    shaped = parts.reshape(rows, size, span // size, size)
    return jnp.swapaxes(shaped, 1, 2).reshape(-1, size, size)


def local(
    stream_in,
    cotangent,
    patch_count,
    pos_index,
    attn_blocks,
    attn_left,
    attn_right,
    ffn_blocks,
    ffn_left,
    ffn_right,
    vectors,
    vectors_mom,
    ffn_bias,
    ffn_bias_mom,
    pos_table,
    pos_mom,
):
    size = attn_blocks.shape[-1]
    width = vectors.shape[1]
    hidden_units = ffn_bias.shape[1]
    slots = stream_in.shape[2]
    row_blocks = width // size
    chunks = hidden_units // width
    rows = round_up(slots, 16)
    seq = round_up(slots + TEXT, 32)
    by_rows = lax.axis_size("dp") == 16 and attn_blocks.shape[0] == row_blocks
    modality = lax.axis_index("mod")
    is_text = modality == 1
    image_flag = (1 - modality).astype(f32)
    along = lax.axis_index("dp")
    is_up = jnp.where(along < lax.axis_size("dp") // 2, 1, 0).astype(jnp.int32)[None]
    is_not = jnp.zeros((1,), jnp.int32)

    core, y, z = place()
    order = range(2 * row_blocks)
    if by_rows:
        order = [ring_order().index(device) for device in order]
    order = tuple(order)
    to_image = [(1, 0)]
    to_text = [(0, 1)]

    if by_rows:
        own_attn = pack_rows(is_not, attn_blocks, row_blocks)[0]
        along_z = [flip(own_attn, bits) for bits in (Z_LOW, Z_HIGH, Z_LOW | Z_HIGH)]
        ffn_rows = pack_rows(is_up, ffn_blocks[0], row_blocks)

    own_vec = lax.dynamic_slice_in_dim(vectors, 3 + 5 * modality, 5, 0)
    vec = jnp.concatenate([own_vec, vectors[0:3]], axis=0)
    up_bias = lax.dynamic_index_in_dim(ffn_bias, modality, 0, keepdims=False)
    up_bias = jnp.swapaxes(up_bias.reshape(row_blocks, chunks, size), 0, 1).reshape(1, hidden_units)
    count = patch_count[0]
    offset = TEXT * (1 - modality)
    first_key = jnp.where(is_text, TEXT, 0)
    end_key = jnp.where(is_text, slots, TEXT + count)
    kept_rows = jnp.where(is_text, slots, count)
    own_core = core if by_rows else 0 * along
    rows_info = jnp.stack([offset, first_key, end_key, modality, kept_rows, own_core])
    rows_info = rows_info.astype(jnp.int32)
    pad = ((0, rows - slots), (0, 0))
    hidden = stream_in[0, 0] + image_flag * jnp.take(pos_table, pos_index[0], axis=0)
    hidden = jnp.pad(hidden, pad)
    pos = jnp.pad(pos_index[0], pad[0], constant_values=-1)[None]
    first = first_norm(rows_info, hidden, vec, seq)
    if by_rows:
        along_z, hidden, first, cotangent, up_bias, pos = sync(
            along_z, hidden, first, cotangent, up_bias, pos
        )
        ffn_parts = lax.all_gather(ffn_rows, "dp", axis=0, axis_index_groups=[ring_order()])
        near = in_order(z % 2, own_attn, along_z[0])
        far = in_order(z % 2, along_z[1], along_z[2])
        attn_z = in_order(z // 2, near, far).reshape(4, size, width)
        upper, lower = attn_z[:, : size * 2 // 3], attn_z[:, size * 2 // 3 :]
        upper_y, lower_x = flip(upper, Y), flip_mod(lower)
    pair_first = lax.ppermute(first[:TEXT], "mod", to_image)
    if by_rows:
        upper_y, lower_x, first, pair_first, cotangent = sync(
            upper_y, lower_x, first, pair_first, cotangent
        )
        upper, lower = in_order(y, upper, upper_y), in_order(modality, lower, lower_x)
        upper_x, lower_y = flip_mod(upper), flip(lower, Y)
    first = lax.dynamic_update_slice(first, jnp.where(is_text, first[:TEXT], pair_first), (0, 0))
    cot = jnp.pad(cotangent[0, 0], pad)

    def by_parts(blocks):
        by_chunk = blocks.reshape(chunks, -1, size, size)
        spread = jnp.swapaxes(blocks.reshape(-1, chunks, size, size), 0, 1)
        return jnp.where(is_up[0] == 1, spread, by_chunk)

    if by_rows:
        ffn_old = [by_parts(part[0]) for part in (ffn_left, ffn_right, ffn_blocks)]
        upper_x, lower_y, first, cot, ffn_old = sync(upper_x, lower_y, first, cot, ffn_old)
        upper, lower = in_order(modality, upper, upper_x), in_order(y, lower, lower_y)
        attn_parts = [upper, flip(upper, CORE), lower, flip(lower, CORE)]
    else:
        attn_all = lax.all_gather(attn_blocks.astype(bf16), ("mod", "dp"), axis=0, tiled=True)
        attn_parts = [square_parts(attn_all, 4 * row_blocks, row_blocks).reshape(4, width, width)]
        ffn_all = lax.all_gather(ffn_blocks[0].astype(bf16), "dp", axis=0, tiled=True)
        shape = (2, row_blocks, row_blocks, chunks, size, size)
        up = ffn_all.reshape(shape)[0].transpose(0, 2, 3, 1, 4)
        down = ffn_all.reshape(2, row_blocks, chunks, row_blocks, size, size)[1]
        down = down.transpose(0, 1, 3, 2, 4)
        ffn_parts = jnp.stack([up, down]).reshape(2 * row_blocks, chunks, size, width)

    qkv, w_attn = project(rows_info, first, vec, attn_parts)
    ctx, lse, pair_ctx = attend(rows_info, qkv)
    pair_ctx = lax.ppermute(pair_ctx, "mod", to_text)
    stream_out, grad_middle, grad_ctx, pair_grad, grad_wo, grad_ffn, late_vec, up_bias_grad = expert(
        rows_info, ctx, pair_ctx, hidden, cot, vec, up_bias, w_attn, ffn_parts, order, slots
    )
    pair_grad = lax.ppermute(pair_grad, "mod", to_image)

    def along_z_of(parts):
        return [flip(part, bits * Z_LOW) for bits, part in enumerate(parts) if bits]

    if by_rows:
        ffn_sum = lax.psum_scatter(
            grad_ffn, "dp", scatter_dimension=0, tiled=True, axis_index_groups=[ring_order()]
        )[0]
    grad_qkv = attend_grad(rows_info, qkv, grad_ctx, pair_grad, ctx, lse)
    attn_keep, attn_send, grad_first, pair_first_grad, sums = project_grad(
        rows_info, grad_qkv, first, w_attn, grad_wo, size
    )
    pair_first_grad = lax.ppermute(pair_first_grad, "mod", to_text)
    up_bias_grad = jnp.swapaxes(up_bias_grad.reshape(chunks, row_blocks, size), 0, 1)
    if by_rows:
        attn_got = flip(attn_send, CORE)
        attn_got, pair_first_grad = sync(attn_got, pair_first_grad)
        both = plus(attn_keep, attn_got).reshape(2, 4, 2, size, width)
        upper, lower = both[..., : size // 2, :], both[..., size // 2 :, :]
        upper_keep, upper_send = pick(upper, modality, 0), pick(upper, 1 - modality, 0)
        lower_keep, lower_send = pick(lower, y, 2), pick(lower, 1 - y, 2)
        upper_keep, upper_send, lower_keep, lower_send, pair_first_grad = sync(
            upper_keep, upper_send, lower_keep, lower_send, pair_first_grad
        )
        upper_got, lower_got = flip_mod(upper_send), flip(lower_send, Y)
    stream_grad, small = first_grad(
        rows_info,
        grad_first,
        pair_first_grad,
        hidden,
        grad_middle,
        vec,
        sums,
        late_vec,
        up_bias_grad.reshape(chunks, width),
        pos,
        slots,
    )
    stream_out = stream_out.reshape(stream_in.shape)
    stream_grad = stream_grad.reshape(stream_in.shape)
    if by_rows:
        small = small.reshape(2, 2, 4, -1, width)
        small_keep, small_send = pick(small, core, 0), pick(small, 1 - core, 0)
        small_got = flip(small_send, CORE)
        upper_got, lower_got, small_got = sync(upper_got, lower_got, small_got)
        upper, lower = plus(upper_keep, upper_got), plus(lower_keep, lower_got)
        small = plus(small_keep, small_got)
        upper = jnp.concatenate([upper, jnp.swapaxes(small, 0, 1)], axis=2)
        upper_keep, upper_send = pick(upper, y, 1), pick(upper, 1 - y, 1)
        lower_keep, lower_send = pick(lower, modality, 0), pick(lower, 1 - modality, 0)
        upper_keep, upper_send, lower_keep, lower_send, ffn_sum = sync(
            upper_keep, upper_send, lower_keep, lower_send, ffn_sum
        )
        upper_got, lower_got = flip(upper_send, Y), flip_mod(lower_send)
        ffn_new = shampoo(is_up, 0, 1, [ffn_sum], *ffn_old)
        upper_got, lower_got, ffn_new = sync(upper_got, lower_got, ffn_new)
        attn = jnp.concatenate([plus(lower_keep, lower_got), plus(upper_keep, upper_got)], axis=1)
        attn_z = [pick(attn, z ^ bits, 0) for bits in range(4)]
        attn_z, ffn_new = sync(attn_z, ffn_new)
        attn_got = along_z_of(attn_z)
        ffn_new = shampoo(is_up, 1, 2, [ffn_sum], *ffn_old, ffn_new)
        attn_got, ffn_new = sync(attn_got, ffn_new)
        small = sum(part[size:].astype(f32) for part in (attn_z[0], *attn_got))
        half = size // 2
        attn_rows = [
            jnp.concatenate([part[half:size], part[:half]], axis=0)[None]
            for part in (attn_z[0], *attn_got)
        ]
        small, attn_rows, ffn_new = sync(small, attn_rows, ffn_new)
        small_got = flip_mod(small)
        ffn_new = shampoo(is_up, 2, 3, [ffn_sum], *ffn_old, ffn_new)
        small_got, ffn_new = sync(small_got, ffn_new)
        small = (small + small_got).astype(bf16)
        small, attn_rows, ffn_new = sync(small, attn_rows, ffn_new)
        small_got = [flip(small, bits * Z_LOW) for bits in (1, 2, 3)]
        attn_old = [part[None] for part in (attn_left, attn_right, attn_blocks)]
        attn_out = shampoo(is_not, 0, 1, attn_rows, *attn_old, mebibytes=56)
        small_got, attn_out = sync(small_got, attn_out)
        near = in_order(z % 2, small, small_got[0])
        far = in_order(z % 2, small_got[1], small_got[2])
        small, ffn_new = sync(in_order(z // 2, near, far), ffn_new)
        small_got = flip(small, Y)
        ffn_out = shampoo(is_up, 3, 4, [ffn_sum], *ffn_old, ffn_new)
        small_got, ffn_out = sync(small_got, ffn_out)
        small = in_order(y, small, small_got)
        small_sum = in_order(core, small, flip(small, CORE)).reshape(-1, width)
    else:
        shape = (row_blocks, chunks, size, row_blocks, size)
        up, down = grad_ffn[:row_blocks].reshape(shape), grad_ffn[row_blocks:].reshape(shape)
        up = up.transpose(0, 3, 1, 2, 4).reshape(-1, size, size)
        down = down.transpose(0, 1, 3, 2, 4).reshape(-1, size, size)
        ffn_sum = lax.psum_scatter(
            jnp.concatenate([up, down], axis=0), "dp", scatter_dimension=0, tiled=True
        )
        attn_full = jnp.stack([attn_keep, attn_send], axis=2).reshape(-1, size, width)
        attn_sum = lax.psum_scatter(
            parts_to_blocks(attn_full), ("mod", "dp"), scatter_dimension=0, tiled=True
        )
        small_sum = lax.psum(small.astype(f32), ("mod", "dp")).astype(bf16)
        ffn_old = [part for part in (ffn_left, ffn_right, ffn_blocks)]
        attn_old = [part[None] for part in (attn_left, attn_right, attn_blocks)]
        ffn_out = shampoo(is_not, 0, 1, [square_parts(ffn_sum, 1, ffn_sum.shape[0])], *ffn_old)
        attn_out = shampoo(is_not, 0, 1, [square_parts(attn_sum, 1, attn_sum.shape[0])], *attn_old)

    items_total = lax.axis_size("dp")
    vector_rate = 0.3 / math.sqrt(items_total * slots)
    pos_rate = 0.5 / math.sqrt(items_total)
    vector_news = momentum_step(
        small_sum, vectors, vectors_mom, ffn_bias, ffn_bias_mom, pos_table, pos_mom, vector_rate, pos_rate
    )
    return (
        stream_out,
        stream_grad,
        *attn_out,
        *(part[None] for part in ffn_out),
        *vector_news,
    )


def solution(mesh):
    items = P("mod", "dp", None, None)
    owned = P(("mod", "dp"), None, None)
    return jax.shard_map(
        local,
        mesh=mesh,
        in_specs=(items, items, P("dp"), P("dp", None), owned, owned, owned, items, items, items)
        + (P(),) * 6,
        out_specs=(items, items, owned, owned, owned, owned, items, items, items, items)
        + (P(),) * 6,
        check_vma=False,
    )
```

```python
import functools
import math

import jax
import jax.numpy as jnp
from jax import lax
from jax.experimental import pallas as pl
from jax.experimental.pallas import tpu as pltpu
from jax.sharding import PartitionSpec as P

HEADS = 12
TEXT = 64
NEWTON = 6
PAIR_LANES = 128
QUERY_TILE = 336
GRAD_TILE = 512

f32 = jnp.float32
bf16 = jnp.bfloat16
norm_eps = 1e-05
stat_decay = 0.5
matrix_rate = 0.25
moment_keep = 0.9
masked_score = -1e30


def dot_nn(left, right):
    return lax.dot_general(left, right, (((1,), (0,)), ((), ())), preferred_element_type=f32)


def dot_nt(left, right):
    return lax.dot_general(left, right, (((1,), (1,)), ((), ())), preferred_element_type=f32)


def dot_tn(left, right):
    return lax.dot_general(left, right, (((0,), (0,)), ((), ())), preferred_element_type=f32)


def params(mebibytes=56):
    return pltpu.CompilerParams(vmem_limit_bytes=mebibytes << 20)


def cost(microseconds):
    return pl.CostEstimate(flops=int(microseconds), bytes_accessed=0, transcendentals=0)


def round_up(value, step):
    return (value + step - 1) // step * step


def whole(shape):
    return pl.BlockSpec(shape, lambda *ids: (0,) * len(shape))


SMEM_SPEC = pl.BlockSpec(memory_space=pltpu.SMEM)


def pack_kernel(up_ref, blocks_ref, out_ref):
    part = pl.program_id(0)
    parts = pl.num_programs(0)
    per_row = blocks_ref.shape[0] // parts
    pieces = []
    for i in range(per_row):
        at = jnp.where(up_ref[0] == 1, i * parts + part, part * per_row + i)
        pieces.append(blocks_ref[at])
    out_ref[0] = jnp.concatenate(pieces, axis=1).astype(bf16)


def pack_rows(is_up, blocks, per_row):
    count, size, _ = blocks.shape
    return pl.pallas_call(
        pack_kernel,
        grid=(count // per_row,),
        in_specs=[SMEM_SPEC, whole(blocks.shape)],
        out_specs=pl.BlockSpec((1, size, per_row * size), lambda i: (i, 0, 0)),
        out_shape=jax.ShapeDtypeStruct((count // per_row, size, per_row * size), bf16),
        compiler_params=params(),
        cost_estimate=cost(3),
        name="pack_rows",
    )(is_up, blocks)


def norm_rows(values):
    centred = values - jnp.mean(values, axis=-1, keepdims=True)
    spread = jnp.mean(centred * centred, axis=-1, keepdims=True)
    inv_std = lax.rsqrt(spread + norm_eps)
    return centred * inv_std, inv_std


def norm_input_grad(grad_out, normal, inv_std, gain):
    grad_norm = grad_out * gain
    mean_grad = jnp.mean(grad_norm, axis=-1, keepdims=True)
    mean_proj = jnp.mean(grad_norm * normal, axis=-1, keepdims=True)
    return inv_std * (grad_norm - mean_grad - normal * mean_proj)


def first_norm_kernel(row_ref, hidden_ref, vec_ref, first_ref):
    rows = hidden_ref.shape[0]
    normal, _ = norm_rows(hidden_ref[...])
    first_ref[...] = jnp.zeros(first_ref.shape, bf16)
    first = normal * vec_ref[0:1, :] + vec_ref[1:2, :]
    first_ref[pl.ds(pl.multiple_of(row_ref[0], 16), rows), :] = first.astype(bf16)


def first_norm(rows_info, hidden, vec, seq):
    return pl.pallas_call(
        first_norm_kernel,
        in_specs=[SMEM_SPEC, whole(hidden.shape), whole(vec.shape)],
        out_specs=whole((seq, hidden.shape[1])),
        out_shape=jax.ShapeDtypeStruct((seq, hidden.shape[1]), bf16),
        compiler_params=params(24),
        cost_estimate=cost(4),
        name="first_norm",
    )(rows_info, hidden, vec)


def project_kernel(row_ref, first_ref, vec_ref, *refs):
    weight_refs, (qkv_ref, w_ref) = refs[:-2], refs[-2:]
    step = pl.program_id(0)
    if len(weight_refs) == 1:
        w_ref[...] = weight_refs[0][...]
    else:
        upper, upper_far, lower, lower_far = weight_refs
        half = upper.shape[3]
        size = half + lower.shape[3]
        on_one = row_ref[5] == 1
        for z in range(2):
            for y in range(2):
                for base, near, far in (
                    (0, upper[0, y, z], upper_far[0, y, z]),
                    (half, lower[y, 0, z], lower_far[y, 0, z]),
                ):
                    start = (4 * z + 2 * y) * size + base
                    end = start + near.shape[0]
                    w_ref[0, start:end, :] = jnp.where(on_one, far, near)
                    w_ref[0, start + size : end + size, :] = jnp.where(on_one, near, far)

    @pl.when(step < 3)
    def _():
        bias = jnp.where(step == 0, vec_ref[5:6, :], jnp.where(step == 2, vec_ref[6:7, :], 0.0))
        qkv_ref[...] = (dot_nn(first_ref[...], w_ref[0]) + bias).astype(bf16)


def project(rows_info, first, vec, attn_parts):
    seq, width = first.shape
    if len(attn_parts) == 1:
        weight_specs = [pl.BlockSpec((1, width, width), lambda i: (i, 0, 0))]
    else:
        rows = [part.shape[3] for part in attn_parts]
        upper = pl.BlockSpec((1, 2, 2, rows[0], width), lambda i: (i // 2, 0, i % 2, 0, 0))
        lower = pl.BlockSpec((2, 1, 2, rows[2], width), lambda i: (0, i // 2, i % 2, 0, 0))
        weight_specs = [upper, upper, lower, lower]
    return pl.pallas_call(
        project_kernel,
        grid=(4,),
        in_specs=[SMEM_SPEC, whole((seq, width)), whole(vec.shape), *weight_specs],
        out_specs=[
            pl.BlockSpec((seq, width), lambda i: (0, jnp.minimum(i, 2))),
            pl.BlockSpec((1, width, width), lambda i: (i, 0, 0)),
        ],
        out_shape=[
            jax.ShapeDtypeStruct((seq, 3 * width), bf16),
            jax.ShapeDtypeStruct((4, width, width), bf16),
        ],
        compiler_params=params(24),
        cost_estimate=cost(8),
        name="project",
    )(rows_info, first, vec, *attn_parts)


def key_bias(row_ref, seq):
    rows = lax.broadcasted_iota(jnp.int32, (seq, 1), 0)
    counts = jnp.logical_and(rows >= row_ref[1], rows < row_ref[2])
    return jnp.where(counts, 0.0, masked_score).astype(f32)


def transposed(values):
    return jnp.transpose(values.astype(f32), (1, 0)).astype(bf16)


def attend_kernel(row_ref, q_ref, k_ref, v_ref, ctx_ref, lse_ref, pair_ref):
    seq = q_ref.shape[0]
    half = PAIR_LANES // 2
    scale = half ** (-0.5)
    lane = lax.broadcasted_iota(jnp.int32, (seq, PAIR_LANES), 1)
    bias = key_bias(row_ref, seq).astype(bf16)
    queries = q_ref[...] * jnp.asarray(scale, bf16)
    keys = k_ref[...]
    values = v_ref[...]
    one = jnp.ones((seq, PAIR_LANES), bf16)
    heads = []
    for head in range(2):
        own = (lane < half) == (head == 0)
        spare = lane == half * (1 - head)
        head_q = jnp.where(own, queries, jnp.where(spare, one, jnp.zeros_like(one)))
        head_k = jnp.where(own, keys, jnp.where(spare, bias, jnp.zeros_like(one)))
        head_v = jnp.where(own, values, one)
        heads.append((head_q, head_k, head_v))
    for start in range(0, seq, QUERY_TILE):
        size = min(QUERY_TILE, seq - start)
        tile = slice(start, start + size)
        parts, lses = [], []
        for head, (head_q, head_k, head_v) in enumerate(heads):
            scores = dot_nt(head_q[tile], head_k)
            top = jnp.max(scores, axis=1, keepdims=True)
            raised = jnp.exp(scores - top).astype(bf16)
            summed = dot_nn(raised, head_v)
            at = half * (1 - head)
            total = summed[:, at : at + 1]
            parts.append(summed * (1.0 / total))
            lses.append(top + jnp.log(total))
        low = lax.broadcasted_iota(jnp.int32, (size, PAIR_LANES), 1) < half
        context = jnp.where(low, parts[0], parts[1]).astype(bf16)
        ctx_ref[tile, :] = context
        if start == 0:
            pair_ref[...] = context[: pair_ref.shape[0]]
        lane8 = lax.broadcasted_iota(jnp.int32, (size, 8), 1)
        lse_ref[0, tile, :] = jnp.where(lane8 == 0, lses[0], lses[1])


def attend(rows_info, qkv):
    seq = qkv.shape[0]
    width = qkv.shape[1] // 3
    pairs = width // PAIR_LANES

    def column(base):
        return pl.BlockSpec((seq, PAIR_LANES), lambda i, base=base: (0, base + i))

    return pl.pallas_call(
        attend_kernel, grid=(pairs,),
        in_specs=[SMEM_SPEC, column(0), column(pairs), column(2 * pairs)],
        out_specs=[column(0), pl.BlockSpec((1, seq, 8), lambda i: (i, 0, 0)), pl.BlockSpec((TEXT, PAIR_LANES), lambda i: (0, i))],
        out_shape=[jax.ShapeDtypeStruct((seq, width), bf16), jax.ShapeDtypeStruct((pairs, seq, 8), f32), jax.ShapeDtypeStruct((TEXT, width), bf16)],
        compiler_params=params(20), cost_estimate=cost(12), name="attend",
    )(rows_info, qkv, qkv, qkv)


def three_parts(values):
    high = values.astype(bf16)
    rest = values - high.astype(f32)
    middle = rest.astype(bf16)
    return high, middle, (rest - middle.astype(f32)).astype(bf16)


def attend_grad_kernel(
    row_ref, q_ref, k_ref, v_ref, g_ref, pair_ref, ctx_ref, lse_ref, out_ref, dk_ref, dv_ref
):
    seq = q_ref.shape[0]
    half = PAIR_LANES // 2
    scale = half ** (-0.5)
    lane = lax.broadcasted_iota(jnp.int32, (seq, PAIR_LANES), 1)
    bias = key_bias(row_ref, seq).astype(bf16)
    queries = q_ref[...]
    scaled = queries * jnp.asarray(scale, bf16)
    keys = k_ref[...]
    values = v_ref[...]
    keys_t = transposed(keys)
    row = lax.broadcasted_iota(jnp.int32, (seq, 1), 0)
    counts = jnp.logical_and(row >= row_ref[1], row < row_ref[2])
    grads = jnp.concatenate([pair_ref[...], g_ref[pair_ref.shape[0] :, :]], axis=0)
    grads = jnp.where(counts, grads, jnp.zeros((seq, PAIR_LANES), bf16))
    products = grads.astype(f32) * ctx_ref[...].astype(f32)
    one = jnp.ones((seq, PAIR_LANES), bf16)
    zero = jnp.zeros((seq, PAIR_LANES), bf16)
    heads = []
    for head in range(2):
        own = (lane < half) == (head == 0)
        spare = lane - half * (1 - head)
        lse = three_parts(-lse_ref[0, :, head : head + 1])
        dots = three_parts(-jnp.sum(jnp.where(own, products, 0.0), axis=1, keepdims=True))
        own_q = jnp.where(own, queries, zero)
        own_g = jnp.where(own, grads, zero)
        head_q = jnp.where(own, scaled, jnp.where(spare == 3, one, zero))
        head_g = own_g
        for i in range(3):
            head_q = jnp.where(spare == i, lse[i], head_q)
            head_g = jnp.where(spare == i, dots[i], head_g)
        head_k = jnp.where(own, keys, jnp.where(spare == 3, bias, one))
        head_v = jnp.where(own, values, one)
        heads.append((head_q, head_g, head_k, head_v, own_q, own_g))
    for start in range(0, seq, GRAD_TILE):
        size = min(GRAD_TILE, seq - start)
        tile = slice(start, start + size)
        parts = []
        for head, (head_q, head_g, head_k, head_v, own_q, own_g) in enumerate(heads):
            probs = jnp.exp(dot_nt(head_k, head_q[tile]))
            grad_scores = (probs * dot_nt(head_v, head_g[tile])).astype(bf16)
            grad_v = dot_nn(probs.astype(bf16), own_g[tile])
            grad_k = dot_nn(grad_scores, own_q[tile])
            if start == 0 and head == 0:
                dv_ref[...] = grad_v
                dk_ref[...] = grad_k
            else:
                dv_ref[...] += grad_v
                dk_ref[...] += grad_k
            parts.append(dot_nn(keys_t[half * head : half * (head + 1), :], grad_scores))
        grad_q = jnp.transpose(jnp.concatenate(parts, axis=0) * scale, (1, 0))
        out_ref[0, tile, :] = grad_q.astype(bf16)
    out_ref[1] = (dk_ref[...] * scale).astype(bf16)
    out_ref[2] = dv_ref[...].astype(bf16)


def attend_grad(rows_info, qkv, grad_ctx, pair_grad, ctx, lse):
    seq = qkv.shape[0]
    width = qkv.shape[1] // 3
    pairs = width // PAIR_LANES

    def column(base):
        return pl.BlockSpec((seq, PAIR_LANES), lambda i, base=base: (0, base + i))

    return pl.pallas_call(
        attend_grad_kernel,
        grid=(pairs,),
        in_specs=[
            SMEM_SPEC,
            column(0),
            column(pairs),
            column(2 * pairs),
            column(0),
            pl.BlockSpec((TEXT, PAIR_LANES), lambda i: (0, i)),
            column(0),
            pl.BlockSpec((1, seq, 8), lambda i: (i, 0, 0)),
        ],
        out_specs=pl.BlockSpec((3, seq, PAIR_LANES), lambda i: (0, 0, i)),
        out_shape=jax.ShapeDtypeStruct((3, seq, width), bf16),
        scratch_shapes=[pltpu.VMEM((seq, PAIR_LANES), f32)] * 2,
        compiler_params=params(20),
        cost_estimate=cost(15),
        name="attend_grad",
    )(rows_info, qkv, qkv, qkv, grad_ctx, pair_grad, ctx, lse)


def gelu_pair(values):
    size = jnp.abs(values)
    tail = 1.0 / (1.0 + (0.3275911 * 0.5**0.5) * size)
    poly = tail * (
        0.254829592
        + tail * (-0.284496736 + tail * (1.421413741 + tail * (-1.453152027 + tail * 1.061405429)))
    )
    bell = jnp.exp(-0.5 * values * values)
    upper = 0.5 * poly * bell
    share = jnp.where(values >= 0.0, 1.0 - upper, upper)
    return values * share, share + values * bell * ((2.0 * math.pi) ** -0.5)


def split_by_core(row_ref, grad, shape):
    size, width = shape[-2:]
    blocks = grad.reshape(-1, 2, size, width)
    near, far = blocks[:, 0], blocks[:, 1]
    on_one = row_ref[5] == 1
    return jnp.where(on_one, far, near).reshape(shape), jnp.where(on_one, near, far).reshape(shape)


def expert_chunk(
    order, second, gbranch, upb, parts_ref, grad_ref, dupb_ref, branch, gsecond, scratch, begin
):
    pre, gact, act, gpre, up, down = scratch
    rows, width = act.shape
    tile = 16
    size = parts_ref.shape[2]
    places = [(which, slice(i * size, (i + 1) * size)) for which in range(2) for i in range(len(order) // 2)]
    for at, (which, span) in zip(order, places):
        (up, down)[which][span, :] = parts_ref[at, 0]
    pre[...] = dot_nn(second[...], up[...])
    gact[...] = dot_nt(gbranch[...], down[...])

    def body(i, total):
        at = pl.ds(pl.multiple_of(i * tile, tile), tile)
        value, slope = gelu_pair(pre[at, :] + upb[...])
        act[at, :] = value.astype(bf16)
        rounded = (gact[at, :] * slope).astype(bf16)
        gpre[at, :] = rounded
        return total + rounded.astype(f32)

    total = lax.fori_loop(0, rows // tile, body, jnp.zeros((tile, width), f32), unroll=True)
    dupb_ref[...] = jnp.sum(total, axis=0, keepdims=True)
    grads = [
        dot_tn(second[...], gpre[...]).astype(bf16),
        dot_tn(act[...], gbranch[...]).astype(bf16),
    ]
    for at, (which, span) in zip(order, places):
        grad_ref[at, 0] = grads[which][span, :]
    own_branch = dot_nn(act[...], down[...])
    own_gsecond = dot_nt(gpre[...], up[...])

    @pl.when(begin)
    def _():
        branch[...] = own_branch
        gsecond[...] = own_gsecond

    @pl.when(jnp.logical_not(begin))
    def _():
        branch[...] += own_branch
        gsecond[...] += own_gsecond


def expert_kernel(
    order,
    row_ref,
    ctx_ref,
    pair_ref,
    hidden_ref,
    cot_ref,
    vec_ref,
    upb_ref,
    wo_ref,
    parts_ref,
    out_ref,
    gmid_ref,
    gctx_ref,
    pair_grad_ref,
    dwo_ref,
    grad_ref,
    dvec_ref,
    dupb_ref,
    own_ctx,
    middle,
    second,
    gbranch,
    branch,
    gsecond,
    *scratch,
):
    step = pl.program_id(0)
    rows, width = hidden_ref.shape
    out_rows = out_ref.shape[0]
    tile = 16

    @pl.when(step == 0)
    def _():
        own_ctx[...] = ctx_ref[pl.ds(pl.multiple_of(row_ref[0], 16), rows), :]

        @pl.when(row_ref[3] == 1)
        def _():
            own_ctx[0 : pair_ref.shape[0], :] = pair_ref[...]

        middle[...] = dot_nn(own_ctx[...], wo_ref[0])

        def body(i, total):
            at = pl.ds(pl.multiple_of(i * tile, tile), tile)
            mid = hidden_ref[at, :] + (middle[at, :] + vec_ref[7:8, :])
            middle[at, :] = mid
            normal, _ = norm_rows(mid)
            second[at, :] = (normal * vec_ref[2:3, :] + vec_ref[3:4, :]).astype(bf16)
            row = lax.broadcasted_iota(jnp.int32, (tile, 1), 0) + i * tile
            kept = jnp.where(row < row_ref[4], cot_ref[at, :], 0.0)
            rounded = kept.astype(bf16)
            gbranch[at, :] = rounded
            return total + rounded.astype(f32)

        total = lax.fori_loop(
            0, rows // tile, body, jnp.zeros((tile, width), f32), unroll=True
        )
        dvec_ref[...] = jnp.zeros(dvec_ref.shape, f32)
        dvec_ref[2:3, :] = jnp.sum(total, axis=0, keepdims=True)

    expert_chunk(
        order,
        second,
        gbranch,
        upb_ref,
        parts_ref,
        grad_ref,
        dupb_ref,
        branch,
        gsecond,
        scratch,
        step == 0,
    )

    @pl.when(step == pl.num_programs(0) - 1)
    def _():
        def body(i, totals):
            at = pl.ds(pl.multiple_of(i * tile, tile), tile)
            mid = middle[at, :]
            normal, inv_std = norm_rows(mid)
            grad_out = gsecond[at, :]
            row = lax.broadcasted_iota(jnp.int32, (tile, 1), 0) + i * tile
            kept = row < row_ref[4]
            branch[at, :] = jnp.where(kept, mid + (branch[at, :] + vec_ref[4:5, :]), 0.0)
            grad_in = norm_input_grad(grad_out, normal, inv_std, vec_ref[2:3, :])
            grad_mid = jnp.where(kept, cot_ref[at, :], 0.0) + grad_in
            gmid_ref[at, :] = grad_mid
            rounded = grad_mid.astype(bf16)
            gbranch[at, :] = rounded
            return (
                totals[0] + grad_out * normal,
                totals[1] + grad_out,
                totals[2] + rounded.astype(f32),
            )

        zero = jnp.zeros((tile, width), f32)
        gains, shifts, biases = lax.fori_loop(
            0, rows // tile, body, (zero, zero, zero), unroll=True
        )
        dvec_ref[0:1, :] = jnp.sum(gains, axis=0, keepdims=True)
        dvec_ref[1:2, :] = jnp.sum(shifts, axis=0, keepdims=True)
        dvec_ref[3:4, :] = jnp.sum(biases, axis=0, keepdims=True)
        out_ref[...] = branch[0:out_rows, :].reshape(out_ref.shape)
        dwo_ref[...] = dot_tn(own_ctx[...], gbranch[...]).astype(bf16)
        grad_ctx = dot_nt(gbranch[...], wo_ref[0]).astype(bf16)
        gctx_ref[...] = jnp.zeros(gctx_ref.shape, bf16)
        gctx_ref[pl.ds(pl.multiple_of(row_ref[0], 16), rows), :] = grad_ctx
        pair_grad_ref[...] = grad_ctx[: pair_grad_ref.shape[0]]


def expert(rows_info, ctx, pair_ctx, hidden, cot, vec, up_bias, w_attn, ffn_parts, order, out_rows):
    rows, width = hidden.shape
    seq = ctx.shape[0]
    blocks, chunks, size, _ = ffn_parts.shape
    parts = pl.BlockSpec((blocks, 1, size, width), lambda i: (0, i, 0, 0))
    return pl.pallas_call(
        functools.partial(expert_kernel, order),
        grid=(chunks,),
        in_specs=[
            SMEM_SPEC,
            whole(ctx.shape),
            whole(pair_ctx.shape),
            whole(hidden.shape),
            whole(cot.shape),
            whole(vec.shape),
            pl.BlockSpec((1, width), lambda i: (0, i)),
            pl.BlockSpec((1, width, width), lambda i: (3, 0, 0)),
            parts,
        ],
        out_specs=[
            whole((out_rows, 1, width)),
            whole((rows, width)),
            whole((seq, width)),
            whole((TEXT, width)),
            whole((width, width)),
            parts,
            whole((8, width)),
            pl.BlockSpec((1, width), lambda i: (0, i)),
        ],
        out_shape=[
            jax.ShapeDtypeStruct((out_rows, 1, width), f32),
            jax.ShapeDtypeStruct((rows, width), f32),
            jax.ShapeDtypeStruct((seq, width), bf16),
            jax.ShapeDtypeStruct((TEXT, width), bf16),
            jax.ShapeDtypeStruct((width, width), bf16),
            jax.ShapeDtypeStruct(ffn_parts.shape, bf16),
            jax.ShapeDtypeStruct((8, width), f32),
            jax.ShapeDtypeStruct((1, chunks * width), f32),
        ],
        scratch_shapes=[
            pltpu.VMEM((rows, width), bf16),
            pltpu.VMEM((rows, width), f32),
            pltpu.VMEM((rows, width), bf16),
            pltpu.VMEM((rows, width), bf16),
            pltpu.VMEM((rows, width), f32),
            pltpu.VMEM((rows, width), f32),
            pltpu.VMEM((rows, width), f32),
            pltpu.VMEM((rows, width), f32),
            pltpu.VMEM((rows, width), bf16),
            pltpu.VMEM((rows, width), bf16),
            pltpu.VMEM((width, width), bf16),
            pltpu.VMEM((width, width), bf16),
        ],
        compiler_params=params(),
        cost_estimate=cost(43),
        name="expert",
    )(rows_info, ctx, pair_ctx, hidden, cot, vec, up_bias, w_attn, ffn_parts)


def project_grad_kernel(
    row_ref, dqkv_ref, first_ref, w_ref, dwo_ref, keep_ref, send_ref, gfirst, pair_ref, sums_ref
):
    step = pl.program_id(0)

    def put(grad):
        keep_ref[0], send_ref[0] = split_by_core(row_ref, grad, keep_ref.shape[1:])

    @pl.when(step < 3)
    def _():
        own = dqkv_ref[0]
        put(dot_tn(first_ref[...], own).astype(bf16))
        share = dot_nt(own, w_ref[0])
        sums = jnp.sum(own.astype(f32), axis=0, keepdims=True)

        @pl.when(step == 0)
        def _():
            gfirst[...] = share
            sums_ref[...] = jnp.zeros(sums_ref.shape, f32)
            sums_ref[0:1, :] = sums

        @pl.when(step > 0)
        def _():
            gfirst[...] += share
            sums_ref[1:2, :] = sums

    @pl.when(step == 3)
    def _():
        put(dwo_ref[...])
        pair_ref[...] = gfirst[0 : pair_ref.shape[0], :]


def project_grad(rows_info, dqkv, first, w_attn, grad_wo, size):
    seq, width = first.shape
    pairs = width // size // 2
    part = pl.BlockSpec((1, pairs, size, width), lambda i: (i, 0, 0, 0))

    def early_index(i):
        return (jnp.minimum(i, 2), 0, 0)

    return pl.pallas_call(
        project_grad_kernel,
        grid=(4,),
        in_specs=[
            SMEM_SPEC,
            pl.BlockSpec((1, seq, width), early_index),
            whole((seq, width)),
            pl.BlockSpec((1, width, width), early_index),
            whole(grad_wo.shape),
        ],
        out_specs=[part, part, whole((seq, width)), whole((TEXT, width)), whole((8, width))],
        out_shape=[
            jax.ShapeDtypeStruct((4, pairs, size, width), bf16),
            jax.ShapeDtypeStruct((4, pairs, size, width), bf16),
            jax.ShapeDtypeStruct((seq, width), f32),
            jax.ShapeDtypeStruct((TEXT, width), f32),
            jax.ShapeDtypeStruct((8, width), f32),
        ],
        compiler_params=params(24),
        cost_estimate=cost(15),
        name="project_grad",
    )(rows_info, dqkv, first, w_attn, grad_wo)


def first_grad_kernel(
    row_ref,
    gfirst_ref,
    pair_ref,
    hidden_ref,
    gmid_ref,
    vec_ref,
    sums_ref,
    late_ref,
    upb_ref,
    pos_ref,
    out_ref,
    small_ref,
    own,
):
    rows, width = hidden_ref.shape
    tile = 16
    own[...] = gfirst_ref[pl.ds(pl.multiple_of(row_ref[0], 16), rows), :]

    @pl.when(row_ref[3] == 1)
    def _():
        own[0 : pair_ref.shape[0], :] = pair_ref[...]

    def body(i, totals):
        at = pl.ds(pl.multiple_of(i * tile, tile), tile)
        normal, inv_std = norm_rows(hidden_ref[at, :])
        grad_out = own[at, :]
        grad_in = norm_input_grad(grad_out, normal, inv_std, vec_ref[0:1, :])
        own[at, :] = gmid_ref[at, :] + grad_in
        return totals[0] + grad_out * normal, totals[1] + grad_out

    zero = jnp.zeros((tile, width), f32)
    gains, shifts = lax.fori_loop(0, rows // tile, body, (zero, zero), unroll=True)
    out_ref[...] = own[0 : out_ref.shape[0], :].reshape(out_ref.shape)
    own_rows = (
        jnp.sum(gains, axis=0, keepdims=True),
        jnp.sum(shifts, axis=0, keepdims=True),
        late_ref[0:1, :],
        late_ref[1:2, :],
        late_ref[2:3, :],
    )
    row = lax.broadcasted_iota(jnp.int32, (16, width), 0)
    top = jnp.where(row == 0, sums_ref[0:1, :], 0.0)
    top = jnp.where(row == 1, sums_ref[1:2, :], top)
    top = jnp.where(row == 2, late_ref[3:4, :], top)
    for i, value in enumerate(own_rows):
        top = jnp.where(row == 3 + 5 * row_ref[3] + i, value, top)
    small_ref[0:16, :] = top.astype(small_ref.dtype)
    row = lax.broadcasted_iota(jnp.int32, (8, width), 0)
    bias = jnp.zeros((8, width), f32)
    for i in range(upb_ref.shape[0]):
        bias = jnp.where(row == upb_ref.shape[0] * row_ref[3] + i, upb_ref[i : i + 1, :], bias)
    small_ref[16:32, :] = jnp.concatenate([bias, jnp.zeros_like(bias)], axis=0).astype(small_ref.dtype)
    grads = own[...]
    high = grads.astype(bf16)
    low = (grads - high.astype(f32)).astype(bf16)
    table = lax.broadcasted_iota(jnp.int32, (rows, rows), 0)
    chosen = jnp.where(row_ref[3] == 0, pos_ref[...], -1) == table
    chosen = jnp.where(chosen, 1.0, 0.0).astype(bf16)
    sums = dot_nn(chosen, high) + dot_nn(chosen, low)
    small_ref[32 : 32 + rows, :] = sums.astype(small_ref.dtype)
    spare = small_ref.shape[0] - 32 - rows
    if spare:
        small_ref[32 + rows :, :] = jnp.zeros((spare, width), small_ref.dtype)


def first_grad(
    rows_info, gfirst, pair_grad, hidden, grad_middle, vec, sums, late, up_bias, pos, out_rows
):
    rows, width = hidden.shape
    small = round_up(32 + rows, 128)
    args = (gfirst, pair_grad, hidden, grad_middle, vec, sums, late, up_bias, pos)
    return pl.pallas_call(
        first_grad_kernel,
        in_specs=[SMEM_SPEC] + [whole(arg.shape) for arg in args],
        out_specs=[whole((out_rows, 1, width)), whole((small, width))],
        out_shape=[
            jax.ShapeDtypeStruct((out_rows, 1, width), f32),
            jax.ShapeDtypeStruct((small, width), bf16),
        ],
        scratch_shapes=[pltpu.VMEM((rows, width), f32)],
        compiler_params=params(24),
        cost_estimate=cost(8),
        name="first_grad",
    )(rows_info, *args)


def widen(values):
    rows, cols = values.shape
    return jnp.concatenate([values, jnp.zeros((rows, PAIR_LANES - cols), f32)], axis=1)


def split_parts(values):
    high = values.astype(bf16)
    return high, (values - high.astype(f32)).astype(bf16)


def left_parts(values):
    return jnp.concatenate(split_parts(values), axis=1)


def right_parts(values):
    high, low = split_parts(values)
    rows, cols = high.shape
    gap = jnp.zeros((cols - rows, cols), bf16)
    near = jnp.concatenate([high, gap, high, gap], axis=0)
    far = jnp.concatenate([low, gap, jnp.zeros((cols, cols), bf16)], axis=0)
    return jnp.concatenate([near, far], axis=1)


def times(left, right):
    both = dot_nn(left, right)
    return both[:, :PAIR_LANES] + both[:, PAIR_LANES:]


def inverse_roots(stats, identity):
    size = stats[0].shape[0]
    mats, factors = [], []
    for stat in stats:
        norm = jnp.sqrt(jnp.sum(stat * stat, keepdims=True))
        mats.append(stat * (1.0 / norm))
        factors.append(lax.rsqrt(jnp.sqrt(norm)))
    for iteration in range(NEWTON):
        steps = [1.25 * identity - 0.25 * mat for mat in mats]
        if iteration == 0:
            factors = [step * factor for step, factor in zip(steps, factors)]
            squares = [times(left_parts(step), right_parts(step)) for step in steps]
        elif iteration < NEWTON - 1:
            both = [
                times(
                    jnp.concatenate([left_parts(step), left_parts(factor)], axis=0),
                    right_parts(step),
                )
                for step, factor in zip(steps, factors)
            ]
            squares = [pair[:size] for pair in both]
            factors = [pair[size:] for pair in both]
        else:
            return [
                times(left_parts(factor), right_parts(step)) for step, factor in zip(steps, factors)
            ]
        fourths = [times(left_parts(square), right_parts(square)) for square in squares]
        mats = [times(left_parts(fourth), right_parts(mat)) for fourth, mat in zip(fourths, mats)]


def shampoo_kernel(group, begin, parts, grad_count, earlier, up_ref, *refs):
    part = begin + pl.program_id(0)
    grad_refs = refs[:grad_count]
    left_ref, right_ref, w_ref = refs[grad_count : grad_count + 3]
    outs = refs[grad_count + 3 + earlier : grad_count + 7 + earlier]
    results, sems = refs[-2:]
    _, count, size, _ = left_ref.shape
    row = lax.broadcasted_iota(jnp.int32, (size, PAIR_LANES), 0)
    col = lax.broadcasted_iota(jnp.int32, (size, PAIR_LANES), 1)
    identity = (row == col).astype(f32)
    copies = []

    def store(kind, i, at, value):
        results[kind, i] = value
        copy = pltpu.make_async_copy(results.at[kind, i], outs[kind].at[at], sems.at[kind, i])
        copy.start()
        copies.append(copy)

    for base in range(0, count, group):
        places, stats, grads = [], [], []
        for i in range(base, base + group):
            at = jnp.where(up_ref[0] == 1, i * parts + part, part * count + i)
            places.append(at)
            span = slice(i * size, (i + 1) * size)
            grad = grad_refs[0][0, :, span].astype(f32)
            for ref in grad_refs[1:]:
                grad = grad + ref[0, :, span].astype(f32)
            store(0, i, at, grad)
            grad = widen(grad)
            grad_t = widen(jnp.transpose(grad, (1, 0))[:size])
            grads.append(grad)
            outer = times(left_parts(grad), right_parts(grad_t))
            inner = times(left_parts(grad_t), right_parts(grad))
            left_new = stat_decay * left_ref[0, i] + (1.0 - stat_decay) * outer[:, :size]
            right_new = stat_decay * right_ref[0, i] + (1.0 - stat_decay) * inner[:, :size]
            store(1, i, at, left_new)
            store(2, i, at, right_new)
            stats += [widen(left_new), widen(right_new)]
        roots = inverse_roots(stats, identity)
        for i, at in enumerate(places):
            half_way = times(left_parts(roots[2 * i]), right_parts(grads[i]))
            update = times(left_parts(half_way), right_parts(roots[2 * i + 1]))
            store(3, base + i, at, w_ref[0, base + i] - matrix_rate * update[:, :size])
    for copy in copies:
        copy.wait()


def shampoo(is_up, begin, end, grad_rows, lefts, rights, weights, earlier=(), mebibytes=24):
    parts, count, size, _ = lefts.shape
    span = count * size
    blocks = pl.BlockSpec((1, count, size, size), lambda i: (begin + i, 0, 0, 0))
    shape = jax.ShapeDtypeStruct((parts * count, size, size), f32)
    anywhere = pl.BlockSpec(memory_space=pl.ANY)
    first_earlier = 4 + len(grad_rows)
    kernel = functools.partial(
        shampoo_kernel, math.gcd(count, 8), begin, parts, len(grad_rows), len(earlier)
    )
    return pl.pallas_call(
        kernel,
        grid=(end - begin,),
        in_specs=[SMEM_SPEC]
        + [pl.BlockSpec((1, size, span), lambda i: (begin + i, 0, 0))] * len(grad_rows)
        + [blocks] * 3
        + [anywhere] * len(earlier),
        out_specs=[anywhere] * 4,
        out_shape=[shape] * 4,
        scratch_shapes=[
            pltpu.VMEM((4, count, size, size), f32),
            pltpu.SemaphoreType.DMA((4, count)),
        ],
        input_output_aliases={first_earlier + i: i for i in range(len(earlier))},
        compiler_params=params(mebibytes),
        cost_estimate=cost(9),
        name="shampoo",
    )(is_up, *grad_rows, lefts, rights, weights, *earlier)


def momentum_kernel(
    vector_rate, pos_rate, sum_ref, v_ref, vm_ref, b_ref, bm_ref, p_ref, pm_ref, vm_out, v_out, bm_out, b_out, pm_out, p_out
):
    width = v_ref.shape[1]
    new = moment_keep * vm_ref[...] + sum_ref[0 : v_ref.shape[0], :].astype(f32)
    vm_out[...] = new
    v_out[...] = v_ref[...] - vector_rate * new
    per_row = b_ref.shape[1] // width
    rows = sum_ref[16:32, :].astype(f32)
    for i in range(b_ref.shape[0]):
        for j in range(per_row):
            at = (slice(i, i + 1), slice(j * width, (j + 1) * width))
            row = i * per_row + j
            new = moment_keep * bm_ref[at] + rows[row : row + 1, :]
            bm_out[at] = new
            b_out[at] = b_ref[at] - vector_rate * new
    new = moment_keep * pm_ref[...] + sum_ref[32 : 32 + p_ref.shape[0], :].astype(f32)
    pm_out[...] = new
    p_out[...] = p_ref[...] - pos_rate * new


def momentum_step(sums, vectors, vectors_mom, bias, bias_mom, table, table_mom, vector_rate, pos_rate):
    args = (sums, vectors, vectors_mom, bias, bias_mom, table, table_mom)
    outs = (vectors, vectors, bias, bias, table, table)
    return pl.pallas_call(
        functools.partial(momentum_kernel, vector_rate, pos_rate),
        in_specs=[whole(arg.shape) for arg in args],
        out_specs=[whole(out.shape) for out in outs],
        out_shape=[jax.ShapeDtypeStruct(out.shape, f32) for out in outs],
        compiler_params=params(24),
        cost_estimate=cost(3),
        name="momentum",
    )(*args)


CORE, Y, Z_LOW, Z_HIGH = 1, 2, 4, 8


def flip(values, bits):
    size = lax.axis_size("dp")
    return lax.ppermute(values, "dp", [(i, i ^ bits) for i in range(size)])


def flip_mod(values):
    return lax.ppermute(values, "mod", [(0, 1), (1, 0)])


def in_order(bit, own, other):
    return jnp.stack([jnp.where(bit == 1, other, own), jnp.where(bit == 1, own, other)])


def ring_order():
    chips = [(z, 0) for z in range(4)] + [(z, 1) for z in reversed(range(4))]
    return [z * 4 + y * 2 + core for z, y in chips for core in range(2)]


def place():
    index = lax.axis_index("dp")
    return index % 2, index // 2 % 2, index // 4


def sync(*values):
    return lax.optimization_barrier(values)


def pick(values, index, axis):
    return lax.dynamic_index_in_dim(values, index, axis, keepdims=False)


def plus(left, right):
    return (left.astype(f32) + right.astype(f32)).astype(bf16)


def square_parts(blocks, rows, cols):
    size = blocks.shape[-1]
    shaped = blocks.reshape(rows, cols, size, size)
    return jnp.swapaxes(shaped, 1, 2).reshape(rows, size, cols * size)


def parts_to_blocks(parts):
    rows, size, span = parts.shape
    shaped = parts.reshape(rows, size, span // size, size)
    return jnp.swapaxes(shaped, 1, 2).reshape(-1, size, size)


def local(
    stream_in,
    cotangent,
    patch_count,
    pos_index,
    attn_blocks,
    attn_left,
    attn_right,
    ffn_blocks,
    ffn_left,
    ffn_right,
    vectors,
    vectors_mom,
    ffn_bias,
    ffn_bias_mom,
    pos_table,
    pos_mom,
):
    size = attn_blocks.shape[-1]
    width = vectors.shape[1]
    hidden_units = ffn_bias.shape[1]
    slots = stream_in.shape[2]
    row_blocks = width // size
    chunks = hidden_units // width
    rows = round_up(slots, 16)
    seq = round_up(slots + TEXT, 32)
    by_rows = lax.axis_size("dp") == 16 and attn_blocks.shape[0] == row_blocks
    modality = lax.axis_index("mod")
    is_text = modality == 1
    image_flag = (1 - modality).astype(f32)
    along = lax.axis_index("dp")
    is_up = jnp.where(along < lax.axis_size("dp") // 2, 1, 0).astype(jnp.int32)[None]
    is_not = jnp.zeros((1,), jnp.int32)

    core, y, z = place()
    order = range(2 * row_blocks)
    if by_rows:
        order = [ring_order().index(device) for device in order]
    order = tuple(order)
    to_image = [(1, 0)]
    to_text = [(0, 1)]

    if by_rows:
        own_attn = pack_rows(is_not, attn_blocks, row_blocks)[0]
        along_z = [flip(own_attn, bits) for bits in (Z_LOW, Z_HIGH, Z_LOW | Z_HIGH)]
        ffn_rows = pack_rows(is_up, ffn_blocks[0], row_blocks)

    own_vec = lax.dynamic_slice_in_dim(vectors, 3 + 5 * modality, 5, 0)
    vec = jnp.concatenate([own_vec, vectors[0:3]], axis=0)
    up_bias = lax.dynamic_index_in_dim(ffn_bias, modality, 0, keepdims=False)
    up_bias = jnp.swapaxes(up_bias.reshape(row_blocks, chunks, size), 0, 1).reshape(1, hidden_units)
    count = patch_count[0]
    offset = TEXT * (1 - modality)
    first_key = jnp.where(is_text, TEXT, 0)
    end_key = jnp.where(is_text, slots, TEXT + count)
    kept_rows = jnp.where(is_text, slots, count)
    own_core = core if by_rows else 0 * along
    rows_info = jnp.stack([offset, first_key, end_key, modality, kept_rows, own_core])
    rows_info = rows_info.astype(jnp.int32)
    pad = ((0, rows - slots), (0, 0))
    hidden = stream_in[0, 0] + image_flag * jnp.take(pos_table, pos_index[0], axis=0)
    hidden = jnp.pad(hidden, pad)
    pos = jnp.pad(pos_index[0], pad[0], constant_values=-1)[None]
    first = first_norm(rows_info, hidden, vec, seq)
    if by_rows:
        along_z, hidden, first, cotangent, up_bias, pos, ffn_rows = sync(
            along_z, hidden, first, cotangent, up_bias, pos, ffn_rows
        )
        ffn_parts = lax.all_gather(ffn_rows, "dp", axis=0, axis_index_groups=[ring_order()])
        near = in_order(z % 2, own_attn, along_z[0])
        far = in_order(z % 2, along_z[1], along_z[2])
        attn_z = in_order(z // 2, near, far).reshape(4, size, width)
        upper, lower = attn_z[:, : size // 2], attn_z[:, size // 2 :]
        upper_y, lower_x = flip(upper, Y), flip_mod(lower)
    pair_first = lax.ppermute(first[:TEXT], "mod", to_image)
    if by_rows:
        upper_y, lower_x, first, pair_first, cotangent = sync(
            upper_y, lower_x, first, pair_first, cotangent
        )
        upper, lower = in_order(y, upper, upper_y), in_order(modality, lower, lower_x)
        upper_x, lower_y = flip_mod(upper), flip(lower, Y)
    first = lax.dynamic_update_slice(first, jnp.where(is_text, first[:TEXT], pair_first), (0, 0))
    cot = jnp.pad(cotangent[0, 0], pad)

    def by_parts(blocks):
        by_chunk = blocks.reshape(chunks, -1, size, size)
        spread = jnp.swapaxes(blocks.reshape(-1, chunks, size, size), 0, 1)
        return jnp.where(is_up[0] == 1, spread, by_chunk)

    if by_rows:
        ffn_old = [by_parts(part[0]) for part in (ffn_left, ffn_right, ffn_blocks)]
        upper_x, lower_y, first, cot, ffn_old = sync(upper_x, lower_y, first, cot, ffn_old)
        upper, lower = in_order(modality, upper, upper_x), in_order(y, lower, lower_y)
        attn_parts = [upper, flip(upper, CORE), lower, flip(lower, CORE)]
    else:
        attn_all = lax.all_gather(attn_blocks.astype(bf16), ("mod", "dp"), axis=0, tiled=True)
        attn_parts = [square_parts(attn_all, 4 * row_blocks, row_blocks).reshape(4, width, width)]
        ffn_all = lax.all_gather(ffn_blocks[0].astype(bf16), "dp", axis=0, tiled=True)
        shape = (2, row_blocks, row_blocks, chunks, size, size)
        up = ffn_all.reshape(shape)[0].transpose(0, 2, 3, 1, 4)
        down = ffn_all.reshape(2, row_blocks, chunks, row_blocks, size, size)[1]
        down = down.transpose(0, 1, 3, 2, 4)
        ffn_parts = jnp.stack([up, down]).reshape(2 * row_blocks, chunks, size, width)

    qkv, w_attn = project(rows_info, first, vec, attn_parts)
    ctx, lse, pair_ctx = attend(rows_info, qkv)
    pair_ctx = lax.ppermute(pair_ctx, "mod", to_text)
    stream_out, grad_middle, grad_ctx, pair_grad, grad_wo, grad_ffn, late_vec, up_bias_grad = expert(
        rows_info, ctx, pair_ctx, hidden, cot, vec, up_bias, w_attn, ffn_parts, order, slots
    )
    pair_grad = lax.ppermute(pair_grad, "mod", to_image)

    def along_z_of(parts):
        return [flip(part, bits * Z_LOW) for bits, part in enumerate(parts) if bits]

    if by_rows:
        ffn_sum = lax.psum_scatter(
            grad_ffn, "dp", scatter_dimension=0, tiled=True, axis_index_groups=[ring_order()]
        )[0]
    grad_qkv = attend_grad(rows_info, qkv, grad_ctx, pair_grad, ctx, lse)
    attn_keep, attn_send, grad_first, pair_first_grad, sums = project_grad(
        rows_info, grad_qkv, first, w_attn, grad_wo, size
    )
    pair_first_grad = lax.ppermute(pair_first_grad, "mod", to_text)
    up_bias_grad = jnp.swapaxes(up_bias_grad.reshape(chunks, row_blocks, size), 0, 1)
    if by_rows:
        attn_got = flip(attn_send, CORE)
        attn_got, pair_first_grad = sync(attn_got, pair_first_grad)
        both = plus(attn_keep, attn_got).reshape(2, 4, 2, size, width)
        upper, lower = both[..., : size // 2, :], both[..., size // 2 :, :]
        upper_keep, upper_send = pick(upper, modality, 0), pick(upper, 1 - modality, 0)
        lower_keep, lower_send = pick(lower, y, 2), pick(lower, 1 - y, 2)
        upper_keep, upper_send, lower_keep, lower_send, pair_first_grad = sync(
            upper_keep, upper_send, lower_keep, lower_send, pair_first_grad
        )
        upper_got, lower_got = flip_mod(upper_send), flip(lower_send, Y)
    stream_grad, small = first_grad(
        rows_info,
        grad_first,
        pair_first_grad,
        hidden,
        grad_middle,
        vec,
        sums,
        late_vec,
        up_bias_grad.reshape(chunks, width),
        pos,
        slots,
    )
    stream_out = stream_out.reshape(stream_in.shape)
    stream_grad = stream_grad.reshape(stream_in.shape)
    if by_rows:
        small = small.reshape(2, 2, 4, -1, width)
        small_keep, small_send = pick(small, core, 0), pick(small, 1 - core, 0)
        small_got = flip(small_send, CORE)
        upper_got, lower_got, small_got = sync(upper_got, lower_got, small_got)
        upper, lower = plus(upper_keep, upper_got), plus(lower_keep, lower_got)
        small = plus(small_keep, small_got)
        upper = jnp.concatenate([upper, jnp.swapaxes(small, 0, 1)], axis=2)
        upper_keep, upper_send = pick(upper, y, 1), pick(upper, 1 - y, 1)
        lower_keep, lower_send = pick(lower, modality, 0), pick(lower, 1 - modality, 0)
        upper_keep, upper_send, lower_keep, lower_send, ffn_sum = sync(
            upper_keep, upper_send, lower_keep, lower_send, ffn_sum
        )
        upper_got, lower_got = flip(upper_send, Y), flip_mod(lower_send)
        ffn_new = shampoo(is_up, 0, 1, [ffn_sum], *ffn_old)
        upper_got, lower_got, ffn_new = sync(upper_got, lower_got, ffn_new)
        attn = jnp.concatenate([plus(lower_keep, lower_got), plus(upper_keep, upper_got)], axis=1)
        attn_z = [pick(attn, z ^ bits, 0) for bits in range(4)]
        attn_z, ffn_new = sync(attn_z, ffn_new)
        attn_got = along_z_of(attn_z)
        ffn_new = shampoo(is_up, 1, 3, [ffn_sum], *ffn_old, ffn_new)
        attn_got, ffn_new = sync(attn_got, ffn_new)
        small = sum(part[size:].astype(f32) for part in (attn_z[0], *attn_got))
        half = size // 2
        attn_rows = [
            jnp.concatenate([part[half:size], part[:half]], axis=0)[None]
            for part in (attn_z[0], *attn_got)
        ]
        small, attn_rows, ffn_new = sync(small, attn_rows, ffn_new)
        small_got = flip_mod(small)
        attn_old = [part[None] for part in (attn_left, attn_right, attn_blocks)]
        attn_out = shampoo(is_not, 0, 1, attn_rows, *attn_old, mebibytes=56)
        small_got, attn_out = sync(small_got, attn_out)
        small = (small + small_got).astype(bf16)
        small, ffn_new = sync(small, ffn_new)
        small_got = [flip(small, bits * Z_LOW) for bits in (1, 2, 3)]
        ffn_out = shampoo(is_up, 3, 4, [ffn_sum], *ffn_old, ffn_new)
        small_got, ffn_out = sync(small_got, ffn_out)
        near = in_order(z % 2, small, small_got[0])
        far = in_order(z % 2, small_got[1], small_got[2])
        small = in_order(z // 2, near, far)
        small = in_order(y, small, flip(small, Y))
        small_sum = in_order(core, small, flip(small, CORE)).reshape(-1, width)
    else:
        shape = (row_blocks, chunks, size, row_blocks, size)
        up, down = grad_ffn[:row_blocks].reshape(shape), grad_ffn[row_blocks:].reshape(shape)
        up = up.transpose(0, 3, 1, 2, 4).reshape(-1, size, size)
        down = down.transpose(0, 1, 3, 2, 4).reshape(-1, size, size)
        ffn_sum = lax.psum_scatter(
            jnp.concatenate([up, down], axis=0), "dp", scatter_dimension=0, tiled=True
        )
        attn_full = jnp.stack([attn_keep, attn_send], axis=2).reshape(-1, size, width)
        attn_sum = lax.psum_scatter(
            parts_to_blocks(attn_full), ("mod", "dp"), scatter_dimension=0, tiled=True
        )
        small_sum = lax.psum(small.astype(f32), ("mod", "dp")).astype(bf16)
        ffn_old = [part for part in (ffn_left, ffn_right, ffn_blocks)]
        attn_old = [part[None] for part in (attn_left, attn_right, attn_blocks)]
        ffn_out = shampoo(is_not, 0, 1, [square_parts(ffn_sum, 1, ffn_sum.shape[0])], *ffn_old)
        attn_out = shampoo(is_not, 0, 1, [square_parts(attn_sum, 1, attn_sum.shape[0])], *attn_old)

    items_total = lax.axis_size("dp")
    vector_rate = 0.3 / math.sqrt(items_total * slots)
    pos_rate = 0.5 / math.sqrt(items_total)
    vector_news = momentum_step(
        small_sum, vectors, vectors_mom, ffn_bias, ffn_bias_mom, pos_table, pos_mom, vector_rate, pos_rate
    )
    return (
        stream_out,
        stream_grad,
        *attn_out,
        *(part[None] for part in ffn_out),
        *vector_news,
    )


def solution(mesh):
    items = P("mod", "dp", None, None)
    owned = P(("mod", "dp"), None, None)
    return jax.shard_map(
        local,
        mesh=mesh,
        in_specs=(items, items, P("dp"), P("dp", None), owned, owned, owned, items, items, items)
        + (P(),) * 6,
        out_specs=(items, items, owned, owned, owned, owned, items, items, items, items)
        + (P(),) * 6,
        check_vma=False,
    )
```

```python
import functools
import math

import jax
import jax.numpy as jnp
from jax import lax
from jax.experimental import pallas as pl
from jax.experimental.pallas import tpu as pltpu
from jax.sharding import PartitionSpec as P

HEADS = 12
TEXT = 64
NEWTON = 6
PAIR_LANES = 128
QUERY_TILE = 336
GRAD_TILE = 512

f32 = jnp.float32
bf16 = jnp.bfloat16
norm_eps = 1e-05
stat_decay = 0.5
matrix_rate = 0.25
moment_keep = 0.9
masked_score = -1e30


def dot_nn(left, right):
    return lax.dot_general(left, right, (((1,), (0,)), ((), ())), preferred_element_type=f32)


def dot_nt(left, right):
    return lax.dot_general(left, right, (((1,), (1,)), ((), ())), preferred_element_type=f32)


def dot_tn(left, right):
    return lax.dot_general(left, right, (((0,), (0,)), ((), ())), preferred_element_type=f32)


def params(mebibytes=56):
    return pltpu.CompilerParams(vmem_limit_bytes=mebibytes << 20)


def cost(microseconds):
    return pl.CostEstimate(flops=int(microseconds), bytes_accessed=0, transcendentals=0)


def round_up(value, step):
    return (value + step - 1) // step * step


def whole(shape):
    return pl.BlockSpec(shape, lambda *ids: (0,) * len(shape))


SMEM_SPEC = pl.BlockSpec(memory_space=pltpu.SMEM)


def pack_kernel(up_ref, blocks_ref, out_ref):
    part = pl.program_id(0)
    parts = pl.num_programs(0)
    per_row = blocks_ref.shape[0] // parts
    pieces = []
    for i in range(per_row):
        at = jnp.where(up_ref[0] == 1, i * parts + part, part * per_row + i)
        pieces.append(blocks_ref[at])
    out_ref[0] = jnp.concatenate(pieces, axis=1).astype(bf16)


def pack_rows(is_up, blocks, per_row):
    count, size, _ = blocks.shape
    return pl.pallas_call(
        pack_kernel,
        grid=(count // per_row,),
        in_specs=[SMEM_SPEC, whole(blocks.shape)],
        out_specs=pl.BlockSpec((1, size, per_row * size), lambda i: (i, 0, 0)),
        out_shape=jax.ShapeDtypeStruct((count // per_row, size, per_row * size), bf16),
        compiler_params=params(),
        cost_estimate=cost(3),
        name="pack_rows",
    )(is_up, blocks)


def norm_rows(values):
    centred = values - jnp.mean(values, axis=-1, keepdims=True)
    spread = jnp.mean(centred * centred, axis=-1, keepdims=True)
    inv_std = lax.rsqrt(spread + norm_eps)
    return centred * inv_std, inv_std


def norm_input_grad(grad_out, normal, inv_std, gain):
    grad_norm = grad_out * gain
    mean_grad = jnp.mean(grad_norm, axis=-1, keepdims=True)
    mean_proj = jnp.mean(grad_norm * normal, axis=-1, keepdims=True)
    return inv_std * (grad_norm - mean_grad - normal * mean_proj)


def first_norm_kernel(row_ref, hidden_ref, vec_ref, first_ref):
    rows = hidden_ref.shape[0]
    normal, _ = norm_rows(hidden_ref[...])
    first_ref[...] = jnp.zeros(first_ref.shape, bf16)
    first = normal * vec_ref[0:1, :] + vec_ref[1:2, :]
    first_ref[pl.ds(pl.multiple_of(row_ref[0], 16), rows), :] = first.astype(bf16)


def first_norm(rows_info, hidden, vec, seq):
    return pl.pallas_call(
        first_norm_kernel,
        in_specs=[SMEM_SPEC, whole(hidden.shape), whole(vec.shape)],
        out_specs=whole((seq, hidden.shape[1])),
        out_shape=jax.ShapeDtypeStruct((seq, hidden.shape[1]), bf16),
        compiler_params=params(24),
        cost_estimate=cost(4),
        name="first_norm",
    )(rows_info, hidden, vec)


def project_kernel(row_ref, first_ref, vec_ref, *refs):
    weight_refs, (qkv_ref, w_ref) = refs[:-2], refs[-2:]
    step = pl.program_id(0)
    if len(weight_refs) == 1:
        w_ref[...] = weight_refs[0][...]
    else:
        upper, upper_far, lower, lower_far = weight_refs
        half = upper.shape[3]
        size = half + lower.shape[3]
        on_one = row_ref[5] == 1
        for z in range(2):
            for y in range(2):
                for base, near, far in (
                    (0, upper[0, y, z], upper_far[0, y, z]),
                    (half, lower[y, 0, z], lower_far[y, 0, z]),
                ):
                    start = (4 * z + 2 * y) * size + base
                    end = start + near.shape[0]
                    w_ref[0, start:end, :] = jnp.where(on_one, far, near)
                    w_ref[0, start + size : end + size, :] = jnp.where(on_one, near, far)

    @pl.when(step < 3)
    def _():
        bias = jnp.where(step == 0, vec_ref[5:6, :], jnp.where(step == 2, vec_ref[6:7, :], 0.0))
        qkv_ref[...] = (dot_nn(first_ref[...], w_ref[0]) + bias).astype(bf16)


def project(rows_info, first, vec, attn_parts):
    seq, width = first.shape
    if len(attn_parts) == 1:
        weight_specs = [pl.BlockSpec((1, width, width), lambda i: (i, 0, 0))]
    else:
        rows = [part.shape[3] for part in attn_parts]
        upper = pl.BlockSpec((1, 2, 2, rows[0], width), lambda i: (i // 2, 0, i % 2, 0, 0))
        lower = pl.BlockSpec((2, 1, 2, rows[2], width), lambda i: (0, i // 2, i % 2, 0, 0))
        weight_specs = [upper, upper, lower, lower]
    return pl.pallas_call(
        project_kernel,
        grid=(4,),
        in_specs=[SMEM_SPEC, whole((seq, width)), whole(vec.shape), *weight_specs],
        out_specs=[
            pl.BlockSpec((seq, width), lambda i: (0, jnp.minimum(i, 2))),
            pl.BlockSpec((1, width, width), lambda i: (i, 0, 0)),
        ],
        out_shape=[
            jax.ShapeDtypeStruct((seq, 3 * width), bf16),
            jax.ShapeDtypeStruct((4, width, width), bf16),
        ],
        compiler_params=params(24),
        cost_estimate=cost(8),
        name="project",
    )(rows_info, first, vec, *attn_parts)


def key_bias(row_ref, seq):
    rows = lax.broadcasted_iota(jnp.int32, (seq, 1), 0)
    counts = jnp.logical_and(rows >= row_ref[1], rows < row_ref[2])
    return jnp.where(counts, 0.0, masked_score).astype(f32)


def transposed(values):
    return jnp.transpose(values.astype(f32), (1, 0)).astype(bf16)


def attend_kernel(row_ref, q_ref, k_ref, v_ref, ctx_ref, lse_ref, pair_ref):
    seq = q_ref.shape[0]
    half = PAIR_LANES // 2
    scale = half ** (-0.5)
    lane = lax.broadcasted_iota(jnp.int32, (seq, PAIR_LANES), 1)
    bias = key_bias(row_ref, seq).astype(bf16)
    queries = q_ref[...] * jnp.asarray(scale, bf16)
    keys = k_ref[...]
    values = v_ref[...]
    one = jnp.ones((seq, PAIR_LANES), bf16)
    heads = []
    for head in range(2):
        own = (lane < half) == (head == 0)
        spare = lane == half * (1 - head)
        head_q = jnp.where(own, queries, jnp.where(spare, one, jnp.zeros_like(one)))
        head_k = jnp.where(own, keys, jnp.where(spare, bias, jnp.zeros_like(one)))
        head_v = jnp.where(own, values, one)
        heads.append((head_q, head_k, head_v))
    for start in range(0, seq, QUERY_TILE):
        size = min(QUERY_TILE, seq - start)
        tile = slice(start, start + size)
        parts, lses = [], []
        for head, (head_q, head_k, head_v) in enumerate(heads):
            scores = dot_nt(head_q[tile], head_k)
            top = jnp.max(scores, axis=1, keepdims=True)
            raised = jnp.exp(scores - top).astype(bf16)
            summed = dot_nn(raised, head_v)
            at = half * (1 - head)
            total = summed[:, at : at + 1]
            parts.append(summed * (1.0 / total))
            lses.append(top + jnp.log(total))
        low = lax.broadcasted_iota(jnp.int32, (size, PAIR_LANES), 1) < half
        context = jnp.where(low, parts[0], parts[1]).astype(bf16)
        ctx_ref[tile, :] = context
        if start == 0:
            pair_ref[...] = context[: pair_ref.shape[0]]
        lane8 = lax.broadcasted_iota(jnp.int32, (size, 8), 1)
        lse_ref[0, tile, :] = jnp.where(lane8 == 0, lses[0], lses[1])


def attend(rows_info, qkv):
    seq = qkv.shape[0]
    width = qkv.shape[1] // 3
    pairs = width // PAIR_LANES

    def column(base):
        return pl.BlockSpec((seq, PAIR_LANES), lambda i, base=base: (0, base + i))

    return pl.pallas_call(
        attend_kernel, grid=(pairs,),
        in_specs=[SMEM_SPEC, column(0), column(pairs), column(2 * pairs)],
        out_specs=[column(0), pl.BlockSpec((1, seq, 8), lambda i: (i, 0, 0)), pl.BlockSpec((TEXT, PAIR_LANES), lambda i: (0, i))],
        out_shape=[jax.ShapeDtypeStruct((seq, width), bf16), jax.ShapeDtypeStruct((pairs, seq, 8), f32), jax.ShapeDtypeStruct((TEXT, width), bf16)],
        compiler_params=params(20), cost_estimate=cost(12), name="attend",
    )(rows_info, qkv, qkv, qkv)


def three_parts(values):
    high = values.astype(bf16)
    rest = values - high.astype(f32)
    middle = rest.astype(bf16)
    return high, middle, (rest - middle.astype(f32)).astype(bf16)


def attend_grad_kernel(
    row_ref, q_ref, k_ref, v_ref, g_ref, pair_ref, ctx_ref, lse_ref, out_ref, dk_ref, dv_ref
):
    seq = q_ref.shape[0]
    half = PAIR_LANES // 2
    scale = half ** (-0.5)
    lane = lax.broadcasted_iota(jnp.int32, (seq, PAIR_LANES), 1)
    bias = key_bias(row_ref, seq).astype(bf16)
    queries = q_ref[...]
    scaled = queries * jnp.asarray(scale, bf16)
    keys = k_ref[...]
    values = v_ref[...]
    keys_t = transposed(keys)
    row = lax.broadcasted_iota(jnp.int32, (seq, 1), 0)
    counts = jnp.logical_and(row >= row_ref[1], row < row_ref[2])
    grads = jnp.concatenate([pair_ref[...], g_ref[pair_ref.shape[0] :, :]], axis=0)
    grads = jnp.where(counts, grads, jnp.zeros((seq, PAIR_LANES), bf16))
    products = grads.astype(f32) * ctx_ref[...].astype(f32)
    one = jnp.ones((seq, PAIR_LANES), bf16)
    zero = jnp.zeros((seq, PAIR_LANES), bf16)
    heads = []
    for head in range(2):
        own = (lane < half) == (head == 0)
        spare = lane - half * (1 - head)
        lse = three_parts(-lse_ref[0, :, head : head + 1])
        dots = three_parts(-jnp.sum(jnp.where(own, products, 0.0), axis=1, keepdims=True))
        own_q = jnp.where(own, queries, zero)
        own_g = jnp.where(own, grads, zero)
        head_q = jnp.where(own, scaled, jnp.where(spare == 3, one, zero))
        head_g = own_g
        for i in range(3):
            head_q = jnp.where(spare == i, lse[i], head_q)
            head_g = jnp.where(spare == i, dots[i], head_g)
        head_k = jnp.where(own, keys, jnp.where(spare == 3, bias, one))
        head_v = jnp.where(own, values, one)
        heads.append((head_q, head_g, head_k, head_v, own_q, own_g))
    for start in range(0, seq, GRAD_TILE):
        size = min(GRAD_TILE, seq - start)
        tile = slice(start, start + size)
        parts = []
        for head, (head_q, head_g, head_k, head_v, own_q, own_g) in enumerate(heads):
            probs = jnp.exp(dot_nt(head_k, head_q[tile]))
            grad_scores = (probs * dot_nt(head_v, head_g[tile])).astype(bf16)
            grad_v = dot_nn(probs.astype(bf16), own_g[tile])
            grad_k = dot_nn(grad_scores, own_q[tile])
            if start == 0 and head == 0:
                dv_ref[...] = grad_v
                dk_ref[...] = grad_k
            else:
                dv_ref[...] += grad_v
                dk_ref[...] += grad_k
            parts.append(dot_nn(keys_t[half * head : half * (head + 1), :], grad_scores))
        grad_q = jnp.transpose(jnp.concatenate(parts, axis=0) * scale, (1, 0))
        out_ref[0, tile, :] = grad_q.astype(bf16)
    out_ref[1] = (dk_ref[...] * scale).astype(bf16)
    out_ref[2] = dv_ref[...].astype(bf16)


def attend_grad(rows_info, qkv, grad_ctx, pair_grad, ctx, lse):
    seq = qkv.shape[0]
    width = qkv.shape[1] // 3
    pairs = width // PAIR_LANES

    def column(base):
        return pl.BlockSpec((seq, PAIR_LANES), lambda i, base=base: (0, base + i))

    return pl.pallas_call(
        attend_grad_kernel,
        grid=(pairs,),
        in_specs=[
            SMEM_SPEC,
            column(0),
            column(pairs),
            column(2 * pairs),
            column(0),
            pl.BlockSpec((TEXT, PAIR_LANES), lambda i: (0, i)),
            column(0),
            pl.BlockSpec((1, seq, 8), lambda i: (i, 0, 0)),
        ],
        out_specs=pl.BlockSpec((3, seq, PAIR_LANES), lambda i: (0, 0, i)),
        out_shape=jax.ShapeDtypeStruct((3, seq, width), bf16),
        scratch_shapes=[pltpu.VMEM((seq, PAIR_LANES), f32)] * 2,
        compiler_params=params(56),
        cost_estimate=cost(15),
        name="attend_grad",
    )(rows_info, qkv, qkv, qkv, grad_ctx, pair_grad, ctx, lse)


def gelu_pair(values):
    size = jnp.abs(values)
    tail = 1.0 / (1.0 + (0.3275911 * 0.5**0.5) * size)
    poly = tail * (
        0.254829592
        + tail * (-0.284496736 + tail * (1.421413741 + tail * (-1.453152027 + tail * 1.061405429)))
    )
    bell = jnp.exp(-0.5 * values * values)
    upper = 0.5 * poly * bell
    share = jnp.where(values >= 0.0, 1.0 - upper, upper)
    return values * share, share + values * bell * ((2.0 * math.pi) ** -0.5)


def split_by_core(row_ref, grad, shape):
    size, width = shape[-2:]
    blocks = grad.reshape(-1, 2, size, width)
    near, far = blocks[:, 0], blocks[:, 1]
    on_one = row_ref[5] == 1
    return jnp.where(on_one, far, near).reshape(shape), jnp.where(on_one, near, far).reshape(shape)


def expert_chunk(
    order, second, gbranch, upb, parts_ref, grad_ref, dupb_ref, branch, gsecond, scratch, begin
):
    pre, gact, act, gpre, up, down = scratch
    rows, width = act.shape
    tile = 16
    size = parts_ref.shape[2]
    places = [(which, slice(i * size, (i + 1) * size)) for which in range(2) for i in range(len(order) // 2)]
    for at, (which, span) in zip(order, places):
        (up, down)[which][span, :] = parts_ref[at, 0]
    pre[...] = dot_nn(second[...], up[...])
    gact[...] = dot_nt(gbranch[...], down[...])

    def body(i, total):
        at = pl.ds(pl.multiple_of(i * tile, tile), tile)
        value, slope = gelu_pair(pre[at, :] + upb[...])
        act[at, :] = value.astype(bf16)
        rounded = (gact[at, :] * slope).astype(bf16)
        gpre[at, :] = rounded
        return total + rounded.astype(f32)

    total = lax.fori_loop(0, rows // tile, body, jnp.zeros((tile, width), f32), unroll=True)
    dupb_ref[...] = jnp.sum(total, axis=0, keepdims=True)
    grads = [
        dot_tn(second[...], gpre[...]).astype(bf16),
        dot_tn(act[...], gbranch[...]).astype(bf16),
    ]
    for at, (which, span) in zip(order, places):
        grad_ref[at, 0] = grads[which][span, :]
    own_branch = dot_nn(act[...], down[...])
    own_gsecond = dot_nt(gpre[...], up[...])

    @pl.when(begin)
    def _():
        branch[...] = own_branch
        gsecond[...] = own_gsecond

    @pl.when(jnp.logical_not(begin))
    def _():
        branch[...] += own_branch
        gsecond[...] += own_gsecond


def expert_kernel(
    order,
    row_ref,
    ctx_ref,
    pair_ref,
    hidden_ref,
    cot_ref,
    vec_ref,
    upb_ref,
    wo_ref,
    parts_ref,
    out_ref,
    gmid_ref,
    gctx_ref,
    pair_grad_ref,
    dwo_ref,
    grad_ref,
    dvec_ref,
    dupb_ref,
    own_ctx,
    middle,
    second,
    gbranch,
    branch,
    gsecond,
    *scratch,
):
    step = pl.program_id(0)
    rows, width = hidden_ref.shape
    out_rows = out_ref.shape[0]
    tile = 16

    @pl.when(step == 0)
    def _():
        own_ctx[...] = ctx_ref[pl.ds(pl.multiple_of(row_ref[0], 16), rows), :]

        @pl.when(row_ref[3] == 1)
        def _():
            own_ctx[0 : pair_ref.shape[0], :] = pair_ref[...]

        middle[...] = dot_nn(own_ctx[...], wo_ref[0])

        def body(i, total):
            at = pl.ds(pl.multiple_of(i * tile, tile), tile)
            mid = hidden_ref[at, :] + (middle[at, :] + vec_ref[7:8, :])
            middle[at, :] = mid
            normal, _ = norm_rows(mid)
            second[at, :] = (normal * vec_ref[2:3, :] + vec_ref[3:4, :]).astype(bf16)
            row = lax.broadcasted_iota(jnp.int32, (tile, 1), 0) + i * tile
            kept = jnp.where(row < row_ref[4], cot_ref[at, :], 0.0)
            rounded = kept.astype(bf16)
            gbranch[at, :] = rounded
            return total + rounded.astype(f32)

        total = lax.fori_loop(
            0, rows // tile, body, jnp.zeros((tile, width), f32), unroll=True
        )
        dvec_ref[...] = jnp.zeros(dvec_ref.shape, f32)
        dvec_ref[2:3, :] = jnp.sum(total, axis=0, keepdims=True)

    expert_chunk(
        order,
        second,
        gbranch,
        upb_ref,
        parts_ref,
        grad_ref,
        dupb_ref,
        branch,
        gsecond,
        scratch,
        step == 0,
    )

    @pl.when(step == pl.num_programs(0) - 1)
    def _():
        def body(i, totals):
            at = pl.ds(pl.multiple_of(i * tile, tile), tile)
            mid = middle[at, :]
            normal, inv_std = norm_rows(mid)
            grad_out = gsecond[at, :]
            row = lax.broadcasted_iota(jnp.int32, (tile, 1), 0) + i * tile
            kept = row < row_ref[4]
            branch[at, :] = jnp.where(kept, mid + (branch[at, :] + vec_ref[4:5, :]), 0.0)
            grad_in = norm_input_grad(grad_out, normal, inv_std, vec_ref[2:3, :])
            grad_mid = jnp.where(kept, cot_ref[at, :], 0.0) + grad_in
            gmid_ref[at, :] = grad_mid
            rounded = grad_mid.astype(bf16)
            gbranch[at, :] = rounded
            return (
                totals[0] + grad_out * normal,
                totals[1] + grad_out,
                totals[2] + rounded.astype(f32),
            )

        zero = jnp.zeros((tile, width), f32)
        gains, shifts, biases = lax.fori_loop(
            0, rows // tile, body, (zero, zero, zero), unroll=True
        )
        dvec_ref[0:1, :] = jnp.sum(gains, axis=0, keepdims=True)
        dvec_ref[1:2, :] = jnp.sum(shifts, axis=0, keepdims=True)
        dvec_ref[3:4, :] = jnp.sum(biases, axis=0, keepdims=True)
        out_ref[...] = branch[0:out_rows, :].reshape(out_ref.shape)
        dwo_ref[...] = dot_tn(own_ctx[...], gbranch[...]).astype(bf16)
        grad_ctx = dot_nt(gbranch[...], wo_ref[0]).astype(bf16)
        gctx_ref[...] = jnp.zeros(gctx_ref.shape, bf16)
        gctx_ref[pl.ds(pl.multiple_of(row_ref[0], 16), rows), :] = grad_ctx
        pair_grad_ref[...] = grad_ctx[: pair_grad_ref.shape[0]]


def expert(rows_info, ctx, pair_ctx, hidden, cot, vec, up_bias, w_attn, ffn_parts, order, out_rows):
    rows, width = hidden.shape
    seq = ctx.shape[0]
    blocks, chunks, size, _ = ffn_parts.shape
    parts = pl.BlockSpec((blocks, 1, size, width), lambda i: (0, i, 0, 0))
    return pl.pallas_call(
        functools.partial(expert_kernel, order),
        grid=(chunks,),
        in_specs=[
            SMEM_SPEC,
            whole(ctx.shape),
            whole(pair_ctx.shape),
            whole(hidden.shape),
            whole(cot.shape),
            whole(vec.shape),
            pl.BlockSpec((1, width), lambda i: (0, i)),
            pl.BlockSpec((1, width, width), lambda i: (3, 0, 0)),
            parts,
        ],
        out_specs=[
            whole((out_rows, 1, width)),
            whole((rows, width)),
            whole((seq, width)),
            whole((TEXT, width)),
            whole((width, width)),
            parts,
            whole((8, width)),
            pl.BlockSpec((1, width), lambda i: (0, i)),
        ],
        out_shape=[
            jax.ShapeDtypeStruct((out_rows, 1, width), f32),
            jax.ShapeDtypeStruct((rows, width), f32),
            jax.ShapeDtypeStruct((seq, width), bf16),
            jax.ShapeDtypeStruct((TEXT, width), bf16),
            jax.ShapeDtypeStruct((width, width), bf16),
            jax.ShapeDtypeStruct(ffn_parts.shape, bf16),
            jax.ShapeDtypeStruct((8, width), f32),
            jax.ShapeDtypeStruct((1, chunks * width), f32),
        ],
        scratch_shapes=[
            pltpu.VMEM((rows, width), bf16),
            pltpu.VMEM((rows, width), f32),
            pltpu.VMEM((rows, width), bf16),
            pltpu.VMEM((rows, width), bf16),
            pltpu.VMEM((rows, width), f32),
            pltpu.VMEM((rows, width), f32),
            pltpu.VMEM((rows, width), f32),
            pltpu.VMEM((rows, width), f32),
            pltpu.VMEM((rows, width), bf16),
            pltpu.VMEM((rows, width), bf16),
            pltpu.VMEM((width, width), bf16),
            pltpu.VMEM((width, width), bf16),
        ],
        compiler_params=params(),
        cost_estimate=cost(43),
        name="expert",
    )(rows_info, ctx, pair_ctx, hidden, cot, vec, up_bias, w_attn, ffn_parts)


def project_grad_kernel(
    row_ref, dqkv_ref, first_ref, w_ref, dwo_ref, keep_ref, send_ref, gfirst, pair_ref, sums_ref
):
    step = pl.program_id(0)

    def put(grad):
        keep_ref[0], send_ref[0] = split_by_core(row_ref, grad, keep_ref.shape[1:])

    @pl.when(step < 3)
    def _():
        own = dqkv_ref[0]
        put(dot_tn(first_ref[...], own).astype(bf16))
        share = dot_nt(own, w_ref[0])
        sums = jnp.sum(own.astype(f32), axis=0, keepdims=True)

        @pl.when(step == 0)
        def _():
            gfirst[...] = share
            sums_ref[...] = jnp.zeros(sums_ref.shape, f32)
            sums_ref[0:1, :] = sums

        @pl.when(step > 0)
        def _():
            gfirst[...] += share
            sums_ref[1:2, :] = sums

    @pl.when(step == 3)
    def _():
        put(dwo_ref[...])
        pair_ref[...] = gfirst[0 : pair_ref.shape[0], :]


def project_grad(rows_info, dqkv, first, w_attn, grad_wo, size):
    seq, width = first.shape
    pairs = width // size // 2
    part = pl.BlockSpec((1, pairs, size, width), lambda i: (i, 0, 0, 0))

    def early_index(i):
        return (jnp.minimum(i, 2), 0, 0)

    return pl.pallas_call(
        project_grad_kernel,
        grid=(4,),
        in_specs=[
            SMEM_SPEC,
            pl.BlockSpec((1, seq, width), early_index),
            whole((seq, width)),
            pl.BlockSpec((1, width, width), early_index),
            whole(grad_wo.shape),
        ],
        out_specs=[part, part, whole((seq, width)), whole((TEXT, width)), whole((8, width))],
        out_shape=[
            jax.ShapeDtypeStruct((4, pairs, size, width), bf16),
            jax.ShapeDtypeStruct((4, pairs, size, width), bf16),
            jax.ShapeDtypeStruct((seq, width), f32),
            jax.ShapeDtypeStruct((TEXT, width), f32),
            jax.ShapeDtypeStruct((8, width), f32),
        ],
        compiler_params=params(56),
        cost_estimate=cost(15),
        name="project_grad",
    )(rows_info, dqkv, first, w_attn, grad_wo)


def first_grad_kernel(
    row_ref,
    gfirst_ref,
    pair_ref,
    hidden_ref,
    gmid_ref,
    vec_ref,
    sums_ref,
    late_ref,
    upb_ref,
    pos_ref,
    out_ref,
    small_ref,
    own,
):
    rows, width = hidden_ref.shape
    tile = 16
    own[...] = gfirst_ref[pl.ds(pl.multiple_of(row_ref[0], 16), rows), :]

    @pl.when(row_ref[3] == 1)
    def _():
        own[0 : pair_ref.shape[0], :] = pair_ref[...]

    def body(i, totals):
        at = pl.ds(pl.multiple_of(i * tile, tile), tile)
        normal, inv_std = norm_rows(hidden_ref[at, :])
        grad_out = own[at, :]
        grad_in = norm_input_grad(grad_out, normal, inv_std, vec_ref[0:1, :])
        own[at, :] = gmid_ref[at, :] + grad_in
        return totals[0] + grad_out * normal, totals[1] + grad_out

    zero = jnp.zeros((tile, width), f32)
    gains, shifts = lax.fori_loop(0, rows // tile, body, (zero, zero), unroll=True)
    out_ref[...] = own[0 : out_ref.shape[0], :].reshape(out_ref.shape)
    own_rows = (
        jnp.sum(gains, axis=0, keepdims=True),
        jnp.sum(shifts, axis=0, keepdims=True),
        late_ref[0:1, :],
        late_ref[1:2, :],
        late_ref[2:3, :],
    )
    row = lax.broadcasted_iota(jnp.int32, (16, width), 0)
    top = jnp.where(row == 0, sums_ref[0:1, :], 0.0)
    top = jnp.where(row == 1, sums_ref[1:2, :], top)
    top = jnp.where(row == 2, late_ref[3:4, :], top)
    for i, value in enumerate(own_rows):
        top = jnp.where(row == 3 + 5 * row_ref[3] + i, value, top)
    small_ref[0:16, :] = top.astype(small_ref.dtype)
    row = lax.broadcasted_iota(jnp.int32, (8, width), 0)
    bias = jnp.zeros((8, width), f32)
    for i in range(upb_ref.shape[0]):
        bias = jnp.where(row == upb_ref.shape[0] * row_ref[3] + i, upb_ref[i : i + 1, :], bias)
    small_ref[16:32, :] = jnp.concatenate([bias, jnp.zeros_like(bias)], axis=0).astype(small_ref.dtype)
    grads = own[...]
    high = grads.astype(bf16)
    low = (grads - high.astype(f32)).astype(bf16)
    table = lax.broadcasted_iota(jnp.int32, (rows, rows), 0)
    chosen = jnp.where(row_ref[3] == 0, pos_ref[...], -1) == table
    chosen = jnp.where(chosen, 1.0, 0.0).astype(bf16)
    sums = dot_nn(chosen, high) + dot_nn(chosen, low)
    small_ref[32 : 32 + rows, :] = sums.astype(small_ref.dtype)
    spare = small_ref.shape[0] - 32 - rows
    if spare:
        small_ref[32 + rows :, :] = jnp.zeros((spare, width), small_ref.dtype)


def first_grad(
    rows_info, gfirst, pair_grad, hidden, grad_middle, vec, sums, late, up_bias, pos, out_rows
):
    rows, width = hidden.shape
    small = round_up(32 + rows, 128)
    args = (gfirst, pair_grad, hidden, grad_middle, vec, sums, late, up_bias, pos)
    return pl.pallas_call(
        first_grad_kernel,
        in_specs=[SMEM_SPEC] + [whole(arg.shape) for arg in args],
        out_specs=[whole((out_rows, 1, width)), whole((small, width))],
        out_shape=[
            jax.ShapeDtypeStruct((out_rows, 1, width), f32),
            jax.ShapeDtypeStruct((small, width), bf16),
        ],
        scratch_shapes=[pltpu.VMEM((rows, width), f32)],
        compiler_params=params(24),
        cost_estimate=cost(8),
        name="first_grad",
    )(rows_info, *args)


def widen(values):
    rows, cols = values.shape
    return jnp.concatenate([values, jnp.zeros((rows, PAIR_LANES - cols), f32)], axis=1)


def split_parts(values):
    high = values.astype(bf16)
    return high, (values - high.astype(f32)).astype(bf16)


def left_parts(values):
    return jnp.concatenate(split_parts(values), axis=1)


def right_parts(values):
    high, low = split_parts(values)
    rows, cols = high.shape
    gap = jnp.zeros((cols - rows, cols), bf16)
    near = jnp.concatenate([high, gap, high, gap], axis=0)
    far = jnp.concatenate([low, gap, jnp.zeros((cols, cols), bf16)], axis=0)
    return jnp.concatenate([near, far], axis=1)


def times(left, right):
    both = dot_nn(left, right)
    return both[:, :PAIR_LANES] + both[:, PAIR_LANES:]


def inverse_roots(stats, identity):
    size = stats[0].shape[0]
    mats, factors = [], []
    for stat in stats:
        norm = jnp.sqrt(jnp.sum(stat * stat, keepdims=True))
        mats.append(stat * (1.0 / norm))
        factors.append(lax.rsqrt(jnp.sqrt(norm)))
    for iteration in range(NEWTON):
        steps = [1.25 * identity - 0.25 * mat for mat in mats]
        if iteration == 0:
            factors = [step * factor for step, factor in zip(steps, factors)]
            squares = [times(left_parts(step), right_parts(step)) for step in steps]
        elif iteration < NEWTON - 1:
            both = [
                times(
                    jnp.concatenate([left_parts(step), left_parts(factor)], axis=0),
                    right_parts(step),
                )
                for step, factor in zip(steps, factors)
            ]
            squares = [pair[:size] for pair in both]
            factors = [pair[size:] for pair in both]
        else:
            return [
                times(left_parts(factor), right_parts(step)) for step, factor in zip(steps, factors)
            ]
        fourths = [times(left_parts(square), right_parts(square)) for square in squares]
        mats = [times(left_parts(fourth), right_parts(mat)) for fourth, mat in zip(fourths, mats)]


def shampoo_kernel(group, begin, parts, grad_count, earlier, up_ref, *refs):
    part = begin + pl.program_id(0)
    grad_refs = refs[:grad_count]
    left_ref, right_ref, w_ref = refs[grad_count : grad_count + 3]
    outs = refs[grad_count + 3 + earlier : grad_count + 7 + earlier]
    results, sems = refs[-2:]
    _, count, size, _ = left_ref.shape
    row = lax.broadcasted_iota(jnp.int32, (size, PAIR_LANES), 0)
    col = lax.broadcasted_iota(jnp.int32, (size, PAIR_LANES), 1)
    identity = (row == col).astype(f32)
    copies = []

    def store(kind, i, at, value):
        results[kind, i] = value
        copy = pltpu.make_async_copy(results.at[kind, i], outs[kind].at[at], sems.at[kind, i])
        copy.start()
        copies.append(copy)

    for base in range(0, count, group):
        places, stats, grads = [], [], []
        for i in range(base, base + group):
            at = jnp.where(up_ref[0] == 1, i * parts + part, part * count + i)
            places.append(at)
            span = slice(i * size, (i + 1) * size)
            grad = grad_refs[0][0, :, span].astype(f32)
            for ref in grad_refs[1:]:
                grad = grad + ref[0, :, span].astype(f32)
            store(0, i, at, grad)
            grad = widen(grad)
            grad_t = widen(jnp.transpose(grad, (1, 0))[:size])
            grads.append(grad)
            outer = times(left_parts(grad), right_parts(grad_t))
            inner = times(left_parts(grad_t), right_parts(grad))
            left_new = stat_decay * left_ref[0, i] + (1.0 - stat_decay) * outer[:, :size]
            right_new = stat_decay * right_ref[0, i] + (1.0 - stat_decay) * inner[:, :size]
            store(1, i, at, left_new)
            store(2, i, at, right_new)
            stats += [widen(left_new), widen(right_new)]
        roots = inverse_roots(stats, identity)
        for i, at in enumerate(places):
            half_way = times(left_parts(roots[2 * i]), right_parts(grads[i]))
            update = times(left_parts(half_way), right_parts(roots[2 * i + 1]))
            store(3, base + i, at, w_ref[0, base + i] - matrix_rate * update[:, :size])
    for copy in copies:
        copy.wait()


def shampoo(is_up, begin, end, grad_rows, lefts, rights, weights, earlier=(), mebibytes=24):
    parts, count, size, _ = lefts.shape
    span = count * size
    blocks = pl.BlockSpec((1, count, size, size), lambda i: (begin + i, 0, 0, 0))
    shape = jax.ShapeDtypeStruct((parts * count, size, size), f32)
    anywhere = pl.BlockSpec(memory_space=pl.ANY)
    first_earlier = 4 + len(grad_rows)
    kernel = functools.partial(
        shampoo_kernel, math.gcd(count, 8), begin, parts, len(grad_rows), len(earlier)
    )
    return pl.pallas_call(
        kernel,
        grid=(end - begin,),
        in_specs=[SMEM_SPEC]
        + [pl.BlockSpec((1, size, span), lambda i: (begin + i, 0, 0))] * len(grad_rows)
        + [blocks] * 3
        + [anywhere] * len(earlier),
        out_specs=[anywhere] * 4,
        out_shape=[shape] * 4,
        scratch_shapes=[
            pltpu.VMEM((4, count, size, size), f32),
            pltpu.SemaphoreType.DMA((4, count)),
        ],
        input_output_aliases={first_earlier + i: i for i in range(len(earlier))},
        compiler_params=params(mebibytes),
        cost_estimate=cost(9),
        name="shampoo",
    )(is_up, *grad_rows, lefts, rights, weights, *earlier)


def momentum_kernel(
    vector_rate, pos_rate, sum_ref, v_ref, vm_ref, b_ref, bm_ref, p_ref, pm_ref, vm_out, v_out, bm_out, b_out, pm_out, p_out
):
    width = v_ref.shape[1]
    new = moment_keep * vm_ref[...] + sum_ref[0 : v_ref.shape[0], :].astype(f32)
    vm_out[...] = new
    v_out[...] = v_ref[...] - vector_rate * new
    per_row = b_ref.shape[1] // width
    rows = sum_ref[16:32, :].astype(f32)
    for i in range(b_ref.shape[0]):
        for j in range(per_row):
            at = (slice(i, i + 1), slice(j * width, (j + 1) * width))
            row = i * per_row + j
            new = moment_keep * bm_ref[at] + rows[row : row + 1, :]
            bm_out[at] = new
            b_out[at] = b_ref[at] - vector_rate * new
    new = moment_keep * pm_ref[...] + sum_ref[32 : 32 + p_ref.shape[0], :].astype(f32)
    pm_out[...] = new
    p_out[...] = p_ref[...] - pos_rate * new


def momentum_step(sums, vectors, vectors_mom, bias, bias_mom, table, table_mom, vector_rate, pos_rate):
    args = (sums, vectors, vectors_mom, bias, bias_mom, table, table_mom)
    outs = (vectors, vectors, bias, bias, table, table)
    return pl.pallas_call(
        functools.partial(momentum_kernel, vector_rate, pos_rate),
        in_specs=[whole(arg.shape) for arg in args],
        out_specs=[whole(out.shape) for out in outs],
        out_shape=[jax.ShapeDtypeStruct(out.shape, f32) for out in outs],
        compiler_params=params(24),
        cost_estimate=cost(3),
        name="momentum",
    )(*args)


CORE, Y, Z_LOW, Z_HIGH = 1, 2, 4, 8


def flip(values, bits):
    size = lax.axis_size("dp")
    return lax.ppermute(values, "dp", [(i, i ^ bits) for i in range(size)])


def flip_mod(values):
    return lax.ppermute(values, "mod", [(0, 1), (1, 0)])


def in_order(bit, own, other):
    return jnp.stack([jnp.where(bit == 1, other, own), jnp.where(bit == 1, own, other)])


def ring_order():
    chips = [(z, 0) for z in range(4)] + [(z, 1) for z in reversed(range(4))]
    return [z * 4 + y * 2 + core for z, y in chips for core in range(2)]


def place():
    index = lax.axis_index("dp")
    return index % 2, index // 2 % 2, index // 4


def sync(*values):
    return lax.optimization_barrier(values)


def pick(values, index, axis):
    return lax.dynamic_index_in_dim(values, index, axis, keepdims=False)


def plus(left, right):
    return (left.astype(f32) + right.astype(f32)).astype(bf16)


def square_parts(blocks, rows, cols):
    size = blocks.shape[-1]
    shaped = blocks.reshape(rows, cols, size, size)
    return jnp.swapaxes(shaped, 1, 2).reshape(rows, size, cols * size)


def parts_to_blocks(parts):
    rows, size, span = parts.shape
    shaped = parts.reshape(rows, size, span // size, size)
    return jnp.swapaxes(shaped, 1, 2).reshape(-1, size, size)


def local(
    stream_in,
    cotangent,
    patch_count,
    pos_index,
    attn_blocks,
    attn_left,
    attn_right,
    ffn_blocks,
    ffn_left,
    ffn_right,
    vectors,
    vectors_mom,
    ffn_bias,
    ffn_bias_mom,
    pos_table,
    pos_mom,
):
    size = attn_blocks.shape[-1]
    width = vectors.shape[1]
    hidden_units = ffn_bias.shape[1]
    slots = stream_in.shape[2]
    row_blocks = width // size
    chunks = hidden_units // width
    rows = round_up(slots, 16)
    seq = round_up(slots + TEXT, 32)
    by_rows = lax.axis_size("dp") == 16 and attn_blocks.shape[0] == row_blocks
    modality = lax.axis_index("mod")
    is_text = modality == 1
    image_flag = (1 - modality).astype(f32)
    along = lax.axis_index("dp")
    is_up = jnp.where(along < lax.axis_size("dp") // 2, 1, 0).astype(jnp.int32)[None]
    is_not = jnp.zeros((1,), jnp.int32)

    core, y, z = place()
    order = range(2 * row_blocks)
    if by_rows:
        order = [ring_order().index(device) for device in order]
    order = tuple(order)
    to_image = [(1, 0)]
    to_text = [(0, 1)]

    if by_rows:
        own_attn = pack_rows(is_not, attn_blocks, row_blocks)[0]
        along_z = [flip(own_attn, bits) for bits in (Z_LOW, Z_HIGH, Z_LOW | Z_HIGH)]
        ffn_rows = pack_rows(is_up, ffn_blocks[0], row_blocks)

    own_vec = lax.dynamic_slice_in_dim(vectors, 3 + 5 * modality, 5, 0)
    vec = jnp.concatenate([own_vec, vectors[0:3]], axis=0)
    up_bias = lax.dynamic_index_in_dim(ffn_bias, modality, 0, keepdims=False)
    up_bias = jnp.swapaxes(up_bias.reshape(row_blocks, chunks, size), 0, 1).reshape(1, hidden_units)
    count = patch_count[0]
    offset = TEXT * (1 - modality)
    first_key = jnp.where(is_text, TEXT, 0)
    end_key = jnp.where(is_text, slots, TEXT + count)
    kept_rows = jnp.where(is_text, slots, count)
    own_core = core if by_rows else 0 * along
    rows_info = jnp.stack([offset, first_key, end_key, modality, kept_rows, own_core])
    rows_info = rows_info.astype(jnp.int32)
    pad = ((0, rows - slots), (0, 0))
    table_rows = jnp.take(pos_table, pos_index[0], axis=0)
    pos = jnp.pad(pos_index[0], pad[0], constant_values=-1)[None]
    if by_rows:
        along_z, table_rows, stream_in, cotangent, up_bias, pos, ffn_rows = sync(
            along_z, table_rows, stream_in, cotangent, up_bias, pos, ffn_rows
        )
        ffn_parts = lax.all_gather(ffn_rows, "dp", axis=0, axis_index_groups=[ring_order()])
        near = in_order(z % 2, own_attn, along_z[0])
        far = in_order(z % 2, along_z[1], along_z[2])
        attn_z = in_order(z // 2, near, far).reshape(4, size, width)
        upper, lower = attn_z[:, : size // 2], attn_z[:, size // 2 :]
        upper_y, lower_x = flip(upper, Y), flip_mod(lower)
    hidden = jnp.pad(stream_in[0, 0] + image_flag * table_rows, pad)
    first = first_norm(rows_info, hidden, vec, seq)
    if by_rows:
        upper_y, lower_x, first, hidden, cotangent = sync(
            upper_y, lower_x, first, hidden, cotangent
        )
        upper, lower = in_order(y, upper, upper_y), in_order(modality, lower, lower_x)
        upper_x, lower_y = flip_mod(upper), flip(lower, Y)
    pair_first = lax.ppermute(first[:TEXT], "mod", to_image)
    first = lax.dynamic_update_slice(first, jnp.where(is_text, first[:TEXT], pair_first), (0, 0))
    cot = jnp.pad(cotangent[0, 0], pad)

    def by_parts(blocks):
        by_chunk = blocks.reshape(chunks, -1, size, size)
        spread = jnp.swapaxes(blocks.reshape(-1, chunks, size, size), 0, 1)
        return jnp.where(is_up[0] == 1, spread, by_chunk)

    if by_rows:
        ffn_old = [by_parts(part[0]) for part in (ffn_left, ffn_right, ffn_blocks)]
        upper_x, lower_y, first, cot, ffn_old = sync(upper_x, lower_y, first, cot, ffn_old)
        upper, lower = in_order(modality, upper, upper_x), in_order(y, lower, lower_y)
        attn_parts = [upper, flip(upper, CORE), lower, flip(lower, CORE)]
    else:
        attn_all = lax.all_gather(attn_blocks.astype(bf16), ("mod", "dp"), axis=0, tiled=True)
        attn_parts = [square_parts(attn_all, 4 * row_blocks, row_blocks).reshape(4, width, width)]
        ffn_all = lax.all_gather(ffn_blocks[0].astype(bf16), "dp", axis=0, tiled=True)
        shape = (2, row_blocks, row_blocks, chunks, size, size)
        up = ffn_all.reshape(shape)[0].transpose(0, 2, 3, 1, 4)
        down = ffn_all.reshape(2, row_blocks, chunks, row_blocks, size, size)[1]
        down = down.transpose(0, 1, 3, 2, 4)
        ffn_parts = jnp.stack([up, down]).reshape(2 * row_blocks, chunks, size, width)

    qkv, w_attn = project(rows_info, first, vec, attn_parts)
    ctx, lse, pair_ctx = attend(rows_info, qkv)
    pair_ctx = lax.ppermute(pair_ctx, "mod", to_text)
    stream_out, grad_middle, grad_ctx, pair_grad, grad_wo, grad_ffn, late_vec, up_bias_grad = expert(
        rows_info, ctx, pair_ctx, hidden, cot, vec, up_bias, w_attn, ffn_parts, order, slots
    )
    pair_grad = lax.ppermute(pair_grad, "mod", to_image)

    def along_z_of(parts):
        return [flip(part, bits * Z_LOW) for bits, part in enumerate(parts) if bits]

    if by_rows:
        ffn_sum = lax.psum_scatter(
            grad_ffn, "dp", scatter_dimension=0, tiled=True, axis_index_groups=[ring_order()]
        )[0]
    grad_qkv = attend_grad(rows_info, qkv, grad_ctx, pair_grad, ctx, lse)
    attn_keep, attn_send, grad_first, pair_first_grad, sums = project_grad(
        rows_info, grad_qkv, first, w_attn, grad_wo, size
    )
    pair_first_grad = lax.ppermute(pair_first_grad, "mod", to_text)
    up_bias_grad = jnp.swapaxes(up_bias_grad.reshape(chunks, row_blocks, size), 0, 1)
    if by_rows:
        attn_got = flip(attn_send, CORE)
        attn_got, pair_first_grad = sync(attn_got, pair_first_grad)
        both = plus(attn_keep, attn_got).reshape(2, 4, 2, size, width)
        upper, lower = both[..., : size // 2, :], both[..., size // 2 :, :]
        upper_keep, upper_send = pick(upper, modality, 0), pick(upper, 1 - modality, 0)
        lower_keep, lower_send = pick(lower, y, 2), pick(lower, 1 - y, 2)
        upper_keep, upper_send, lower_keep, lower_send, pair_first_grad = sync(
            upper_keep, upper_send, lower_keep, lower_send, pair_first_grad
        )
        upper_got, lower_got = flip_mod(upper_send), flip(lower_send, Y)
    stream_grad, small = first_grad(
        rows_info,
        grad_first,
        pair_first_grad,
        hidden,
        grad_middle,
        vec,
        sums,
        late_vec,
        up_bias_grad.reshape(chunks, width),
        pos,
        slots,
    )
    stream_out = stream_out.reshape(stream_in.shape)
    stream_grad = stream_grad.reshape(stream_in.shape)
    if by_rows:
        small = small.reshape(2, 2, 4, -1, width)
        small_keep, small_send = pick(small, core, 0), pick(small, 1 - core, 0)
        small_got = flip(small_send, CORE)
        upper_got, lower_got, small_got = sync(upper_got, lower_got, small_got)
        upper, lower = plus(upper_keep, upper_got), plus(lower_keep, lower_got)
        small = plus(small_keep, small_got)
        upper = jnp.concatenate([upper, jnp.swapaxes(small, 0, 1)], axis=2)
        upper_keep, upper_send = pick(upper, y, 1), pick(upper, 1 - y, 1)
        lower_keep, lower_send = pick(lower, modality, 0), pick(lower, 1 - modality, 0)
        upper_keep, upper_send, lower_keep, lower_send = sync(
            upper_keep, upper_send, lower_keep, lower_send
        )
        upper_got, lower_got = flip(upper_send, Y), flip_mod(lower_send)
        ffn_new = shampoo(is_up, 0, 1, [ffn_sum], *ffn_old, mebibytes=56)
        upper_got, lower_got, ffn_new = sync(upper_got, lower_got, ffn_new)
        upper, lower = plus(upper_keep, upper_got), plus(lower_keep, lower_got)
        half = size // 2
        attn = jnp.concatenate([upper[:, :half], lower, upper[:, half:]], axis=1)
        attn_z = [pick(attn, z ^ bits, 0) for bits in range(4)]
        attn_z, ffn_new = sync(attn_z, ffn_new)
        attn_got = along_z_of(attn_z)
        ffn_new = shampoo(is_up, 1, 3, [ffn_sum], *ffn_old, ffn_new)
        attn_got, ffn_new = sync(attn_got, ffn_new)
        small = sum(part[size:].astype(f32) for part in (attn_z[0], *attn_got))
        attn_rows = [part[None] for part in (attn_z[0], *attn_got)]
        small, attn_rows, ffn_new = sync(small, attn_rows, ffn_new)
        small_got = flip_mod(small)
        attn_old = [part[None] for part in (attn_left, attn_right, attn_blocks)]
        attn_out = shampoo(is_not, 0, 1, attn_rows, *attn_old, mebibytes=56)
        small_got, attn_out = sync(small_got, attn_out)
        small = (small + small_got).astype(bf16)
        small, ffn_new = sync(small, ffn_new)
        small_got = [flip(small, bits * Z_LOW) for bits in (1, 2, 3)]
        ffn_out = shampoo(is_up, 3, 4, [ffn_sum], *ffn_old, ffn_new)
        small_got, ffn_out = sync(small_got, ffn_out)
        near = in_order(z % 2, small, small_got[0])
        far = in_order(z % 2, small_got[1], small_got[2])
        small = in_order(z // 2, near, far)
        small = in_order(y, small, flip(small, Y))
        small_sum = in_order(core, small, flip(small, CORE)).reshape(-1, width)
    else:
        shape = (row_blocks, chunks, size, row_blocks, size)
        up, down = grad_ffn[:row_blocks].reshape(shape), grad_ffn[row_blocks:].reshape(shape)
        up = up.transpose(0, 3, 1, 2, 4).reshape(-1, size, size)
        down = down.transpose(0, 1, 3, 2, 4).reshape(-1, size, size)
        ffn_sum = lax.psum_scatter(
            jnp.concatenate([up, down], axis=0), "dp", scatter_dimension=0, tiled=True
        )
        attn_full = jnp.stack([attn_keep, attn_send], axis=2).reshape(-1, size, width)
        attn_sum = lax.psum_scatter(
            parts_to_blocks(attn_full), ("mod", "dp"), scatter_dimension=0, tiled=True
        )
        small_sum = lax.psum(small.astype(f32), ("mod", "dp")).astype(bf16)
        ffn_old = [part for part in (ffn_left, ffn_right, ffn_blocks)]
        attn_old = [part[None] for part in (attn_left, attn_right, attn_blocks)]
        ffn_out = shampoo(is_not, 0, 1, [square_parts(ffn_sum, 1, ffn_sum.shape[0])], *ffn_old)
        attn_out = shampoo(is_not, 0, 1, [square_parts(attn_sum, 1, attn_sum.shape[0])], *attn_old)

    items_total = lax.axis_size("dp")
    vector_rate = 0.3 / math.sqrt(items_total * slots)
    pos_rate = 0.5 / math.sqrt(items_total)
    vector_news = momentum_step(
        small_sum, vectors, vectors_mom, ffn_bias, ffn_bias_mom, pos_table, pos_mom, vector_rate, pos_rate
    )
    return (
        stream_out,
        stream_grad,
        *attn_out,
        *(part[None] for part in ffn_out),
        *vector_news,
    )


def solution(mesh):
    items = P("mod", "dp", None, None)
    owned = P(("mod", "dp"), None, None)
    return jax.shard_map(
        local,
        mesh=mesh,
        in_specs=(items, items, P("dp"), P("dp", None), owned, owned, owned, items, items, items)
        + (P(),) * 6,
        out_specs=(items, items, owned, owned, owned, owned, items, items, items, items)
        + (P(),) * 6,
        check_vma=False,
    )
```

```python
import functools
import math

import jax
import jax.numpy as jnp
from jax import lax
from jax.experimental import pallas as pl
from jax.experimental.pallas import tpu as pltpu
from jax.sharding import PartitionSpec as P

HEADS = 12
TEXT = 64
NEWTON = 6
PAIR_LANES = 128
QUERY_TILE = 336
GRAD_TILE = 512

f32 = jnp.float32
bf16 = jnp.bfloat16
norm_eps = 1e-05
stat_decay = 0.5
matrix_rate = 0.25
moment_keep = 0.9
masked_score = -1e30


def dot_nn(left, right):
    return lax.dot_general(left, right, (((1,), (0,)), ((), ())), preferred_element_type=f32)


def dot_nt(left, right):
    return lax.dot_general(left, right, (((1,), (1,)), ((), ())), preferred_element_type=f32)


def dot_tn(left, right):
    return lax.dot_general(left, right, (((0,), (0,)), ((), ())), preferred_element_type=f32)


def params(mebibytes=56):
    return pltpu.CompilerParams(vmem_limit_bytes=mebibytes << 20)


def cost(microseconds):
    return pl.CostEstimate(flops=int(microseconds), bytes_accessed=0, transcendentals=0)


def round_up(value, step):
    return (value + step - 1) // step * step


def whole(shape):
    return pl.BlockSpec(shape, lambda *ids: (0,) * len(shape))


SMEM_SPEC = pl.BlockSpec(memory_space=pltpu.SMEM)


def pack_kernel(up_ref, blocks_ref, out_ref):
    part = pl.program_id(0)
    parts = pl.num_programs(0)
    per_row = blocks_ref.shape[0] // parts
    pieces = []
    for i in range(per_row):
        at = jnp.where(up_ref[0] == 1, i * parts + part, part * per_row + i)
        pieces.append(blocks_ref[at])
    out_ref[0] = jnp.concatenate(pieces, axis=1).astype(bf16)


def pack_rows(is_up, blocks, per_row):
    count, size, _ = blocks.shape
    return pl.pallas_call(
        pack_kernel,
        grid=(count // per_row,),
        in_specs=[SMEM_SPEC, whole(blocks.shape)],
        out_specs=pl.BlockSpec((1, size, per_row * size), lambda i: (i, 0, 0)),
        out_shape=jax.ShapeDtypeStruct((count // per_row, size, per_row * size), bf16),
        compiler_params=params(),
        cost_estimate=cost(3),
        name="pack_rows",
    )(is_up, blocks)


def norm_rows(values):
    centred = values - jnp.mean(values, axis=-1, keepdims=True)
    spread = jnp.mean(centred * centred, axis=-1, keepdims=True)
    inv_std = lax.rsqrt(spread + norm_eps)
    return centred * inv_std, inv_std


def norm_input_grad(grad_out, normal, inv_std, gain):
    grad_norm = grad_out * gain
    mean_grad = jnp.mean(grad_norm, axis=-1, keepdims=True)
    mean_proj = jnp.mean(grad_norm * normal, axis=-1, keepdims=True)
    return inv_std * (grad_norm - mean_grad - normal * mean_proj)


def first_norm_kernel(row_ref, hidden_ref, vec_ref, first_ref):
    rows = hidden_ref.shape[0]
    normal, _ = norm_rows(hidden_ref[...])
    first_ref[...] = jnp.zeros(first_ref.shape, bf16)
    first = normal * vec_ref[0:1, :] + vec_ref[1:2, :]
    first_ref[pl.ds(pl.multiple_of(row_ref[0], 16), rows), :] = first.astype(bf16)


def first_norm(rows_info, hidden, vec, seq):
    return pl.pallas_call(
        first_norm_kernel,
        in_specs=[SMEM_SPEC, whole(hidden.shape), whole(vec.shape)],
        out_specs=whole((seq, hidden.shape[1])),
        out_shape=jax.ShapeDtypeStruct((seq, hidden.shape[1]), bf16),
        compiler_params=params(24),
        cost_estimate=cost(4),
        name="first_norm",
    )(rows_info, hidden, vec)


def project_kernel(row_ref, first_ref, vec_ref, *refs):
    weight_refs, (qkv_ref, w_ref) = refs[:-2], refs[-2:]
    step = pl.program_id(0)
    if len(weight_refs) == 1:
        w_ref[...] = weight_refs[0][...]
    else:
        upper, upper_far, lower, lower_far = weight_refs
        half = upper.shape[3]
        size = half + lower.shape[3]
        on_one = row_ref[5] == 1
        for z in range(2):
            for y in range(2):
                for base, near, far in (
                    (0, upper[0, y, z], upper_far[0, y, z]),
                    (half, lower[y, 0, z], lower_far[y, 0, z]),
                ):
                    start = (4 * z + 2 * y) * size + base
                    end = start + near.shape[0]
                    w_ref[0, start:end, :] = jnp.where(on_one, far, near)
                    w_ref[0, start + size : end + size, :] = jnp.where(on_one, near, far)

    @pl.when(step < 3)
    def _():
        bias = jnp.where(step == 0, vec_ref[5:6, :], jnp.where(step == 2, vec_ref[6:7, :], 0.0))
        qkv_ref[...] = (dot_nn(first_ref[...], w_ref[0]) + bias).astype(bf16)


def project(rows_info, first, vec, attn_parts):
    seq, width = first.shape
    if len(attn_parts) == 1:
        weight_specs = [pl.BlockSpec((1, width, width), lambda i: (i, 0, 0))]
    else:
        rows = [part.shape[3] for part in attn_parts]
        upper = pl.BlockSpec((1, 2, 2, rows[0], width), lambda i: (i // 2, 0, i % 2, 0, 0))
        lower = pl.BlockSpec((2, 1, 2, rows[2], width), lambda i: (0, i // 2, i % 2, 0, 0))
        weight_specs = [upper, upper, lower, lower]
    return pl.pallas_call(
        project_kernel,
        grid=(4,),
        in_specs=[SMEM_SPEC, whole((seq, width)), whole(vec.shape), *weight_specs],
        out_specs=[
            pl.BlockSpec((seq, width), lambda i: (0, jnp.minimum(i, 2))),
            pl.BlockSpec((1, width, width), lambda i: (i, 0, 0)),
        ],
        out_shape=[
            jax.ShapeDtypeStruct((seq, 3 * width), bf16),
            jax.ShapeDtypeStruct((4, width, width), bf16),
        ],
        compiler_params=params(24),
        cost_estimate=cost(8),
        name="project",
    )(rows_info, first, vec, *attn_parts)


def key_bias(row_ref, seq):
    rows = lax.broadcasted_iota(jnp.int32, (seq, 1), 0)
    counts = jnp.logical_and(rows >= row_ref[1], rows < row_ref[2])
    return jnp.where(counts, 0.0, masked_score).astype(f32)


def transposed(values):
    return jnp.transpose(values.astype(f32), (1, 0)).astype(bf16)


def attend_kernel(row_ref, q_ref, k_ref, v_ref, ctx_ref, lse_ref, pair_ref):
    seq = q_ref.shape[0]
    half = PAIR_LANES // 2
    scale = half ** (-0.5)
    lane = lax.broadcasted_iota(jnp.int32, (seq, PAIR_LANES), 1)
    bias = key_bias(row_ref, seq).astype(bf16)
    queries = q_ref[...] * jnp.asarray(scale, bf16)
    keys = k_ref[...]
    values = v_ref[...]
    one = jnp.ones((seq, PAIR_LANES), bf16)
    heads = []
    for head in range(2):
        own = (lane < half) == (head == 0)
        spare = lane == half * (1 - head)
        head_q = jnp.where(own, queries, jnp.where(spare, one, jnp.zeros_like(one)))
        head_k = jnp.where(own, keys, jnp.where(spare, bias, jnp.zeros_like(one)))
        head_v = jnp.where(own, values, one)
        heads.append((head_q, head_k, head_v))
    for start in range(0, seq, QUERY_TILE):
        size = min(QUERY_TILE, seq - start)
        tile = slice(start, start + size)
        parts, lses = [], []
        for head, (head_q, head_k, head_v) in enumerate(heads):
            scores = dot_nt(head_q[tile], head_k)
            top = jnp.max(scores, axis=1, keepdims=True)
            raised = jnp.exp(scores - top).astype(bf16)
            summed = dot_nn(raised, head_v)
            at = half * (1 - head)
            total = summed[:, at : at + 1]
            parts.append(summed * (1.0 / total))
            lses.append(top + jnp.log(total))
        low = lax.broadcasted_iota(jnp.int32, (size, PAIR_LANES), 1) < half
        context = jnp.where(low, parts[0], parts[1]).astype(bf16)
        ctx_ref[tile, :] = context
        if start == 0:
            pair_ref[...] = context[: pair_ref.shape[0]]
        column = lax.broadcasted_iota(jnp.int32, (size, PAIR_LANES), 1) - 2 * pl.program_id(0)
        others = jnp.where(column < 0, lse_ref[tile, :], 0.0)
        lse_ref[tile, :] = jnp.where(column == 0, lses[0], jnp.where(column == 1, lses[1], others))


def attend(rows_info, qkv):
    seq = qkv.shape[0]
    width = qkv.shape[1] // 3
    pairs = width // PAIR_LANES

    def column(base):
        return pl.BlockSpec((seq, PAIR_LANES), lambda i, base=base: (0, base + i))

    return pl.pallas_call(
        attend_kernel, grid=(pairs,),
        in_specs=[SMEM_SPEC, column(0), column(pairs), column(2 * pairs)],
        out_specs=[column(0), whole((seq, PAIR_LANES)), pl.BlockSpec((TEXT, PAIR_LANES), lambda i: (0, i))],
        out_shape=[jax.ShapeDtypeStruct((seq, width), bf16), jax.ShapeDtypeStruct((seq, PAIR_LANES), f32), jax.ShapeDtypeStruct((TEXT, width), bf16)],
        compiler_params=params(20), cost_estimate=cost(12), name="attend",
    )(rows_info, qkv, qkv, qkv)


def three_parts(values):
    high = values.astype(bf16)
    rest = values - high.astype(f32)
    middle = rest.astype(bf16)
    return high, middle, (rest - middle.astype(f32)).astype(bf16)


def attend_grad_kernel(
    row_ref, q_ref, k_ref, v_ref, g_ref, pair_ref, ctx_ref, lse_ref, out_ref, dk_ref, dv_ref
):
    seq = q_ref.shape[0]
    half = PAIR_LANES // 2
    scale = half ** (-0.5)
    lane = lax.broadcasted_iota(jnp.int32, (seq, PAIR_LANES), 1)
    bias = key_bias(row_ref, seq).astype(bf16)
    queries = q_ref[...]
    scaled = queries * jnp.asarray(scale, bf16)
    keys = k_ref[...]
    values = v_ref[...]
    keys_t = transposed(keys)
    row = lax.broadcasted_iota(jnp.int32, (seq, 1), 0)
    counts = jnp.logical_and(row >= row_ref[1], row < row_ref[2])
    grads = jnp.concatenate([pair_ref[...], g_ref[pair_ref.shape[0] :, :]], axis=0)
    grads = jnp.where(counts, grads, jnp.zeros((seq, PAIR_LANES), bf16))
    products = grads.astype(f32) * ctx_ref[...].astype(f32)
    one = jnp.ones((seq, PAIR_LANES), bf16)
    zero = jnp.zeros((seq, PAIR_LANES), bf16)
    heads = []
    for head in range(2):
        own = (lane < half) == (head == 0)
        spare = lane - half * (1 - head)
        held = jnp.where(lane == 2 * pl.program_id(0) + head, lse_ref[...], 0.0)
        lse = three_parts(-jnp.sum(held, axis=1, keepdims=True))
        dots = three_parts(-jnp.sum(jnp.where(own, products, 0.0), axis=1, keepdims=True))
        own_q = jnp.where(own, queries, zero)
        own_g = jnp.where(own, grads, zero)
        head_q = jnp.where(own, scaled, jnp.where(spare == 3, one, zero))
        head_g = own_g
        for i in range(3):
            head_q = jnp.where(spare == i, lse[i], head_q)
            head_g = jnp.where(spare == i, dots[i], head_g)
        head_k = jnp.where(own, keys, jnp.where(spare == 3, bias, one))
        head_v = jnp.where(own, values, one)
        heads.append((head_q, head_g, head_k, head_v, own_q, own_g))
    for start in range(0, seq, GRAD_TILE):
        size = min(GRAD_TILE, seq - start)
        tile = slice(start, start + size)
        parts = []
        for head, (head_q, head_g, head_k, head_v, own_q, own_g) in enumerate(heads):
            probs = jnp.exp(dot_nt(head_k, head_q[tile]))
            grad_scores = (probs * dot_nt(head_v, head_g[tile])).astype(bf16)
            grad_v = dot_nn(probs.astype(bf16), own_g[tile])
            grad_k = dot_nn(grad_scores, own_q[tile])
            if start == 0 and head == 0:
                dv_ref[...] = grad_v
                dk_ref[...] = grad_k
            else:
                dv_ref[...] += grad_v
                dk_ref[...] += grad_k
            parts.append(dot_nn(keys_t[half * head : half * (head + 1), :], grad_scores))
        grad_q = jnp.transpose(jnp.concatenate(parts, axis=0) * scale, (1, 0))
        out_ref[0, tile, :] = grad_q.astype(bf16)
    out_ref[1] = (dk_ref[...] * scale).astype(bf16)
    out_ref[2] = dv_ref[...].astype(bf16)


def attend_grad(rows_info, qkv, grad_ctx, pair_grad, ctx, lse):
    seq = qkv.shape[0]
    width = qkv.shape[1] // 3
    pairs = width // PAIR_LANES

    def column(base):
        return pl.BlockSpec((seq, PAIR_LANES), lambda i, base=base: (0, base + i))

    return pl.pallas_call(
        attend_grad_kernel,
        grid=(pairs,),
        in_specs=[
            SMEM_SPEC,
            column(0),
            column(pairs),
            column(2 * pairs),
            column(0),
            pl.BlockSpec((TEXT, PAIR_LANES), lambda i: (0, i)),
            column(0),
            whole((seq, PAIR_LANES)),
        ],
        out_specs=pl.BlockSpec((3, seq, PAIR_LANES), lambda i: (0, 0, i)),
        out_shape=jax.ShapeDtypeStruct((3, seq, width), bf16),
        scratch_shapes=[pltpu.VMEM((seq, PAIR_LANES), f32)] * 2,
        compiler_params=params(56),
        cost_estimate=cost(15),
        name="attend_grad",
    )(rows_info, qkv, qkv, qkv, grad_ctx, pair_grad, ctx, lse)


def gelu_pair(values):
    size = jnp.abs(values)
    tail = 1.0 / (1.0 + (0.3275911 * 0.5**0.5) * size)
    poly = tail * (
        0.254829592
        + tail * (-0.284496736 + tail * (1.421413741 + tail * (-1.453152027 + tail * 1.061405429)))
    )
    bell = jnp.exp(-0.5 * values * values)
    upper = 0.5 * poly * bell
    share = jnp.where(values >= 0.0, 1.0 - upper, upper)
    return values * share, share + values * bell * ((2.0 * math.pi) ** -0.5)


def split_by_core(row_ref, grad, shape):
    size, width = shape[-2:]
    blocks = grad.reshape(-1, 2, size, width)
    near, far = blocks[:, 0], blocks[:, 1]
    on_one = row_ref[5] == 1
    return jnp.where(on_one, far, near).reshape(shape), jnp.where(on_one, near, far).reshape(shape)


def expert_chunk(
    order, second, gbranch, upb, parts_ref, grad_ref, dupb_ref, branch, gsecond, scratch, begin
):
    pre, gact, act, gpre, up, down = scratch
    rows, width = act.shape
    tile = 16
    size = parts_ref.shape[2]
    places = [(which, slice(i * size, (i + 1) * size)) for which in range(2) for i in range(len(order) // 2)]
    for at, (which, span) in zip(order, places):
        (up, down)[which][span, :] = parts_ref[at, 0]
    pre[...] = dot_nn(second[...], up[...])
    gact[...] = dot_nt(gbranch[...], down[...])

    def body(i, total):
        at = pl.ds(pl.multiple_of(i * tile, tile), tile)
        value, slope = gelu_pair(pre[at, :] + upb[...])
        act[at, :] = value.astype(bf16)
        rounded = (gact[at, :] * slope).astype(bf16)
        gpre[at, :] = rounded
        return total + rounded.astype(f32)

    total = lax.fori_loop(0, rows // tile, body, jnp.zeros((tile, width), f32), unroll=True)
    dupb_ref[...] = jnp.sum(total, axis=0, keepdims=True)
    grads = [
        dot_tn(second[...], gpre[...]).astype(bf16),
        dot_tn(act[...], gbranch[...]).astype(bf16),
    ]
    for at, (which, span) in zip(order, places):
        grad_ref[at, 0] = grads[which][span, :]
    own_branch = dot_nn(act[...], down[...])
    own_gsecond = dot_nt(gpre[...], up[...])

    @pl.when(begin)
    def _():
        branch[...] = own_branch
        gsecond[...] = own_gsecond

    @pl.when(jnp.logical_not(begin))
    def _():
        branch[...] += own_branch
        gsecond[...] += own_gsecond


def expert_kernel(
    order,
    row_ref,
    ctx_ref,
    pair_ref,
    hidden_ref,
    cot_ref,
    vec_ref,
    upb_ref,
    wo_ref,
    parts_ref,
    out_ref,
    gmid_ref,
    gctx_ref,
    pair_grad_ref,
    dwo_ref,
    grad_ref,
    dvec_ref,
    dupb_ref,
    own_ctx,
    middle,
    second,
    gbranch,
    branch,
    gsecond,
    *scratch,
):
    step = pl.program_id(0)
    rows, width = hidden_ref.shape
    out_rows = out_ref.shape[0]
    tile = 16

    @pl.when(step == 0)
    def _():
        own_ctx[...] = ctx_ref[pl.ds(pl.multiple_of(row_ref[0], 16), rows), :]

        @pl.when(row_ref[3] == 1)
        def _():
            own_ctx[0 : pair_ref.shape[0], :] = pair_ref[...]

        middle[...] = dot_nn(own_ctx[...], wo_ref[0])

        def body(i, total):
            at = pl.ds(pl.multiple_of(i * tile, tile), tile)
            mid = hidden_ref[at, :] + (middle[at, :] + vec_ref[7:8, :])
            middle[at, :] = mid
            normal, _ = norm_rows(mid)
            second[at, :] = (normal * vec_ref[2:3, :] + vec_ref[3:4, :]).astype(bf16)
            row = lax.broadcasted_iota(jnp.int32, (tile, 1), 0) + i * tile
            kept = jnp.where(row < row_ref[4], cot_ref[at, :], 0.0)
            rounded = kept.astype(bf16)
            gbranch[at, :] = rounded
            return total + rounded.astype(f32)

        total = lax.fori_loop(
            0, rows // tile, body, jnp.zeros((tile, width), f32), unroll=True
        )
        dvec_ref[...] = jnp.zeros(dvec_ref.shape, f32)
        dvec_ref[2:3, :] = jnp.sum(total, axis=0, keepdims=True)

    expert_chunk(
        order,
        second,
        gbranch,
        upb_ref,
        parts_ref,
        grad_ref,
        dupb_ref,
        branch,
        gsecond,
        scratch,
        step == 0,
    )

    @pl.when(step == pl.num_programs(0) - 1)
    def _():
        def body(i, totals):
            at = pl.ds(pl.multiple_of(i * tile, tile), tile)
            mid = middle[at, :]
            normal, inv_std = norm_rows(mid)
            grad_out = gsecond[at, :]
            row = lax.broadcasted_iota(jnp.int32, (tile, 1), 0) + i * tile
            kept = row < row_ref[4]
            branch[at, :] = jnp.where(kept, mid + (branch[at, :] + vec_ref[4:5, :]), 0.0)
            grad_in = norm_input_grad(grad_out, normal, inv_std, vec_ref[2:3, :])
            grad_mid = jnp.where(kept, cot_ref[at, :], 0.0) + grad_in
            gmid_ref[at, :] = grad_mid
            rounded = grad_mid.astype(bf16)
            gbranch[at, :] = rounded
            return (
                totals[0] + grad_out * normal,
                totals[1] + grad_out,
                totals[2] + rounded.astype(f32),
            )

        zero = jnp.zeros((tile, width), f32)
        gains, shifts, biases = lax.fori_loop(
            0, rows // tile, body, (zero, zero, zero), unroll=True
        )
        dvec_ref[0:1, :] = jnp.sum(gains, axis=0, keepdims=True)
        dvec_ref[1:2, :] = jnp.sum(shifts, axis=0, keepdims=True)
        dvec_ref[3:4, :] = jnp.sum(biases, axis=0, keepdims=True)
        out_ref[...] = branch[0:out_rows, :].reshape(out_ref.shape)
        dwo_ref[...] = dot_tn(own_ctx[...], gbranch[...]).astype(bf16)
        grad_ctx = dot_nt(gbranch[...], wo_ref[0]).astype(bf16)
        gctx_ref[...] = jnp.zeros(gctx_ref.shape, bf16)
        gctx_ref[pl.ds(pl.multiple_of(row_ref[0], 16), rows), :] = grad_ctx
        pair_grad_ref[...] = grad_ctx[: pair_grad_ref.shape[0]]


def expert(rows_info, ctx, pair_ctx, hidden, cot, vec, up_bias, w_attn, ffn_parts, order, out_rows):
    rows, width = hidden.shape
    seq = ctx.shape[0]
    blocks, chunks, size, _ = ffn_parts.shape
    parts = pl.BlockSpec((blocks, 1, size, width), lambda i: (0, i, 0, 0))
    return pl.pallas_call(
        functools.partial(expert_kernel, order),
        grid=(chunks,),
        in_specs=[
            SMEM_SPEC,
            whole(ctx.shape),
            whole(pair_ctx.shape),
            whole(hidden.shape),
            whole(cot.shape),
            whole(vec.shape),
            pl.BlockSpec((1, width), lambda i: (0, i)),
            pl.BlockSpec((1, width, width), lambda i: (3, 0, 0)),
            parts,
        ],
        out_specs=[
            whole((out_rows, 1, width)),
            whole((rows, width)),
            whole((seq, width)),
            whole((TEXT, width)),
            whole((width, width)),
            parts,
            whole((8, width)),
            pl.BlockSpec((1, width), lambda i: (0, i)),
        ],
        out_shape=[
            jax.ShapeDtypeStruct((out_rows, 1, width), f32),
            jax.ShapeDtypeStruct((rows, width), f32),
            jax.ShapeDtypeStruct((seq, width), bf16),
            jax.ShapeDtypeStruct((TEXT, width), bf16),
            jax.ShapeDtypeStruct((width, width), bf16),
            jax.ShapeDtypeStruct(ffn_parts.shape, bf16),
            jax.ShapeDtypeStruct((8, width), f32),
            jax.ShapeDtypeStruct((1, chunks * width), f32),
        ],
        scratch_shapes=[
            pltpu.VMEM((rows, width), bf16),
            pltpu.VMEM((rows, width), f32),
            pltpu.VMEM((rows, width), bf16),
            pltpu.VMEM((rows, width), bf16),
            pltpu.VMEM((rows, width), f32),
            pltpu.VMEM((rows, width), f32),
            pltpu.VMEM((rows, width), f32),
            pltpu.VMEM((rows, width), f32),
            pltpu.VMEM((rows, width), bf16),
            pltpu.VMEM((rows, width), bf16),
            pltpu.VMEM((width, width), bf16),
            pltpu.VMEM((width, width), bf16),
        ],
        compiler_params=params(),
        cost_estimate=cost(43),
        name="expert",
    )(rows_info, ctx, pair_ctx, hidden, cot, vec, up_bias, w_attn, ffn_parts)


def project_grad_kernel(
    row_ref, dqkv_ref, first_ref, w_ref, dwo_ref, keep_ref, send_ref, gfirst, pair_ref, sums_ref
):
    step = pl.program_id(0)

    def put(grad):
        keep_ref[0], send_ref[0] = split_by_core(row_ref, grad, keep_ref.shape[1:])

    @pl.when(step < 3)
    def _():
        own = dqkv_ref[0]
        put(dot_tn(first_ref[...], own).astype(bf16))
        share = dot_nt(own, w_ref[0])
        sums = jnp.sum(own.astype(f32), axis=0, keepdims=True)

        @pl.when(step == 0)
        def _():
            gfirst[...] = share
            sums_ref[...] = jnp.zeros(sums_ref.shape, f32)
            sums_ref[0:1, :] = sums

        @pl.when(step > 0)
        def _():
            gfirst[...] += share
            sums_ref[1:2, :] = sums

    @pl.when(step == 3)
    def _():
        put(dwo_ref[...])
        pair_ref[...] = gfirst[0 : pair_ref.shape[0], :]


def project_grad(rows_info, dqkv, first, w_attn, grad_wo, size):
    seq, width = first.shape
    pairs = width // size // 2
    part = pl.BlockSpec((1, pairs, size, width), lambda i: (i, 0, 0, 0))

    def early_index(i):
        return (jnp.minimum(i, 2), 0, 0)

    return pl.pallas_call(
        project_grad_kernel,
        grid=(4,),
        in_specs=[
            SMEM_SPEC,
            pl.BlockSpec((1, seq, width), early_index),
            whole((seq, width)),
            pl.BlockSpec((1, width, width), early_index),
            whole(grad_wo.shape),
        ],
        out_specs=[part, part, whole((seq, width)), whole((TEXT, width)), whole((8, width))],
        out_shape=[
            jax.ShapeDtypeStruct((4, pairs, size, width), bf16),
            jax.ShapeDtypeStruct((4, pairs, size, width), bf16),
            jax.ShapeDtypeStruct((seq, width), f32),
            jax.ShapeDtypeStruct((TEXT, width), f32),
            jax.ShapeDtypeStruct((8, width), f32),
        ],
        compiler_params=params(56),
        cost_estimate=cost(15),
        name="project_grad",
    )(rows_info, dqkv, first, w_attn, grad_wo)


def first_grad_kernel(
    row_ref,
    gfirst_ref,
    pair_ref,
    hidden_ref,
    gmid_ref,
    vec_ref,
    sums_ref,
    late_ref,
    upb_ref,
    pos_ref,
    out_ref,
    small_ref,
    own,
):
    rows, width = hidden_ref.shape
    tile = 16
    own[...] = gfirst_ref[pl.ds(pl.multiple_of(row_ref[0], 16), rows), :]

    @pl.when(row_ref[3] == 1)
    def _():
        own[0 : pair_ref.shape[0], :] = pair_ref[...]

    def body(i, totals):
        at = pl.ds(pl.multiple_of(i * tile, tile), tile)
        normal, inv_std = norm_rows(hidden_ref[at, :])
        grad_out = own[at, :]
        grad_in = norm_input_grad(grad_out, normal, inv_std, vec_ref[0:1, :])
        own[at, :] = gmid_ref[at, :] + grad_in
        return totals[0] + grad_out * normal, totals[1] + grad_out

    zero = jnp.zeros((tile, width), f32)
    gains, shifts = lax.fori_loop(0, rows // tile, body, (zero, zero), unroll=True)
    out_ref[...] = own[0 : out_ref.shape[0], :].reshape(out_ref.shape)
    own_rows = (
        jnp.sum(gains, axis=0, keepdims=True),
        jnp.sum(shifts, axis=0, keepdims=True),
        late_ref[0:1, :],
        late_ref[1:2, :],
        late_ref[2:3, :],
    )
    row = lax.broadcasted_iota(jnp.int32, (16, width), 0)
    top = jnp.where(row == 0, sums_ref[0:1, :], 0.0)
    top = jnp.where(row == 1, sums_ref[1:2, :], top)
    top = jnp.where(row == 2, late_ref[3:4, :], top)
    for i, value in enumerate(own_rows):
        top = jnp.where(row == 3 + 5 * row_ref[3] + i, value, top)
    small_ref[0:16, :] = top.astype(small_ref.dtype)
    row = lax.broadcasted_iota(jnp.int32, (8, width), 0)
    bias = jnp.zeros((8, width), f32)
    for i in range(upb_ref.shape[0]):
        bias = jnp.where(row == upb_ref.shape[0] * row_ref[3] + i, upb_ref[i : i + 1, :], bias)
    small_ref[16:32, :] = jnp.concatenate([bias, jnp.zeros_like(bias)], axis=0).astype(small_ref.dtype)
    grads = own[...]
    high = grads.astype(bf16)
    low = (grads - high.astype(f32)).astype(bf16)
    table = lax.broadcasted_iota(jnp.int32, (rows, rows), 0)
    chosen = jnp.where(row_ref[3] == 0, pos_ref[...], -1) == table
    chosen = jnp.where(chosen, 1.0, 0.0).astype(bf16)
    sums = dot_nn(chosen, high) + dot_nn(chosen, low)
    small_ref[32 : 32 + rows, :] = sums.astype(small_ref.dtype)
    spare = small_ref.shape[0] - 32 - rows
    if spare:
        small_ref[32 + rows :, :] = jnp.zeros((spare, width), small_ref.dtype)


def first_grad(
    rows_info, gfirst, pair_grad, hidden, grad_middle, vec, sums, late, up_bias, pos, out_rows
):
    rows, width = hidden.shape
    small = round_up(32 + rows, 128)
    args = (gfirst, pair_grad, hidden, grad_middle, vec, sums, late, up_bias, pos)
    return pl.pallas_call(
        first_grad_kernel,
        in_specs=[SMEM_SPEC] + [whole(arg.shape) for arg in args],
        out_specs=[whole((out_rows, 1, width)), whole((small, width))],
        out_shape=[
            jax.ShapeDtypeStruct((out_rows, 1, width), f32),
            jax.ShapeDtypeStruct((small, width), bf16),
        ],
        scratch_shapes=[pltpu.VMEM((rows, width), f32)],
        compiler_params=params(24),
        cost_estimate=cost(8),
        name="first_grad",
    )(rows_info, *args)


def widen(values):
    rows, cols = values.shape
    return jnp.concatenate([values, jnp.zeros((rows, PAIR_LANES - cols), f32)], axis=1)


def split_parts(values):
    high = values.astype(bf16)
    return high, (values - high.astype(f32)).astype(bf16)


def left_parts(values):
    return jnp.concatenate(split_parts(values), axis=1)


def right_parts(values):
    high, low = split_parts(values)
    rows, cols = high.shape
    gap = jnp.zeros((cols - rows, cols), bf16)
    near = jnp.concatenate([high, gap, high, gap], axis=0)
    far = jnp.concatenate([low, gap, jnp.zeros((cols, cols), bf16)], axis=0)
    return jnp.concatenate([near, far], axis=1)


def times(left, right):
    both = dot_nn(left, right)
    return both[:, :PAIR_LANES] + both[:, PAIR_LANES:]


def inverse_roots(stats, identity):
    size = stats[0].shape[0]
    mats, factors = [], []
    for stat in stats:
        norm = jnp.sqrt(jnp.sum(stat * stat, keepdims=True))
        mats.append(stat * (1.0 / norm))
        factors.append(lax.rsqrt(jnp.sqrt(norm)))
    for iteration in range(NEWTON):
        steps = [1.25 * identity - 0.25 * mat for mat in mats]
        if iteration == 0:
            factors = [step * factor for step, factor in zip(steps, factors)]
            squares = [times(left_parts(step), right_parts(step)) for step in steps]
        elif iteration < NEWTON - 1:
            both = [
                times(
                    jnp.concatenate([left_parts(step), left_parts(factor)], axis=0),
                    right_parts(step),
                )
                for step, factor in zip(steps, factors)
            ]
            squares = [pair[:size] for pair in both]
            factors = [pair[size:] for pair in both]
        else:
            return [
                times(left_parts(factor), right_parts(step)) for step, factor in zip(steps, factors)
            ]
        fourths = [times(left_parts(square), right_parts(square)) for square in squares]
        mats = [times(left_parts(fourth), right_parts(mat)) for fourth, mat in zip(fourths, mats)]


def shampoo_kernel(group, begin, parts, grad_count, earlier, up_ref, *refs):
    part = begin + pl.program_id(0)
    grad_refs = refs[:grad_count]
    left_ref, right_ref, w_ref = refs[grad_count : grad_count + 3]
    outs = refs[grad_count + 3 + earlier : grad_count + 7 + earlier]
    results, sems = refs[-2:]
    _, count, size, _ = left_ref.shape
    row = lax.broadcasted_iota(jnp.int32, (size, PAIR_LANES), 0)
    col = lax.broadcasted_iota(jnp.int32, (size, PAIR_LANES), 1)
    identity = (row == col).astype(f32)
    copies = []

    def store(kind, i, at, value):
        results[kind, i] = value
        copy = pltpu.make_async_copy(results.at[kind, i], outs[kind].at[at], sems.at[kind, i])
        copy.start()
        copies.append(copy)

    for base in range(0, count, group):
        places, stats, grads = [], [], []
        for i in range(base, base + group):
            at = jnp.where(up_ref[0] == 1, i * parts + part, part * count + i)
            places.append(at)
            span = slice(i * size, (i + 1) * size)
            grad = grad_refs[0][0, :, span].astype(f32)
            for ref in grad_refs[1:]:
                grad = grad + ref[0, :, span].astype(f32)
            store(0, i, at, grad)
            grad = widen(grad)
            grad_t = widen(jnp.transpose(grad, (1, 0))[:size])
            grads.append(grad)
            outer = times(left_parts(grad), right_parts(grad_t))
            inner = times(left_parts(grad_t), right_parts(grad))
            left_new = stat_decay * left_ref[0, i] + (1.0 - stat_decay) * outer[:, :size]
            right_new = stat_decay * right_ref[0, i] + (1.0 - stat_decay) * inner[:, :size]
            store(1, i, at, left_new)
            store(2, i, at, right_new)
            stats += [widen(left_new), widen(right_new)]
        roots = inverse_roots(stats, identity)
        for i, at in enumerate(places):
            half_way = times(left_parts(roots[2 * i]), right_parts(grads[i]))
            update = times(left_parts(half_way), right_parts(roots[2 * i + 1]))
            store(3, base + i, at, w_ref[0, base + i] - matrix_rate * update[:, :size])
    for copy in copies:
        copy.wait()


def shampoo(is_up, begin, end, grad_rows, lefts, rights, weights, earlier=(), mebibytes=24):
    parts, count, size, _ = lefts.shape
    span = count * size
    blocks = pl.BlockSpec((1, count, size, size), lambda i: (begin + i, 0, 0, 0))
    shape = jax.ShapeDtypeStruct((parts * count, size, size), f32)
    anywhere = pl.BlockSpec(memory_space=pl.ANY)
    first_earlier = 4 + len(grad_rows)
    kernel = functools.partial(
        shampoo_kernel, math.gcd(count, 8), begin, parts, len(grad_rows), len(earlier)
    )
    return pl.pallas_call(
        kernel,
        grid=(end - begin,),
        in_specs=[SMEM_SPEC]
        + [pl.BlockSpec((1, size, span), lambda i: (begin + i, 0, 0))] * len(grad_rows)
        + [blocks] * 3
        + [anywhere] * len(earlier),
        out_specs=[anywhere] * 4,
        out_shape=[shape] * 4,
        scratch_shapes=[
            pltpu.VMEM((4, count, size, size), f32),
            pltpu.SemaphoreType.DMA((4, count)),
        ],
        input_output_aliases={first_earlier + i: i for i in range(len(earlier))},
        compiler_params=params(mebibytes),
        cost_estimate=cost(9),
        name="shampoo",
    )(is_up, *grad_rows, lefts, rights, weights, *earlier)


def momentum_kernel(
    vector_rate, pos_rate, sum_ref, v_ref, vm_ref, b_ref, bm_ref, p_ref, pm_ref, vm_out, v_out, bm_out, b_out, pm_out, p_out
):
    width = v_ref.shape[1]
    new = moment_keep * vm_ref[...] + sum_ref[0 : v_ref.shape[0], :].astype(f32)
    vm_out[...] = new
    v_out[...] = v_ref[...] - vector_rate * new
    per_row = b_ref.shape[1] // width
    rows = sum_ref[16:32, :].astype(f32)
    for i in range(b_ref.shape[0]):
        for j in range(per_row):
            at = (slice(i, i + 1), slice(j * width, (j + 1) * width))
            row = i * per_row + j
            new = moment_keep * bm_ref[at] + rows[row : row + 1, :]
            bm_out[at] = new
            b_out[at] = b_ref[at] - vector_rate * new
    new = moment_keep * pm_ref[...] + sum_ref[32 : 32 + p_ref.shape[0], :].astype(f32)
    pm_out[...] = new
    p_out[...] = p_ref[...] - pos_rate * new


def momentum_step(sums, vectors, vectors_mom, bias, bias_mom, table, table_mom, vector_rate, pos_rate):
    args = (sums, vectors, vectors_mom, bias, bias_mom, table, table_mom)
    outs = (vectors, vectors, bias, bias, table, table)
    return pl.pallas_call(
        functools.partial(momentum_kernel, vector_rate, pos_rate),
        in_specs=[whole(arg.shape) for arg in args],
        out_specs=[whole(out.shape) for out in outs],
        out_shape=[jax.ShapeDtypeStruct(out.shape, f32) for out in outs],
        compiler_params=params(24),
        cost_estimate=cost(3),
        name="momentum",
    )(*args)


CORE, Y, Z_LOW, Z_HIGH = 1, 2, 4, 8


def flip(values, bits):
    size = lax.axis_size("dp")
    return lax.ppermute(values, "dp", [(i, i ^ bits) for i in range(size)])


def flip_mod(values):
    return lax.ppermute(values, "mod", [(0, 1), (1, 0)])


def in_order(bit, own, other):
    return jnp.stack([jnp.where(bit == 1, other, own), jnp.where(bit == 1, own, other)])


def ring_order():
    chips = [(z, 0) for z in range(4)] + [(z, 1) for z in reversed(range(4))]
    return [z * 4 + y * 2 + core for z, y in chips for core in range(2)]


def place():
    index = lax.axis_index("dp")
    return index % 2, index // 2 % 2, index // 4


def sync(*values):
    return lax.optimization_barrier(values)


def pick(values, index, axis):
    return lax.dynamic_index_in_dim(values, index, axis, keepdims=False)


def plus(left, right):
    return (left.astype(f32) + right.astype(f32)).astype(bf16)


def square_parts(blocks, rows, cols):
    size = blocks.shape[-1]
    shaped = blocks.reshape(rows, cols, size, size)
    return jnp.swapaxes(shaped, 1, 2).reshape(rows, size, cols * size)


def parts_to_blocks(parts):
    rows, size, span = parts.shape
    shaped = parts.reshape(rows, size, span // size, size)
    return jnp.swapaxes(shaped, 1, 2).reshape(-1, size, size)


def local(
    stream_in,
    cotangent,
    patch_count,
    pos_index,
    attn_blocks,
    attn_left,
    attn_right,
    ffn_blocks,
    ffn_left,
    ffn_right,
    vectors,
    vectors_mom,
    ffn_bias,
    ffn_bias_mom,
    pos_table,
    pos_mom,
):
    size = attn_blocks.shape[-1]
    width = vectors.shape[1]
    hidden_units = ffn_bias.shape[1]
    slots = stream_in.shape[2]
    row_blocks = width // size
    chunks = hidden_units // width
    rows = round_up(slots, 16)
    seq = round_up(slots + TEXT, 32)
    by_rows = lax.axis_size("dp") == 16 and attn_blocks.shape[0] == row_blocks
    modality = lax.axis_index("mod")
    is_text = modality == 1
    image_flag = (1 - modality).astype(f32)
    along = lax.axis_index("dp")
    is_up = jnp.where(along < lax.axis_size("dp") // 2, 1, 0).astype(jnp.int32)[None]
    is_not = jnp.zeros((1,), jnp.int32)

    core, y, z = place()
    order = range(2 * row_blocks)
    if by_rows:
        order = [ring_order().index(device) for device in order]
    order = tuple(order)
    to_image = [(1, 0)]
    to_text = [(0, 1)]

    if by_rows:
        own_attn = pack_rows(is_not, attn_blocks, row_blocks)[0]
        along_z = [flip(own_attn, bits) for bits in (Z_LOW, Z_HIGH, Z_LOW | Z_HIGH)]
        ffn_rows = pack_rows(is_up, ffn_blocks[0], row_blocks)

    own_vec = lax.dynamic_slice_in_dim(vectors, 3 + 5 * modality, 5, 0)
    vec = jnp.concatenate([own_vec, vectors[0:3]], axis=0)
    up_bias = lax.dynamic_index_in_dim(ffn_bias, modality, 0, keepdims=False)
    up_bias = jnp.swapaxes(up_bias.reshape(row_blocks, chunks, size), 0, 1).reshape(1, hidden_units)
    count = patch_count[0]
    offset = TEXT * (1 - modality)
    first_key = jnp.where(is_text, TEXT, 0)
    end_key = jnp.where(is_text, slots, TEXT + count)
    kept_rows = jnp.where(is_text, slots, count)
    own_core = core if by_rows else 0 * along
    rows_info = jnp.stack([offset, first_key, end_key, modality, kept_rows, own_core])
    rows_info = rows_info.astype(jnp.int32)
    pad = ((0, rows - slots), (0, 0))
    pos = jnp.pad(pos_index[0], pad[0], constant_values=-1)[None]
    if by_rows:
        along_z, pos_index, stream_in, cotangent, up_bias, pos, ffn_rows = sync(
            along_z, pos_index, stream_in, cotangent, up_bias, pos, ffn_rows
        )
        ffn_parts = lax.all_gather(ffn_rows, "dp", axis=0, axis_index_groups=[ring_order()])
        near = in_order(z % 2, own_attn, along_z[0])
        far = in_order(z % 2, along_z[1], along_z[2])
        attn_z = in_order(z // 2, near, far).reshape(4, size, width)
        upper, lower = attn_z[:, : size // 2], attn_z[:, size // 2 :]
        upper_y, lower_x = flip(upper, Y), flip_mod(lower)
    table_rows = jnp.take(pos_table, pos_index[0], axis=0)
    if by_rows:
        upper_y, lower_x, table_rows, stream_in, cotangent = sync(
            upper_y, lower_x, table_rows, stream_in, cotangent
        )
        upper, lower = in_order(y, upper, upper_y), in_order(modality, lower, lower_x)
        upper_x, lower_y = flip_mod(upper), flip(lower, Y)
    hidden = jnp.pad(stream_in[0, 0] + image_flag * table_rows, pad)
    first = first_norm(rows_info, hidden, vec, seq)
    pair_first = lax.ppermute(first[:TEXT], "mod", to_image)
    first = lax.dynamic_update_slice(first, jnp.where(is_text, first[:TEXT], pair_first), (0, 0))
    cot = jnp.pad(cotangent[0, 0], pad)

    def by_parts(blocks):
        by_chunk = blocks.reshape(chunks, -1, size, size)
        spread = jnp.swapaxes(blocks.reshape(-1, chunks, size, size), 0, 1)
        return jnp.where(is_up[0] == 1, spread, by_chunk)

    if by_rows:
        ffn_old = [by_parts(part[0]) for part in (ffn_left, ffn_right, ffn_blocks)]
        upper_x, lower_y, first, cot, ffn_old = sync(upper_x, lower_y, first, cot, ffn_old)
        upper, lower = in_order(modality, upper, upper_x), in_order(y, lower, lower_y)
        attn_parts = [upper, flip(upper, CORE), lower, flip(lower, CORE)]
    else:
        attn_all = lax.all_gather(attn_blocks.astype(bf16), ("mod", "dp"), axis=0, tiled=True)
        attn_parts = [square_parts(attn_all, 4 * row_blocks, row_blocks).reshape(4, width, width)]
        ffn_all = lax.all_gather(ffn_blocks[0].astype(bf16), "dp", axis=0, tiled=True)
        shape = (2, row_blocks, row_blocks, chunks, size, size)
        up = ffn_all.reshape(shape)[0].transpose(0, 2, 3, 1, 4)
        down = ffn_all.reshape(2, row_blocks, chunks, row_blocks, size, size)[1]
        down = down.transpose(0, 1, 3, 2, 4)
        ffn_parts = jnp.stack([up, down]).reshape(2 * row_blocks, chunks, size, width)

    qkv, w_attn = project(rows_info, first, vec, attn_parts)
    ctx, lse, pair_ctx = attend(rows_info, qkv)
    pair_ctx = lax.ppermute(pair_ctx, "mod", to_text)
    stream_out, grad_middle, grad_ctx, pair_grad, grad_wo, grad_ffn, late_vec, up_bias_grad = expert(
        rows_info, ctx, pair_ctx, hidden, cot, vec, up_bias, w_attn, ffn_parts, order, slots
    )
    pair_grad = lax.ppermute(pair_grad, "mod", to_image)

    def along_z_of(parts):
        return [flip(part, bits * Z_LOW) for bits, part in enumerate(parts) if bits]

    if by_rows:
        ffn_sum = lax.psum_scatter(
            grad_ffn, "dp", scatter_dimension=0, tiled=True, axis_index_groups=[ring_order()]
        )[0]
    grad_qkv = attend_grad(rows_info, qkv, grad_ctx, pair_grad, ctx, lse)
    attn_keep, attn_send, grad_first, pair_first_grad, sums = project_grad(
        rows_info, grad_qkv, first, w_attn, grad_wo, size
    )
    pair_first_grad = lax.ppermute(pair_first_grad, "mod", to_text)
    up_bias_grad = jnp.swapaxes(up_bias_grad.reshape(chunks, row_blocks, size), 0, 1)
    if by_rows:
        attn_got = flip(attn_send, CORE)
        attn_got, pair_first_grad = sync(attn_got, pair_first_grad)
        both = plus(attn_keep, attn_got).reshape(2, 4, 2, size, width)
        upper, lower = both[..., : size // 2, :], both[..., size // 2 :, :]
        upper_keep, upper_send = pick(upper, modality, 0), pick(upper, 1 - modality, 0)
        lower_keep, lower_send = pick(lower, y, 2), pick(lower, 1 - y, 2)
        upper_keep, upper_send, lower_keep, lower_send, pair_first_grad = sync(
            upper_keep, upper_send, lower_keep, lower_send, pair_first_grad
        )
        upper_got, lower_got = flip_mod(upper_send), flip(lower_send, Y)
    stream_grad, small = first_grad(
        rows_info,
        grad_first,
        pair_first_grad,
        hidden,
        grad_middle,
        vec,
        sums,
        late_vec,
        up_bias_grad.reshape(chunks, width),
        pos,
        slots,
    )
    stream_out = stream_out.reshape(stream_in.shape)
    stream_grad = stream_grad.reshape(stream_in.shape)
    if by_rows:
        small = small.reshape(2, 2, 4, -1, width)
        small_keep, small_send = pick(small, core, 0), pick(small, 1 - core, 0)
        small_got = flip(small_send, CORE)
        upper_got, lower_got, small_got = sync(upper_got, lower_got, small_got)
        upper, lower = plus(upper_keep, upper_got), plus(lower_keep, lower_got)
        small = plus(small_keep, small_got)
        upper = jnp.concatenate([upper, jnp.swapaxes(small, 0, 1)], axis=2)
        upper_keep, upper_send = pick(upper, y, 1), pick(upper, 1 - y, 1)
        lower_keep, lower_send = pick(lower, modality, 0), pick(lower, 1 - modality, 0)
        upper_keep, upper_send, lower_keep, lower_send = sync(
            upper_keep, upper_send, lower_keep, lower_send
        )
        upper_got, lower_got = flip(upper_send, Y), flip_mod(lower_send)
        ffn_new = shampoo(is_up, 0, 1, [ffn_sum], *ffn_old, mebibytes=56)
        upper_got, lower_got, ffn_new = sync(upper_got, lower_got, ffn_new)
        upper, lower = plus(upper_keep, upper_got), plus(lower_keep, lower_got)
        half = size // 2
        attn = jnp.concatenate([upper[:, :half], lower, upper[:, half:]], axis=1)
        attn_z = [pick(attn, z ^ bits, 0) for bits in range(4)]
        attn_z, ffn_new = sync(attn_z, ffn_new)
        attn_got = along_z_of(attn_z)
        ffn_new = shampoo(is_up, 1, 3, [ffn_sum], *ffn_old, ffn_new)
        attn_got, ffn_new = sync(attn_got, ffn_new)
        small = sum(part[size:].astype(f32) for part in (attn_z[0], *attn_got))
        attn_rows = [part[None] for part in (attn_z[0], *attn_got)]
        small, attn_rows, ffn_new = sync(small, attn_rows, ffn_new)
        small_got = flip_mod(small)
        attn_old = [part[None] for part in (attn_left, attn_right, attn_blocks)]
        attn_out = shampoo(is_not, 0, 1, attn_rows, *attn_old, mebibytes=56)
        small_got, attn_out = sync(small_got, attn_out)
        small = (small + small_got).astype(bf16)
        small, ffn_new = sync(small, ffn_new)
        small_got = [flip(small, bits * Z_LOW) for bits in (1, 2, 3)]
        ffn_out = shampoo(is_up, 3, 4, [ffn_sum], *ffn_old, ffn_new)
        small_got, ffn_out = sync(small_got, ffn_out)
        near = in_order(z % 2, small, small_got[0])
        far = in_order(z % 2, small_got[1], small_got[2])
        small = in_order(z // 2, near, far)
        small = in_order(y, small, flip(small, Y))
        small_sum = in_order(core, small, flip(small, CORE)).reshape(-1, width)
    else:
        shape = (row_blocks, chunks, size, row_blocks, size)
        up, down = grad_ffn[:row_blocks].reshape(shape), grad_ffn[row_blocks:].reshape(shape)
        up = up.transpose(0, 3, 1, 2, 4).reshape(-1, size, size)
        down = down.transpose(0, 1, 3, 2, 4).reshape(-1, size, size)
        ffn_sum = lax.psum_scatter(
            jnp.concatenate([up, down], axis=0), "dp", scatter_dimension=0, tiled=True
        )
        attn_full = jnp.stack([attn_keep, attn_send], axis=2).reshape(-1, size, width)
        attn_sum = lax.psum_scatter(
            parts_to_blocks(attn_full), ("mod", "dp"), scatter_dimension=0, tiled=True
        )
        small_sum = lax.psum(small.astype(f32), ("mod", "dp")).astype(bf16)
        ffn_old = [part for part in (ffn_left, ffn_right, ffn_blocks)]
        attn_old = [part[None] for part in (attn_left, attn_right, attn_blocks)]
        ffn_out = shampoo(is_not, 0, 1, [square_parts(ffn_sum, 1, ffn_sum.shape[0])], *ffn_old)
        attn_out = shampoo(is_not, 0, 1, [square_parts(attn_sum, 1, attn_sum.shape[0])], *attn_old)

    items_total = lax.axis_size("dp")
    vector_rate = 0.3 / math.sqrt(items_total * slots)
    pos_rate = 0.5 / math.sqrt(items_total)
    vector_news = momentum_step(
        small_sum, vectors, vectors_mom, ffn_bias, ffn_bias_mom, pos_table, pos_mom, vector_rate, pos_rate
    )
    return (
        stream_out,
        stream_grad,
        *attn_out,
        *(part[None] for part in ffn_out),
        *vector_news,
    )


def solution(mesh):
    items = P("mod", "dp", None, None)
    owned = P(("mod", "dp"), None, None)
    return jax.shard_map(
        local,
        mesh=mesh,
        in_specs=(items, items, P("dp"), P("dp", None), owned, owned, owned, items, items, items)
        + (P(),) * 6,
        out_specs=(items, items, owned, owned, owned, owned, items, items, items, items)
        + (P(),) * 6,
        check_vma=False,
    )
```

```python
import functools
import math

import jax
import jax.numpy as jnp
from jax import lax
from jax.experimental import pallas as pl
from jax.experimental.pallas import tpu as pltpu
from jax.sharding import PartitionSpec as P

HEADS = 12
TEXT = 64
NEWTON = 6
PAIR_LANES = 128
QUERY_TILE = 336
GRAD_TILE = 512

f32 = jnp.float32
bf16 = jnp.bfloat16
norm_eps = 1e-05
stat_decay = 0.5
matrix_rate = 0.25
moment_keep = 0.9
masked_score = -1e30


def dot_nn(left, right):
    return lax.dot_general(left, right, (((1,), (0,)), ((), ())), preferred_element_type=f32)


def dot_nt(left, right):
    return lax.dot_general(left, right, (((1,), (1,)), ((), ())), preferred_element_type=f32)


def dot_tn(left, right):
    return lax.dot_general(left, right, (((0,), (0,)), ((), ())), preferred_element_type=f32)


def params(mebibytes=56):
    return pltpu.CompilerParams(vmem_limit_bytes=mebibytes << 20)


def cost(microseconds):
    return pl.CostEstimate(flops=int(microseconds), bytes_accessed=0, transcendentals=0)


def round_up(value, step):
    return (value + step - 1) // step * step


def whole(shape):
    return pl.BlockSpec(shape, lambda *ids: (0,) * len(shape))


SMEM_SPEC = pl.BlockSpec(memory_space=pltpu.SMEM)


def pack_kernel(up_ref, blocks_ref, out_ref):
    part = pl.program_id(0)
    parts = pl.num_programs(0)
    per_row = blocks_ref.shape[0] // parts
    pieces = []
    for i in range(per_row):
        at = jnp.where(up_ref[0] == 1, i * parts + part, part * per_row + i)
        pieces.append(blocks_ref[at])
    out_ref[0] = jnp.concatenate(pieces, axis=1).astype(bf16)


def pack_rows(is_up, blocks, per_row):
    count, size, _ = blocks.shape
    return pl.pallas_call(
        pack_kernel,
        grid=(count // per_row,),
        in_specs=[SMEM_SPEC, whole(blocks.shape)],
        out_specs=pl.BlockSpec((1, size, per_row * size), lambda i: (i, 0, 0)),
        out_shape=jax.ShapeDtypeStruct((count // per_row, size, per_row * size), bf16),
        compiler_params=params(),
        cost_estimate=cost(3),
        name="pack_rows",
    )(is_up, blocks)


def norm_rows(values):
    centred = values - jnp.mean(values, axis=-1, keepdims=True)
    spread = jnp.mean(centred * centred, axis=-1, keepdims=True)
    inv_std = lax.rsqrt(spread + norm_eps)
    return centred * inv_std, inv_std


def norm_input_grad(grad_out, normal, inv_std, gain):
    grad_norm = grad_out * gain
    mean_grad = jnp.mean(grad_norm, axis=-1, keepdims=True)
    mean_proj = jnp.mean(grad_norm * normal, axis=-1, keepdims=True)
    return inv_std * (grad_norm - mean_grad - normal * mean_proj)


def first_norm_kernel(row_ref, hidden_ref, vec_ref, first_ref):
    rows = hidden_ref.shape[0]
    normal, _ = norm_rows(hidden_ref[...])
    first_ref[...] = jnp.zeros(first_ref.shape, bf16)
    first = normal * vec_ref[0:1, :] + vec_ref[1:2, :]
    first_ref[pl.ds(pl.multiple_of(row_ref[0], 16), rows), :] = first.astype(bf16)


def first_norm(rows_info, hidden, vec, seq):
    return pl.pallas_call(
        first_norm_kernel,
        in_specs=[SMEM_SPEC, whole(hidden.shape), whole(vec.shape)],
        out_specs=whole((seq, hidden.shape[1])),
        out_shape=jax.ShapeDtypeStruct((seq, hidden.shape[1]), bf16),
        compiler_params=params(24),
        cost_estimate=cost(4),
        name="first_norm",
    )(rows_info, hidden, vec)


def project_kernel(row_ref, first_ref, vec_ref, *refs):
    weight_refs, (qkv_ref, w_ref) = refs[:-2], refs[-2:]
    step = pl.program_id(0)
    if len(weight_refs) == 1:
        w_ref[...] = weight_refs[0][...]
    else:
        upper, upper_far, lower, lower_far = weight_refs
        half = upper.shape[3]
        size = half + lower.shape[3]
        on_one = row_ref[5] == 1
        for z in range(2):
            for y in range(2):
                for base, near, far in (
                    (0, upper[0, y, z], upper_far[0, y, z]),
                    (half, lower[y, 0, z], lower_far[y, 0, z]),
                ):
                    start = (4 * z + 2 * y) * size + base
                    end = start + near.shape[0]
                    w_ref[0, start:end, :] = jnp.where(on_one, far, near)
                    w_ref[0, start + size : end + size, :] = jnp.where(on_one, near, far)

    @pl.when(step < 3)
    def _():
        bias = jnp.where(step == 0, vec_ref[5:6, :], jnp.where(step == 2, vec_ref[6:7, :], 0.0))
        qkv_ref[...] = (dot_nn(first_ref[...], w_ref[0]) + bias).astype(bf16)


def project(rows_info, first, vec, attn_parts):
    seq, width = first.shape
    if len(attn_parts) == 1:
        weight_specs = [pl.BlockSpec((1, width, width), lambda i: (i, 0, 0))]
    else:
        rows = [part.shape[3] for part in attn_parts]
        upper = pl.BlockSpec((1, 2, 2, rows[0], width), lambda i: (i // 2, 0, i % 2, 0, 0))
        lower = pl.BlockSpec((2, 1, 2, rows[2], width), lambda i: (0, i // 2, i % 2, 0, 0))
        weight_specs = [upper, upper, lower, lower]
    return pl.pallas_call(
        project_kernel,
        grid=(4,),
        in_specs=[SMEM_SPEC, whole((seq, width)), whole(vec.shape), *weight_specs],
        out_specs=[
            pl.BlockSpec((seq, width), lambda i: (0, jnp.minimum(i, 2))),
            pl.BlockSpec((1, width, width), lambda i: (i, 0, 0)),
        ],
        out_shape=[
            jax.ShapeDtypeStruct((seq, 3 * width), bf16),
            jax.ShapeDtypeStruct((4, width, width), bf16),
        ],
        compiler_params=params(24),
        cost_estimate=cost(8),
        name="project",
    )(rows_info, first, vec, *attn_parts)


def key_bias(row_ref, seq):
    rows = lax.broadcasted_iota(jnp.int32, (seq, 1), 0)
    counts = jnp.logical_and(rows >= row_ref[1], rows < row_ref[2])
    return jnp.where(counts, 0.0, masked_score).astype(f32)


def transposed(values):
    return jnp.transpose(values.astype(f32), (1, 0)).astype(bf16)


def attend_kernel(row_ref, q_ref, k_ref, v_ref, ctx_ref, lse_ref, pair_ref):
    seq = q_ref.shape[0]
    half = PAIR_LANES // 2
    scale = half ** (-0.5)
    lane = lax.broadcasted_iota(jnp.int32, (seq, PAIR_LANES), 1)
    bias = key_bias(row_ref, seq).astype(bf16)
    queries = q_ref[...] * jnp.asarray(scale, bf16)
    keys = k_ref[...]
    values = v_ref[...]
    one = jnp.ones((seq, PAIR_LANES), bf16)
    heads = []
    for head in range(2):
        own = (lane < half) == (head == 0)
        spare = lane == half * (1 - head)
        head_q = jnp.where(own, queries, jnp.where(spare, one, jnp.zeros_like(one)))
        head_k = jnp.where(own, keys, jnp.where(spare, bias, jnp.zeros_like(one)))
        head_v = jnp.where(own, values, one)
        heads.append((head_q, head_k, head_v))
    for start in range(0, seq, QUERY_TILE):
        size = min(QUERY_TILE, seq - start)
        tile = slice(start, start + size)
        parts, lses = [], []
        for head, (head_q, head_k, head_v) in enumerate(heads):
            scores = dot_nt(head_q[tile], head_k)
            top = jnp.max(scores, axis=1, keepdims=True)
            raised = jnp.exp(scores - top).astype(bf16)
            summed = dot_nn(raised, head_v)
            at = half * (1 - head)
            total = summed[:, at : at + 1]
            parts.append(summed * (1.0 / total))
            lses.append(top + jnp.log(total))
        low = lax.broadcasted_iota(jnp.int32, (size, PAIR_LANES), 1) < half
        context = jnp.where(low, parts[0], parts[1]).astype(bf16)
        ctx_ref[tile, :] = context
        if start == 0:
            pair_ref[...] = context[: pair_ref.shape[0]]
        column = lax.broadcasted_iota(jnp.int32, (size, PAIR_LANES), 1) - 2 * pl.program_id(0)
        others = jnp.where(column < 0, lse_ref[tile, :], 0.0)
        lse_ref[tile, :] = jnp.where(column == 0, lses[0], jnp.where(column == 1, lses[1], others))


def attend(rows_info, qkv):
    seq = qkv.shape[0]
    width = qkv.shape[1] // 3
    pairs = width // PAIR_LANES

    def column(base):
        return pl.BlockSpec((seq, PAIR_LANES), lambda i, base=base: (0, base + i))

    return pl.pallas_call(
        attend_kernel, grid=(pairs,),
        in_specs=[SMEM_SPEC, column(0), column(pairs), column(2 * pairs)],
        out_specs=[column(0), whole((seq, PAIR_LANES)), pl.BlockSpec((TEXT, PAIR_LANES), lambda i: (0, i))],
        out_shape=[jax.ShapeDtypeStruct((seq, width), bf16), jax.ShapeDtypeStruct((seq, PAIR_LANES), f32), jax.ShapeDtypeStruct((TEXT, width), bf16)],
        compiler_params=params(20), cost_estimate=cost(12), name="attend",
    )(rows_info, qkv, qkv, qkv)


def three_parts(values):
    high = values.astype(bf16)
    rest = values - high.astype(f32)
    middle = rest.astype(bf16)
    return high, middle, (rest - middle.astype(f32)).astype(bf16)


def attend_grad_kernel(
    row_ref, q_ref, k_ref, v_ref, g_ref, pair_ref, ctx_ref, lse_ref, out_ref, dk_ref, dv_ref
):
    seq = q_ref.shape[0]
    half = PAIR_LANES // 2
    scale = half ** (-0.5)
    lane = lax.broadcasted_iota(jnp.int32, (seq, PAIR_LANES), 1)
    bias = key_bias(row_ref, seq).astype(bf16)
    queries = q_ref[...]
    scaled = queries * jnp.asarray(scale, bf16)
    keys = k_ref[...]
    values = v_ref[...]
    keys_t = transposed(keys)
    row = lax.broadcasted_iota(jnp.int32, (seq, 1), 0)
    counts = jnp.logical_and(row >= row_ref[1], row < row_ref[2])
    grads = jnp.concatenate([pair_ref[...], g_ref[pair_ref.shape[0] :, :]], axis=0)
    grads = jnp.where(counts, grads, jnp.zeros((seq, PAIR_LANES), bf16))
    products = grads.astype(f32) * ctx_ref[...].astype(f32)
    one = jnp.ones((seq, PAIR_LANES), bf16)
    zero = jnp.zeros((seq, PAIR_LANES), bf16)
    heads = []
    for head in range(2):
        own = (lane < half) == (head == 0)
        spare = lane - half * (1 - head)
        held = jnp.where(lane == 2 * pl.program_id(0) + head, lse_ref[...], 0.0)
        lse = three_parts(-jnp.sum(held, axis=1, keepdims=True))
        dots = three_parts(-jnp.sum(jnp.where(own, products, 0.0), axis=1, keepdims=True))
        own_q = jnp.where(own, queries, zero)
        own_g = jnp.where(own, grads, zero)
        head_q = jnp.where(own, scaled, jnp.where(spare == 3, one, zero))
        head_g = own_g
        for i in range(3):
            head_q = jnp.where(spare == i, lse[i], head_q)
            head_g = jnp.where(spare == i, dots[i], head_g)
        head_k = jnp.where(own, keys, jnp.where(spare == 3, bias, one))
        head_v = jnp.where(own, values, one)
        heads.append((head_q, head_g, head_k, head_v, own_q, own_g))
    for start in range(0, seq, GRAD_TILE):
        size = min(GRAD_TILE, seq - start)
        tile = slice(start, start + size)
        parts = []
        for head, (head_q, head_g, head_k, head_v, own_q, own_g) in enumerate(heads):
            probs = jnp.exp(dot_nt(head_k, head_q[tile]))
            grad_scores = (probs * dot_nt(head_v, head_g[tile])).astype(bf16)
            grad_v = dot_nn(probs.astype(bf16), own_g[tile])
            grad_k = dot_nn(grad_scores, own_q[tile])
            if start == 0 and head == 0:
                dv_ref[...] = grad_v
                dk_ref[...] = grad_k
            else:
                dv_ref[...] += grad_v
                dk_ref[...] += grad_k
            parts.append(dot_nn(keys_t[half * head : half * (head + 1), :], grad_scores))
        grad_q = jnp.transpose(jnp.concatenate(parts, axis=0) * scale, (1, 0))
        out_ref[0, tile, :] = grad_q.astype(bf16)
    out_ref[1] = (dk_ref[...] * scale).astype(bf16)
    out_ref[2] = dv_ref[...].astype(bf16)


def attend_grad(rows_info, qkv, grad_ctx, pair_grad, ctx, lse):
    seq = qkv.shape[0]
    width = qkv.shape[1] // 3
    pairs = width // PAIR_LANES

    def column(base):
        return pl.BlockSpec((seq, PAIR_LANES), lambda i, base=base: (0, base + i))

    return pl.pallas_call(
        attend_grad_kernel,
        grid=(pairs,),
        in_specs=[
            SMEM_SPEC,
            column(0),
            column(pairs),
            column(2 * pairs),
            column(0),
            pl.BlockSpec((TEXT, PAIR_LANES), lambda i: (0, i)),
            column(0),
            whole((seq, PAIR_LANES)),
        ],
        out_specs=pl.BlockSpec((3, seq, PAIR_LANES), lambda i: (0, 0, i)),
        out_shape=jax.ShapeDtypeStruct((3, seq, width), bf16),
        scratch_shapes=[pltpu.VMEM((seq, PAIR_LANES), f32)] * 2,
        compiler_params=params(56),
        cost_estimate=cost(15),
        name="attend_grad",
    )(rows_info, qkv, qkv, qkv, grad_ctx, pair_grad, ctx, lse)


def gelu_pair(values):
    size = jnp.abs(values)
    tail = 1.0 / (1.0 + (0.3275911 * 0.5**0.5) * size)
    poly = tail * (
        0.254829592
        + tail * (-0.284496736 + tail * (1.421413741 + tail * (-1.453152027 + tail * 1.061405429)))
    )
    bell = jnp.exp(-0.5 * values * values)
    upper = 0.5 * poly * bell
    share = jnp.where(values >= 0.0, 1.0 - upper, upper)
    return values * share, share + values * bell * ((2.0 * math.pi) ** -0.5)


def split_by_core(row_ref, grad, shape):
    size, width = shape[-2:]
    blocks = grad.reshape(-1, 2, size, width)
    near, far = blocks[:, 0], blocks[:, 1]
    on_one = row_ref[5] == 1
    return jnp.where(on_one, far, near).reshape(shape), jnp.where(on_one, near, far).reshape(shape)


def expert_chunk(
    order, second, gbranch, upb, parts_ref, grad_ref, dupb_ref, branch, gsecond, scratch, begin
):
    pre, gact, act, gpre, up, down = scratch
    rows, width = act.shape
    tile = 16
    size = parts_ref.shape[2]
    places = [(which, slice(i * size, (i + 1) * size)) for which in range(2) for i in range(len(order) // 2)]
    for at, (which, span) in zip(order, places):
        (up, down)[which][span, :] = parts_ref[at, 0]
    pre[...] = dot_nn(second[...], up[...])
    gact[...] = dot_nt(gbranch[...], down[...])

    def body(i, total):
        at = pl.ds(pl.multiple_of(i * tile, tile), tile)
        value, slope = gelu_pair(pre[at, :] + upb[...])
        act[at, :] = value.astype(bf16)
        rounded = (gact[at, :] * slope).astype(bf16)
        gpre[at, :] = rounded
        return total + rounded.astype(f32)

    total = lax.fori_loop(0, rows // tile, body, jnp.zeros((tile, width), f32), unroll=True)
    dupb_ref[...] = jnp.sum(total, axis=0, keepdims=True)
    grads = [
        dot_tn(second[...], gpre[...]).astype(bf16),
        dot_tn(act[...], gbranch[...]).astype(bf16),
    ]
    for at, (which, span) in zip(order, places):
        grad_ref[at, 0] = grads[which][span, :]
    own_branch = dot_nn(act[...], down[...])
    own_gsecond = dot_nt(gpre[...], up[...])

    @pl.when(begin)
    def _():
        branch[...] = own_branch
        gsecond[...] = own_gsecond

    @pl.when(jnp.logical_not(begin))
    def _():
        branch[...] += own_branch
        gsecond[...] += own_gsecond


def expert_kernel(
    order,
    row_ref,
    ctx_ref,
    pair_ref,
    hidden_ref,
    cot_ref,
    vec_ref,
    upb_ref,
    wo_ref,
    parts_ref,
    out_ref,
    gmid_ref,
    gctx_ref,
    pair_grad_ref,
    dwo_ref,
    grad_ref,
    dvec_ref,
    dupb_ref,
    own_ctx,
    middle,
    second,
    gbranch,
    branch,
    gsecond,
    *scratch,
):
    step = pl.program_id(0)
    rows, width = hidden_ref.shape
    out_rows = out_ref.shape[0]
    tile = 16

    @pl.when(step == 0)
    def _():
        own_ctx[...] = ctx_ref[pl.ds(pl.multiple_of(row_ref[0], 16), rows), :]

        @pl.when(row_ref[3] == 1)
        def _():
            own_ctx[0 : pair_ref.shape[0], :] = pair_ref[...]

        middle[...] = dot_nn(own_ctx[...], wo_ref[0])

        def body(i, total):
            at = pl.ds(pl.multiple_of(i * tile, tile), tile)
            mid = hidden_ref[at, :] + (middle[at, :] + vec_ref[7:8, :])
            middle[at, :] = mid
            normal, _ = norm_rows(mid)
            second[at, :] = (normal * vec_ref[2:3, :] + vec_ref[3:4, :]).astype(bf16)
            row = lax.broadcasted_iota(jnp.int32, (tile, 1), 0) + i * tile
            kept = jnp.where(row < row_ref[4], cot_ref[at, :], 0.0)
            rounded = kept.astype(bf16)
            gbranch[at, :] = rounded
            return total + rounded.astype(f32)

        total = lax.fori_loop(
            0, rows // tile, body, jnp.zeros((tile, width), f32), unroll=True
        )
        dvec_ref[...] = jnp.zeros(dvec_ref.shape, f32)
        dvec_ref[2:3, :] = jnp.sum(total, axis=0, keepdims=True)

    expert_chunk(
        order,
        second,
        gbranch,
        upb_ref,
        parts_ref,
        grad_ref,
        dupb_ref,
        branch,
        gsecond,
        scratch,
        step == 0,
    )

    @pl.when(step == pl.num_programs(0) - 1)
    def _():
        def body(i, totals):
            at = pl.ds(pl.multiple_of(i * tile, tile), tile)
            mid = middle[at, :]
            normal, inv_std = norm_rows(mid)
            grad_out = gsecond[at, :]
            row = lax.broadcasted_iota(jnp.int32, (tile, 1), 0) + i * tile
            kept = row < row_ref[4]
            branch[at, :] = jnp.where(kept, mid + (branch[at, :] + vec_ref[4:5, :]), 0.0)
            grad_in = norm_input_grad(grad_out, normal, inv_std, vec_ref[2:3, :])
            grad_mid = jnp.where(kept, cot_ref[at, :], 0.0) + grad_in
            gmid_ref[at, :] = grad_mid
            rounded = grad_mid.astype(bf16)
            gbranch[at, :] = rounded
            return (
                totals[0] + grad_out * normal,
                totals[1] + grad_out,
                totals[2] + rounded.astype(f32),
            )

        zero = jnp.zeros((tile, width), f32)
        gains, shifts, biases = lax.fori_loop(
            0, rows // tile, body, (zero, zero, zero), unroll=True
        )
        dvec_ref[0:1, :] = jnp.sum(gains, axis=0, keepdims=True)
        dvec_ref[1:2, :] = jnp.sum(shifts, axis=0, keepdims=True)
        dvec_ref[3:4, :] = jnp.sum(biases, axis=0, keepdims=True)
        out_ref[...] = branch[0:out_rows, :].reshape(out_ref.shape)
        dwo_ref[...] = dot_tn(own_ctx[...], gbranch[...]).astype(bf16)
        grad_ctx = dot_nt(gbranch[...], wo_ref[0]).astype(bf16)
        gctx_ref[...] = jnp.zeros(gctx_ref.shape, bf16)
        gctx_ref[pl.ds(pl.multiple_of(row_ref[0], 16), rows), :] = grad_ctx
        pair_grad_ref[...] = grad_ctx[: pair_grad_ref.shape[0]]


def expert(rows_info, ctx, pair_ctx, hidden, cot, vec, up_bias, w_attn, ffn_parts, order, out_rows):
    rows, width = hidden.shape
    seq = ctx.shape[0]
    blocks, chunks, size, _ = ffn_parts.shape
    parts = pl.BlockSpec((blocks, 1, size, width), lambda i: (0, i, 0, 0))
    return pl.pallas_call(
        functools.partial(expert_kernel, order),
        grid=(chunks,),
        in_specs=[
            SMEM_SPEC,
            whole(ctx.shape),
            whole(pair_ctx.shape),
            whole(hidden.shape),
            whole(cot.shape),
            whole(vec.shape),
            pl.BlockSpec((1, width), lambda i: (0, i)),
            pl.BlockSpec((1, width, width), lambda i: (3, 0, 0)),
            parts,
        ],
        out_specs=[
            whole((out_rows, 1, width)),
            whole((rows, width)),
            whole((seq, width)),
            whole((TEXT, width)),
            whole((width, width)),
            parts,
            whole((8, width)),
            pl.BlockSpec((1, width), lambda i: (0, i)),
        ],
        out_shape=[
            jax.ShapeDtypeStruct((out_rows, 1, width), f32),
            jax.ShapeDtypeStruct((rows, width), f32),
            jax.ShapeDtypeStruct((seq, width), bf16),
            jax.ShapeDtypeStruct((TEXT, width), bf16),
            jax.ShapeDtypeStruct((width, width), bf16),
            jax.ShapeDtypeStruct(ffn_parts.shape, bf16),
            jax.ShapeDtypeStruct((8, width), f32),
            jax.ShapeDtypeStruct((1, chunks * width), f32),
        ],
        scratch_shapes=[
            pltpu.VMEM((rows, width), bf16),
            pltpu.VMEM((rows, width), f32),
            pltpu.VMEM((rows, width), bf16),
            pltpu.VMEM((rows, width), bf16),
            pltpu.VMEM((rows, width), f32),
            pltpu.VMEM((rows, width), f32),
            pltpu.VMEM((rows, width), f32),
            pltpu.VMEM((rows, width), f32),
            pltpu.VMEM((rows, width), bf16),
            pltpu.VMEM((rows, width), bf16),
            pltpu.VMEM((width, width), bf16),
            pltpu.VMEM((width, width), bf16),
        ],
        compiler_params=params(),
        cost_estimate=cost(43),
        name="expert",
    )(rows_info, ctx, pair_ctx, hidden, cot, vec, up_bias, w_attn, ffn_parts)


def project_grad_kernel(
    row_ref, dqkv_ref, first_ref, w_ref, dwo_ref, keep_ref, send_ref, gfirst, pair_ref, sums_ref
):
    step = pl.program_id(0)

    def put(grad):
        keep_ref[0], send_ref[0] = split_by_core(row_ref, grad, keep_ref.shape[1:])

    @pl.when(step < 3)
    def _():
        own = dqkv_ref[0]
        put(dot_tn(first_ref[...], own).astype(bf16))
        share = dot_nt(own, w_ref[0])
        sums = jnp.sum(own.astype(f32), axis=0, keepdims=True)

        @pl.when(step == 0)
        def _():
            gfirst[...] = share
            sums_ref[...] = jnp.zeros(sums_ref.shape, f32)
            sums_ref[0:1, :] = sums

        @pl.when(step > 0)
        def _():
            gfirst[...] += share
            sums_ref[1:2, :] = sums

    @pl.when(step == 3)
    def _():
        put(dwo_ref[...])
        pair_ref[...] = gfirst[0 : pair_ref.shape[0], :]


def project_grad(rows_info, dqkv, first, w_attn, grad_wo, size):
    seq, width = first.shape
    pairs = width // size // 2
    part = pl.BlockSpec((1, pairs, size, width), lambda i: (i, 0, 0, 0))

    def early_index(i):
        return (jnp.minimum(i, 2), 0, 0)

    return pl.pallas_call(
        project_grad_kernel,
        grid=(4,),
        in_specs=[
            SMEM_SPEC,
            pl.BlockSpec((1, seq, width), early_index),
            whole((seq, width)),
            pl.BlockSpec((1, width, width), early_index),
            whole(grad_wo.shape),
        ],
        out_specs=[part, part, whole((seq, width)), whole((TEXT, width)), whole((8, width))],
        out_shape=[
            jax.ShapeDtypeStruct((4, pairs, size, width), bf16),
            jax.ShapeDtypeStruct((4, pairs, size, width), bf16),
            jax.ShapeDtypeStruct((seq, width), f32),
            jax.ShapeDtypeStruct((TEXT, width), f32),
            jax.ShapeDtypeStruct((8, width), f32),
        ],
        compiler_params=params(56),
        cost_estimate=cost(15),
        name="project_grad",
    )(rows_info, dqkv, first, w_attn, grad_wo)


def first_grad_kernel(
    row_ref,
    gfirst_ref,
    pair_ref,
    hidden_ref,
    gmid_ref,
    vec_ref,
    sums_ref,
    late_ref,
    upb_ref,
    pos_ref,
    out_ref,
    small_ref,
    own,
):
    rows, width = hidden_ref.shape
    tile = 16
    own[...] = gfirst_ref[pl.ds(pl.multiple_of(row_ref[0], 16), rows), :]

    @pl.when(row_ref[3] == 1)
    def _():
        own[0 : pair_ref.shape[0], :] = pair_ref[...]

    def body(i, totals):
        at = pl.ds(pl.multiple_of(i * tile, tile), tile)
        normal, inv_std = norm_rows(hidden_ref[at, :])
        grad_out = own[at, :]
        grad_in = norm_input_grad(grad_out, normal, inv_std, vec_ref[0:1, :])
        own[at, :] = gmid_ref[at, :] + grad_in
        return totals[0] + grad_out * normal, totals[1] + grad_out

    zero = jnp.zeros((tile, width), f32)
    gains, shifts = lax.fori_loop(0, rows // tile, body, (zero, zero), unroll=True)
    out_ref[...] = own[0 : out_ref.shape[0], :].reshape(out_ref.shape)
    own_rows = (
        jnp.sum(gains, axis=0, keepdims=True),
        jnp.sum(shifts, axis=0, keepdims=True),
        late_ref[0:1, :],
        late_ref[1:2, :],
        late_ref[2:3, :],
    )
    row = lax.broadcasted_iota(jnp.int32, (16, width), 0)
    top = jnp.where(row == 0, sums_ref[0:1, :], 0.0)
    top = jnp.where(row == 1, sums_ref[1:2, :], top)
    top = jnp.where(row == 2, late_ref[3:4, :], top)
    for i, value in enumerate(own_rows):
        top = jnp.where(row == 3 + 5 * row_ref[3] + i, value, top)
    small_ref[0:16, :] = top.astype(small_ref.dtype)
    row = lax.broadcasted_iota(jnp.int32, (8, width), 0)
    bias = jnp.zeros((8, width), f32)
    for i in range(upb_ref.shape[0]):
        bias = jnp.where(row == upb_ref.shape[0] * row_ref[3] + i, upb_ref[i : i + 1, :], bias)
    small_ref[16:32, :] = jnp.concatenate([bias, jnp.zeros_like(bias)], axis=0).astype(small_ref.dtype)
    grads = own[...]
    high = grads.astype(bf16)
    low = (grads - high.astype(f32)).astype(bf16)
    table = lax.broadcasted_iota(jnp.int32, (rows, rows), 0)
    chosen = jnp.where(row_ref[3] == 0, pos_ref[...], -1) == table
    chosen = jnp.where(chosen, 1.0, 0.0).astype(bf16)
    sums = dot_nn(chosen, high) + dot_nn(chosen, low)
    small_ref[32 : 32 + rows, :] = sums.astype(small_ref.dtype)
    spare = small_ref.shape[0] - 32 - rows
    if spare:
        small_ref[32 + rows :, :] = jnp.zeros((spare, width), small_ref.dtype)


def first_grad(
    rows_info, gfirst, pair_grad, hidden, grad_middle, vec, sums, late, up_bias, pos, out_rows
):
    rows, width = hidden.shape
    small = round_up(32 + rows, 128)
    args = (gfirst, pair_grad, hidden, grad_middle, vec, sums, late, up_bias, pos)
    return pl.pallas_call(
        first_grad_kernel,
        in_specs=[SMEM_SPEC] + [whole(arg.shape) for arg in args],
        out_specs=[whole((out_rows, 1, width)), whole((small, width))],
        out_shape=[
            jax.ShapeDtypeStruct((out_rows, 1, width), f32),
            jax.ShapeDtypeStruct((small, width), bf16),
        ],
        scratch_shapes=[pltpu.VMEM((rows, width), f32)],
        compiler_params=params(24),
        cost_estimate=cost(8),
        name="first_grad",
    )(rows_info, *args)


def widen(values):
    rows, cols = values.shape
    return jnp.concatenate([values, jnp.zeros((rows, PAIR_LANES - cols), f32)], axis=1)


def split_parts(values):
    high = values.astype(bf16)
    return high, (values - high.astype(f32)).astype(bf16)


def left_parts(values):
    return jnp.concatenate(split_parts(values), axis=1)


def right_parts(values):
    high, low = split_parts(values)
    rows, cols = high.shape
    gap = jnp.zeros((cols - rows, cols), bf16)
    near = jnp.concatenate([high, gap, high, gap], axis=0)
    far = jnp.concatenate([low, gap, jnp.zeros((cols, cols), bf16)], axis=0)
    return jnp.concatenate([near, far], axis=1)


def times(left, right):
    both = dot_nn(left, right)
    return both[:, :PAIR_LANES] + both[:, PAIR_LANES:]


def inverse_roots(stats, identity):
    size = stats[0].shape[0]
    mats, factors = [], []
    for stat in stats:
        norm = jnp.sqrt(jnp.sum(stat * stat, keepdims=True))
        mats.append(stat * (1.0 / norm))
        factors.append(lax.rsqrt(jnp.sqrt(norm)))
    for iteration in range(NEWTON):
        steps = [1.25 * identity - 0.25 * mat for mat in mats]
        if iteration == 0:
            factors = [step * factor for step, factor in zip(steps, factors)]
            squares = [times(left_parts(step), right_parts(step)) for step in steps]
        elif iteration < NEWTON - 1:
            both = [
                times(
                    jnp.concatenate([left_parts(step), left_parts(factor)], axis=0),
                    right_parts(step),
                )
                for step, factor in zip(steps, factors)
            ]
            squares = [pair[:size] for pair in both]
            factors = [pair[size:] for pair in both]
        else:
            return [
                times(left_parts(factor), right_parts(step)) for step, factor in zip(steps, factors)
            ]
        fourths = [times(left_parts(square), right_parts(square)) for square in squares]
        mats = [times(left_parts(fourth), right_parts(mat)) for fourth, mat in zip(fourths, mats)]


def shampoo_kernel(group, begin, parts, grad_count, earlier, up_ref, *refs):
    part = begin + pl.program_id(0)
    grad_refs = refs[:grad_count]
    left_ref, right_ref, w_ref = refs[grad_count : grad_count + 3]
    outs = refs[grad_count + 3 + earlier : grad_count + 7 + earlier]
    results, sems = refs[-2:]
    _, count, size, _ = left_ref.shape
    row = lax.broadcasted_iota(jnp.int32, (size, PAIR_LANES), 0)
    col = lax.broadcasted_iota(jnp.int32, (size, PAIR_LANES), 1)
    identity = (row == col).astype(f32)
    copies = []

    def store(kind, i, at, value):
        results[kind, i] = value
        copy = pltpu.make_async_copy(results.at[kind, i], outs[kind].at[at], sems.at[kind, i])
        copy.start()
        copies.append(copy)

    for base in range(0, count, group):
        places, stats, grads = [], [], []
        for i in range(base, base + group):
            at = jnp.where(up_ref[0] == 1, i * parts + part, part * count + i)
            places.append(at)
            span = slice(i * size, (i + 1) * size)
            grad = grad_refs[0][0, :, span].astype(f32)
            for ref in grad_refs[1:]:
                grad = grad + ref[0, :, span].astype(f32)
            store(0, i, at, grad)
            grad = widen(grad)
            grad_t = widen(jnp.transpose(grad, (1, 0))[:size])
            grads.append(grad)
            outer = times(left_parts(grad), right_parts(grad_t))
            inner = times(left_parts(grad_t), right_parts(grad))
            left_new = stat_decay * left_ref[0, i] + (1.0 - stat_decay) * outer[:, :size]
            right_new = stat_decay * right_ref[0, i] + (1.0 - stat_decay) * inner[:, :size]
            store(1, i, at, left_new)
            store(2, i, at, right_new)
            stats += [widen(left_new), widen(right_new)]
        roots = inverse_roots(stats, identity)
        for i, at in enumerate(places):
            half_way = times(left_parts(roots[2 * i]), right_parts(grads[i]))
            update = times(left_parts(half_way), right_parts(roots[2 * i + 1]))
            store(3, base + i, at, w_ref[0, base + i] - matrix_rate * update[:, :size])
    for copy in copies:
        copy.wait()


def shampoo(is_up, begin, end, grad_rows, lefts, rights, weights, earlier=(), mebibytes=24):
    parts, count, size, _ = lefts.shape
    span = count * size
    blocks = pl.BlockSpec((1, count, size, size), lambda i: (begin + i, 0, 0, 0))
    shape = jax.ShapeDtypeStruct((parts * count, size, size), f32)
    anywhere = pl.BlockSpec(memory_space=pl.ANY)
    first_earlier = 4 + len(grad_rows)
    kernel = functools.partial(
        shampoo_kernel, math.gcd(count, 8), begin, parts, len(grad_rows), len(earlier)
    )
    return pl.pallas_call(
        kernel,
        grid=(end - begin,),
        in_specs=[SMEM_SPEC]
        + [pl.BlockSpec((1, size, span), lambda i: (begin + i, 0, 0))] * len(grad_rows)
        + [blocks] * 3
        + [anywhere] * len(earlier),
        out_specs=[anywhere] * 4,
        out_shape=[shape] * 4,
        scratch_shapes=[
            pltpu.VMEM((4, count, size, size), f32),
            pltpu.SemaphoreType.DMA((4, count)),
        ],
        input_output_aliases={first_earlier + i: i for i in range(len(earlier))},
        compiler_params=params(mebibytes),
        cost_estimate=cost(9),
        name="shampoo",
    )(is_up, *grad_rows, lefts, rights, weights, *earlier)


def momentum_kernel(
    vector_rate, pos_rate, sum_ref, v_ref, vm_ref, b_ref, bm_ref, p_ref, pm_ref, vm_out, v_out, bm_out, b_out, pm_out, p_out
):
    width = v_ref.shape[1]
    new = moment_keep * vm_ref[...] + sum_ref[0 : v_ref.shape[0], :].astype(f32)
    vm_out[...] = new
    v_out[...] = v_ref[...] - vector_rate * new
    per_row = b_ref.shape[1] // width
    rows = sum_ref[16:32, :].astype(f32)
    for i in range(b_ref.shape[0]):
        for j in range(per_row):
            at = (slice(i, i + 1), slice(j * width, (j + 1) * width))
            row = i * per_row + j
            new = moment_keep * bm_ref[at] + rows[row : row + 1, :]
            bm_out[at] = new
            b_out[at] = b_ref[at] - vector_rate * new
    new = moment_keep * pm_ref[...] + sum_ref[32 : 32 + p_ref.shape[0], :].astype(f32)
    pm_out[...] = new
    p_out[...] = p_ref[...] - pos_rate * new


def momentum_step(sums, vectors, vectors_mom, bias, bias_mom, table, table_mom, vector_rate, pos_rate):
    args = (sums, vectors, vectors_mom, bias, bias_mom, table, table_mom)
    outs = (vectors, vectors, bias, bias, table, table)
    return pl.pallas_call(
        functools.partial(momentum_kernel, vector_rate, pos_rate),
        in_specs=[whole(arg.shape) for arg in args],
        out_specs=[whole(out.shape) for out in outs],
        out_shape=[jax.ShapeDtypeStruct(out.shape, f32) for out in outs],
        compiler_params=params(24),
        cost_estimate=cost(3),
        name="momentum",
    )(*args)


CORE, Y, Z_LOW, Z_HIGH = 1, 2, 4, 8


def flip(values, bits):
    size = lax.axis_size("dp")
    return lax.ppermute(values, "dp", [(i, i ^ bits) for i in range(size)])


def flip_mod(values):
    return lax.ppermute(values, "mod", [(0, 1), (1, 0)])


def in_order(bit, own, other):
    return jnp.stack([jnp.where(bit == 1, other, own), jnp.where(bit == 1, own, other)])


def ring_order():
    chips = [(z, 0) for z in range(4)] + [(z, 1) for z in reversed(range(4))]
    return [z * 4 + y * 2 + core for z, y in chips for core in range(2)]


def place():
    index = lax.axis_index("dp")
    return index % 2, index // 2 % 2, index // 4


def sync(*values):
    return lax.optimization_barrier(values)


def pick(values, index, axis):
    return lax.dynamic_index_in_dim(values, index, axis, keepdims=False)


def plus(left, right):
    return (left.astype(f32) + right.astype(f32)).astype(bf16)


def square_parts(blocks, rows, cols):
    size = blocks.shape[-1]
    shaped = blocks.reshape(rows, cols, size, size)
    return jnp.swapaxes(shaped, 1, 2).reshape(rows, size, cols * size)


def parts_to_blocks(parts):
    rows, size, span = parts.shape
    shaped = parts.reshape(rows, size, span // size, size)
    return jnp.swapaxes(shaped, 1, 2).reshape(-1, size, size)


def local(
    stream_in,
    cotangent,
    patch_count,
    pos_index,
    attn_blocks,
    attn_left,
    attn_right,
    ffn_blocks,
    ffn_left,
    ffn_right,
    vectors,
    vectors_mom,
    ffn_bias,
    ffn_bias_mom,
    pos_table,
    pos_mom,
):
    size = attn_blocks.shape[-1]
    width = vectors.shape[1]
    hidden_units = ffn_bias.shape[1]
    slots = stream_in.shape[2]
    row_blocks = width // size
    chunks = hidden_units // width
    rows = round_up(slots, 16)
    seq = round_up(slots + TEXT, 32)
    by_rows = lax.axis_size("dp") == 16 and attn_blocks.shape[0] == row_blocks
    modality = lax.axis_index("mod")
    is_text = modality == 1
    image_flag = (1 - modality).astype(f32)
    along = lax.axis_index("dp")
    is_up = jnp.where(along < lax.axis_size("dp") // 2, 1, 0).astype(jnp.int32)[None]
    is_not = jnp.zeros((1,), jnp.int32)

    core, y, z = place()
    order = range(2 * row_blocks)
    if by_rows:
        order = [ring_order().index(device) for device in order]
    order = tuple(order)
    to_image = [(1, 0)]
    to_text = [(0, 1)]

    if by_rows:
        own_attn = pack_rows(is_not, attn_blocks, row_blocks)[0]
        along_z = [flip(own_attn, bits) for bits in (Z_LOW, Z_HIGH, Z_LOW | Z_HIGH)]
        ffn_rows = pack_rows(is_up, ffn_blocks[0], row_blocks)

    own_vec = lax.dynamic_slice_in_dim(vectors, 3 + 5 * modality, 5, 0)
    vec = jnp.concatenate([own_vec, vectors[0:3]], axis=0)
    up_bias = lax.dynamic_index_in_dim(ffn_bias, modality, 0, keepdims=False)
    up_bias = jnp.swapaxes(up_bias.reshape(row_blocks, chunks, size), 0, 1).reshape(1, hidden_units)
    count = patch_count[0]
    offset = TEXT * (1 - modality)
    first_key = jnp.where(is_text, TEXT, 0)
    end_key = jnp.where(is_text, slots, TEXT + count)
    kept_rows = jnp.where(is_text, slots, count)
    own_core = core if by_rows else 0 * along
    rows_info = jnp.stack([offset, first_key, end_key, modality, kept_rows, own_core])
    rows_info = rows_info.astype(jnp.int32)
    pad = ((0, rows - slots), (0, 0))
    pos = jnp.pad(pos_index[0], pad[0], constant_values=-1)[None]
    if by_rows:
        along_z[0], ffn_rows = sync(along_z[0], ffn_rows)
        along_z, pos_index, stream_in, cotangent, up_bias, pos = sync(
            along_z, pos_index, stream_in, cotangent, up_bias, pos
        )
        ffn_parts = lax.all_gather(ffn_rows, "dp", axis=0, axis_index_groups=[ring_order()])
        near = in_order(z % 2, own_attn, along_z[0])
        far = in_order(z % 2, along_z[1], along_z[2])
        attn_z = in_order(z // 2, near, far).reshape(4, size, width)
        upper, lower = attn_z[:, : size // 2], attn_z[:, size // 2 :]
        upper_y, lower_x = flip(upper, Y), flip_mod(lower)
    table_rows = jnp.take(pos_table, pos_index[0], axis=0)
    if by_rows:
        upper_y, lower_x, table_rows, stream_in, cotangent = sync(
            upper_y, lower_x, table_rows, stream_in, cotangent
        )
        upper, lower = in_order(y, upper, upper_y), in_order(modality, lower, lower_x)
        upper_x, lower_y = flip_mod(upper), flip(lower, Y)
    hidden = jnp.pad(stream_in[0, 0] + image_flag * table_rows, pad)
    first = first_norm(rows_info, hidden, vec, seq)
    pair_first = lax.ppermute(first[:TEXT], "mod", to_image)
    first = lax.dynamic_update_slice(first, jnp.where(is_text, first[:TEXT], pair_first), (0, 0))
    cot = jnp.pad(cotangent[0, 0], pad)

    def by_parts(blocks):
        by_chunk = blocks.reshape(chunks, -1, size, size)
        spread = jnp.swapaxes(blocks.reshape(-1, chunks, size, size), 0, 1)
        return jnp.where(is_up[0] == 1, spread, by_chunk)

    if by_rows:
        ffn_old = [by_parts(part[0]) for part in (ffn_left, ffn_right, ffn_blocks)]
        upper_x, lower_y, first, cot, ffn_old = sync(upper_x, lower_y, first, cot, ffn_old)
        upper, lower = in_order(modality, upper, upper_x), in_order(y, lower, lower_y)
        attn_parts = [upper, flip(upper, CORE), lower, flip(lower, CORE)]
    else:
        attn_all = lax.all_gather(attn_blocks.astype(bf16), ("mod", "dp"), axis=0, tiled=True)
        attn_parts = [square_parts(attn_all, 4 * row_blocks, row_blocks).reshape(4, width, width)]
        ffn_all = lax.all_gather(ffn_blocks[0].astype(bf16), "dp", axis=0, tiled=True)
        shape = (2, row_blocks, row_blocks, chunks, size, size)
        up = ffn_all.reshape(shape)[0].transpose(0, 2, 3, 1, 4)
        down = ffn_all.reshape(2, row_blocks, chunks, row_blocks, size, size)[1]
        down = down.transpose(0, 1, 3, 2, 4)
        ffn_parts = jnp.stack([up, down]).reshape(2 * row_blocks, chunks, size, width)

    qkv, w_attn = project(rows_info, first, vec, attn_parts)
    ctx, lse, pair_ctx = attend(rows_info, qkv)
    pair_ctx = lax.ppermute(pair_ctx, "mod", to_text)
    stream_out, grad_middle, grad_ctx, pair_grad, grad_wo, grad_ffn, late_vec, up_bias_grad = expert(
        rows_info, ctx, pair_ctx, hidden, cot, vec, up_bias, w_attn, ffn_parts, order, slots
    )
    pair_grad = lax.ppermute(pair_grad, "mod", to_image)

    def along_z_of(parts):
        return [flip(part, bits * Z_LOW) for bits, part in enumerate(parts) if bits]

    if by_rows:
        ffn_sum = lax.psum_scatter(
            grad_ffn, "dp", scatter_dimension=0, tiled=True, axis_index_groups=[ring_order()]
        )[0]
    grad_qkv = attend_grad(rows_info, qkv, grad_ctx, pair_grad, ctx, lse)
    attn_keep, attn_send, grad_first, pair_first_grad, sums = project_grad(
        rows_info, grad_qkv, first, w_attn, grad_wo, size
    )
    pair_first_grad = lax.ppermute(pair_first_grad, "mod", to_text)
    up_bias_grad = jnp.swapaxes(up_bias_grad.reshape(chunks, row_blocks, size), 0, 1)
    if by_rows:
        attn_got = flip(attn_send, CORE)
        attn_got, pair_first_grad = sync(attn_got, pair_first_grad)
        both = plus(attn_keep, attn_got).reshape(2, 4, 2, size, width)
        upper, lower = both[..., : size // 2, :], both[..., size // 2 :, :]
        upper_keep, upper_send = pick(upper, modality, 0), pick(upper, 1 - modality, 0)
        lower_keep, lower_send = pick(lower, y, 2), pick(lower, 1 - y, 2)
        upper_keep, upper_send, lower_keep, lower_send, pair_first_grad = sync(
            upper_keep, upper_send, lower_keep, lower_send, pair_first_grad
        )
        upper_got, lower_got = flip_mod(upper_send), flip(lower_send, Y)
    stream_grad, small = first_grad(
        rows_info,
        grad_first,
        pair_first_grad,
        hidden,
        grad_middle,
        vec,
        sums,
        late_vec,
        up_bias_grad.reshape(chunks, width),
        pos,
        slots,
    )
    stream_out = stream_out.reshape(stream_in.shape)
    stream_grad = stream_grad.reshape(stream_in.shape)
    if by_rows:
        small = small.reshape(2, 2, 4, -1, width)
        small_keep, small_send = pick(small, core, 0), pick(small, 1 - core, 0)
        small_got = flip(small_send, CORE)
        upper_got, lower_got, small_got = sync(upper_got, lower_got, small_got)
        upper, lower = plus(upper_keep, upper_got), plus(lower_keep, lower_got)
        small = plus(small_keep, small_got)
        upper = jnp.concatenate([upper, jnp.swapaxes(small, 0, 1)], axis=2)
        upper_keep, upper_send = pick(upper, y, 1), pick(upper, 1 - y, 1)
        lower_keep, lower_send = pick(lower, modality, 0), pick(lower, 1 - modality, 0)
        upper_keep, upper_send, lower_keep, lower_send = sync(
            upper_keep, upper_send, lower_keep, lower_send
        )
        upper_got, lower_got = flip(upper_send, Y), flip_mod(lower_send)
        ffn_new = shampoo(is_up, 0, 1, [ffn_sum], *ffn_old, mebibytes=56)
        upper_got, lower_got, ffn_new = sync(upper_got, lower_got, ffn_new)
        upper, lower = plus(upper_keep, upper_got), plus(lower_keep, lower_got)
        half = size // 2
        attn = jnp.concatenate([upper[:, :half], lower, upper[:, half:]], axis=1)
        attn_z = [pick(attn, z ^ bits, 0) for bits in range(4)]
        attn_z, ffn_new = sync(attn_z, ffn_new)
        attn_got = along_z_of(attn_z)
        ffn_new = shampoo(is_up, 1, 3, [ffn_sum], *ffn_old, ffn_new)
        attn_got, ffn_new = sync(attn_got, ffn_new)
        small = sum(part[size:].astype(f32) for part in (attn_z[0], *attn_got))
        attn_rows = [part[None] for part in (attn_z[0], *attn_got)]
        small, attn_rows, ffn_new = sync(small, attn_rows, ffn_new)
        small_got = flip_mod(small)
        attn_old = [part[None] for part in (attn_left, attn_right, attn_blocks)]
        attn_out = shampoo(is_not, 0, 1, attn_rows, *attn_old, mebibytes=56)
        small_got, attn_out = sync(small_got, attn_out)
        small = (small + small_got).astype(bf16)
        small, ffn_new = sync(small, ffn_new)
        small_got = [flip(small, bits * Z_LOW) for bits in (1, 2, 3)]
        ffn_out = shampoo(is_up, 3, 4, [ffn_sum], *ffn_old, ffn_new)
        small_got, ffn_out = sync(small_got, ffn_out)
        near = in_order(z % 2, small, small_got[0])
        far = in_order(z % 2, small_got[1], small_got[2])
        small = in_order(z // 2, near, far)
        small = in_order(y, small, flip(small, Y))
        small_sum = in_order(core, small, flip(small, CORE)).reshape(-1, width)
    else:
        shape = (row_blocks, chunks, size, row_blocks, size)
        up, down = grad_ffn[:row_blocks].reshape(shape), grad_ffn[row_blocks:].reshape(shape)
        up = up.transpose(0, 3, 1, 2, 4).reshape(-1, size, size)
        down = down.transpose(0, 1, 3, 2, 4).reshape(-1, size, size)
        ffn_sum = lax.psum_scatter(
            jnp.concatenate([up, down], axis=0), "dp", scatter_dimension=0, tiled=True
        )
        attn_full = jnp.stack([attn_keep, attn_send], axis=2).reshape(-1, size, width)
        attn_sum = lax.psum_scatter(
            parts_to_blocks(attn_full), ("mod", "dp"), scatter_dimension=0, tiled=True
        )
        small_sum = lax.psum(small.astype(f32), ("mod", "dp")).astype(bf16)
        ffn_old = [part for part in (ffn_left, ffn_right, ffn_blocks)]
        attn_old = [part[None] for part in (attn_left, attn_right, attn_blocks)]
        ffn_out = shampoo(is_not, 0, 1, [square_parts(ffn_sum, 1, ffn_sum.shape[0])], *ffn_old)
        attn_out = shampoo(is_not, 0, 1, [square_parts(attn_sum, 1, attn_sum.shape[0])], *attn_old)

    items_total = lax.axis_size("dp")
    vector_rate = 0.3 / math.sqrt(items_total * slots)
    pos_rate = 0.5 / math.sqrt(items_total)
    vector_news = momentum_step(
        small_sum, vectors, vectors_mom, ffn_bias, ffn_bias_mom, pos_table, pos_mom, vector_rate, pos_rate
    )
    return (
        stream_out,
        stream_grad,
        *attn_out,
        *(part[None] for part in ffn_out),
        *vector_news,
    )


def solution(mesh):
    items = P("mod", "dp", None, None)
    owned = P(("mod", "dp"), None, None)
    return jax.shard_map(
        local,
        mesh=mesh,
        in_specs=(items, items, P("dp"), P("dp", None), owned, owned, owned, items, items, items)
        + (P(),) * 6,
        out_specs=(items, items, owned, owned, owned, owned, items, items, items, items)
        + (P(),) * 6,
        check_vma=False,
    )
```
